32 devices in a mesh: section: 2 (over y), fsdp: 16 (over z, x, core).
Axes of the slice: x: 2, y: 2, z: 4, core: 2. Of those that a mesh axis runs over, the one named last changes fastest.
Arguments:
- token_ids: int32 [2, 8192], P('section', 'fsdp'), may hold values from 0 to 49151
- scored: int32 [2, 32, 32], P('section', 'fsdp'), may hold values from 0 to 127
- targets: int32 [2, 32, 32], P('section'), may hold values from 0 to 49151
- pairs: int32 [64], replicated, may hold values from 0 to 63, each once
- table: float32 [49152, 960], P('fsdp')
- w_qkv: float32 [2, 960, 1600], P('section', 'fsdp'), may hold values from -0.1875 to 0.1875
- w_out: float32 [2, 960, 960], P('section', 'fsdp'), may hold values from -0.75 to 0.75
- w_gu: float32 [2, 960, 5120], P('section', 'fsdp'), may hold values from -0.1875 to 0.1875
- w_down: float32 [2, 2560, 960], P('section', 'fsdp'), may hold values from -0.125 to 0.125
- gains: float32 [2, 2, 960], P('section', None, 'fsdp'), may hold values from 0.5 to 1.5
- final_gain: float32 [960], P('fsdp'), may hold values from 0.5 to 1.5
- first_table: float32 [49152, 960], P('fsdp'), may hold values from -3.8146973e-05 to 3.8146973e-05
- first_qkv: float32 [2, 960, 1600], P('section', 'fsdp'), may hold values from -7.6293945e-05 to 7.6293945e-05
- first_out: float32 [2, 960, 960], P('section', 'fsdp'), may hold values from -7.6293945e-05 to 7.6293945e-05
- first_gu: float32 [2, 960, 5120], P('section', 'fsdp'), may hold values from -7.6293945e-05 to 7.6293945e-05
- first_down: float32 [2, 2560, 960], P('section', 'fsdp'), may hold values from -7.6293945e-05 to 7.6293945e-05
- first_gains: float32 [2, 2, 960], P('section', None, 'fsdp'), may hold values from -0.0008544922 to 0.0008544922
- first_final: float32 [960], P('fsdp'), may hold values from -0.0008544922 to 0.0008544922
- second_table: float32 [49152, 960], P('fsdp'), may hold values from 3.739631e-11 to 1.5108108e-10
- second_qkv: float32 [2, 960, 1600], P('section', 'fsdp'), may hold values from 1.5108108e-10 to 6.043243e-10
- second_out: float32 [2, 960, 960], P('section', 'fsdp'), may hold values from 1.5108108e-10 to 6.043243e-10
- second_gu: float32 [2, 960, 5120], P('section', 'fsdp'), may hold values from 1.5108108e-10 to 6.043243e-10
- second_down: float32 [2, 2560, 960], P('section', 'fsdp'), may hold values from 1.5108108e-10 to 6.043243e-10
- second_gains: float32 [2, 2, 960], P('section', None, 'fsdp'), may hold values from 1.5108109e-08 to 6.0432434e-08
- second_final: float32 [960], P('fsdp'), may hold values from 1.5108109e-08 to 6.0432434e-08
Outputs:
- loss: float32 [], replicated
- grad_norm: float32 [], replicated
- matrix_norms: float32 [2, 14], replicated
- new_table: float32 [49152, 960], P('fsdp')
- new_first_table: float32 [49152, 960], P('fsdp')
- new_second_table: float32 [49152, 960], P('fsdp')
- new_qkv: float32 [2, 960, 1600], P('section', 'fsdp')
- new_first_qkv: float32 [2, 960, 1600], P('section', 'fsdp')
- new_second_qkv: float32 [2, 960, 1600], P('section', 'fsdp')
- new_out: float32 [2, 960, 960], P('section', 'fsdp')
- new_first_out: float32 [2, 960, 960], P('section', 'fsdp')
- new_second_out: float32 [2, 960, 960], P('section', 'fsdp')
- new_gu: float32 [2, 960, 5120], P('section', 'fsdp')
- new_first_gu: float32 [2, 960, 5120], P('section', 'fsdp')
- new_second_gu: float32 [2, 960, 5120], P('section', 'fsdp')
- new_down: float32 [2, 2560, 960], P('section', 'fsdp')
- new_first_down: float32 [2, 2560, 960], P('section', 'fsdp')
- new_second_down: float32 [2, 2560, 960], P('section', 'fsdp')
- new_gains: float32 [2, 2, 960], P('section', None, 'fsdp')
- new_first_gains: float32 [2, 2, 960], P('section', None, 'fsdp')
- new_second_gains: float32 [2, 2, 960], P('section', None, 'fsdp')
- new_final: float32 [960], P('fsdp')
- new_first_final: float32 [960], P('fsdp')
- new_second_final: float32 [960], P('fsdp')
- table_half: bfloat16 [49152, 960], P('fsdp')
- qkv_half: bfloat16 [2, 960, 1600], P('section', 'fsdp')
- out_half: bfloat16 [2, 960, 960], P('section', 'fsdp')
- gu_half: bfloat16 [2, 960, 5120], P('section', 'fsdp')
- down_half: bfloat16 [2, 2560, 960], P('section', 'fsdp')
The draws below stay inside these ranges and needn't reach their ends.
Inputs may be any that keep to these rules, and one draw needn't show every extreme that they name: `pairs`: each continuation appears once.
All inputs are finite; a program needn't handle non-finite values.
Results may differ from the reference program's by a relative error of at most 0.022.
Values may be sent and summed in bfloat16 or wider, within the bound.
A program may use at most 896 MiB of HBM per device.

```python
import math
import jax
import jax.numpy as jnp
import numpy as np
from jax import lax

D = 960
HEADS = 15
KV = 5
HD = 64
FF = 2560
VOCAB = 49152
PROMPT = 256
NCONT = 2
CONT = 128
SCORED = 32
STEP = 10
MICRO = 2
TOK_MB = 512
CONTS = 64
N_SECTION = 2
N_FSDP = 16


def draw_table(key, part):
    key = jax.random.fold_in(key, 7)
    place = jnp.arange(VOCAB).astype(jnp.float32)[:, None] / VOCAB
    base = jax.random.normal(key, (VOCAB, D), jnp.float32)
    rise = 1.0 + 2.0 * place
    return base * rise * D ** (-0.5)


def plant(values, stream_key, low, top_value):
    longest = values.shape.index(max(values.shape))
    spots = []
    for shift in (0, 1):
        where = [jax.random.randint(jax.random.fold_in(stream_key, axis), (), 0, length) for axis, length in enumerate(values.shape)]
        where[longest] = (where[longest] + shift) % values.shape[longest]
        spots.append(tuple(where))
    return values.at[spots[0]].set(low).at[spots[1]].set(top_value)


def block_levels(own_key, dims, split, smallest, largest):
    def one(dim, shards_of):
        steps = jax.random.uniform(jax.random.fold_in(jax.random.fold_in(own_key, 6), dim), (shards_of,), jnp.float32, smallest / len(split), largest / len(split))
        return jnp.repeat(jnp.exp(steps), dims[dim] // shards_of).reshape((-1,) + (1,) * (len(dims) - dim - 1))

    gain = one(*split[0])
    for cut in split[1:]:
        gain = gain * one(*cut)
    return gain


def cumulative_ranks(count, skew):
    weights = [(1 << 20) // math.isqrt(standing ** skew) + 1 for standing in range(1, count + 1)]
    scale = 1 + sum(weights) // (1 << 30)
    return np.cumsum(np.array([max(1, weight // scale) for weight in weights]))


def skewed_ids(rng, extent, count, skew):
    grid = cumulative_ranks(count, skew)
    ticket = jax.random.randint(jax.random.fold_in(rng, 1), extent, 0, int(grid[count - 1]))
    standing = jnp.searchsorted(jnp.asarray(grid, jnp.int32), ticket, side="right")
    return jax.random.permutation(jax.random.fold_in(rng, 2), count)[standing].astype(jnp.int32)


def scatter_about(rng, extent, scale, most, shards=(), held_as=jnp.bfloat16):
    entries = jax.random.normal(rng, extent, jnp.float32) * scale
    if len(shards) > 0:
        entries = block_levels(rng, extent, shards, -0.22, 0.18) * entries
    return jnp.clip(entries, min=-most, max=most).astype(held_as)


def setup_inputs(seed: int = 0) -> dict:
    splits = jax.random.split(jax.random.key(seed), 26)
    token_ids = plant(skewed_ids(splits[0], (MICRO, N_FSDP * TOK_MB), VOCAB, 2), jax.random.fold_in(splits[0], 3), 0, VOCAB - 1).astype(jnp.int32)
    scored = plant(jax.random.randint(splits[1], (MICRO, N_FSDP * NCONT, SCORED), 0, CONT), jax.random.fold_in(splits[1], 1), 0, CONT - 1).astype(jnp.int32)
    targets = plant(skewed_ids(splits[2], (MICRO, N_FSDP * NCONT, SCORED), VOCAB, 2), jax.random.fold_in(splits[2], 3), 0, VOCAB - 1).astype(jnp.int32)
    pairs = jax.random.permutation(splits[3], CONTS).astype(jnp.int32)
    table = draw_table(jax.random.fold_in(splits[25], 71), 0)
    w_qkv = scatter_about(splits[5], (N_SECTION, D, HEADS * HD + 2 * KV * HD), D ** -0.5, 0.1875, ((0, 2), (1, 16)), jnp.float32)
    w_out = scatter_about(splits[6], (N_SECTION, HEADS * HD, D), (D // 16) ** -0.5, 0.75, ((0, 2), (1, 16)), jnp.float32)
    w_gu = scatter_about(splits[7], (N_SECTION, D, 2 * FF), D ** -0.5, 0.1875, ((0, 2), (1, 16)), jnp.float32)
    w_down = scatter_about(splits[8], (N_SECTION, FF, D), FF ** -0.5, 0.125, ((0, 2), (1, 16)), jnp.float32)
    gains = jnp.clip(1.0 + 0.1 * jax.random.normal(splits[9], (N_SECTION, 2, D), jnp.float32), 0.5, 1.5)
    final_gain = jnp.clip(1.0 + 0.1 * jax.random.normal(splits[10], (D,), jnp.float32), 0.5, 1.5)
    first_table = scatter_about(splits[11], (VOCAB, D), (0.055 * (VOCAB * D + N_SECTION * (D * (2 * HEADS * HD + 2 * KV * HD + 3 * FF) + 2 * D) + D) ** -0.5), 3.814697265625e-05, ((0, 16),), jnp.float32)
    first_qkv = scatter_about(splits[12], (N_SECTION, D, HEADS * HD + 2 * KV * HD), (0.111 * (VOCAB * D + N_SECTION * (D * (2 * HEADS * HD + 2 * KV * HD + 3 * FF) + 2 * D) + D) ** -0.5), 7.62939453125e-05, ((0, 2), (1, 16)), jnp.float32)
    first_out = scatter_about(splits[13], (N_SECTION, HEADS * HD, D), (0.111 * (VOCAB * D + N_SECTION * (D * (2 * HEADS * HD + 2 * KV * HD + 3 * FF) + 2 * D) + D) ** -0.5), 7.62939453125e-05, ((0, 2), (1, 16)), jnp.float32)
    first_gu = scatter_about(splits[14], (N_SECTION, D, 2 * FF), (0.111 * (VOCAB * D + N_SECTION * (D * (2 * HEADS * HD + 2 * KV * HD + 3 * FF) + 2 * D) + D) ** -0.5), 7.62939453125e-05, ((0, 2), (1, 16)), jnp.float32)
    first_down = scatter_about(splits[15], (N_SECTION, FF, D), (0.111 * (VOCAB * D + N_SECTION * (D * (2 * HEADS * HD + 2 * KV * HD + 3 * FF) + 2 * D) + D) ** -0.5), 7.62939453125e-05, ((0, 2), (1, 16)), jnp.float32)
    first_gains = scatter_about(splits[16], (N_SECTION, 2, D), (1.11 * (VOCAB * D + N_SECTION * (D * (2 * HEADS * HD + 2 * KV * HD + 3 * FF) + 2 * D) + D) ** -0.5), 0.0008544922, ((0, 2), (2, 16)), jnp.float32)
    first_final = scatter_about(splits[17], (D,), (1.11 * (VOCAB * D + N_SECTION * (D * (2 * HEADS * HD + 2 * KV * HD + 3 * FF) + 2 * D) + D) ** -0.5), 0.0008544922, ((0, 16),), jnp.float32)
    second_table = jnp.clip(jnp.exp(math.log(1.510810782034966e-10) - 1.3962446 * jax.random.uniform(splits[18], (VOCAB, D), jnp.float32) ** block_levels(splits[18], (VOCAB, D), ((0, 16),), -0.2, 0.2)), 3.739630827226392e-11, 1.510810782034966e-10)
    second_qkv = jnp.clip(jnp.exp(math.log(6.043243128139864e-10) - 1.3862944 * jax.random.uniform(splits[19], (N_SECTION, D, HEADS * HD + 2 * KV * HD), jnp.float32) ** block_levels(splits[19], (N_SECTION, D, HEADS * HD + 2 * KV * HD), ((0, 2), (1, 16)), -0.2, 0.2)), 1.510810782034966e-10, 6.043243128139864e-10)
    second_out = jnp.clip(jnp.exp(math.log(6.043243128139864e-10) - 1.3862944 * jax.random.uniform(splits[20], (N_SECTION, HEADS * HD, D), jnp.float32) ** block_levels(splits[20], (N_SECTION, HEADS * HD, D), ((0, 2), (1, 16)), -0.2, 0.2)), 1.510810782034966e-10, 6.043243128139864e-10)
    second_gu = jnp.clip(jnp.exp(math.log(6.043243128139864e-10) - 1.3862944 * jax.random.uniform(splits[21], (N_SECTION, D, 2 * FF), jnp.float32) ** block_levels(splits[21], (N_SECTION, D, 2 * FF), ((0, 2), (1, 16)), -0.2, 0.2)), 1.510810782034966e-10, 6.043243128139864e-10)
    second_down = jnp.clip(jnp.exp(math.log(6.043243128139864e-10) - 1.3862944 * jax.random.uniform(splits[22], (N_SECTION, FF, D), jnp.float32) ** block_levels(splits[22], (N_SECTION, FF, D), ((0, 2), (1, 16)), -0.2, 0.2)), 1.510810782034966e-10, 6.043243128139864e-10)
    second_gains = jnp.clip(jnp.exp(math.log(6.04324341679785e-08) - 1.3862944 * jax.random.uniform(splits[23], (N_SECTION, 2, D), jnp.float32) ** block_levels(splits[23], (N_SECTION, 2, D), ((0, 2), (2, 16)), -0.2, 0.2)), 1.5108108541994625e-08, 6.04324341679785e-08)
    second_final = jnp.clip(jnp.exp(math.log(6.04324341679785e-08) - 1.3862944 * jax.random.uniform(splits[24], (D,), jnp.float32) ** block_levels(splits[24], (D,), ((0, 16),), -0.2, 0.2)), 1.5108108541994625e-08, 6.04324341679785e-08)
    return dict(token_ids=token_ids, scored=scored, targets=targets, pairs=pairs, table=table, w_qkv=w_qkv, w_out=w_out, w_gu=w_gu, w_down=w_down, gains=gains, final_gain=final_gain, first_table=first_table, first_qkv=first_qkv, first_out=first_out, first_gu=first_gu, first_down=first_down, first_gains=first_gains, first_final=first_final, second_table=second_table, second_qkv=second_qkv, second_out=second_out, second_gu=second_gu, second_down=second_down, second_gains=second_gains, second_final=second_final)


EPS = 1e-05
SCALE = 0.125
THETA = 100000.0
BETA = 0.1
CLIP = 1.0
RATE = 0.3
BETA_ONE = 0.9
BETA_TWO = 0.99
ADAM_EPS = 1e-08
DECAY = 0.01
HI = lax.Precision.HIGHEST

@jax.custom_vjp
def low(v):
    return lax.optimization_barrier(v.astype(jnp.bfloat16)).astype(jnp.float32)

@jax.custom_vjp
def low_back(v):
    return v

def low_keep(v):
    return (low(v), None)

def low_pass(kept, grad):
    return (grad,)

def back_keep(v):
    return (v, None)

def back_low(kept, grad):
    return (low(grad),)
low.defvjp(low_keep, low_pass)
low_back.defvjp(back_keep, back_low)

def normed(x):
    return x * lax.rsqrt(lax.optimization_barrier(jnp.mean(x * x, axis=-1, keepdims=True)) + EPS)

def rotate(x, cosine, sine):
    half = x.shape[-1] // 2
    first, second = (x[..., :half], x[..., half:])
    return jnp.concatenate([first * cosine - second * sine, second * cosine + first * sine], axis=-1)

def layer_tables():
    place = jnp.arange(TOK_MB)
    segment = jnp.where(place >= PROMPT, 1 + (place - PROMPT) // CONT, 0)
    rotary = jnp.where(place >= PROMPT, PROMPT + (place - PROMPT) % CONT, place).astype(jnp.float32)
    freq = THETA ** (-2.0 * jnp.arange(HD // 2).astype(jnp.float32) / HD)
    angle = rotary[:, None] * freq[None, :]
    allowed = (place[None, :] <= place[:, None]) & ((segment[None, :] == 0) | (segment[None, :] == segment[:, None]))
    return (jnp.cos(angle)[:, None, :], jnp.sin(angle)[:, None, :], allowed)

def layer(x, w_qkv, w_out, w_gu, w_down, gains, cosine, sine, allowed):
    width = HEADS * HD
    kv_width = KV * HD
    a = low(normed(x) * gains[0])
    qkv = low_back(jnp.dot(a, w_qkv, precision=HI))
    query = low(rotate(qkv[:, :width].reshape(-1, HEADS, HD), cosine, sine)).reshape(-1, KV, HEADS // KV, HD)
    key = low(rotate(qkv[:, width:width + kv_width].reshape(-1, KV, HD), cosine, sine))
    value = low(qkv[:, width + kv_width:].reshape(-1, KV, HD))
    scores = low_back(jnp.einsum('qhgd,khd->hgqk', query, key, precision=HI) * SCALE)
    scores = jnp.where(allowed, scores, -1e+30)
    expo = jnp.exp(scores - lax.optimization_barrier(jnp.max(scores, axis=-1, keepdims=True)))
    probs = low(expo / lax.optimization_barrier(jnp.sum(expo, axis=-1, keepdims=True)))
    attended = jnp.einsum('hgqk,khd->qhgd', probs, value, precision=HI).reshape(-1, width)
    attended = low_back(low(attended))
    mixed = x + low_back(jnp.dot(attended, w_out, precision=HI))
    b = low(normed(mixed) * gains[1])
    gate_up = low_back(jnp.dot(b, w_gu, precision=HI))
    hidden = low(jax.nn.silu(gate_up[:, :FF]) * gate_up[:, FF:])
    return mixed + low_back(jnp.dot(hidden, w_down, precision=HI))

def group_rows(weights, ids, scored, cosine, sine, allowed):
    table, w_qkv, w_out, w_gu, w_down, gains, final_gain = weights
    x = table[ids]
    for section_index in range(N_SECTION):
        x = layer(x, w_qkv[section_index], w_out[section_index], w_gu[section_index], w_down[section_index], gains[section_index], cosine, sine, allowed)
    z = low(normed(x) * final_gain)
    rows = PROMPT + CONT * jnp.arange(NCONT)[:, None] + scored
    return z[rows.reshape(-1)]

def total_loss(weights32, token_ids, scored, targets, pairs):
    weights = tuple((low(w) for w in weights32))
    cosine, sine, allowed = layer_tables()

    def one_group(args):
        return group_rows(weights, args[0], args[1], cosine, sine, allowed)
    rows = lax.map(jax.checkpoint(one_group), (token_ids.reshape(-1, TOK_MB), scored.reshape(-1, NCONT, SCORED)))
    rows = rows.reshape(-1, D)
    block = min(512, rows.shape[0])
    table = weights[0]

    def one_block(args):
        part, wanted = args
        logits = low_back(jnp.dot(part, table.T, precision=HI))
        top = lax.optimization_barrier(jnp.max(logits, axis=-1, keepdims=True))
        total = top[:, 0] + jnp.log(lax.optimization_barrier(jnp.sum(jnp.exp(logits - top), axis=-1)))
        picked = jnp.take_along_axis(logits, wanted[:, None], axis=1)[:, 0]
        return picked - total
    logp = lax.map(jax.checkpoint(one_block), (rows.reshape(-1, block, D), targets.reshape(-1, block)))
    seq = lax.optimization_barrier(jnp.sum(logp.reshape(-1, SCORED), axis=1))
    pair = pairs.reshape(-1, 2)
    delta = seq[pair[:, 0]] - seq[pair[:, 1]]
    return jnp.sum(jax.nn.softplus(-BETA * delta))

def slot_norms(arrays):
    table, w_qkv, w_out, w_gu, w_down, gains, final_gain = arrays
    rows_each_section = jnp.stack([lax.optimization_barrier(jnp.sum(w_qkv ** 2, axis=(1, 2))), lax.optimization_barrier(jnp.sum(w_out ** 2, axis=(1, 2))), lax.optimization_barrier(jnp.sum(w_gu ** 2, axis=(1, 2))), lax.optimization_barrier(jnp.sum(w_down ** 2, axis=(1, 2))), lax.optimization_barrier(jnp.sum(gains[:, 0] ** 2, axis=1)), lax.optimization_barrier(jnp.sum(gains[:, 1] ** 2, axis=1))], axis=1)
    common_prompt = jnp.stack([jnp.sum(table ** 2), jnp.sum(final_gain ** 2)])
    return jnp.sqrt(jnp.concatenate([rows_each_section.reshape(-1), common_prompt]))

def spread(scale):
    rows_each_section = scale[:6 * N_SECTION].reshape(N_SECTION, 6)
    return (scale[6 * N_SECTION], rows_each_section[:, 0][:, None, None], rows_each_section[:, 1][:, None, None], rows_each_section[:, 2][:, None, None], rows_each_section[:, 3][:, None, None], rows_each_section[:, 4:6][:, :, None], scale[6 * N_SECTION + 1])

def lamb_parts(weight, grad, first, second, decay):
    first_new = BETA_ONE * first + (1.0 - BETA_ONE) * grad
    second_new = BETA_TWO * second + (1.0 - BETA_TWO) * grad * grad
    update = first_new / (1.0 - BETA_ONE ** STEP) / (jnp.sqrt(second_new / (1.0 - BETA_TWO ** STEP)) + ADAM_EPS) + decay * weight
    return (first_new, second_new, update)

def reference(token_ids, scored, targets, pairs, table, w_qkv, w_out, w_gu, w_down, gains, final_gain, first_table, first_qkv, first_out, first_gu, first_down, first_gains, first_final, second_table, second_qkv, second_out, second_gu, second_down, second_gains, second_final):
    weights = (table, w_qkv, w_out, w_gu, w_down, gains, final_gain)
    firsts = (first_table, first_qkv, first_out, first_gu, first_down, first_gains, first_final)
    seconds = (second_table, second_qkv, second_out, second_gu, second_down, second_gains, second_final)
    loss, pull = jax.vjp(lambda *w: total_loss(w, token_ids, scored, targets, pairs), *weights)
    grads = pull(jnp.ones_like(loss))
    grad_norm = jnp.sqrt(sum((jnp.sum(g * g) for g in grads)))
    clip = jnp.minimum(1.0, CLIP / grad_norm)
    decays = (DECAY, DECAY, DECAY, DECAY, DECAY, 0.0, 0.0)
    parts = [lamb_parts(w, clip * g, m, v, d) for w, g, m, v, d in zip(weights, grads, firsts, seconds, decays)]
    updates = tuple((p[2] for p in parts))
    weight_norms = slot_norms(weights)
    update_norms = slot_norms(updates)
    trust_ratio = spread(weight_norms / update_norms)
    new = [w - RATE * t * u for w, t, u in zip(weights, trust_ratio, updates)]
    matrix_norms = jnp.stack([weight_norms, update_norms])
    return (loss, grad_norm, matrix_norms, new[0], parts[0][0], parts[0][1], new[1], parts[1][0], parts[1][1], new[2], parts[2][0], parts[2][1], new[3], parts[3][0], parts[3][1], new[4], parts[4][0], parts[4][1], new[5], parts[5][0], parts[5][1], new[6], parts[6][0], parts[6][1], new[0].astype(jnp.bfloat16), new[1].astype(jnp.bfloat16), new[2].astype(jnp.bfloat16), new[3].astype(jnp.bfloat16), new[4].astype(jnp.bfloat16))
```

```python
import jax
import jax.numpy as jnp
from jax import lax
from jax.sharding import PartitionSpec as P

HEADS = 15
KV = 5
HD = 64
FF = 2560
PROMPT = 256
NCONT = 2
CONT = 128
SCORED = 32
STEP = 10
TOK_MB = 512

EPS = 1e-05
SCALE = 0.125
THETA = 100000.0
BETA = 0.1
CLIP = 1.0
RATE = 0.3
BETA_ONE = 0.9
BETA_TWO = 0.99
ADAM_EPS = 1e-08
DECAY = 0.01

WIDTH = HEADS * HD
KVW = KV * HD
BOTH = ("section", "fsdp")
HI = lax.Precision.HIGHEST
LOW = jnp.bfloat16


def up16(count):
    return -(-count // 16) * 16


def dense(left, right):
    return jnp.dot(left, right, preferred_element_type=jnp.float32)


def dense_t(left, right):
    return lax.dot_general(
        left, right, (((0,), (0,)), ((), ())), preferred_element_type=jnp.float32
    )


def dense_nt(left, right):
    return lax.dot_general(
        left, right, (((1,), (1,)), ((), ())), preferred_element_type=jnp.float32
    )


def spread_matrix(parts, real, padded):
    feature = jnp.arange(parts * real)
    place = feature // real * padded + feature % real
    return (place[:, None] == jnp.arange(parts * padded)[None, :]).astype(LOW)


def inverse_rms(x, width):
    return lax.rsqrt(jnp.sum(x * x, axis=-1, keepdims=True) / width + EPS)


def norm_back(x, scale, gain, upstream, width):
    inner = upstream * gain
    grad_gain = jnp.sum(upstream * x * scale, axis=0)
    mean = jnp.sum(inner * x, axis=-1, keepdims=True) / width
    return (scale * inner - x * scale**3 * mean, grad_gain)


def rotate(x, cosine, sine):
    half = x.shape[-1] // 2
    first, second = (x[..., :half], x[..., half:])
    return jnp.concatenate(
        [first * cosine - second * sine, second * cosine + first * sine], axis=-1
    )


def rotate_back(grad, cosine, sine):
    return rotate(grad, cosine, -sine)


def rotary_angles(place):
    rotary = jnp.where(place >= PROMPT, PROMPT + (place - PROMPT) % CONT, place).astype(jnp.float32)
    freq = THETA ** (-2.0 * jnp.arange(HD // 2).astype(jnp.float32) / HD)
    angle = rotary[:, None] * freq[None, :]
    return (jnp.cos(angle)[:, None, :], jnp.sin(angle)[:, None, :])


def may_attend(place):
    keys = jnp.arange(TOK_MB)

    def segment(p):
        return jnp.where(p >= PROMPT, 1 + (p - PROMPT) // CONT, 0)

    return (keys[None, :] <= place[:, None]) & (
        (segment(keys)[None, :] == 0) | (segment(keys)[None, :] == segment(place)[:, None])
    )


def attend(query, key, value, allowed):
    scores = jnp.einsum("qhgd,khd->hgqk", query, key, preferred_element_type=jnp.float32) * SCALE
    scores = jnp.where(allowed, scores, -1e30)
    expo = jnp.exp(scores - jnp.max(scores, axis=-1, keepdims=True))
    probs = expo / jnp.sum(expo, axis=-1, keepdims=True)
    out = jnp.einsum("hgqk,khd->qhgd", probs.astype(LOW), value, preferred_element_type=jnp.float32)
    return (out.reshape(-1, WIDTH).astype(LOW), probs)


def attend_back(query, key, value, probs, grad):
    grad = grad.reshape(-1, KV, HEADS // KV, HD)
    grad_probs = jnp.einsum("qhgd,khd->hgqk", grad, value, preferred_element_type=jnp.float32)
    grad_scores = probs * (grad_probs - jnp.sum(grad_probs * probs, axis=-1, keepdims=True))
    grad_scores = grad_scores.astype(LOW)
    grad_query = (
        jnp.einsum("hgqk,khd->qhgd", grad_scores, key, preferred_element_type=jnp.float32) * SCALE
    )
    grad_key = (
        jnp.einsum("hgqk,qhgd->khd", grad_scores, query, preferred_element_type=jnp.float32) * SCALE
    )
    grad_value = jnp.einsum(
        "hgqk,qhgd->khd", probs.astype(LOW), grad, preferred_element_type=jnp.float32
    )
    return (grad_query.reshape(-1, HEADS, HD), grad_key, grad_value)


def heads_of(q, cosine, sine):
    return (
        rotate(q.reshape(-1, HEADS, HD), cosine, sine).astype(LOW).reshape(-1, KV, HEADS // KV, HD)
    )


def keys_values(kv, cosine, sine):
    key = rotate(kv[:, :KVW].reshape(-1, KV, HD), cosine, sine).astype(LOW)
    return (key, kv[:, KVW:].reshape(-1, KV, HD).astype(LOW))


def mlp(b, w_gu, w_down):
    gate_up = dense(b, w_gu)
    half = gate_up.shape[1] // 2
    gate, upper = (gate_up[:, :half], gate_up[:, half:])
    hidden = (jax.nn.silu(gate) * upper).astype(LOW)
    return (dense(hidden, w_down), gate, upper, hidden)


def mlp_back(branch, b, gate, upper, hidden, w_gu, w_down):
    grad_down = dense_t(hidden, branch)
    grad_hidden = dense_nt(branch, w_down)
    sig = jax.nn.sigmoid(gate)
    grad_gate = grad_hidden * upper * sig * (1.0 + gate * (1.0 - sig))
    grad_upper = grad_hidden * gate * sig
    grad_gate_up = jnp.concatenate([grad_gate, grad_upper], axis=1).astype(LOW)
    return (grad_down, dense_t(b, grad_gate_up), dense_nt(grad_gate_up, w_gu))


def lamb_parts(weight, grad, first, second, decay):
    first_new = BETA_ONE * first + (1.0 - BETA_ONE) * grad
    second_new = BETA_TWO * second + (1.0 - BETA_TWO) * grad * grad
    update = (
        first_new
        / (1.0 - BETA_ONE**STEP)
        / (jnp.sqrt(second_new / (1.0 - BETA_TWO**STEP)) + ADAM_EPS)
        + decay * weight
    )
    return (first_new, second_new, update)


def lookup_ranks(ids, vshard):
    place = jnp.arange(ids.shape[0])
    same = ids[:, None] == ids[None, :]
    first = jnp.min(jnp.where(same, place[None, :], ids.shape[0]), axis=1)
    owner = ids // vshard
    before = (
        (owner[:, None] == owner[None, :])
        & (first == place)[None, :]
        & (place[None, :] < first[:, None])
    )
    return (owner, jnp.sum(before.astype(jnp.int32), axis=1))


def lookup_round(ids, owner, rank, turn, slots, parts, vshard):
    slot = jnp.where(rank // slots == turn, owner * slots + rank - turn * slots, -1)
    onehot = slot[:, None] == jnp.arange(parts * slots)[None, :]
    wanted = jnp.max(jnp.where(onehot, (ids - owner * vshard)[:, None], -1), axis=0)
    return (onehot.astype(LOW), wanted)


def shards(
    token_ids,
    scored,
    targets,
    pairs,
    table,
    w_qkv,
    w_out,
    w_gu,
    w_down,
    gains,
    final_gain,
    first_table,
    first_qkv,
    first_out,
    first_gu,
    first_down,
    first_gains,
    first_final,
    second_table,
    second_qkv,
    second_out,
    second_gu,
    second_down,
    second_gains,
    second_final,
):
    n = lax.axis_size("fsdp")
    sections = lax.axis_size("section")
    section_index = lax.axis_index("section")
    fsdp_index = lax.axis_index("fsdp")
    leader = section_index == 0
    vshard, width = table.shape
    vstart = fsdp_index * vshard
    r = w_qkv.shape[1]
    rp = up16(r)
    rd = w_down.shape[1]
    rdp = up16(rd)
    wide = n * rp
    ffp = n * rdp
    slots = up16(768 // n)
    sel = spread_matrix(n, r, rp)

    qkv_block = jnp.pad(w_qkv[0].astype(LOW), ((0, rp - r), (0, 0)))
    out_block = jnp.pad(dense(w_out[0].astype(LOW), sel).astype(LOW), ((0, rp - r), (0, 0)))
    gu_block = w_gu[0].astype(LOW)
    if rdp != rd:
        gu_block = jnp.pad(gu_block.reshape(r, 2, n, rd), ((0, 0), (0, 0), (0, 0), (0, rdp - rd)))
    gu_block = jnp.pad(gu_block.reshape(r, 2 * ffp), ((0, rp - r), (0, 0)))
    down_block = jnp.pad(dense(w_down[0].astype(LOW), sel).astype(LOW), ((0, rdp - rd), (0, 0)))
    gain_block = jnp.pad(
        jnp.concatenate([gains[0], final_gain[None]], axis=0).astype(LOW), ((0, 0), (0, rp - r))
    )

    ids = token_ids[0]
    owner, rank = lookup_ranks(ids, vshard)
    onehot, wanted = lookup_round(ids, owner, rank, 0, slots, n, vshard)
    note = jnp.concatenate([wanted, jnp.full((128,), jnp.max(rank) // slots + 1, jnp.int32)])
    notes = lax.all_gather(note, BOTH, axis=0)
    turns = jnp.max(notes[:, n * slots])

    def asked(all_wanted):
        mine = lax.dynamic_slice_in_dim(all_wanted.reshape(sections, n, n, slots), fsdp_index, 1, 2)
        return mine[:, :, 0]

    def fetch(all_asked, choose):
        here = lax.dynamic_index_in_dim(all_asked, section_index, 0, keepdims=False).reshape(-1)
        rows = jnp.take(table, jnp.maximum(here, 0), axis=0).astype(LOW)
        got = lax.all_to_all(rows.reshape(n, slots, width), "fsdp", 0, 0).reshape(n * slots, width)
        return dense(dense(choose, got).astype(LOW), sel)

    asked_first = asked(notes[:, : n * slots])
    x0 = fetch(asked_first, onehot)

    def fetch_more(state):
        turn, total = state
        choose, more = lookup_round(ids, owner, rank, turn, slots, n, vshard)
        return (turn + 1, total + fetch(asked(lax.all_gather(more, BOTH, axis=0)), choose))

    x0 = lax.while_loop(lambda state: state[0] < turns, fetch_more, (jnp.int32(1), x0))[1]

    def everywhere(block):
        return lax.all_gather(block, BOTH, axis=0, tiled=True).reshape(
            sections, n * block.shape[0], block.shape[1]
        )

    qkv_all = everywhere(qkv_block)
    out_all = everywhere(out_block)
    gu_all = everywhere(gu_block)
    down_all = everywhere(down_block)
    gain_all = lax.all_gather(gain_block, BOTH, axis=0).reshape(sections, n, 3, rp)
    gain_all = jnp.moveaxis(gain_all, 2, 1).reshape(sections, 3, wide).astype(jnp.float32)
    final_all = gain_all[0, 2]
    wanted_rows = lax.all_gather(targets[0].reshape(-1), "section", axis=0, tiled=True)

    everyone = jnp.arange(TOK_MB)
    cosine, sine = rotary_angles(everyone)
    allowed = may_attend(everyone)
    x = x0
    kept = []
    for layer in range(sections - 1):
        scale_a = inverse_rms(x, width)
        a = (x * scale_a * gain_all[layer, 0]).astype(LOW)
        qkv = dense(a, qkv_all[layer])
        query = heads_of(qkv[:, :WIDTH], cosine, sine)
        key, value = keys_values(qkv[:, WIDTH:], cosine, sine)
        attended, probs = attend(query, key, value, allowed)
        attended = dense(attended, sel).astype(LOW)
        mixed = x + dense(attended, out_all[layer])
        scale_b = inverse_rms(mixed, width)
        b = (mixed * scale_b * gain_all[layer, 1]).astype(LOW)
        branch, gate, upper, hidden = mlp(b, gu_all[layer], down_all[layer])
        kept.append(
            (x, scale_a, a, query, key, value, probs, attended, mixed, scale_b, b, gate, upper, hidden)
        )
        x = mixed + branch

    last = sections - 1
    place = (PROMPT + CONT * jnp.arange(NCONT)[:, None] + scored[0]).reshape(-1)
    pick = (place[:, None] == everyone[None, :]).astype(LOW)
    pick32 = pick.astype(jnp.float32)
    cosine_s, sine_s = rotary_angles(place)
    allowed_s = may_attend(place)
    scale_last = inverse_rms(x, width)
    a_last = (x * scale_last * gain_all[last, 0]).astype(LOW)
    key_last, value_last = keys_values(dense(a_last, qkv_all[last][:, WIDTH:]), cosine, sine)
    a_s = dense(pick, a_last).astype(LOW)
    x_s = jnp.dot(pick32, x, precision=HI)
    query_s = heads_of(dense(a_s, qkv_all[last][:, :WIDTH]), cosine_s, sine_s)
    attended_s, probs_s = attend(query_s, key_last, value_last, allowed_s)
    attended_s = dense(attended_s, sel).astype(LOW)
    mixed_s = x_s + dense(attended_s, out_all[last])
    scale_s = inverse_rms(mixed_s, width)
    b_s = (mixed_s * scale_s * gain_all[last, 1]).astype(LOW)
    branch_s, gate_s, upper_s, hidden_s = mlp(b_s, gu_all[last], down_all[last])
    y_s = mixed_s + branch_s
    scale_y = inverse_rms(y_s, width)
    head_in = dense_nt((y_s * scale_y * final_all).astype(LOW), sel).astype(LOW)

    rows_all = lax.all_gather(head_in, BOTH, axis=0, tiled=True)
    own_rows = rows_all.shape[0] // sections
    table_low = table.astype(LOW)
    logits = dense_nt(rows_all, table_low)
    hit = jnp.arange(vshard)[None, :] == (wanted_rows - vstart)[:, None]
    top_here = jnp.max(logits, axis=1)
    total_here = jnp.sum(jnp.exp(logits - top_here[:, None]), axis=1)
    target_here = jnp.sum(jnp.where(hit, logits, 0.0), axis=1)
    stats = lax.all_gather(jnp.stack([top_here, total_here, target_here]), "fsdp", axis=0)
    top = jnp.max(stats[:, 0], axis=0)
    total = jnp.sum(stats[:, 1] * jnp.exp(stats[:, 0] - top), axis=0)
    row_logp = jnp.sum(stats[:, 2], axis=0) - top - jnp.log(total)
    seq = jnp.sum(row_logp.reshape(-1, SCORED), axis=1)
    pair = pairs.reshape(-1, 2)
    conts = jnp.arange(seq.shape[0])
    chosen = (pair[:, 0][:, None] == conts[None, :]).astype(jnp.float32)
    passed = (pair[:, 1][:, None] == conts[None, :]).astype(jnp.float32)
    delta = jnp.sum((chosen - passed) * seq[None, :], axis=1)
    loss = jnp.sum(jax.nn.softplus(-BETA * delta))
    push = BETA * jax.nn.sigmoid(-BETA * delta)
    grad_seq = jnp.sum((passed - chosen) * push[:, None], axis=0)
    grad_row = jnp.repeat(grad_seq, SCORED)
    prob = jnp.exp(logits - top[:, None]) * (1.0 / total)[:, None]
    grad_logits = (grad_row[:, None] * (hit.astype(jnp.float32) - prob)).astype(LOW)
    grad_table = dense_t(grad_logits, rows_all)
    own_grads = lax.dynamic_slice_in_dim(grad_logits, section_index * own_rows, own_rows)
    grad_head = lax.psum_scatter(
        dense(own_grads, table_low).astype(LOW), "fsdp", scatter_dimension=0, tiled=True
    )
    grad_y, grad_final = norm_back(y_s, scale_y, final_all, dense(grad_head, sel), width)

    grads = [None] * sections
    g_down, g_gu, grad_b = mlp_back(
        grad_y.astype(LOW), b_s, gate_s, upper_s, hidden_s, gu_all[last], down_all[last]
    )
    grad_mid, gain_two = norm_back(mixed_s, scale_s, gain_all[last, 1], grad_b, width)
    grad_mixed = grad_mid + grad_y
    branch = grad_mixed.astype(LOW)
    g_out = dense_t(attended_s, branch)
    grad_att = dense_nt(dense_nt(branch, out_all[last]).astype(LOW), sel).astype(LOW)
    grad_query, grad_key, grad_value = attend_back(query_s, key_last, value_last, probs_s, grad_att)
    grad_q = rotate_back(grad_query, cosine_s, sine_s).reshape(-1, WIDTH).astype(LOW)
    grad_kv = jnp.concatenate(
        [rotate_back(grad_key, cosine, sine).reshape(-1, KVW), grad_value.reshape(-1, KVW)], axis=1
    ).astype(LOW)
    g_qkv = jnp.concatenate([dense_t(a_s, grad_q), dense_t(a_last, grad_kv)], axis=1)
    grad_a_s = dense_nt(grad_q, qkv_all[last][:, :WIDTH])
    spread_back = lax.dot_general(
        pick32,
        jnp.concatenate([grad_a_s, grad_mixed], axis=1),
        (((0,), (0,)), ((), ())),
        precision=HI,
    )
    grad_a = dense_nt(grad_kv, qkv_all[last][:, WIDTH:]) + spread_back[:, :wide]
    grad_in, gain_one = norm_back(x, scale_last, gain_all[last, 0], grad_a, width)
    upstream = grad_in + spread_back[:, wide:]
    grads[last] = (g_qkv, g_out, g_gu, g_down, jnp.stack([gain_one, gain_two]))

    for layer in range(sections - 2, -1, -1):
        (x, scale_a, a, query, key, value, probs, attended, mixed, scale_b, b, gate, upper, hidden) = kept[
            layer
        ]
        g_down, g_gu, grad_b = mlp_back(
            upstream.astype(LOW), b, gate, upper, hidden, gu_all[layer], down_all[layer]
        )
        grad_mid, gain_two = norm_back(mixed, scale_b, gain_all[layer, 1], grad_b, width)
        grad_mixed = grad_mid + upstream
        branch = grad_mixed.astype(LOW)
        g_out = dense_t(attended, branch)
        grad_att = dense_nt(dense_nt(branch, out_all[layer]).astype(LOW), sel).astype(LOW)
        grad_query, grad_key, grad_value = attend_back(query, key, value, probs, grad_att)
        grad_qkv = jnp.concatenate(
            [
                rotate_back(grad_query, cosine, sine).reshape(-1, WIDTH),
                rotate_back(grad_key, cosine, sine).reshape(-1, KVW),
                grad_value.reshape(-1, KVW),
            ],
            axis=1,
        ).astype(LOW)
        g_qkv = dense_t(a, grad_qkv)
        grad_in, gain_one = norm_back(
            x, scale_a, gain_all[layer, 0], dense_nt(grad_qkv, qkv_all[layer]), width
        )
        upstream = grad_in + grad_mixed
        grads[layer] = (g_qkv, g_out, g_gu, g_down, jnp.stack([gain_one, gain_two]))

    grad_x0 = dense_nt(upstream.astype(LOW), sel).astype(LOW)

    def give(grad_rows, all_asked, choose):
        rows = dense_t(choose, grad_x0).astype(LOW)
        got = lax.all_to_all(rows.reshape(n, slots, width), "fsdp", 0, 0)
        every = lax.all_gather(got, "section", axis=0).reshape(-1, width)
        place_of = (jnp.arange(vshard)[:, None] == all_asked.reshape(-1)[None, :]).astype(LOW)
        return grad_rows + dense(place_of, every)

    grad_table = give(grad_table, asked_first, onehot)

    def give_more(state):
        turn, grad_rows = state
        choose, more = lookup_round(ids, owner, rank, turn, slots, n, vshard)
        return (turn + 1, give(grad_rows, asked(lax.all_gather(more, BOTH, axis=0)), choose))

    grad_table = lax.while_loop(lambda state: state[0] < turns, give_more, (jnp.int32(1), grad_table))[1]

    def to_owner(which, rows_each):
        stacked = jnp.concatenate([grads[layer][which].astype(LOW) for layer in range(sections)], axis=0)
        return lax.psum_scatter(stacked, BOTH, scatter_dimension=0, tiled=True).astype(jnp.float32)

    s_qkv = to_owner(0, rp)[:r]
    s_out = to_owner(1, rp)[:r].reshape(r, n, rp)[:, :, :r].reshape(r, width)
    s_gu = to_owner(2, rp)[:r].reshape(r, 2, n, rdp)[:, :, :, :rd].reshape(r, 2 * n * rd)
    s_down = to_owner(3, rdp)[:rd].reshape(rd, n, rp)[:, :, :r].reshape(rd, width)
    small = lax.psum(
        jnp.concatenate([grads[layer][4] for layer in range(sections)] + [grad_final[None]], axis=0), BOTH
    )
    small = lax.dynamic_index_in_dim(
        small.reshape(2 * sections + 1, n, rp), fsdp_index, 1, keepdims=False
    )[:, :r]
    s_gains = lax.dynamic_slice_in_dim(small, 2 * section_index, 2)
    s_final = small[2 * sections]

    grads_all = (
        grad_table,
        s_qkv[None],
        s_out[None],
        s_gu[None],
        s_down[None],
        s_gains[None],
        s_final,
    )
    weights_all = (table, w_qkv, w_out, w_gu, w_down, gains, final_gain)
    firsts = (first_table, first_qkv, first_out, first_gu, first_down, first_gains, first_final)
    seconds = (
        second_table,
        second_qkv,
        second_out,
        second_gu,
        second_down,
        second_gains,
        second_final,
    )
    slot_total = 6 * sections + 2
    shared_share = jnp.where(leader, 1.0, 0.0)

    def slot_squares(arrays):
        rows_each_section = jnp.stack(
            [
                jnp.sum(arrays[1] ** 2),
                jnp.sum(arrays[2] ** 2),
                jnp.sum(arrays[3] ** 2),
                jnp.sum(arrays[4] ** 2),
                jnp.sum(arrays[5][0, 0] ** 2),
                jnp.sum(arrays[5][0, 1] ** 2),
            ]
        )
        slot_entries = 6 * section_index + jnp.arange(6)
        positioned_rows = jnp.sum(
            jnp.where(
                slot_entries[:, None] == jnp.arange(slot_total)[None, :],
                rows_each_section[:, None],
                0.0,
            ),
            axis=0,
        )
        common_prompt = shared_share * jnp.stack([jnp.sum(arrays[0] ** 2), jnp.sum(arrays[6] ** 2)])
        return positioned_rows + jnp.concatenate(
            [jnp.zeros((slot_total - 2,), jnp.float32), common_prompt]
        )

    grad_sq = lax.psum(slot_squares(grads_all), BOTH)
    grad_norm = jnp.sqrt(jnp.sum(grad_sq))
    clip = jnp.minimum(1.0, CLIP / grad_norm)
    decays = (DECAY, DECAY, DECAY, DECAY, DECAY, 0.0, 0.0)
    parts = [
        lamb_parts(w, clip * g, m, v, d)
        for w, g, m, v, d in zip(weights_all, grads_all, firsts, seconds, decays)
    ]
    squares = lax.psum(
        jnp.stack([slot_squares(weights_all), slot_squares(tuple((p[2] for p in parts)))]), BOTH
    )
    weight_norms, update_norms = (jnp.sqrt(squares[0]), jnp.sqrt(squares[1]))
    trust_ratio = weight_norms / update_norms
    own = lax.dynamic_slice_in_dim(trust_ratio, 6 * section_index, 6)
    scales = (
        trust_ratio[slot_total - 2],
        own[0],
        own[1],
        own[2],
        own[3],
        own[4:6][None, :, None],
        trust_ratio[slot_total - 1],
    )
    new = [w - RATE * s * p[2] for w, s, p in zip(weights_all, scales, parts)]
    matrix_norms = jnp.stack([weight_norms, update_norms])
    outs = [loss, grad_norm, matrix_norms]
    for k in range(7):
        outs += [new[k], parts[k][0], parts[k][1]]
    return tuple(outs + [new[k].astype(LOW) for k in range(5)])


def solution(mesh):
    tall, layered, gainy, flat = (
        P("fsdp", None),
        P("section", "fsdp", None),
        P("section", None, "fsdp"),
        P("fsdp"),
    )
    weights = (tall, layered, layered, layered, layered, gainy, flat)
    placed = (
        P("section", "fsdp"),
        P("section", "fsdp", None),
        P("section", None, None),
        P(),
    ) + weights * 3
    results = (P(), P(), P())
    for spec in weights:
        results += (spec, spec, spec)
    return jax.shard_map(
        shards, mesh=mesh, in_specs=placed, out_specs=results + weights[:5], check_vma=False
    )
```

```python
import functools

import jax
import jax.numpy as jnp
from jax import lax
from jax.experimental import pallas as pl
from jax.experimental.pallas import tpu as pltpu
from jax.sharding import PartitionSpec as P

HEADS = 15
KV = 5
HD = 64
FF = 2560
PROMPT = 256
NCONT = 2
CONT = 128
SCORED = 32
STEP = 10
TOK_MB = 512

EPS = 1e-05
SCALE = 0.125
THETA = 100000.0
BETA = 0.1
CLIP = 1.0
RATE = 0.3
BETA_ONE = 0.9
BETA_TWO = 0.99
ADAM_EPS = 1e-08
DECAY = 0.01

WIDTH = HEADS * HD
KVW = KV * HD
BOTH = ("section", "fsdp")
HI = lax.Precision.HIGHEST
LOW = jnp.bfloat16

WEIGHT_PIECES = [
    (0, 0, 64, 0),
    (1, 0, 64, 1),
    (2, 0, 16, 0),
    (2, 16, 16, 1),
    (2, 32, 16, 0),
    (2, 48, 16, 1),
    (3, 0, 80, 0),
    (3, 80, 80, 1),
    (4, 0, 16, 1),
]

MESH = pl.DeviceIdType.MESH
ANYWHERE = pl.BlockSpec(memory_space=pl.ANY)
IN_VMEM = pl.BlockSpec(memory_space=pltpu.VMEM)
TILE_R, TILE_C = 32, 1024


def coords():
    f = lax.axis_index("fsdp")
    return (lax.axis_index("section"), f // 4, f // 2 % 2, f % 2)


def device(y, z, x, c):
    return (y, z * 4 + x * 2 + c)


def greet(peers):
    barrier = pltpu.get_barrier_semaphore()
    for peer in peers:
        pl.semaphore_signal(barrier, inc=1, device_id=peer, device_id_type=MESH)
    pl.semaphore_wait(barrier, len(peers))


def send(src, dst, send_sem, recv_sem, peer):
    pltpu.make_async_remote_copy(
        src_ref=src,
        dst_ref=dst,
        send_sem=send_sem,
        recv_sem=recv_sem,
        device_id=peer,
        device_id_type=MESH,
    ).start()


def settle(ref, sem):
    pltpu.make_async_copy(ref, ref, sem).wait()


def gather_kernel(pieces, count, *refs):
    blocks, outs = (refs[:count], refs[count : 2 * count])
    send_sem, recv_sem, sib_sem, own_sem = refs[2 * count :]
    y, z, x, c = coords()
    to_x, to_y, to_sib = (device(y, z, 1 - x, c), device(1 - y, z, x, c), device(y, z, x, 1 - c))
    zs = [(z + k) % 4 for k in range(4)]
    greet([to_x, to_y, to_sib] + [device(y, zz, x, c) for zz in zs[1:]])

    def part(ref, p):
        return ref.at[pl.ds(pieces[p][1], pieces[p][2])]

    def there(p, o):
        return part(outs[pieces[p][0]].at[o[0] * 16 + o[1] * 4 + o[2] * 2 + c], p)

    def mark(p, o):
        return recv_sem.at[p, o[0] * 8 + o[1] * 2 + o[2]]

    def push(p, o, peer, own=False, sib=False):
        src = part(blocks[pieces[p][0]], p) if own else there(p, o)
        send(src, there(p, o), send_sem.at[p], sib_sem.at[p] if sib else mark(p, o), peer)

    every = range(len(pieces))
    for p in every:
        me = (y, z, x)
        push(p, me, to_x, own=True)
        push(p, me, to_y, own=True)
        for zz in zs[1:]:
            push(p, me, device(y, zz, x, c), own=True)
        push(p, me, to_sib, own=True, sib=True)
        pltpu.make_async_copy(part(blocks[pieces[p][0]], p), there(p, me), own_sem).start()

    def from_x(p, zz):
        o = (y, zz, 1 - x)
        settle(there(p, o), mark(p, o))
        if pieces[p][3] == 0:
            push(p, o, to_y)
        push(p, o, to_sib, sib=True)

    def from_y(p, zz):
        o = (1 - y, zz, x)
        settle(there(p, o), mark(p, o))
        if pieces[p][3] == 1:
            push(p, o, to_x)
        push(p, o, to_sib, sib=True)

    for p in every:
        for zz in zs[1:]:
            o = (y, zz, x)
            settle(there(p, o), mark(p, o))
            push(p, o, to_x)
            push(p, o, to_y)
            push(p, o, to_sib, sib=True)
        from_x(p, z)
        from_y(p, z)
    for p in every:
        for zz in zs[1:]:
            from_x(p, zz)
            from_y(p, zz)
    for p in every:
        for zz in zs:
            o = (1 - y, zz, 1 - x)
            settle(there(p, o), mark(p, o))
            push(p, o, to_sib, sib=True)
    for p in every:
        a, start, rows, unused = pieces[p]
        own = part(blocks[a], p)
        settle(own, own_sem)
        settle(outs[a].at[pl.ds(0, 31), pl.ds(start, rows)], send_sem.at[p])
        settle(outs[a].at[pl.ds(0, 16), pl.ds(start, rows)], sib_sem.at[p])


def gather_all(blocks, pieces, name):
    many = len(pieces)
    return pl.pallas_call(
        functools.partial(gather_kernel, pieces, len(blocks)),
        out_shape=[jax.ShapeDtypeStruct((32,) + b.shape, b.dtype) for b in blocks],
        in_specs=[ANYWHERE] * len(blocks),
        out_specs=[ANYWHERE] * len(blocks),
        scratch_shapes=[
            pltpu.SemaphoreType.DMA((many,)),
            pltpu.SemaphoreType.DMA((many, 16)),
            pltpu.SemaphoreType.DMA((many,)),
            pltpu.SemaphoreType.DMA,
        ],
        compiler_params=pltpu.CompilerParams(collective_id=name, has_side_effects=True),
    )(*blocks)


def reduce_pieces(shapes):
    out = []
    for a, (rows, cols) in enumerate(shapes):
        for row in range(0, rows, TILE_R):
            for col in range(0, cols, TILE_C):
                out.append((a, row, col, min(TILE_C, cols - col)))
    return out


def reduce_kernel(pieces, count, lag, *refs):
    grads = (refs[:count], refs[count : 2 * count])
    outs = refs[2 * count : 3 * count]
    held, from_one, from_two, from_z, mine = refs[3 * count : 3 * count + 5]
    sib_recv, sib_send, recv_one, send_one, recv_two, send_two, recv_z, send_z, own_sem = refs[
        3 * count + 5 :
    ]
    y, z, x, c = coords()
    to_x, to_y, to_sib = (device(y, z, 1 - x, c), device(1 - y, z, x, c), device(y, z, x, 1 - c))
    zs = [(z + k) % 4 for k in range(4)]
    greet([to_x, to_y, to_sib] + [device(y, zz, x, c) for zz in zs[1:]])
    many = len(pieces)

    def source(p, yo, xo, core):
        a, row, col, cols = pieces[p]
        return grads[yo][a].at[:, xo, core, pl.ds(row, TILE_R), pl.ds(col, cols)]

    def cut(ref, p):
        cols = pieces[p][3]
        return ref if cols == TILE_C else ref.at[..., pl.ds(0, cols)]

    def fetch(p):
        for yo in range(2):
            for xo in range(2):
                pltpu.make_async_copy(
                    source(p, yo, xo, c), cut(mine.at[p % 2, yo, xo], p), own_sem.at[p % 2]
                ).start()

    for p in range(many):
        for yo in range(2):
            for xo in range(2):
                send(
                    source(p, yo, xo, 1 - c),
                    cut(held.at[p, yo, xo], p),
                    sib_send.at[p],
                    sib_recv.at[p],
                    to_sib,
                )
        if p == 0:
            fetch(0)

    def add(dst, src, p):
        cols = pl.ds(0, pieces[p][3])
        dst[:, cols] = (dst[:, cols].astype(jnp.float32) + src[:, cols].astype(jnp.float32)).astype(LOW)

    def two_cores(p):
        if p + 1 < many:
            fetch(p + 1)
        settle(cut(mine.at[p % 2], p), own_sem.at[p % 2])
        settle(cut(held.at[p], p), sib_recv.at[p])

        def each(i, carry):
            yo, xo, zo = (i // 8, i // 4 % 2, i % 4)
            add(held.at[p, yo, xo, zo], mine.at[p % 2, yo, xo, zo], p)
            return carry

        lax.fori_loop(0, 16, each, 0)
        if p % 2 == 0:
            send(cut(held.at[p, 1 - y], p), cut(from_one.at[p], p), send_one.at[p], recv_one.at[p], to_y)
        else:
            for yo in range(2):
                send(
                    cut(held.at[p, yo, 1 - x], p),
                    cut(from_one.at[p, yo], p),
                    send_one.at[p],
                    recv_one.at[p],
                    to_x,
                )

    def first_axis(p):
        settle(cut(from_one.at[p], p), recv_one.at[p])

        def each(i, carry):
            if p % 2 == 0:
                add(held.at[p, y, i // 4, i % 4], from_one.at[p, i // 4, i % 4], p)
            else:
                add(held.at[p, i // 4, x, i % 4], from_one.at[p, i // 4, i % 4], p)
            return carry

        lax.fori_loop(0, 8, each, 0)
        if p % 2 == 0:
            src, peer = (held.at[p, y, 1 - x], to_x)
        else:
            src, peer = (held.at[p, 1 - y, x], to_y)
        send(cut(src, p), cut(from_two.at[p], p), send_two.at[p], recv_two.at[p], peer)

    def second_axis(p):
        settle(cut(from_two.at[p], p), recv_two.at[p])

        def each(i, carry):
            add(held.at[p, y, x, i], from_two.at[p, i], p)
            return carry

        lax.fori_loop(0, 4, each, 0)
        for k in range(1, 4):
            send(
                cut(held.at[p, y, x, zs[k]], p),
                cut(from_z.at[p, 3 - k], p),
                send_z.at[p],
                recv_z.at[p],
                device(y, zs[k], x, c),
            )

    def along_z(p):
        settle(cut(from_z.at[p], p), recv_z.at[p])
        a, row, col, cols = pieces[p]
        part = pl.ds(0, cols)
        total = held[p, y, x, z, :, part].astype(jnp.float32)
        for k in range(3):
            total = total + from_z[p, k, :, part].astype(jnp.float32)
        outs[a][pl.ds(row, TILE_R), pl.ds(col, cols)] = total

    for step in range(many + 3 * lag):
        for k, stage in enumerate((two_cores, first_axis, second_axis, along_z)):
            if 0 <= step - k * lag < many:
                stage(step - k * lag)
    for p in range(many):
        settle(cut(held.at[p], p), sib_send.at[p])
        settle(cut(from_one.at[p], p), send_one.at[p])
        settle(cut(from_two.at[p], p), send_two.at[p])
        settle(cut(from_z.at[p], p), send_z.at[p])


def reduce_all(grads, name, lag):
    count = len(grads[0])
    shapes = [(g.shape[0] // 16, g.shape[1]) for g in grads[0]]
    pieces = reduce_pieces(shapes)
    many = len(pieces)
    views = [g.reshape(4, 2, 2, g.shape[0] // 16, g.shape[1]) for layer in grads for g in layer]
    return pl.pallas_call(
        functools.partial(reduce_kernel, pieces, count, lag),
        out_shape=[jax.ShapeDtypeStruct(s, jnp.float32) for s in shapes],
        in_specs=[ANYWHERE] * len(views),
        out_specs=[IN_VMEM] * count,
        scratch_shapes=[
            pltpu.VMEM((many, 2, 2, 4, TILE_R, TILE_C), LOW),
            pltpu.VMEM((many, 2, 4, TILE_R, TILE_C), LOW),
            pltpu.VMEM((many, 4, TILE_R, TILE_C), LOW),
            pltpu.VMEM((many, 3, TILE_R, TILE_C), LOW),
            pltpu.VMEM((2, 2, 2, 4, TILE_R, TILE_C), LOW),
        ]
        + [pltpu.SemaphoreType.DMA((many,)) for unused in range(8)]
        + [pltpu.SemaphoreType.DMA((2,))],
        compiler_params=pltpu.CompilerParams(
            collective_id=name,
            has_side_effects=True,
            vmem_limit_bytes=(12 + 3 * many) * 2**20 if many < 16 else 58 * 2**20,
        ),
    )(*views)


def exchange_kernel(whole, src, out, send_sem, recv_sem, own_sem):
    y, f = (lax.axis_index("section"), lax.axis_index("fsdp"))
    count = 32 if whole else 16
    me = y * 16 + f if whole else f
    peers = [(me + k) % count for k in range(1, count)]
    where = [(p // 16, p % 16) if whole else (y, p) for p in peers]
    greet(where)
    for peer in where:
        send(src, out.at[me], send_sem, recv_sem, peer)
    own = pltpu.make_async_copy(src, out.at[me], own_sem)
    own.start()
    own.wait()
    settle(out.at[pl.ds(0, count - 1)], send_sem)
    settle(out.at[pl.ds(0, count - 1)], recv_sem)


def exchange(small, name, whole=True):
    return pl.pallas_call(
        functools.partial(exchange_kernel, whole),
        out_shape=jax.ShapeDtypeStruct((32 if whole else 16,) + small.shape, small.dtype),
        in_specs=[IN_VMEM],
        out_specs=IN_VMEM,
        scratch_shapes=[pltpu.SemaphoreType.DMA] * 3,
        compiler_params=pltpu.CompilerParams(collective_id=name, has_side_effects=True),
    )(small)


def up16(count):
    return -(-count // 16) * 16


def dense(left, right):
    return jnp.dot(left, right, preferred_element_type=jnp.float32)


def dense_t(left, right):
    return lax.dot_general(
        left, right, (((0,), (0,)), ((), ())), preferred_element_type=jnp.float32
    )


def dense_nt(left, right):
    return lax.dot_general(
        left, right, (((1,), (1,)), ((), ())), preferred_element_type=jnp.float32
    )


def spread_matrix(parts, real, padded):
    feature = jnp.arange(parts * real)
    place = feature // real * padded + feature % real
    return (place[:, None] == jnp.arange(parts * padded)[None, :]).astype(LOW)


def inverse_rms(x, width):
    return lax.rsqrt(jnp.sum(x * x, axis=-1, keepdims=True) / width + EPS)


def norm_back(x, scale, gain, upstream, width):
    inner = upstream * gain
    grad_gain = jnp.sum(upstream * x * scale, axis=0)
    mean = jnp.sum(inner * x, axis=-1, keepdims=True) / width
    return (scale * inner - x * scale**3 * mean, grad_gain)


def rotate(x, cosine, sine):
    half = x.shape[-1] // 2
    first, second = (x[..., :half], x[..., half:])
    return jnp.concatenate(
        [first * cosine - second * sine, second * cosine + first * sine], axis=-1
    )


def rotate_back(grad, cosine, sine):
    return rotate(grad, cosine, -sine)


def rotary_angles(place):
    rotary = jnp.where(place >= PROMPT, PROMPT + (place - PROMPT) % CONT, place).astype(jnp.float32)
    freq = THETA ** (-2.0 * jnp.arange(HD // 2).astype(jnp.float32) / HD)
    angle = rotary[:, None] * freq[None, :]
    return (jnp.cos(angle)[:, None, :], jnp.sin(angle)[:, None, :])


def may_attend(place):
    keys = jnp.arange(TOK_MB)

    def segment(p):
        return jnp.where(p >= PROMPT, 1 + (p - PROMPT) // CONT, 0)

    return (keys[None, :] <= place[:, None]) & (
        (segment(keys)[None, :] == 0) | (segment(keys)[None, :] == segment(place)[:, None])
    )


def attend(query, key, value, allowed):
    scores = jnp.einsum("qhgd,khd->hgqk", query, key, preferred_element_type=jnp.float32) * SCALE
    scores = jnp.where(allowed, scores, -1e30)
    expo = jnp.exp(scores - jnp.max(scores, axis=-1, keepdims=True))
    probs = expo / jnp.sum(expo, axis=-1, keepdims=True)
    out = jnp.einsum("hgqk,khd->qhgd", probs.astype(LOW), value, preferred_element_type=jnp.float32)
    return (out.reshape(-1, WIDTH).astype(LOW), probs)


def attend_back(query, key, value, probs, grad):
    grad = grad.reshape(-1, KV, HEADS // KV, HD)
    grad_probs = jnp.einsum("qhgd,khd->hgqk", grad, value, preferred_element_type=jnp.float32)
    grad_scores = probs * (grad_probs - jnp.sum(grad_probs * probs, axis=-1, keepdims=True))
    grad_scores = grad_scores.astype(LOW)
    grad_query = (
        jnp.einsum("hgqk,khd->qhgd", grad_scores, key, preferred_element_type=jnp.float32) * SCALE
    )
    grad_key = (
        jnp.einsum("hgqk,qhgd->khd", grad_scores, query, preferred_element_type=jnp.float32) * SCALE
    )
    grad_value = jnp.einsum(
        "hgqk,qhgd->khd", probs.astype(LOW), grad, preferred_element_type=jnp.float32
    )
    return (grad_query.reshape(-1, HEADS, HD), grad_key, grad_value)


def heads_of(q, cosine, sine):
    return (
        rotate(q.reshape(-1, HEADS, HD), cosine, sine).astype(LOW).reshape(-1, KV, HEADS // KV, HD)
    )


def keys_values(kv, cosine, sine):
    key = rotate(kv[:, :KVW].reshape(-1, KV, HD), cosine, sine).astype(LOW)
    return (key, kv[:, KVW:].reshape(-1, KV, HD).astype(LOW))


def mlp(b, w_gu, w_down):
    gate_up = dense(b, w_gu)
    half = gate_up.shape[1] // 2
    gate, upper = (gate_up[:, :half], gate_up[:, half:])
    hidden = (jax.nn.silu(gate) * upper).astype(LOW)
    return (dense(hidden, w_down), gate, upper, hidden)


def mlp_back(branch, b, gate, upper, hidden, w_gu, w_down):
    grad_down = dense_t(hidden, branch)
    grad_hidden = dense_nt(branch, w_down)
    sig = jax.nn.sigmoid(gate)
    grad_gate = grad_hidden * upper * sig * (1.0 + gate * (1.0 - sig))
    grad_upper = grad_hidden * gate * sig
    grad_gate_up = jnp.concatenate([grad_gate, grad_upper], axis=1).astype(LOW)
    return (grad_down, dense_t(b, grad_gate_up), dense_nt(grad_gate_up, w_gu))


def lamb_parts(weight, grad, first, second, decay):
    first_new = BETA_ONE * first + (1.0 - BETA_ONE) * grad
    second_new = BETA_TWO * second + (1.0 - BETA_TWO) * grad * grad
    update = (
        first_new
        / (1.0 - BETA_ONE**STEP)
        / (jnp.sqrt(second_new / (1.0 - BETA_TWO**STEP)) + ADAM_EPS)
        + decay * weight
    )
    return (first_new, second_new, update)


def lookup_ranks(ids, vshard):
    place = jnp.arange(ids.shape[0])
    same = ids[:, None] == ids[None, :]
    first = jnp.min(jnp.where(same, place[None, :], ids.shape[0]), axis=1)
    owner = ids // vshard
    before = (
        (owner[:, None] == owner[None, :])
        & (first == place)[None, :]
        & (place[None, :] < first[:, None])
    )
    return (owner, jnp.sum(before.astype(jnp.int32), axis=1))


def lookup_round(ids, owner, rank, turn, slots, parts, vshard):
    slot = jnp.where(rank // slots == turn, owner * slots + rank - turn * slots, -1)
    onehot = slot[:, None] == jnp.arange(parts * slots)[None, :]
    wanted = jnp.max(jnp.where(onehot, (ids - owner * vshard)[:, None], -1), axis=0)
    return (onehot.astype(LOW), wanted)


def shards(
    token_ids,
    scored,
    targets,
    pairs,
    table,
    w_qkv,
    w_out,
    w_gu,
    w_down,
    gains,
    final_gain,
    first_table,
    first_qkv,
    first_out,
    first_gu,
    first_down,
    first_gains,
    first_final,
    second_table,
    second_qkv,
    second_out,
    second_gu,
    second_down,
    second_gains,
    second_final,
):
    n = lax.axis_size("fsdp")
    sections = lax.axis_size("section")
    section_index = lax.axis_index("section")
    fsdp_index = lax.axis_index("fsdp")
    leader = section_index == 0
    vshard, width = table.shape
    vstart = fsdp_index * vshard
    r = w_qkv.shape[1]
    rp = up16(r)
    rd = w_down.shape[1]
    rdp = up16(rd)
    wide = n * rp
    ffp = n * rdp
    slots = up16(768 // n)
    sel = spread_matrix(n, r, rp)
    fast = (sections, n) == (2, 16)
    qkv_wide = -(-w_qkv.shape[2] // 128) * 128

    qkv_block = jnp.pad(
        w_qkv[0].astype(LOW), ((0, rp - r), (0, qkv_wide - w_qkv.shape[2]))
    )
    out_block = jnp.pad(dense(w_out[0].astype(LOW), sel).astype(LOW), ((0, rp - r), (0, 0)))
    gu_block = w_gu[0].astype(LOW)
    if rdp != rd:
        gu_block = jnp.pad(gu_block.reshape(r, 2, n, rd), ((0, 0), (0, 0), (0, 0), (0, rdp - rd)))
    gu_block = jnp.pad(gu_block.reshape(r, 2 * ffp), ((0, rp - r), (0, 0)))
    down_block = jnp.pad(dense(w_down[0].astype(LOW), sel).astype(LOW), ((0, rdp - rd), (0, 0)))
    gain_block = jnp.pad(
        jnp.concatenate([gains[0], final_gain[None]], axis=0).astype(LOW),
        ((0, 13), (0, 128 - r)),
    )

    ids = token_ids[0]
    owner, rank = lookup_ranks(ids, vshard)
    onehot, wanted = lookup_round(ids, owner, rank, 0, slots, n, vshard)
    turns_here = jnp.max(rank) // slots + 1
    own_targets = lax.dynamic_slice_in_dim(targets[0], fsdp_index * NCONT, NCONT).reshape(-1)
    note = jnp.concatenate(
        [wanted, jnp.pad(own_targets, (0, 128 - NCONT * SCORED)), jnp.full((128,), turns_here, jnp.int32)]
    )
    if fast:
        notes = exchange(note.reshape(-1, 128), 0).reshape(sections * n, -1)
    else:
        notes = lax.all_gather(note, BOTH, axis=0)
    turns = jnp.max(notes[:, -1])
    wanted_rows = notes[:, n * slots : n * slots + NCONT * SCORED].reshape(-1)

    def asked(all_wanted):
        mine = lax.dynamic_slice_in_dim(all_wanted.reshape(sections, n, n, slots), fsdp_index, 1, 2)
        return mine[:, :, 0]

    def fetch(all_asked, choose):
        here = lax.dynamic_index_in_dim(all_asked, section_index, 0, keepdims=False).reshape(-1)
        rows = jnp.take(table, jnp.maximum(here, 0), axis=0).astype(LOW)
        got = lax.all_to_all(rows.reshape(n, slots, width), "fsdp", 0, 0).reshape(n * slots, width)
        return dense(dense(choose, got).astype(LOW), sel)

    asked_first = asked(notes[:, : n * slots])
    x0 = fetch(asked_first, onehot)

    def fetch_more(state):
        turn, total = state
        choose, more = lookup_round(ids, owner, rank, turn, slots, n, vshard)
        return (turn + 1, total + fetch(asked(lax.all_gather(more, BOTH, axis=0)), choose))

    x0 = lax.while_loop(lambda state: state[0] < turns, fetch_more, (jnp.int32(1), x0))[1]

    blocks = (qkv_block, out_block, gu_block, down_block, gain_block)
    if fast:
        gathered = gather_all(blocks, WEIGHT_PIECES, 1)
    else:
        gathered = [lax.all_gather(block, BOTH, axis=0) for block in blocks]
    qkv_all, out_all, gu_all, down_all = [
        g.reshape(sections, n * g.shape[1], g.shape[2]) for g in gathered[:4]
    ]
    gain_all = gathered[4].reshape(sections, n, 16, 128)[:, :, :3, :rp]
    gain_all = jnp.moveaxis(gain_all, 2, 1).reshape(sections, 3, wide).astype(jnp.float32)
    final_all = gain_all[0, 2]

    everyone = jnp.arange(TOK_MB)
    cosine, sine = rotary_angles(everyone)
    allowed = may_attend(everyone)
    x = x0
    kept = []
    for layer in range(sections - 1):
        scale_a = inverse_rms(x, width)
        a = (x * scale_a * gain_all[layer, 0]).astype(LOW)
        qkv = dense(a, qkv_all[layer])
        query = heads_of(qkv[:, :WIDTH], cosine, sine)
        key, value = keys_values(qkv[:, WIDTH : WIDTH + 2 * KVW], cosine, sine)
        attended, probs = attend(query, key, value, allowed)
        attended = dense(attended, sel).astype(LOW)
        mixed = x + dense(attended, out_all[layer])
        scale_b = inverse_rms(mixed, width)
        b = (mixed * scale_b * gain_all[layer, 1]).astype(LOW)
        branch, gate, upper, hidden = mlp(b, gu_all[layer], down_all[layer])
        kept.append(
            (x, scale_a, a, query, key, value, probs, attended, mixed, scale_b, b, gate, upper, hidden)
        )
        x = mixed + branch

    last = sections - 1
    place = (PROMPT + CONT * jnp.arange(NCONT)[:, None] + scored[0]).reshape(-1)
    pick = (place[:, None] == everyone[None, :]).astype(LOW)
    pick32 = pick.astype(jnp.float32)
    cosine_s, sine_s = rotary_angles(place)
    allowed_s = may_attend(place)
    scale_last = inverse_rms(x, width)
    a_last = (x * scale_last * gain_all[last, 0]).astype(LOW)
    qkv_last = qkv_all[last][:, WIDTH : WIDTH + 2 * KVW]
    key_last, value_last = keys_values(dense(a_last, qkv_last), cosine, sine)
    a_s = dense(pick, a_last).astype(LOW)
    x_s = jnp.dot(pick32, x, precision=HI)
    query_s = heads_of(dense(a_s, qkv_all[last][:, :WIDTH]), cosine_s, sine_s)
    attended_s, probs_s = attend(query_s, key_last, value_last, allowed_s)
    attended_s = dense(attended_s, sel).astype(LOW)
    mixed_s = x_s + dense(attended_s, out_all[last])
    scale_s = inverse_rms(mixed_s, width)
    b_s = (mixed_s * scale_s * gain_all[last, 1]).astype(LOW)
    branch_s, gate_s, upper_s, hidden_s = mlp(b_s, gu_all[last], down_all[last])
    y_s = mixed_s + branch_s
    scale_y = inverse_rms(y_s, width)
    head_in = (y_s * scale_y * final_all).astype(LOW)

    if fast:
        rows_all = gather_all([head_in], [(0, 16 * k, 16, k % 2) for k in range(4)], 2)[0]
    else:
        rows_all = lax.all_gather(head_in, BOTH, axis=0)
    rows_all = dense_nt(rows_all.reshape(-1, wide), sel).astype(LOW)
    own_rows = rows_all.shape[0] // sections
    table_low = table.astype(LOW)
    logits = dense_nt(rows_all, table_low)
    hit = jnp.arange(vshard)[None, :] == (wanted_rows - vstart)[:, None]
    top_here = jnp.max(logits, axis=1)
    total_here = jnp.sum(jnp.exp(logits - top_here[:, None]), axis=1)
    target_here = jnp.sum(jnp.where(hit, logits, 0.0), axis=1)
    stats = jnp.stack([top_here, total_here, target_here])
    if fast:
        stats = exchange(stats.reshape(-1, 128), 3, whole=False).reshape(n, 3, -1)
    else:
        stats = lax.all_gather(stats, "fsdp", axis=0)
    top = jnp.max(stats[:, 0], axis=0)
    total = jnp.sum(stats[:, 1] * jnp.exp(stats[:, 0] - top), axis=0)
    row_logp = jnp.sum(stats[:, 2], axis=0) - top - jnp.log(total)
    seq = jnp.sum(row_logp.reshape(-1, SCORED), axis=1)
    pair = pairs.reshape(-1, 2)
    conts = jnp.arange(seq.shape[0])
    chosen = (pair[:, 0][:, None] == conts[None, :]).astype(jnp.float32)
    passed = (pair[:, 1][:, None] == conts[None, :]).astype(jnp.float32)
    delta = jnp.sum((chosen - passed) * seq[None, :], axis=1)
    loss = jnp.sum(jax.nn.softplus(-BETA * delta))
    push = BETA * jax.nn.sigmoid(-BETA * delta)
    grad_seq = jnp.sum((passed - chosen) * push[:, None], axis=0)
    grad_row = jnp.repeat(grad_seq, SCORED)
    prob = jnp.exp(logits - top[:, None]) * (1.0 / total)[:, None]
    grad_logits = (grad_row[:, None] * (hit.astype(jnp.float32) - prob)).astype(LOW)
    grad_table = dense_t(grad_logits, rows_all)
    own_vocab = vshard // sections
    own_grads = lax.dynamic_slice_in_dim(grad_logits, section_index * own_vocab, own_vocab, 1)
    own_table = lax.dynamic_slice_in_dim(table_low, section_index * own_vocab, own_vocab)
    grad_rows = dense(dense(own_grads, own_table).astype(LOW), sel).astype(LOW)
    if fast:
        halves = [[grad_rows[k * own_rows : (k + 1) * own_rows]] for k in range(sections)]
        grad_head = reduce_all(halves, 4, 1)[0]
    else:
        grad_head = lax.psum_scatter(grad_rows, BOTH, scatter_dimension=0, tiled=True)
    grad_y, grad_final = norm_back(y_s, scale_y, final_all, grad_head.astype(jnp.float32), width)

    grads = [None] * sections
    g_down, g_gu, grad_b = mlp_back(
        grad_y.astype(LOW), b_s, gate_s, upper_s, hidden_s, gu_all[last], down_all[last]
    )
    grad_mid, gain_two = norm_back(mixed_s, scale_s, gain_all[last, 1], grad_b, width)
    grad_mixed = grad_mid + grad_y
    branch = grad_mixed.astype(LOW)
    g_out = dense_t(attended_s, branch)
    grad_att = dense_nt(dense_nt(branch, out_all[last]).astype(LOW), sel).astype(LOW)
    grad_query, grad_key, grad_value = attend_back(query_s, key_last, value_last, probs_s, grad_att)
    grad_q = rotate_back(grad_query, cosine_s, sine_s).reshape(-1, WIDTH).astype(LOW)
    grad_kv = jnp.concatenate(
        [rotate_back(grad_key, cosine, sine).reshape(-1, KVW), grad_value.reshape(-1, KVW)], axis=1
    ).astype(LOW)
    g_qkv = dense_t(
        jnp.concatenate([a_s, a_last], axis=0),
        jnp.concatenate(
            [
                jnp.pad(grad_q, ((0, 0), (0, qkv_wide - WIDTH))),
                jnp.pad(grad_kv, ((0, 0), (WIDTH, qkv_wide - WIDTH - 2 * KVW))),
            ],
            axis=0,
        ),
    )
    grad_a_s = dense_nt(grad_q, qkv_all[last][:, :WIDTH])
    spread_back = lax.dot_general(
        pick32,
        jnp.concatenate([grad_a_s, grad_mixed], axis=1),
        (((0,), (0,)), ((), ())),
        precision=HI,
    )
    grad_a = dense_nt(grad_kv, qkv_last) + spread_back[:, :wide]
    grad_in, gain_one = norm_back(x, scale_last, gain_all[last, 0], grad_a, width)
    upstream = grad_in + spread_back[:, wide:]
    grads[last] = (g_qkv, g_out, g_gu, g_down, jnp.stack([gain_one, gain_two]))

    for layer in range(sections - 2, -1, -1):
        (x, scale_a, a, query, key, value, probs, attended, mixed, scale_b, b, gate, upper, hidden) = kept[
            layer
        ]
        g_down, g_gu, grad_b = mlp_back(
            upstream.astype(LOW), b, gate, upper, hidden, gu_all[layer], down_all[layer]
        )
        grad_mid, gain_two = norm_back(mixed, scale_b, gain_all[layer, 1], grad_b, width)
        grad_mixed = grad_mid + upstream
        branch = grad_mixed.astype(LOW)
        g_out = dense_t(attended, branch)
        grad_att = dense_nt(dense_nt(branch, out_all[layer]).astype(LOW), sel).astype(LOW)
        grad_query, grad_key, grad_value = attend_back(query, key, value, probs, grad_att)
        grad_qkv = jnp.concatenate(
            [
                rotate_back(grad_query, cosine, sine).reshape(-1, WIDTH),
                rotate_back(grad_key, cosine, sine).reshape(-1, KVW),
                grad_value.reshape(-1, KVW),
                jnp.zeros((TOK_MB, qkv_wide - WIDTH - 2 * KVW), jnp.float32),
            ],
            axis=1,
        ).astype(LOW)
        g_qkv = dense_t(a, grad_qkv)
        grad_in, gain_one = norm_back(
            x, scale_a, gain_all[layer, 0], dense_nt(grad_qkv, qkv_all[layer]), width
        )
        upstream = grad_in + grad_mixed
        grads[layer] = (g_qkv, g_out, g_gu, g_down, jnp.stack([gain_one, gain_two]))

    grad_x0 = dense_nt(upstream.astype(LOW), sel).astype(LOW)

    def give(grad_rows, all_asked, choose):
        rows = dense_t(choose, grad_x0).astype(LOW)
        got = lax.all_to_all(rows.reshape(n, slots, width), "fsdp", 0, 0)
        every = lax.all_gather(got, "section", axis=0).reshape(-1, width)
        place_of = (jnp.arange(vshard)[:, None] == all_asked.reshape(-1)[None, :]).astype(LOW)
        return grad_rows + dense(place_of, every)

    grad_table = give(grad_table, asked_first, onehot)

    def give_more(state):
        turn, grad_rows = state
        choose, more = lookup_round(ids, owner, rank, turn, slots, n, vshard)
        return (turn + 1, give(grad_rows, asked(lax.all_gather(more, BOTH, axis=0)), choose))

    grad_table = lax.while_loop(lambda state: state[0] < turns, give_more, (jnp.int32(1), grad_table))[1]

    def gain_rows(layer):
        rows = jnp.concatenate([grads[layer][4], grad_final[None]], axis=0).reshape(3, n, rp)
        rows = jnp.pad(jnp.moveaxis(rows, 0, 1), ((0, 0), (0, TILE_R - 3), (0, 128 - rp)))
        return rows.reshape(n * TILE_R, 128)

    outward = [
        [g.astype(LOW) for g in grads[layer][:4] + (gain_rows(layer),)] for layer in range(sections)
    ]
    if fast:
        summed = reduce_all(outward, 5, 2)
    else:
        summed = [
            lax.psum_scatter(
                jnp.concatenate(arrays, axis=0), BOTH, scatter_dimension=0, tiled=True
            ).astype(jnp.float32)
            for arrays in zip(*outward)
        ]
    s_qkv = summed[0][:r, : w_qkv.shape[2]]
    s_out = summed[1][:r].reshape(r, n, rp)[:, :, :r].reshape(r, width)
    s_gu = summed[2][:r].reshape(r, 2, n, rdp)[:, :, :, :rd].reshape(r, 2 * n * rd)
    s_down = summed[3][:rd].reshape(rd, n, rp)[:, :, :r].reshape(rd, width)
    s_gains = summed[4][:2, :r]
    s_final = summed[4][2, :r]

    grads_all = (
        grad_table,
        s_qkv[None],
        s_out[None],
        s_gu[None],
        s_down[None],
        s_gains[None],
        s_final,
    )
    weights_all = (table, w_qkv, w_out, w_gu, w_down, gains, final_gain)
    firsts = (first_table, first_qkv, first_out, first_gu, first_down, first_gains, first_final)
    seconds = (
        second_table,
        second_qkv,
        second_out,
        second_gu,
        second_down,
        second_gains,
        second_final,
    )
    slot_total = 6 * sections + 2
    shared_share = jnp.where(leader, 1.0, 0.0)

    def slot_squares(arrays):
        rows_each_section = jnp.stack(
            [
                jnp.sum(arrays[1] ** 2),
                jnp.sum(arrays[2] ** 2),
                jnp.sum(arrays[3] ** 2),
                jnp.sum(arrays[4] ** 2),
                jnp.sum(arrays[5][0, 0] ** 2),
                jnp.sum(arrays[5][0, 1] ** 2),
            ]
        )
        slot_entries = 6 * section_index + jnp.arange(6)
        positioned_rows = jnp.sum(
            jnp.where(
                slot_entries[:, None] == jnp.arange(slot_total)[None, :],
                rows_each_section[:, None],
                0.0,
            ),
            axis=0,
        )
        common_prompt = shared_share * jnp.stack([jnp.sum(arrays[0] ** 2), jnp.sum(arrays[6] ** 2)])
        return positioned_rows + jnp.concatenate(
            [jnp.zeros((slot_total - 2,), jnp.float32), common_prompt]
        )

    def everyones(sums, name):
        if not fast:
            return lax.psum(sums, BOTH)
        flat = sums.reshape(-1)
        small = jnp.broadcast_to(jnp.pad(flat, (0, 128 - flat.shape[0])), (8, 128))
        return jnp.sum(exchange(small, name)[:, 0], axis=0)[: flat.shape[0]].reshape(sums.shape)

    grad_sq = everyones(slot_squares(grads_all), 6)
    grad_norm = jnp.sqrt(jnp.sum(grad_sq))
    clip = jnp.minimum(1.0, CLIP / grad_norm)
    decays = (DECAY, DECAY, DECAY, DECAY, DECAY, 0.0, 0.0)
    parts = [
        lamb_parts(w, clip * g, m, v, d)
        for w, g, m, v, d in zip(weights_all, grads_all, firsts, seconds, decays)
    ]
    squares = everyones(
        jnp.stack([slot_squares(weights_all), slot_squares(tuple((p[2] for p in parts)))]), 7
    )
    weight_norms, update_norms = (jnp.sqrt(squares[0]), jnp.sqrt(squares[1]))
    trust_ratio = weight_norms / update_norms
    own = lax.dynamic_slice_in_dim(trust_ratio, 6 * section_index, 6)
    scales = (
        trust_ratio[slot_total - 2],
        own[0],
        own[1],
        own[2],
        own[3],
        own[4:6][None, :, None],
        trust_ratio[slot_total - 1],
    )
    new = [w - RATE * s * p[2] for w, s, p in zip(weights_all, scales, parts)]
    matrix_norms = jnp.stack([weight_norms, update_norms])
    outs = [loss, grad_norm, matrix_norms]
    for k in range(7):
        outs += [new[k], parts[k][0], parts[k][1]]
    return tuple(outs + [new[k].astype(LOW) for k in range(5)])


def solution(mesh):
    tall, layered, gainy, flat = (
        P("fsdp", None),
        P("section", "fsdp", None),
        P("section", None, "fsdp"),
        P("fsdp"),
    )
    weights = (tall, layered, layered, layered, layered, gainy, flat)
    placed = (
        P("section", "fsdp"),
        P("section", "fsdp", None),
        P("section", None, None),
        P(),
    ) + weights * 3
    results = (P(), P(), P())
    for spec in weights:
        results += (spec, spec, spec)
    return jax.shard_map(
        shards, mesh=mesh, in_specs=placed, out_specs=results + weights[:5], check_vma=False
    )
```

```python
import functools

import jax
import jax.numpy as jnp
from jax import lax
from jax.experimental import pallas as pl
from jax.experimental.pallas import tpu as pltpu
from jax.sharding import PartitionSpec as P

HEADS = 15
KV = 5
HD = 64
FF = 2560
PROMPT = 256
NCONT = 2
CONT = 128
SCORED = 32
STEP = 10
TOK_MB = 512

EPS = 1e-05
SCALE = 0.125
THETA = 100000.0
BETA = 0.1
CLIP = 1.0
RATE = 0.3
BETA_ONE = 0.9
BETA_TWO = 0.99
ADAM_EPS = 1e-08
DECAY = 0.01

WIDTH = HEADS * HD
KVW = KV * HD
BOTH = ("section", "fsdp")
HI = lax.Precision.HIGHEST
LOW = jnp.bfloat16

WEIGHT_PIECES = [
    (0, 0, 64, 0),
    (1, 0, 64, 1),
    (2, 0, 16, 0),
    (2, 16, 16, 1),
    (2, 32, 16, 0),
    (2, 48, 16, 1),
    (3, 0, 80, 0),
    (3, 80, 80, 1),
    (4, 0, 16, 1),
]

MESH = pl.DeviceIdType.MESH
ANYWHERE = pl.BlockSpec(memory_space=pl.ANY)
IN_VMEM = pl.BlockSpec(memory_space=pltpu.VMEM)
TILE_R, TILE_C = 32, 1024


def coords():
    f = lax.axis_index("fsdp")
    return (lax.axis_index("section"), f // 4, f // 2 % 2, f % 2)


def device(y, z, x, c):
    return (y, z * 4 + x * 2 + c)


def greet(peers):
    barrier = pltpu.get_barrier_semaphore()
    for peer in peers:
        pl.semaphore_signal(barrier, inc=1, device_id=peer, device_id_type=MESH)
    pl.semaphore_wait(barrier, len(peers))


def send(src, dst, send_sem, recv_sem, peer):
    pltpu.make_async_remote_copy(
        src_ref=src,
        dst_ref=dst,
        send_sem=send_sem,
        recv_sem=recv_sem,
        device_id=peer,
        device_id_type=MESH,
    ).start()


def settle(ref, sem):
    pltpu.make_async_copy(ref, ref, sem).wait()


def gather_kernel(pieces, count, carried, *refs):
    y, f = (lax.axis_index("section"), lax.axis_index("fsdp"))
    z, x, c = coords()[1:]
    in_line = [((z + k) % 4) * 4 + x * 2 + c for k in range(1, 4)]
    near = [f + 2 - 4 * x, f + 1 - 2 * c]
    away = [(f + k) % 16 for k in range(1, 16)] if carried else in_line + near
    greet([device(1 - y, z, x, c)] + [(y, peer) for peer in away])
    for section in range(2):
        pl.when(y == section)(functools.partial(gather_section, section, pieces, count, carried, *refs))


def gather_section(y, pieces, count, carried, *refs):
    given = count + carried
    blocks, outs = (refs[:count], refs[given : given + 2 * count])
    send_sem, recv_sem, sib_sem, own_sem, carry_sem = refs[given + 2 * count + carried :]
    z, x, c = coords()[1:]
    to_x, to_y, to_sib = (device(y, z, 1 - x, c), device(1 - y, z, x, c), device(y, z, x, 1 - c))
    zs = [(z + k) % 4 for k in range(4)]

    def part(ref, p):
        return ref.at[pl.ds(pieces[p][1], pieces[p][2])]

    def there(p, o):
        return part(outs[o[0] * count + pieces[p][0]].at[o[1] * 4 + o[2] * 2 + c], p)

    def mark(p, o):
        return recv_sem.at[p, o[0] * 8 + o[1] * 2 + o[2]]

    def push(p, o, peer, own=False, sib=False):
        src = part(blocks[pieces[p][0]], p) if own else there(p, o)
        send(src, there(p, o), send_sem.at[p], sib_sem.at[p] if sib else mark(p, o), peer)

    every = range(len(pieces))
    for p in every:
        me = (y, z, x)
        push(p, me, to_x, own=True)
        push(p, me, to_y, own=True)
        for zz in zs[1:]:
            push(p, me, device(y, zz, x, c), own=True)
        push(p, me, to_sib, own=True, sib=True)
        pltpu.make_async_copy(part(blocks[pieces[p][0]], p), there(p, me), own_sem).start()
    if carried:
        rows, got = (refs[count], refs[given + 2 * count])
        f = lax.axis_index("fsdp")
        for k in range(1, 16):
            peer = (f + k) % 16
            send(rows.at[peer], got.at[f], carry_sem.at[0], carry_sem.at[1], (y, peer))
        pltpu.make_async_copy(rows.at[f], got.at[f], carry_sem.at[2]).start()

    def from_x(p, zz):
        o = (y, zz, 1 - x)
        settle(there(p, o), mark(p, o))
        if pieces[p][3] == 0:
            push(p, o, to_y)
        push(p, o, to_sib, sib=True)

    def from_y(p, zz):
        o = (1 - y, zz, x)
        settle(there(p, o), mark(p, o))
        if pieces[p][3] == 1:
            push(p, o, to_x)
        push(p, o, to_sib, sib=True)

    for p in every:
        for zz in zs[1:]:
            o = (y, zz, x)
            settle(there(p, o), mark(p, o))
            push(p, o, to_x)
            push(p, o, to_y)
            push(p, o, to_sib, sib=True)
        from_x(p, z)
        from_y(p, z)
    for p in every:
        for zz in zs[1:]:
            from_x(p, zz)
            from_y(p, zz)
    for p in every:
        for zz in zs:
            o = (1 - y, zz, 1 - x)
            settle(there(p, o), mark(p, o))
            push(p, o, to_sib, sib=True)
    for p in every:
        a, start, rows_each, unused = pieces[p]
        settle(part(blocks[a], p), own_sem)
        for times in (16, 15):
            settle(outs[a].at[pl.ds(0, times), pl.ds(start, rows_each)], send_sem.at[p])
        settle(outs[a].at[pl.ds(0, 16), pl.ds(start, rows_each)], sib_sem.at[p])
    if carried:
        settle(rows.at[pl.ds(0, 15)], carry_sem.at[0])
        settle(rows.at[pl.ds(0, 15)], carry_sem.at[1])
        settle(rows.at[0], carry_sem.at[2])


def gather_all(blocks, pieces, name, rows=None):
    many = len(pieces)
    extra = [] if rows is None else [rows]
    shapes = [jax.ShapeDtypeStruct((16,) + b.shape, b.dtype) for b in blocks] * 2
    shapes += [jax.ShapeDtypeStruct(e.shape, e.dtype) for e in extra]
    return pl.pallas_call(
        functools.partial(gather_kernel, pieces, len(blocks), len(extra)),
        out_shape=shapes,
        in_specs=[ANYWHERE] * (len(blocks) + len(extra)),
        out_specs=[ANYWHERE] * len(shapes),
        scratch_shapes=[
            pltpu.SemaphoreType.DMA((many,)),
            pltpu.SemaphoreType.DMA((many, 16)),
            pltpu.SemaphoreType.DMA((many,)),
            pltpu.SemaphoreType.DMA,
            pltpu.SemaphoreType.DMA((3,)),
        ],
        compiler_params=pltpu.CompilerParams(collective_id=name, has_side_effects=True),
    )(*blocks, *extra)


def reduce_pieces(shapes):
    out = []
    for a, (rows, cols) in enumerate(shapes):
        for row in range(0, rows, TILE_R):
            for col in range(0, cols, TILE_C):
                out.append((a, row, col, min(TILE_C, cols - col)))
    return out


def reduce_kernel(pieces, count, carried, lag, *refs):
    grads = (refs[:count], refs[count : 2 * count])
    outs = refs[2 * count + carried : 3 * count + carried]
    held, from_one, from_two, from_z, mine = refs[3 * count + 2 * carried : 3 * count + 2 * carried + 5]
    sib_recv, sib_send, recv_one, send_one, recv_two, send_two, recv_z, send_z, own_sem, carry_sem = refs[
        3 * count + 2 * carried + 5 :
    ]
    y, z, x, c = coords()
    to_x, to_y, to_sib = (device(y, z, 1 - x, c), device(1 - y, z, x, c), device(y, z, x, 1 - c))
    zs = [(z + k) % 4 for k in range(4)]
    many = len(pieces)
    f = lax.axis_index("fsdp")
    alike = [(y, (f + k) % 16) for k in range(1, 16)]
    near = [to_x, to_sib] + [device(y, zz, x, c) for zz in zs[1:]]
    greet([to_y] + (alike if carried else near))

    def source(p, yo, xo, core):
        a, row, col, cols = pieces[p]
        return grads[yo][a].at[:, xo, core, pl.ds(row, TILE_R), pl.ds(col, cols)]

    def cut(ref, p):
        cols = pieces[p][3]
        return ref if cols == TILE_C else ref.at[..., pl.ds(0, cols)]

    def fetch(p):
        for yo in range(2):
            for xo in range(2):
                pltpu.make_async_copy(
                    source(p, yo, xo, c), cut(mine.at[p % 2, yo, xo], p), own_sem.at[p % 2]
                ).start()

    for p in range(many):
        for yo in range(2):
            for xo in range(2):
                send(
                    source(p, yo, xo, 1 - c),
                    cut(held.at[p, yo, xo], p),
                    sib_send.at[p],
                    sib_recv.at[p],
                    to_sib,
                )
        if p == 0:
            fetch(0)
    if carried:
        rows, got = (refs[2 * count], refs[3 * count + carried])
        for peer in alike:
            send(rows.at[peer[1]], got.at[y * 16 + f], carry_sem.at[0], carry_sem.at[1], peer)
        pltpu.make_async_copy(rows.at[f], got.at[y * 16 + f], carry_sem.at[2]).start()

    def pass_on():
        settle(rows.at[pl.ds(0, 15)], carry_sem.at[1])
        settle(rows.at[0], carry_sem.at[2])
        ours = got.at[pl.ds(y * 16, 16)]
        send(ours, ours, carry_sem.at[3], carry_sem.at[4], to_y)

    def y_first(p):
        return p % 2 == 0

    def add(dst, src, p):
        cols = pl.ds(0, pieces[p][3])
        dst[:, cols] = (dst[:, cols].astype(jnp.float32) + src[:, cols].astype(jnp.float32)).astype(LOW)

    def two_cores(p):
        if p + 1 < many:
            fetch(p + 1)
        settle(cut(mine.at[p % 2], p), own_sem.at[p % 2])
        settle(cut(held.at[p], p), sib_recv.at[p])

        def each(i, carry):
            yo, xo, zo = (i // 8, i // 4 % 2, i % 4)
            add(held.at[p, yo, xo, zo], mine.at[p % 2, yo, xo, zo], p)
            return carry

        lax.fori_loop(0, 16, each, 0)
        if y_first(p):
            send(cut(held.at[p, 1 - y], p), cut(from_one.at[p], p), send_one.at[p], recv_one.at[p], to_y)
        else:
            for yo in range(2):
                send(
                    cut(held.at[p, yo, 1 - x], p),
                    cut(from_one.at[p, yo], p),
                    send_one.at[p],
                    recv_one.at[p],
                    to_x,
                )

    def first_axis(p):
        settle(cut(from_one.at[p], p), recv_one.at[p])

        def each(i, carry):
            if y_first(p):
                add(held.at[p, y, i // 4, i % 4], from_one.at[p, i // 4, i % 4], p)
            else:
                add(held.at[p, i // 4, x, i % 4], from_one.at[p, i // 4, i % 4], p)
            return carry

        lax.fori_loop(0, 8, each, 0)
        if y_first(p):
            src, peer = (held.at[p, y, 1 - x], to_x)
        else:
            src, peer = (held.at[p, 1 - y, x], to_y)
        send(cut(src, p), cut(from_two.at[p], p), send_two.at[p], recv_two.at[p], peer)

    def second_axis(p):
        settle(cut(from_two.at[p], p), recv_two.at[p])

        def each(i, carry):
            add(held.at[p, y, x, i], from_two.at[p, i], p)
            return carry

        lax.fori_loop(0, 4, each, 0)
        for k in range(1, 4):
            send(
                cut(held.at[p, y, x, zs[k]], p),
                cut(from_z.at[p, 3 - k], p),
                send_z.at[p],
                recv_z.at[p],
                device(y, zs[k], x, c),
            )

    def along_z(p):
        settle(cut(from_z.at[p], p), recv_z.at[p])
        a, row, col, cols = pieces[p]
        part = pl.ds(0, cols)
        total = held[p, y, x, z, :, part].astype(jnp.float32)
        for k in range(3):
            total = total + from_z[p, k, :, part].astype(jnp.float32)
        outs[a][pl.ds(row, TILE_R), pl.ds(col, cols)] = total

    for step in range(many + 3 * lag):
        if carried and step == many // 2:
            pass_on()
        for k, stage in enumerate((two_cores, first_axis, second_axis, along_z)):
            if 0 <= step - k * lag < many:
                stage(step - k * lag)
    for p in range(many):
        settle(cut(held.at[p], p), sib_send.at[p])
        settle(cut(from_one.at[p], p), send_one.at[p])
        settle(cut(from_two.at[p], p), send_two.at[p])
        settle(cut(from_z.at[p], p), send_z.at[p])
    if carried:
        settle(rows.at[pl.ds(0, 15)], carry_sem.at[0])
        settle(rows, carry_sem.at[3])
        settle(rows, carry_sem.at[4])


def reduce_all(grads, name, lag, rows=None):
    count = len(grads[0])
    shapes = [(g.shape[0] // 16, g.shape[1]) for g in grads[0]]
    pieces = reduce_pieces(shapes)
    many = len(pieces)
    views = [g.reshape(4, 2, 2, g.shape[0] // 16, g.shape[1]) for layer in grads for g in layer]
    extra = [] if rows is None else [rows]
    return pl.pallas_call(
        functools.partial(reduce_kernel, pieces, count, len(extra), lag),
        out_shape=[jax.ShapeDtypeStruct(s, jnp.float32) for s in shapes]
        + [jax.ShapeDtypeStruct((32,) + e.shape[1:], e.dtype) for e in extra],
        in_specs=[ANYWHERE] * (len(views) + len(extra)),
        out_specs=[IN_VMEM] * count + [ANYWHERE] * len(extra),
        scratch_shapes=[
            pltpu.VMEM((many, 2, 2, 4, TILE_R, TILE_C), LOW),
            pltpu.VMEM((many, 2, 4, TILE_R, TILE_C), LOW),
            pltpu.VMEM((many, 4, TILE_R, TILE_C), LOW),
            pltpu.VMEM((many, 3, TILE_R, TILE_C), LOW),
            pltpu.VMEM((2, 2, 2, 4, TILE_R, TILE_C), LOW),
        ]
        + [pltpu.SemaphoreType.DMA((many,)) for unused in range(8)]
        + [pltpu.SemaphoreType.DMA((2,)), pltpu.SemaphoreType.DMA((5,))],
        compiler_params=pltpu.CompilerParams(
            collective_id=name,
            has_side_effects=True,
            vmem_limit_bytes=(12 + 3 * many) * 2**20 if many < 16 else 58 * 2**20,
        ),
    )(*views, *extra)


def exchange_kernel(whole, src, out, send_sem, recv_sem, own_sem):
    y, f = (lax.axis_index("section"), lax.axis_index("fsdp"))
    count = 32 if whole else 16
    me = y * 16 + f if whole else f
    peers = [(me + k) % count for k in range(1, count)]
    where = [(p // 16, p % 16) if whole else (y, p) for p in peers]
    greet(where)
    for peer in where:
        send(src, out.at[me], send_sem, recv_sem, peer)
    own = pltpu.make_async_copy(src, out.at[me], own_sem)
    own.start()
    own.wait()
    settle(out.at[pl.ds(0, count - 1)], send_sem)
    settle(out.at[pl.ds(0, count - 1)], recv_sem)


def exchange(small, name, whole=True):
    return pl.pallas_call(
        functools.partial(exchange_kernel, whole),
        out_shape=jax.ShapeDtypeStruct((32 if whole else 16,) + small.shape, small.dtype),
        in_specs=[IN_VMEM],
        out_specs=IN_VMEM,
        scratch_shapes=[pltpu.SemaphoreType.DMA] * 3,
        compiler_params=pltpu.CompilerParams(collective_id=name, has_side_effects=True),
    )(small)


def tall_of(height, sections=2):
    return 256 if height % (256 * sections) == 0 else 128


def whole(shape):
    return pl.BlockSpec(shape, lambda *unused: (0,) * len(shape), pipeline_mode=pl.Buffered(1))


def striped(tall, cols):
    return pl.BlockSpec((tall, cols), lambda i: (i, 0))


def lined(rows, wide):
    return pl.BlockSpec((rows, wide), lambda i: (0, i))


def squares_of(value):
    return jnp.sum(jnp.sum(value * value, axis=1, keepdims=True), axis=0, keepdims=True)


def padded_table_kernel(asked, sel, table, low, rows, total):
    step = pl.program_id(0)

    @pl.when(step == 0)
    def start():
        total[...] = jnp.zeros_like(total)

    width, tall = table.shape
    low[:, pl.ds(low.shape[1] - 128, 128)] = jnp.zeros((tall, 128), LOW)
    eye = lax.broadcasted_iota(jnp.int32, (tall, tall), 0) == lax.broadcasted_iota(jnp.int32, (tall, tall), 1)
    low[:, pl.ds(0, width)] = dense_nt(eye.astype(LOW), table[...].astype(LOW)).astype(LOW)
    place = lax.broadcasted_iota(jnp.int32, (asked.shape[0], tall), 1) + step * tall
    total[...] += dense((asked[...] == place).astype(LOW), low[...])

    @pl.when(step == pl.num_programs(0) - 1)
    def end():
        rows[...] = dense(total[...].astype(LOW), sel[...]).astype(LOW)


def padded_table(asked, sel, table):
    width, height = table.shape
    wide = sel.shape[0]
    count = asked.shape[0]
    tall = tall_of(height)
    return pl.pallas_call(
        padded_table_kernel,
        grid=(height // tall,),
        out_shape=[
            jax.ShapeDtypeStruct((height, wide), LOW),
            jax.ShapeDtypeStruct((count, sel.shape[1]), LOW),
        ],
        in_specs=[whole((count, 1)), whole(sel.shape), lined(width, tall)],
        out_specs=[striped(tall, wide), whole((count, sel.shape[1]))],
        scratch_shapes=[pltpu.VMEM((count, wide), jnp.float32)],
        compiler_params=pltpu.CompilerParams(vmem_limit_bytes=48 * 2**20),
    )(asked[:, None], sel, table)


def logits_kernel(wanted, rows, table, logits, top, total, target):
    step = pl.program_id(0)

    @pl.when(step == 0)
    def start():
        top[...] = jnp.full_like(top, -jnp.inf)
        total[...] = jnp.zeros_like(total)
        target[...] = jnp.zeros_like(target)

    here = dense_nt(table[...], rows[...])
    logits[...] = here
    higher = jnp.maximum(top[...], jnp.max(here, axis=0, keepdims=True))
    total[...] = total[...] * jnp.exp(top[...] - higher) + jnp.sum(
        jnp.exp(here - higher), axis=0, keepdims=True
    )
    top[...] = higher
    place = lax.broadcasted_iota(jnp.int32, here.shape, 0) + step * here.shape[0]
    target[...] += jnp.sum(jnp.where(place == wanted[...], here, 0.0), axis=0, keepdims=True)


def logits_of(wanted, rows, table):
    height, wide = table.shape
    count = rows.shape[0]
    tall = tall_of(height)
    line = jax.ShapeDtypeStruct((1, count), jnp.float32)
    return pl.pallas_call(
        logits_kernel,
        grid=(height // tall,),
        out_shape=[jax.ShapeDtypeStruct((height, count), jnp.float32), line, line, line],
        in_specs=[whole((1, count)), whole(rows.shape), striped(tall, wide)],
        out_specs=[striped(tall, count)] + [whole((1, count))] * 3,
        compiler_params=pltpu.CompilerParams(vmem_limit_bytes=48 * 2**20),
    )(wanted[None], rows, table)


def logits_back_kernel(share, section, wanted, top, scale, push, logits, table, grad, rows, total):
    step = pl.program_id(1)
    mine = (step >= section[0] * share) & (step < (section[0] + 1) * share)

    @pl.when(step == 0)
    def start():
        total[...] = jnp.zeros_like(total)

    here = logits[...]
    place = lax.broadcasted_iota(jnp.int32, here.shape, 0) + step * here.shape[0]
    hit = jnp.where(place == wanted[...], push[...], 0.0)
    low = (hit - jnp.exp(here - top[...]) * scale[...]).astype(LOW)
    grad[...] = low

    @pl.when(mine)
    def add():
        total[...] += dense_t(low, table[...])

    @pl.when(step == pl.num_programs(1) - 1)
    def end():
        rows[...] = total[...].astype(LOW)


def logits_back(section, wanted, top, scale, push, logits, table, sections):
    height, wide = table.shape
    count = logits.shape[1]
    tall = tall_of(height, sections)
    block = min(count, 2048)
    line = pl.BlockSpec((1, block), lambda j, i: (0, j))
    tile = pl.BlockSpec((tall, block), lambda j, i: (i, j))
    return pl.pallas_call(
        functools.partial(logits_back_kernel, height // tall // sections),
        grid=(count // block, height // tall),
        out_shape=[
            jax.ShapeDtypeStruct((height, count), LOW),
            jax.ShapeDtypeStruct((count, wide), LOW),
        ],
        in_specs=[
            pl.BlockSpec(memory_space=pltpu.SMEM),
            line,
            line,
            line,
            line,
            tile,
            pl.BlockSpec((tall, wide), lambda j, i: (i, 0)),
        ],
        out_specs=[tile, pl.BlockSpec((block, wide), lambda j, i: (j, 0))],
        scratch_shapes=[pltpu.VMEM((block, wide), jnp.float32)],
        compiler_params=pltpu.CompilerParams(vmem_limit_bytes=56 * 2**20),
    )(section[None], wanted[None], top[None], scale[None], push[None], logits, table)


def table_grad_kernel(leader, asked, got, rows, grad_logits, *refs):
    *others, grad, squares = refs
    step = pl.program_id(0)

    @pl.when(step == 0)
    def start():
        gains = others[-1][...]
        total = squares_of(gains[:2]) + leader[0] * squares_of(gains[2:3])
        for other in others[:-1]:
            total += squares_of(other[...])
        squares[...] = jnp.broadcast_to(total, squares.shape)

    width, tall = grad.shape
    place = lax.broadcasted_iota(jnp.int32, (tall, asked.shape[1]), 0) + step * tall
    here = dense_nt(rows[...], grad_logits[...]) + dense_nt(got[...], (asked[...] == place).astype(LOW))
    here = here[:width]
    grad[...] = here
    squares[pl.ds(0, 1)] += leader[0] * squares_of(here)


def table_grad(leader, asked, got, rows, grad_logits, others, width):
    height, count = grad_logits.shape
    tall = tall_of(height)
    return pl.pallas_call(
        table_grad_kernel,
        grid=(height // tall,),
        out_shape=[
            jax.ShapeDtypeStruct((width, height), jnp.float32),
            jax.ShapeDtypeStruct((8, 128), jnp.float32),
        ],
        in_specs=[
            pl.BlockSpec(memory_space=pltpu.SMEM),
            whole((1, asked.shape[0])),
            whole(got.shape),
            whole(rows.shape),
            striped(tall, count),
        ]
        + [whole(o.shape) for o in others],
        out_specs=[lined(width, tall), whole((8, 128))],
        compiler_params=pltpu.CompilerParams(vmem_limit_bytes=56 * 2**20),
    )(leader[None], asked[None], got, rows, grad_logits, *others)


def exact_product(left, onehot):
    high = left.astype(LOW)
    rest = left - high.astype(jnp.float32)
    middle = rest.astype(LOW)
    lowest = (rest - middle.astype(jnp.float32)).astype(LOW)
    return dense_nt(high, onehot) + (dense_nt(middle, onehot) + dense_nt(lowest, onehot))


ROWED = 3
SPREAD = (1, 3)


def moments_kernel(decays, clip, sel, *refs):
    weights, grads, firsts, seconds = (refs[7 * k : 7 * k + 7] for k in range(4))
    new_firsts, new_seconds, updates = (refs[28 + 7 * k : 35 + 7 * k] for k in range(3))
    kept, sums, *scratch = refs[49:49 + ROWED] , refs[49 + ROWED], *refs[50 + ROWED:]
    staged = [scratch[5 * k : 5 * k + 5] for k in range(ROWED)]
    in_sem, out_sem = scratch[5 * ROWED :]
    step, steps = (pl.program_id(0), pl.num_programs(0))

    def copies(k, inward):
        w, m, v, new_m, new_v = staged[k]
        if inward:
            pairs = [(weights[k + 1].at[:, 0], w), (firsts[k + 1].at[:, 0], m), (seconds[k + 1].at[:, 0], v)]
        else:
            pairs = [(new_m, new_firsts[k + 1].at[:, 0]), (new_v, new_seconds[k + 1].at[:, 0])]
        return [
            pltpu.make_async_copy(src, dst, (in_sem if inward else out_sem).at[k, i])
            for i, (src, dst) in enumerate(pairs)
        ]

    @pl.when(step == 0)
    def start():
        sums[...] = jnp.zeros_like(sums)
        for k in range(ROWED):
            for copy in copies(k, True):
                copy.start()

    def one(weight, grad, first, second, decay):
        return (weight,) + lamb_parts(weight, clip[0] * grad, first, second, decay)

    weight, new_firsts[0][...], new_seconds[0][...], update = one(
        weights[0][...], grads[0][...], firsts[0][...], seconds[0][...], decays[0]
    )
    updates[0][...] = update
    sums[pl.ds(0, 1)] += squares_of(weight)
    sums[pl.ds(8, 1)] += squares_of(update)

    def tensor(k):
        rows, cols = updates[k + 1].shape
        grad = grads[k + 1][pl.ds(0, rows)]
        grad = exact_product(grad, sel[...]) if k in SPREAD else grad[:, :cols]
        if k < ROWED:
            for copy in copies(k, True):
                copy.wait()
            w, m, v, new_m, new_v = staged[k]
        else:
            w, m, v, new_m, new_v = (t[k + 1] for t in (weights, firsts, seconds, new_firsts, new_seconds))
        weight, new_m[...], new_v[...], update = one(w[...], grad, m[...], v[...], decays[k + 1])
        updates[k + 1][...] = update
        if k < ROWED:
            kept[k][...] = weight
            for copy in copies(k, False):
                copy.start()
        for row in range(rows if k == 4 else 1):
            part = slice(row, row + 1) if k == 4 else slice(None)
            line = k + 1 + row + (k > 4)
            sums[pl.ds(line, 1)] += squares_of(weight[part])
            sums[pl.ds(8 + line, 1)] += squares_of(update[part])

    for k in range(6):
        pl.when(step == min(k + 1, 5) % steps)(functools.partial(tensor, k))

    @pl.when(step == steps - 1)
    def end():
        for k in range(ROWED):
            for copy in copies(k, False):
                copy.wait()


def moments(clip, sel, weights, grads, firsts, seconds, decays):
    width, height = weights[0].shape
    tall = tall_of(height)
    flat = [w.shape if w.ndim == 2 else w.shape[::2] for w in weights]

    def specs(arrays, results=False):
        out = [lined(width, tall)]
        for a in arrays[1:]:
            out.append(ANYWHERE if a.ndim == 3 else whole(a.shape))
        return out

    line = [jax.ShapeDtypeStruct(w.shape, jnp.float32) for w in weights]
    plain = [jax.ShapeDtypeStruct(s, jnp.float32) for s in flat]
    kept = plain[1 : 1 + ROWED]
    out = pl.pallas_call(
        functools.partial(moments_kernel, decays),
        grid=(height // tall,),
        out_shape=line * 2 + plain + kept + [jax.ShapeDtypeStruct((16, 128), jnp.float32)],
        in_specs=[pl.BlockSpec(memory_space=pltpu.SMEM), whole(sel.shape)]
        + specs(weights)
        + specs(grads)
        + specs(firsts)
        + specs(seconds),
        out_specs=specs(line) * 2 + specs(plain) + [whole(s.shape) for s in kept] + [whole((16, 128))],
        scratch_shapes=[pltpu.VMEM(s.shape, jnp.float32) for s in kept for unused in range(5)]
        + [pltpu.SemaphoreType.DMA((ROWED, 3)), pltpu.SemaphoreType.DMA((ROWED, 2))],
        compiler_params=pltpu.CompilerParams(vmem_limit_bytes=60 * 2**20),
    )(clip[None], sel, *weights, *grads, *firsts, *seconds)
    return (out[:7], out[7:14], out[14:21], out[21 : 21 + ROWED], out[21 + ROWED])


def apply_kernel(scales, *refs):
    weights, updates, new, half = (refs[5 * k : 5 * k + 5] for k in range(4))
    staged, sem = (refs[20 : 20 + ROWED], refs[20 + ROWED])
    step, steps = (pl.program_id(0), pl.num_programs(0))

    def copy(k):
        return pltpu.make_async_copy(staged[k - 1], new[k].at[:, 0], sem.at[k - 1])

    def one(k):
        value = weights[k][...] - RATE * scales[k] * updates[k][...]
        half[k][...] = value.astype(LOW)
        if 0 < k <= ROWED:
            staged[k - 1][...] = value
            copy(k).start()
        else:
            new[k][...] = value

    one(0)
    for k in range(1, 5):
        pl.when(step == (k - 1) % steps)(functools.partial(one, k))

    @pl.when(step == steps - 1)
    def end():
        for k in range(1, 1 + ROWED):
            copy(k).wait()


def apply_updates(scales, weights, updates, shapes):
    width, height = weights[0].shape
    tall = tall_of(height)
    plain = [lined(width, tall)] + [whole(w.shape) for w in weights[1:]]
    out = pl.pallas_call(
        apply_kernel,
        grid=(height // tall,),
        out_shape=[jax.ShapeDtypeStruct(s, jnp.float32) for s in shapes]
        + [jax.ShapeDtypeStruct(w.shape, LOW) for w in weights],
        in_specs=[pl.BlockSpec(memory_space=pltpu.SMEM)] + plain * 2,
        out_specs=plain[:1] + [ANYWHERE] * ROWED + plain[1 + ROWED :] + plain,
        scratch_shapes=[pltpu.VMEM(w.shape, jnp.float32) for w in weights[1 : 1 + ROWED]]
        + [pltpu.SemaphoreType.DMA((ROWED,))],
        compiler_params=pltpu.CompilerParams(vmem_limit_bytes=56 * 2**20),
    )(scales, *weights, *updates)
    return (out[:5], out[5:])


def up16(count):
    return -(-count // 16) * 16


def dense(left, right):
    return jnp.dot(left, right, preferred_element_type=jnp.float32)


def dense_t(left, right):
    return lax.dot_general(
        left, right, (((0,), (0,)), ((), ())), preferred_element_type=jnp.float32
    )


def dense_nt(left, right):
    return lax.dot_general(
        left, right, (((1,), (1,)), ((), ())), preferred_element_type=jnp.float32
    )


def spread_matrix(parts, real, padded):
    feature = jnp.arange(parts * real)
    place = feature // real * padded + feature % real
    return (place[:, None] == jnp.arange(parts * padded)[None, :]).astype(LOW)


def inverse_rms(x, width):
    return lax.rsqrt(jnp.sum(x * x, axis=-1, keepdims=True) / width + EPS)


def norm_back(x, scale, gain, upstream, width):
    inner = upstream * gain
    grad_gain = jnp.sum(upstream * x * scale, axis=0)
    mean = jnp.sum(inner * x, axis=-1, keepdims=True) / width
    return (scale * inner - x * scale**3 * mean, grad_gain)


def rotate(x, cosine, sine):
    half = x.shape[-1] // 2
    first, second = (x[..., :half], x[..., half:])
    return jnp.concatenate(
        [first * cosine - second * sine, second * cosine + first * sine], axis=-1
    )


def rotate_back(grad, cosine, sine):
    return rotate(grad, cosine, -sine)


def rotary_angles(place):
    rotary = jnp.where(place >= PROMPT, PROMPT + (place - PROMPT) % CONT, place).astype(jnp.float32)
    freq = THETA ** (-2.0 * jnp.arange(HD // 2).astype(jnp.float32) / HD)
    angle = rotary[:, None] * freq[None, :]
    return (jnp.cos(angle)[:, None, :], jnp.sin(angle)[:, None, :])


def may_attend(place):
    keys = jnp.arange(TOK_MB)

    def segment(p):
        return jnp.where(p >= PROMPT, 1 + (p - PROMPT) // CONT, 0)

    return (keys[None, :] <= place[:, None]) & (
        (segment(keys)[None, :] == 0) | (segment(keys)[None, :] == segment(place)[:, None])
    )


def attend(query, key, value, allowed):
    scores = jnp.einsum("qhgd,khd->hgqk", query, key, preferred_element_type=jnp.float32) * SCALE
    scores = jnp.where(allowed, scores, -1e30)
    expo = jnp.exp(scores - jnp.max(scores, axis=-1, keepdims=True))
    probs = expo / jnp.sum(expo, axis=-1, keepdims=True)
    out = jnp.einsum("hgqk,khd->qhgd", probs.astype(LOW), value, preferred_element_type=jnp.float32)
    return (out.reshape(-1, WIDTH).astype(LOW), probs)


def attend_back(query, key, value, probs, grad):
    grad = grad.reshape(-1, KV, HEADS // KV, HD)
    grad_probs = jnp.einsum("qhgd,khd->hgqk", grad, value, preferred_element_type=jnp.float32)
    grad_scores = probs * (grad_probs - jnp.sum(grad_probs * probs, axis=-1, keepdims=True))
    grad_scores = grad_scores.astype(LOW)
    grad_query = (
        jnp.einsum("hgqk,khd->qhgd", grad_scores, key, preferred_element_type=jnp.float32) * SCALE
    )
    grad_key = (
        jnp.einsum("hgqk,qhgd->khd", grad_scores, query, preferred_element_type=jnp.float32) * SCALE
    )
    grad_value = jnp.einsum(
        "hgqk,qhgd->khd", probs.astype(LOW), grad, preferred_element_type=jnp.float32
    )
    return (grad_query.reshape(-1, HEADS, HD), grad_key, grad_value)


def heads_of(q, cosine, sine):
    return (
        rotate(q.reshape(-1, HEADS, HD), cosine, sine).astype(LOW).reshape(-1, KV, HEADS // KV, HD)
    )


def keys_values(kv, cosine, sine):
    key = rotate(kv[:, :KVW].reshape(-1, KV, HD), cosine, sine).astype(LOW)
    return (key, kv[:, KVW:].reshape(-1, KV, HD).astype(LOW))


def mlp(b, w_gu, w_down):
    gate_up = dense(b, w_gu)
    half = gate_up.shape[1] // 2
    gate, upper = (gate_up[:, :half], gate_up[:, half:])
    hidden = (jax.nn.silu(gate) * upper).astype(LOW)
    return (dense(hidden, w_down), gate, upper, hidden)


def mlp_back(branch, b, gate, upper, hidden, w_gu, w_down):
    grad_down = dense_t(hidden, branch)
    grad_hidden = dense_nt(branch, w_down)
    sig = jax.nn.sigmoid(gate)
    grad_gate = grad_hidden * upper * sig * (1.0 + gate * (1.0 - sig))
    grad_upper = grad_hidden * gate * sig
    grad_gate_up = jnp.concatenate([grad_gate, grad_upper], axis=1).astype(LOW)
    return (grad_down, dense_t(b, grad_gate_up), dense_nt(grad_gate_up, w_gu))


def lamb_parts(weight, grad, first, second, decay):
    first_new = BETA_ONE * first + (1.0 - BETA_ONE) * grad
    second_new = BETA_TWO * second + (1.0 - BETA_TWO) * grad * grad
    root = (1.0 - BETA_TWO**STEP) ** 0.5
    scale = root / (1.0 - BETA_ONE**STEP)
    update = first_new * scale / (second_new * lax.rsqrt(second_new) + ADAM_EPS * root) + decay * weight
    return (first_new, second_new, update)


def lookup_ranks(ids, vshard):
    place = jnp.arange(ids.shape[0])
    same = ids[:, None] == ids[None, :]
    first = jnp.min(jnp.where(same, place[None, :], ids.shape[0]), axis=1)
    owner = ids // vshard
    before = (
        (owner[:, None] == owner[None, :])
        & (first == place)[None, :]
        & (place[None, :] < first[:, None])
    )
    return (owner, jnp.sum(before.astype(jnp.int32), axis=1))


def lookup_round(ids, owner, rank, turn, slots, parts, vshard):
    slot = jnp.where(rank // slots == turn, owner * slots + rank - turn * slots, -1)
    onehot = slot[:, None] == jnp.arange(parts * slots)[None, :]
    wanted = jnp.max(jnp.where(onehot, (ids - owner * vshard)[:, None], -1), axis=0)
    return (onehot.astype(LOW), wanted)


def shards(
    token_ids,
    scored,
    targets,
    pairs,
    table,
    w_qkv,
    w_out,
    w_gu,
    w_down,
    gains,
    final_gain,
    first_table,
    first_qkv,
    first_out,
    first_gu,
    first_down,
    first_gains,
    first_final,
    second_table,
    second_qkv,
    second_out,
    second_gu,
    second_down,
    second_gains,
    second_final,
):
    n = lax.axis_size("fsdp")
    sections = lax.axis_size("section")
    section_index = lax.axis_index("section")
    fsdp_index = lax.axis_index("fsdp")
    leader = section_index == 0
    vshard, width = table.shape
    vstart = fsdp_index * vshard
    r = w_qkv.shape[1]
    rp = up16(r)
    rd = w_down.shape[1]
    rdp = up16(rd)
    wide = n * rp
    ffp = n * rdp
    slots = up16(768 // n)
    sel = spread_matrix(n, r, rp)
    sel_wide = jnp.pad(sel, ((0, wide - width), (0, 0)))
    fast = (sections, n) == (2, 16)
    qkv_wide = -(-w_qkv.shape[2] // 128) * 128

    qkv_block = jnp.pad(
        w_qkv[0].astype(LOW), ((0, rp - r), (0, qkv_wide - w_qkv.shape[2]))
    )
    out_block = jnp.pad(dense(w_out[0].astype(LOW), sel).astype(LOW), ((0, rp - r), (0, 0)))
    gu_block = w_gu[0].astype(LOW)
    if rdp != rd:
        gu_block = jnp.pad(gu_block.reshape(r, 2, n, rd), ((0, 0), (0, 0), (0, 0), (0, rdp - rd)))
    gu_block = jnp.pad(gu_block.reshape(r, 2 * ffp), ((0, rp - r), (0, 0)))
    down_block = jnp.pad(dense(w_down[0].astype(LOW), sel).astype(LOW), ((0, rdp - rd), (0, 0)))
    gain_block = jnp.pad(
        jnp.concatenate([gains[0], final_gain[None]], axis=0).astype(LOW),
        ((0, 13), (0, 128 - r)),
    )

    ids = token_ids[0]
    owner, rank = lookup_ranks(ids, vshard)
    onehot, wanted = lookup_round(ids, owner, rank, 0, slots, n, vshard)
    turns_here = jnp.max(rank) // slots + 1
    own_targets = lax.dynamic_slice_in_dim(targets[0], fsdp_index * NCONT, NCONT).reshape(-1)
    note = jnp.concatenate(
        [wanted, jnp.pad(own_targets, (0, 128 - NCONT * SCORED)), jnp.full((128,), turns_here, jnp.int32)]
    )
    if fast:
        notes = exchange(note.reshape(-1, 128), 0).reshape(sections * n, -1)
    else:
        notes = lax.all_gather(note, BOTH, axis=0)
    turns = jnp.max(notes[:, -1])
    wanted_rows = notes[:, n * slots : n * slots + NCONT * SCORED].reshape(-1)

    def asked(all_wanted):
        mine = lax.dynamic_slice_in_dim(all_wanted.reshape(sections, n, n, slots), fsdp_index, 1, 2)
        return mine[:, :, 0]

    asked_first = asked(notes[:, : n * slots])
    asked_here = lax.dynamic_index_in_dim(asked_first, section_index, 0, keepdims=False).reshape(-1)
    table_low, rows = padded_table(asked_here, sel_wide, table.T)
    rows = rows.reshape(n, slots, wide)

    blocks = (qkv_block, out_block, gu_block, down_block, gain_block)
    if fast:
        gathered = gather_all(blocks, WEIGHT_PIECES, 1, rows)
        got = gathered[10]
        gathered = (gathered[:5], gathered[5:10])
    else:
        got = lax.all_to_all(rows, "fsdp", 0, 0)
        gathered = [lax.all_gather(block, BOTH, axis=0) for block in blocks]
        gathered = [[g[k * n : (k + 1) * n] for g in gathered] for k in range(sections)]
    qkv_all, out_all, gu_all, down_all, gain_all = [
        [section[k].reshape(n * blocks[k].shape[0], -1) for section in gathered] for k in range(5)
    ]
    gain_all = jnp.stack([g.reshape(n, 16, 128)[:, :3, :rp] for g in gain_all])
    gain_all = jnp.moveaxis(gain_all, 2, 1).reshape(sections, 3, wide).astype(jnp.float32)
    final_all = gain_all[0, 2]
    x0 = dense(onehot, got.reshape(n * slots, wide))

    def fetch_more(state):
        turn, total = state
        choose, more = lookup_round(ids, owner, rank, turn, slots, n, vshard)
        here = asked(lax.all_gather(more, BOTH, axis=0))
        here = lax.dynamic_index_in_dim(here, section_index, 0, keepdims=False).reshape(-1)
        rows = dense(jnp.take(table, jnp.maximum(here, 0), axis=0).astype(LOW), sel).astype(LOW)
        got = lax.all_to_all(rows.reshape(n, slots, wide), "fsdp", 0, 0).reshape(n * slots, wide)
        return (turn + 1, total + dense(choose, got))

    x0 = lax.while_loop(lambda state: state[0] < turns, fetch_more, (jnp.int32(1), x0))[1]

    everyone = jnp.arange(TOK_MB)
    cosine, sine = rotary_angles(everyone)
    allowed = may_attend(everyone)
    x = x0
    kept = []
    for layer in range(sections - 1):
        scale_a = inverse_rms(x, width)
        a = (x * scale_a * gain_all[layer, 0]).astype(LOW)
        qkv = dense(a, qkv_all[layer])
        query = heads_of(qkv[:, :WIDTH], cosine, sine)
        key, value = keys_values(qkv[:, WIDTH : WIDTH + 2 * KVW], cosine, sine)
        attended, probs = attend(query, key, value, allowed)
        attended = dense(attended, sel).astype(LOW)
        mixed = x + dense(attended, out_all[layer])
        scale_b = inverse_rms(mixed, width)
        b = (mixed * scale_b * gain_all[layer, 1]).astype(LOW)
        branch, gate, upper, hidden = mlp(b, gu_all[layer], down_all[layer])
        kept.append(
            (x, scale_a, a, query, key, value, probs, attended, mixed, scale_b, b, gate, upper, hidden)
        )
        x = mixed + branch

    last = sections - 1
    place = (PROMPT + CONT * jnp.arange(NCONT)[:, None] + scored[0]).reshape(-1)
    pick = (place[:, None] == everyone[None, :]).astype(LOW)
    pick32 = pick.astype(jnp.float32)
    cosine_s, sine_s = rotary_angles(place)
    allowed_s = may_attend(place)
    scale_last = inverse_rms(x, width)
    a_last = (x * scale_last * gain_all[last, 0]).astype(LOW)
    qkv_last = qkv_all[last][:, WIDTH : WIDTH + 2 * KVW]
    key_last, value_last = keys_values(dense(a_last, qkv_last), cosine, sine)
    a_s = dense(pick, a_last).astype(LOW)
    x_s = jnp.dot(pick32, x, precision=HI)
    query_s = heads_of(dense(a_s, qkv_all[last][:, :WIDTH]), cosine_s, sine_s)
    attended_s, probs_s = attend(query_s, key_last, value_last, allowed_s)
    attended_s = dense(attended_s, sel).astype(LOW)
    mixed_s = x_s + dense(attended_s, out_all[last])
    scale_s = inverse_rms(mixed_s, width)
    b_s = (mixed_s * scale_s * gain_all[last, 1]).astype(LOW)
    branch_s, gate_s, upper_s, hidden_s = mlp(b_s, gu_all[last], down_all[last])
    y_s = mixed_s + branch_s
    scale_y = inverse_rms(y_s, width)
    head_in = dense_nt((y_s * scale_y * final_all).astype(LOW), sel_wide).astype(LOW)

    if fast:
        rows_all = jnp.concatenate(gather_all([head_in], [(0, 16 * k, 16, k % 2) for k in range(4)], 2))
    else:
        rows_all = lax.all_gather(head_in, BOTH, axis=0)
    rows_all = rows_all.reshape(-1, wide)
    own_rows = rows_all.shape[0] // sections
    wanted_here = wanted_rows - vstart
    logits, top_here, total_here, target_here = logits_of(wanted_here, rows_all, table_low)
    stats = jnp.concatenate([top_here, total_here, target_here])
    if fast:
        stats = exchange(stats.reshape(-1, 128), 3, whole=False).reshape(n, 3, -1)
    else:
        stats = lax.all_gather(stats, "fsdp", axis=0)
    top = jnp.max(stats[:, 0], axis=0)
    total = jnp.sum(stats[:, 1] * jnp.exp(stats[:, 0] - top), axis=0)
    row_logp = jnp.sum(stats[:, 2], axis=0) - top - jnp.log(total)
    seq = jnp.sum(row_logp.reshape(-1, SCORED), axis=1)
    pair = pairs.reshape(-1, 2)
    conts = jnp.arange(seq.shape[0])
    chosen = (pair[:, 0][:, None] == conts[None, :]).astype(jnp.float32)
    passed = (pair[:, 1][:, None] == conts[None, :]).astype(jnp.float32)
    delta = jnp.sum((chosen - passed) * seq[None, :], axis=1)
    loss = jnp.sum(jax.nn.softplus(-BETA * delta))
    push = BETA * jax.nn.sigmoid(-BETA * delta)
    grad_seq = jnp.sum((passed - chosen) * push[:, None], axis=0)
    grad_row = jnp.repeat(grad_seq, SCORED)
    grad_logits, grad_rows = logits_back(
        section_index, wanted_here, top, grad_row / total, grad_row, logits, table_low, sections
    )
    if fast:
        halves = [[grad_rows[k * own_rows : (k + 1) * own_rows]] for k in range(sections)]
        grad_head = reduce_all(halves, 4, 1)[0]
    else:
        grad_head = lax.psum_scatter(grad_rows, BOTH, scatter_dimension=0, tiled=True)
    grad_y, grad_final = norm_back(
        y_s, scale_y, final_all, jnp.dot(grad_head.astype(jnp.float32), sel_wide.astype(jnp.float32), precision=HI), width
    )

    grads = [None] * sections
    g_down, g_gu, grad_b = mlp_back(
        grad_y.astype(LOW), b_s, gate_s, upper_s, hidden_s, gu_all[last], down_all[last]
    )
    grad_mid, gain_two = norm_back(mixed_s, scale_s, gain_all[last, 1], grad_b, width)
    grad_mixed = grad_mid + grad_y
    branch = grad_mixed.astype(LOW)
    g_out = dense_t(attended_s, branch)
    grad_att = dense_nt(dense_nt(branch, out_all[last]).astype(LOW), sel).astype(LOW)
    grad_query, grad_key, grad_value = attend_back(query_s, key_last, value_last, probs_s, grad_att)
    grad_q = rotate_back(grad_query, cosine_s, sine_s).reshape(-1, WIDTH).astype(LOW)
    grad_kv = jnp.concatenate(
        [rotate_back(grad_key, cosine, sine).reshape(-1, KVW), grad_value.reshape(-1, KVW)], axis=1
    ).astype(LOW)
    g_qkv = dense_t(
        jnp.concatenate([a_s, a_last], axis=0),
        jnp.concatenate(
            [
                jnp.pad(grad_q, ((0, 0), (0, qkv_wide - WIDTH))),
                jnp.pad(grad_kv, ((0, 0), (WIDTH, qkv_wide - WIDTH - 2 * KVW))),
            ],
            axis=0,
        ),
    )
    grad_a_s = dense_nt(grad_q, qkv_all[last][:, :WIDTH])
    spread_back = lax.dot_general(
        pick32,
        jnp.concatenate([grad_a_s, grad_mixed], axis=1),
        (((0,), (0,)), ((), ())),
        precision=HI,
    )
    grad_a = dense_nt(grad_kv, qkv_last) + spread_back[:, :wide]
    grad_in, gain_one = norm_back(x, scale_last, gain_all[last, 0], grad_a, width)
    upstream = grad_in + spread_back[:, wide:]
    grads[last] = (g_qkv, g_out, g_gu, g_down, jnp.stack([gain_one, gain_two]))

    for layer in range(sections - 2, -1, -1):
        (x, scale_a, a, query, key, value, probs, attended, mixed, scale_b, b, gate, upper, hidden) = kept[
            layer
        ]
        g_down, g_gu, grad_b = mlp_back(
            upstream.astype(LOW), b, gate, upper, hidden, gu_all[layer], down_all[layer]
        )
        grad_mid, gain_two = norm_back(mixed, scale_b, gain_all[layer, 1], grad_b, width)
        grad_mixed = grad_mid + upstream
        branch = grad_mixed.astype(LOW)
        g_out = dense_t(attended, branch)
        grad_att = dense_nt(dense_nt(branch, out_all[layer]).astype(LOW), sel).astype(LOW)
        grad_query, grad_key, grad_value = attend_back(query, key, value, probs, grad_att)
        grad_qkv = jnp.concatenate(
            [
                rotate_back(grad_query, cosine, sine).reshape(-1, WIDTH),
                rotate_back(grad_key, cosine, sine).reshape(-1, KVW),
                grad_value.reshape(-1, KVW),
                jnp.zeros((TOK_MB, qkv_wide - WIDTH - 2 * KVW), jnp.float32),
            ],
            axis=1,
        ).astype(LOW)
        g_qkv = dense_t(a, grad_qkv)
        grad_in, gain_one = norm_back(
            x, scale_a, gain_all[layer, 0], dense_nt(grad_qkv, qkv_all[layer]), width
        )
        upstream = grad_in + grad_mixed
        grads[layer] = (g_qkv, g_out, g_gu, g_down, jnp.stack([gain_one, gain_two]))

    grad_x0 = dense_nt(upstream.astype(LOW), sel_wide).astype(LOW)

    def give(all_asked, choose):
        rows = dense_t(choose, grad_x0).astype(LOW)
        got = lax.all_to_all(rows.reshape(n, slots, wide), "fsdp", 0, 0)
        return (all_asked.reshape(-1), lax.all_gather(got, "section", axis=0).reshape(-1, wide))

    def give_more(state):
        turn, grad, squares = state
        choose, more = lookup_round(ids, owner, rank, turn, slots, n, vshard)
        places, got = give(asked(lax.all_gather(more, BOTH, axis=0)), choose)
        place_of = (jnp.arange(vshard)[:, None] == places[None, :]).astype(LOW)
        new = grad + lax.dot_general(
            got[:, :width], place_of, (((0,), (1,)), ((), ())), preferred_element_type=jnp.float32
        )
        every = squares[1] + jnp.where(leader, jnp.sum(new**2), 0.0)
        return (turn + 1, new, squares.at[0].set(every))

    def gain_rows(layer):
        rows = jnp.concatenate([grads[layer][4], grad_final[None]], axis=0).reshape(3, n, rp)
        rows = jnp.pad(jnp.moveaxis(rows, 0, 1), ((0, 0), (0, TILE_R - 3), (0, 128 - rp)))
        return rows.reshape(n * TILE_R, 128)

    outward = [
        [g.astype(LOW) for g in grads[layer][:4] + (gain_rows(layer),)] for layer in range(sections)
    ]
    if fast:
        rows = dense_t(onehot, grad_x0).astype(LOW).reshape(n, slots, wide)
        *summed, got = reduce_all(outward, 5, 2, rows)
    else:
        summed = [
            lax.psum_scatter(
                jnp.concatenate(arrays, axis=0), BOTH, scatter_dimension=0, tiled=True
            ).astype(jnp.float32)
            for arrays in zip(*outward)
        ]
        got = give(asked_first, onehot)[1]
    if rdp != rd:
        summed[2] = summed[2].reshape(rp, 2, n, rdp)[:, :, :, :rd].reshape(rp, 2 * n * rd)
    grad_table, grad_squares = table_grad(
        leader.astype(jnp.float32),
        asked_first.reshape(-1),
        got.reshape(-1, wide).T,
        rows_all.T,
        grad_logits,
        summed,
        width,
    )
    grad_table, grad_squares = lax.while_loop(
        lambda state: state[0] < turns, give_more, (jnp.int32(1), grad_table, grad_squares)
    )[1:]

    def everyones(sums, name):
        if fast:
            return exchange(sums, name)
        return lax.all_gather(sums, BOTH, axis=0)

    grad_norm = jnp.sqrt(jnp.sum(everyones(grad_squares, 6)[:, 0, 0]))
    clip = jnp.minimum(1.0, CLIP / grad_norm)

    def views(arrays):
        out = [arrays[0].T] + [a.transpose(1, 0, 2) for a in arrays[1:4]]
        return out + [arrays[4][0], arrays[5][0], arrays[6][None]]

    weights_all = views((table, w_qkv, w_out, w_gu, w_down, gains, final_gain))
    grads_all = [grad_table] + summed[:4] + [summed[4][:2, :r], summed[4][2:3, :r]]
    new_firsts, new_seconds, updates, kept_weights, sums = moments(
        clip,
        sel,
        weights_all,
        grads_all,
        views((first_table, first_qkv, first_out, first_gu, first_down, first_gains, first_final)),
        views((second_table, second_qkv, second_out, second_gu, second_down, second_gains, second_final)),
        (DECAY,) * 5 + (0.0, 0.0),
    )
    sums = everyones(sums, 7)[:, :, 0].reshape(sections, n, 2, 8)
    sums = jnp.sum(sums, axis=1)
    layered = jnp.moveaxis(sums[:, :, 1:7], 1, 0).reshape(2, -1)
    matrix_norms = jnp.sqrt(jnp.concatenate([layered, sums[0, :, 0:1], sums[0, :, 7:8]], axis=1))
    trust_ratio = matrix_norms[0] / matrix_norms[1]
    own = lax.dynamic_slice_in_dim(trust_ratio, 6 * section_index, 6)
    last_two = trust_ratio[6 * sections :]
    new, half = apply_updates(
        jnp.concatenate([last_two[:1], own[:4]]),
        [weights_all[0], *kept_weights, weights_all[4]],
        updates[:5],
        [w.shape for w in weights_all[:5]],
    )
    new = list(new) + [
        weights_all[5] - RATE * own[4:6][:, None] * updates[5],
        weights_all[6] - RATE * last_two[1] * updates[6],
    ]

    def back(k, array):
        if k == 0:
            return array.T
        if k == 6:
            return array[0]
        return array.transpose(1, 0, 2) if array.ndim == 3 else array[None]

    outs = [loss, grad_norm, matrix_norms]
    for k in range(7):
        outs += [back(k, t[k]) for t in (new, new_firsts, new_seconds)]
    return tuple(outs + [back(k, half[k]) for k in range(5)])


def solution(mesh):
    tall, layered, gainy, flat = (
        P("fsdp", None),
        P("section", "fsdp", None),
        P("section", None, "fsdp"),
        P("fsdp"),
    )
    weights = (tall, layered, layered, layered, layered, gainy, flat)
    placed = (
        P("section", "fsdp"),
        P("section", "fsdp", None),
        P("section", None, None),
        P(),
    ) + weights * 3
    results = (P(), P(), P())
    for spec in weights:
        results += (spec, spec, spec)
    return jax.shard_map(
        shards, mesh=mesh, in_specs=placed, out_specs=results + weights[:5], check_vma=False
    )
```

```python
import functools

import jax
import jax.numpy as jnp
from jax import lax
from jax.experimental import pallas as pl
from jax.experimental.pallas import tpu as pltpu
from jax.sharding import PartitionSpec as P

HEADS = 15
KV = 5
HD = 64
FF = 2560
PROMPT = 256
NCONT = 2
CONT = 128
SCORED = 32
STEP = 10
TOK_MB = 512

EPS = 1e-05
SCALE = 0.125
THETA = 100000.0
BETA = 0.1
CLIP = 1.0
RATE = 0.3
BETA_ONE = 0.9
BETA_TWO = 0.99
ADAM_EPS = 1e-08
DECAY = 0.01

WIDTH = HEADS * HD
KVW = KV * HD
BOTH = ("section", "fsdp")
HI = lax.Precision.HIGHEST
LOW = jnp.bfloat16

WEIGHT_PIECES = [
    (0, 0, 64, 0),
    (1, 0, 64, 1),
    (2, 0, 16, 0),
    (2, 16, 16, 1),
    (2, 32, 16, 0),
    (2, 48, 16, 1),
    (3, 0, 80, 0),
    (3, 80, 80, 1),
    (4, 0, 16, 1),
]

MESH = pl.DeviceIdType.MESH
ANYWHERE = pl.BlockSpec(memory_space=pl.ANY)
IN_VMEM = pl.BlockSpec(memory_space=pltpu.VMEM)
TILE_R, TILE_C = 32, 1024


def coords():
    f = lax.axis_index("fsdp")
    return (lax.axis_index("section"), f // 4, f // 2 % 2, f % 2)


def device(y, z, x, c):
    return (y, z * 4 + x * 2 + c)


def greet(peers):
    barrier = pltpu.get_barrier_semaphore()
    for peer in peers:
        pl.semaphore_signal(barrier, inc=1, device_id=peer, device_id_type=MESH)
    pl.semaphore_wait(barrier, len(peers))


def send(src, dst, send_sem, recv_sem, peer):
    pltpu.make_async_remote_copy(
        src_ref=src,
        dst_ref=dst,
        send_sem=send_sem,
        recv_sem=recv_sem,
        device_id=peer,
        device_id_type=MESH,
    ).start()


def settle(ref, sem):
    pltpu.make_async_copy(ref, ref, sem).wait()


def gather_kernel(pieces, count, carried, *refs):
    y, f = (lax.axis_index("section"), lax.axis_index("fsdp"))
    z, x, c = coords()[1:]
    in_line = [((z + k) % 4) * 4 + x * 2 + c for k in range(1, 4)]
    near = [f + 2 - 4 * x, f + 1 - 2 * c]
    away = [(f + k) % 16 for k in range(1, 16)] if carried else in_line + near
    greet([device(1 - y, z, x, c)] + [(y, peer) for peer in away])
    for section in range(2):
        pl.when(y == section)(functools.partial(gather_section, section, pieces, count, carried, *refs))


def gather_section(y, pieces, count, carried, *refs):
    given = count + carried
    blocks, outs = (refs[:count], refs[given : given + 2 * count])
    send_sem, recv_sem, sib_sem, own_sem, carry_sem = refs[given + 2 * count + carried :]
    z, x, c = coords()[1:]
    to_x, to_y, to_sib = (device(y, z, 1 - x, c), device(1 - y, z, x, c), device(y, z, x, 1 - c))
    zs = [(z + k) % 4 for k in range(4)]

    def part(ref, p):
        return ref.at[pl.ds(pieces[p][1], pieces[p][2])]

    def there(p, o):
        return part(outs[o[0] * count + pieces[p][0]].at[o[1] * 4 + o[2] * 2 + c], p)

    def mark(p, o):
        return recv_sem.at[p, o[0] * 8 + o[1] * 2 + o[2]]

    def push(p, o, peer, own=False, sib=False):
        src = part(blocks[pieces[p][0]], p) if own else there(p, o)
        send(src, there(p, o), send_sem.at[p], sib_sem.at[p] if sib else mark(p, o), peer)

    every = range(len(pieces))
    for p in every:
        me = (y, z, x)
        push(p, me, to_x, own=True)
        push(p, me, to_y, own=True)
        for zz in zs[1:]:
            push(p, me, device(y, zz, x, c), own=True)
        push(p, me, to_sib, own=True, sib=True)
        pltpu.make_async_copy(part(blocks[pieces[p][0]], p), there(p, me), own_sem).start()
    if carried:
        rows, got = (refs[count], refs[given + 2 * count])
        f = lax.axis_index("fsdp")
        for k in range(1, 16):
            peer = (f + k) % 16
            send(rows.at[peer], got.at[f], carry_sem.at[0], carry_sem.at[1], (y, peer))
        pltpu.make_async_copy(rows.at[f], got.at[f], carry_sem.at[2]).start()

    def from_x(p, zz):
        o = (y, zz, 1 - x)
        settle(there(p, o), mark(p, o))
        if pieces[p][3] == 0:
            push(p, o, to_y)
        push(p, o, to_sib, sib=True)

    def from_y(p, zz):
        o = (1 - y, zz, x)
        settle(there(p, o), mark(p, o))
        if pieces[p][3] == 1:
            push(p, o, to_x)
        push(p, o, to_sib, sib=True)

    for p in every:
        for zz in zs[1:]:
            o = (y, zz, x)
            settle(there(p, o), mark(p, o))
            push(p, o, to_x)
            push(p, o, to_y)
            push(p, o, to_sib, sib=True)
        from_x(p, z)
        from_y(p, z)
    for p in every:
        for zz in zs[1:]:
            from_x(p, zz)
            from_y(p, zz)
    for p in every:
        for zz in zs:
            o = (1 - y, zz, 1 - x)
            settle(there(p, o), mark(p, o))
            push(p, o, to_sib, sib=True)
    for p in every:
        a, start, rows_each, unused = pieces[p]
        settle(part(blocks[a], p), own_sem)
        for times in (16, 15):
            settle(outs[a].at[pl.ds(0, times), pl.ds(start, rows_each)], send_sem.at[p])
        settle(outs[a].at[pl.ds(0, 16), pl.ds(start, rows_each)], sib_sem.at[p])
    if carried:
        settle(rows.at[pl.ds(0, 15)], carry_sem.at[0])
        settle(rows.at[pl.ds(0, 15)], carry_sem.at[1])
        settle(rows.at[0], carry_sem.at[2])


def gather_all(blocks, pieces, name, rows=None):
    many = len(pieces)
    extra = [] if rows is None else [rows]
    shapes = [jax.ShapeDtypeStruct((16,) + b.shape, b.dtype) for b in blocks] * 2
    shapes += [jax.ShapeDtypeStruct(e.shape, e.dtype) for e in extra]
    return pl.pallas_call(
        functools.partial(gather_kernel, pieces, len(blocks), len(extra)),
        out_shape=shapes,
        in_specs=[ANYWHERE] * (len(blocks) + len(extra)),
        out_specs=[ANYWHERE] * len(shapes),
        scratch_shapes=[
            pltpu.SemaphoreType.DMA((many,)),
            pltpu.SemaphoreType.DMA((many, 16)),
            pltpu.SemaphoreType.DMA((many,)),
            pltpu.SemaphoreType.DMA,
            pltpu.SemaphoreType.DMA((3,)),
        ],
        compiler_params=pltpu.CompilerParams(collective_id=name, has_side_effects=True),
    )(*blocks, *extra)


def reduce_pieces(shapes, tile):
    out = []
    for a, (rows, cols) in enumerate(shapes):
        for row in range(0, rows, tile):
            for col in range(0, cols, TILE_C):
                out.append((a, row, col, min(TILE_C, cols - col)))
    return out


def reduce_kernel(pieces, tile, count, carried, lag, *refs):
    grads = (refs[:count], refs[count : 2 * count])
    outs = refs[2 * count + carried : 3 * count + carried]
    held, from_one, from_two, from_z, mine = refs[3 * count + 2 * carried : 3 * count + 2 * carried + 5]
    sib_recv, sib_send, recv_one, send_one, recv_two, send_two, recv_z, send_z, own_sem, carry_sem = refs[
        3 * count + 2 * carried + 5 :
    ]
    y, z, x, c = coords()
    to_x, to_y, to_sib = (device(y, z, 1 - x, c), device(1 - y, z, x, c), device(y, z, x, 1 - c))
    zs = [(z + k) % 4 for k in range(4)]
    many = len(pieces)
    f = lax.axis_index("fsdp")
    alike = [(y, (f + k) % 16) for k in range(1, 16)]
    near = [to_x, to_sib] + [device(y, zz, x, c) for zz in zs[1:]]
    greet([to_y] + (alike if carried else near))

    def source(p, yo, xo, core):
        a, row, col, cols = pieces[p]
        return grads[yo][a].at[:, xo, core, pl.ds(row, tile), pl.ds(col, cols)]

    def cut(ref, p):
        cols = pieces[p][3]
        return ref if cols == TILE_C else ref.at[..., pl.ds(0, cols)]

    def fetch(p):
        for yo in range(2):
            for xo in range(2):
                pltpu.make_async_copy(
                    source(p, yo, xo, c), cut(mine.at[p % 2, yo, xo], p), own_sem.at[p % 2]
                ).start()

    for p in range(many):
        for yo in range(2):
            for xo in range(2):
                send(
                    source(p, yo, xo, 1 - c),
                    cut(held.at[p, yo, xo], p),
                    sib_send.at[p],
                    sib_recv.at[p],
                    to_sib,
                )
        if p == 0:
            fetch(0)
    if carried:
        rows, got = (refs[2 * count], refs[3 * count + carried])
        for peer in alike:
            send(rows.at[peer[1]], got.at[y * 16 + f], carry_sem.at[0], carry_sem.at[1], peer)
        pltpu.make_async_copy(rows.at[f], got.at[y * 16 + f], carry_sem.at[2]).start()

    def pass_on():
        settle(rows.at[pl.ds(0, 15)], carry_sem.at[1])
        settle(rows.at[0], carry_sem.at[2])
        ours = got.at[pl.ds(y * 16, 16)]
        send(ours, ours, carry_sem.at[3], carry_sem.at[4], to_y)

    def y_first(p):
        return p % 2 == 0

    def add(dst, src, p):
        cols = pl.ds(0, pieces[p][3])
        dst[:, cols] = (dst[:, cols].astype(jnp.float32) + src[:, cols].astype(jnp.float32)).astype(LOW)

    def two_cores(p):
        if p + 1 < many:
            fetch(p + 1)
        settle(cut(mine.at[p % 2], p), own_sem.at[p % 2])
        settle(cut(held.at[p], p), sib_recv.at[p])

        def each(i, carry):
            yo, xo, zo = (i // 8, i // 4 % 2, i % 4)
            add(held.at[p, yo, xo, zo], mine.at[p % 2, yo, xo, zo], p)
            return carry

        lax.fori_loop(0, 16, each, 0)
        if y_first(p):
            send(cut(held.at[p, 1 - y], p), cut(from_one.at[p], p), send_one.at[p], recv_one.at[p], to_y)
        else:
            for yo in range(2):
                send(
                    cut(held.at[p, yo, 1 - x], p),
                    cut(from_one.at[p, yo], p),
                    send_one.at[p],
                    recv_one.at[p],
                    to_x,
                )

    def first_axis(p):
        settle(cut(from_one.at[p], p), recv_one.at[p])

        def each(i, carry):
            if y_first(p):
                add(held.at[p, y, i // 4, i % 4], from_one.at[p, i // 4, i % 4], p)
            else:
                add(held.at[p, i // 4, x, i % 4], from_one.at[p, i // 4, i % 4], p)
            return carry

        lax.fori_loop(0, 8, each, 0)
        if y_first(p):
            src, peer = (held.at[p, y, 1 - x], to_x)
        else:
            src, peer = (held.at[p, 1 - y, x], to_y)
        send(cut(src, p), cut(from_two.at[p], p), send_two.at[p], recv_two.at[p], peer)

    def second_axis(p):
        settle(cut(from_two.at[p], p), recv_two.at[p])

        def each(i, carry):
            add(held.at[p, y, x, i], from_two.at[p, i], p)
            return carry

        lax.fori_loop(0, 4, each, 0)
        for k in range(1, 4):
            send(
                cut(held.at[p, y, x, zs[k]], p),
                cut(from_z.at[p, 3 - k], p),
                send_z.at[p],
                recv_z.at[p],
                device(y, zs[k], x, c),
            )

    def along_z(p):
        settle(cut(from_z.at[p], p), recv_z.at[p])
        a, row, col, cols = pieces[p]
        part = pl.ds(0, cols)
        total = held[p, y, x, z, :, part].astype(jnp.float32)
        for k in range(3):
            total = total + from_z[p, k, :, part].astype(jnp.float32)
        outs[a][pl.ds(row, tile), pl.ds(col, cols)] = total

    for step in range(many + 3 * lag):
        if carried and step == many // 2:
            pass_on()
        for k, stage in enumerate((two_cores, first_axis, second_axis, along_z)):
            if 0 <= step - k * lag < many:
                stage(step - k * lag)
    for p in range(many):
        settle(cut(held.at[p], p), sib_send.at[p])
        settle(cut(from_one.at[p], p), send_one.at[p])
        settle(cut(from_two.at[p], p), send_two.at[p])
        settle(cut(from_z.at[p], p), send_z.at[p])
    if carried:
        settle(rows.at[pl.ds(0, 15)], carry_sem.at[0])
        settle(rows, carry_sem.at[3])
        settle(rows, carry_sem.at[4])


def reduce_all(grads, name, lag, rows=None, tile=TILE_R):
    count = len(grads[0])
    shapes = [(g.shape[0] // 16, g.shape[1]) for g in grads[0]]
    pieces = reduce_pieces(shapes, tile)
    many = len(pieces)
    views = [g.reshape(4, 2, 2, g.shape[0] // 16, g.shape[1]) for layer in grads for g in layer]
    extra = [] if rows is None else [rows]
    return pl.pallas_call(
        functools.partial(reduce_kernel, pieces, tile, count, len(extra), lag),
        out_shape=[jax.ShapeDtypeStruct(s, jnp.float32) for s in shapes]
        + [jax.ShapeDtypeStruct((32,) + e.shape[1:], e.dtype) for e in extra],
        in_specs=[ANYWHERE] * (len(views) + len(extra)),
        out_specs=[IN_VMEM] * count + [ANYWHERE] * len(extra),
        scratch_shapes=[
            pltpu.VMEM((many, 2, 2, 4, tile, TILE_C), LOW),
            pltpu.VMEM((many, 2, 4, tile, TILE_C), LOW),
            pltpu.VMEM((many, 4, tile, TILE_C), LOW),
            pltpu.VMEM((many, 3, tile, TILE_C), LOW),
            pltpu.VMEM((2, 2, 2, 4, tile, TILE_C), LOW),
        ]
        + [pltpu.SemaphoreType.DMA((many,)) for unused in range(8)]
        + [pltpu.SemaphoreType.DMA((2,)), pltpu.SemaphoreType.DMA((5,))],
        compiler_params=pltpu.CompilerParams(
            collective_id=name,
            has_side_effects=True,
            vmem_limit_bytes=(12 + 3 * many) * 2**20 if many < 16 else 58 * 2**20,
        ),
    )(*views, *extra)


def exchange_kernel(whole, src, out, send_sem, recv_sem, own_sem):
    y, f = (lax.axis_index("section"), lax.axis_index("fsdp"))
    count = 32 if whole else 16
    me = y * 16 + f if whole else f
    peers = [(me + k) % count for k in range(1, count)]
    where = [(p // 16, p % 16) if whole else (y, p) for p in peers]
    greet(where)
    for peer in where:
        send(src, out.at[me], send_sem, recv_sem, peer)
    own = pltpu.make_async_copy(src, out.at[me], own_sem)
    own.start()
    own.wait()
    settle(out.at[pl.ds(0, count - 1)], send_sem)
    settle(out.at[pl.ds(0, count - 1)], recv_sem)


def exchange(small, name, whole=True):
    return pl.pallas_call(
        functools.partial(exchange_kernel, whole),
        out_shape=jax.ShapeDtypeStruct((32 if whole else 16,) + small.shape, small.dtype),
        in_specs=[IN_VMEM],
        out_specs=IN_VMEM,
        scratch_shapes=[pltpu.SemaphoreType.DMA] * 3,
        compiler_params=pltpu.CompilerParams(collective_id=name, has_side_effects=True),
    )(small)


def tall_of(height, sections=2):
    return 256 if height % (256 * sections) == 0 else 128


def whole(shape):
    return pl.BlockSpec(shape, lambda *unused: (0,) * len(shape), pipeline_mode=pl.Buffered(1))


def striped(tall, cols):
    return pl.BlockSpec((tall, cols), lambda i: (i, 0))


def lined(rows, wide):
    return pl.BlockSpec((rows, wide), lambda i: (0, i))


def squares_of(value):
    return jnp.sum(jnp.sum(value * value, axis=1, keepdims=True), axis=0, keepdims=True)


def padded_table_kernel(asked, sel, table, low, rows, total):
    step = pl.program_id(0)

    @pl.when(step == 0)
    def start():
        total[...] = jnp.zeros_like(total)

    width, tall = table.shape
    low[:, pl.ds(low.shape[1] - 128, 128)] = jnp.zeros((tall, 128), LOW)
    eye = lax.broadcasted_iota(jnp.int32, (tall, tall), 0) == lax.broadcasted_iota(jnp.int32, (tall, tall), 1)
    low[:, pl.ds(0, width)] = dense_nt(eye.astype(LOW), table[...].astype(LOW)).astype(LOW)
    place = lax.broadcasted_iota(jnp.int32, (asked.shape[0], tall), 1) + step * tall
    total[...] += dense((asked[...] == place).astype(LOW), low[...])

    @pl.when(step == pl.num_programs(0) - 1)
    def end():
        rows[...] = dense(total[...].astype(LOW), sel[...]).astype(LOW)


def padded_table(asked, sel, table):
    width, height = table.shape
    wide = sel.shape[0]
    count = asked.shape[0]
    tall = tall_of(height)
    return pl.pallas_call(
        padded_table_kernel,
        grid=(height // tall,),
        out_shape=[
            jax.ShapeDtypeStruct((height, wide), LOW),
            jax.ShapeDtypeStruct((count, sel.shape[1]), LOW),
        ],
        in_specs=[whole((count, 1)), whole(sel.shape), lined(width, tall)],
        out_specs=[striped(tall, wide), whole((count, sel.shape[1]))],
        scratch_shapes=[pltpu.VMEM((count, wide), jnp.float32)],
        compiler_params=pltpu.CompilerParams(vmem_limit_bytes=48 * 2**20),
    )(asked[:, None], sel, table)


def logits_kernel(wanted, rows, table, logits, top, total, target):
    step = pl.program_id(0)

    @pl.when(step == 0)
    def start():
        top[...] = jnp.full_like(top, -jnp.inf)
        total[...] = jnp.zeros_like(total)
        target[...] = jnp.zeros_like(target)

    here = dense_nt(table[...], rows[...])
    logits[...] = here
    higher = jnp.maximum(top[...], jnp.max(here, axis=0, keepdims=True))
    total[...] = total[...] * jnp.exp(top[...] - higher) + jnp.sum(
        jnp.exp(here - higher), axis=0, keepdims=True
    )
    top[...] = higher
    place = lax.broadcasted_iota(jnp.int32, here.shape, 0) + step * here.shape[0]
    target[...] += jnp.sum(jnp.where(place == wanted[...], here, 0.0), axis=0, keepdims=True)


def logits_of(wanted, rows, table):
    height, wide = table.shape
    count = rows.shape[0]
    tall = tall_of(height)
    line = jax.ShapeDtypeStruct((1, count), jnp.float32)
    return pl.pallas_call(
        logits_kernel,
        grid=(height // tall,),
        out_shape=[jax.ShapeDtypeStruct((height, count), jnp.float32), line, line, line],
        in_specs=[whole((1, count)), whole(rows.shape), striped(tall, wide)],
        out_specs=[striped(tall, count)] + [whole((1, count))] * 3,
        compiler_params=pltpu.CompilerParams(vmem_limit_bytes=48 * 2**20),
    )(wanted[None], rows, table)


def logits_back_kernel(share, section, wanted, top, scale, push, logits, table, grad, rows, total):
    step = pl.program_id(1)
    mine = (step >= section[0] * share) & (step < (section[0] + 1) * share)

    @pl.when(step == 0)
    def start():
        total[...] = jnp.zeros_like(total)

    here = logits[...]
    place = lax.broadcasted_iota(jnp.int32, here.shape, 0) + step * here.shape[0]
    hit = jnp.where(place == wanted[...], push[...], 0.0)
    low = (hit - jnp.exp(here - top[...]) * scale[...]).astype(LOW)
    grad[...] = low

    @pl.when(mine)
    def add():
        total[...] += dense_t(low, table[...])

    @pl.when(step == pl.num_programs(1) - 1)
    def end():
        rows[...] = total[...].astype(LOW)


def logits_back(section, wanted, top, scale, push, logits, table, sections):
    height, wide = table.shape
    count = logits.shape[1]
    tall = tall_of(height, sections)
    block = min(count, 2048)
    line = pl.BlockSpec((1, block), lambda j, i: (0, j))
    tile = pl.BlockSpec((tall, block), lambda j, i: (i, j))
    return pl.pallas_call(
        functools.partial(logits_back_kernel, height // tall // sections),
        grid=(count // block, height // tall),
        out_shape=[
            jax.ShapeDtypeStruct((height, count), LOW),
            jax.ShapeDtypeStruct((count, wide), LOW),
        ],
        in_specs=[
            pl.BlockSpec(memory_space=pltpu.SMEM),
            line,
            line,
            line,
            line,
            tile,
            pl.BlockSpec((tall, wide), lambda j, i: (i, 0)),
        ],
        out_specs=[tile, pl.BlockSpec((block, wide), lambda j, i: (j, 0))],
        scratch_shapes=[pltpu.VMEM((block, wide), jnp.float32)],
        compiler_params=pltpu.CompilerParams(vmem_limit_bytes=56 * 2**20),
    )(section[None], wanted[None], top[None], scale[None], push[None], logits, table)


def table_grad_kernel(leader, asked, got, rows, grad_logits, *refs):
    *others, grad, squares = refs
    step = pl.program_id(0)

    @pl.when(step == 0)
    def start():
        gains = others[-1][...]
        total = squares_of(gains[:2]) + leader[0] * squares_of(gains[2:3])
        for other in others[:-1]:
            total += squares_of(other[...])
        squares[...] = jnp.broadcast_to(total, squares.shape)

    width, tall = grad.shape
    place = lax.broadcasted_iota(jnp.int32, (tall, asked.shape[1]), 0) + step * tall
    here = dense_nt(rows[...], grad_logits[...]) + dense_nt(got[...], (asked[...] == place).astype(LOW))
    here = here[:width]
    grad[...] = here.astype(LOW)
    squares[pl.ds(0, 1)] += leader[0] * squares_of(here)


def table_grad(leader, asked, got, rows, grad_logits, others, width):
    height, count = grad_logits.shape
    tall = tall_of(height)
    return pl.pallas_call(
        table_grad_kernel,
        grid=(height // tall,),
        out_shape=[
            jax.ShapeDtypeStruct((width, height), LOW),
            jax.ShapeDtypeStruct((8, 128), jnp.float32),
        ],
        in_specs=[
            pl.BlockSpec(memory_space=pltpu.SMEM),
            whole((1, asked.shape[0])),
            whole(got.shape),
            whole(rows.shape),
            striped(tall, count),
        ]
        + [whole(o.shape) for o in others],
        out_specs=[lined(width, tall), whole((8, 128))],
        compiler_params=pltpu.CompilerParams(vmem_limit_bytes=56 * 2**20),
    )(leader[None], asked[None], got, rows, grad_logits, *others)


def exact_product(left, onehot):
    high = left.astype(LOW)
    rest = left - high.astype(jnp.float32)
    middle = rest.astype(LOW)
    lowest = (rest - middle.astype(jnp.float32)).astype(LOW)
    return dense_nt(high, onehot) + (dense_nt(middle, onehot) + dense_nt(lowest, onehot))


ROWED = 3
SPREAD = (1, 3)


def moments_kernel(decays, clip, sel, *refs):
    weights, grads, firsts, seconds = (refs[7 * k : 7 * k + 7] for k in range(4))
    new_firsts, new_seconds, updates = (refs[28 + 7 * k : 35 + 7 * k] for k in range(3))
    kept, sums, *scratch = refs[49:49 + ROWED] , refs[49 + ROWED], *refs[50 + ROWED:]
    staged = [scratch[5 * k : 5 * k + 5] for k in range(ROWED)]
    in_sem, out_sem = scratch[5 * ROWED :]
    step, steps = (pl.program_id(0), pl.num_programs(0))

    def copies(k, inward):
        w, m, v, new_m, new_v = staged[k]
        if inward:
            pairs = [(weights[k + 1].at[:, 0], w), (firsts[k + 1].at[:, 0], m), (seconds[k + 1].at[:, 0], v)]
        else:
            pairs = [(new_m, new_firsts[k + 1].at[:, 0]), (new_v, new_seconds[k + 1].at[:, 0])]
        return [
            pltpu.make_async_copy(src, dst, (in_sem if inward else out_sem).at[k, i])
            for i, (src, dst) in enumerate(pairs)
        ]

    @pl.when(step == 0)
    def start():
        sums[...] = jnp.zeros_like(sums)
        for k in range(ROWED):
            for copy in copies(k, True):
                copy.start()

    def one(weight, grad, first, second, decay):
        return (weight,) + lamb_parts(weight, clip[0] * grad.astype(jnp.float32), first, second, decay)

    weight, new_firsts[0][...], new_seconds[0][...], update = one(
        weights[0][...], grads[0][...], firsts[0][...], seconds[0][...], decays[0]
    )
    updates[0][...] = update.astype(LOW)
    sums[pl.ds(0, 1)] += squares_of(weight)
    sums[pl.ds(8, 1)] += squares_of(update)

    def tensor(k):
        rows, cols = updates[k + 1].shape
        grad = grads[k + 1][pl.ds(0, rows)]
        grad = exact_product(grad, sel[...]) if k in SPREAD else grad[:, :cols]
        if k < ROWED:
            for copy in copies(k, True):
                copy.wait()
            w, m, v, new_m, new_v = staged[k]
        else:
            w, m, v, new_m, new_v = (t[k + 1] for t in (weights, firsts, seconds, new_firsts, new_seconds))
        weight, new_m[...], new_v[...], update = one(w[...], grad, m[...], v[...], decays[k + 1])
        updates[k + 1][...] = update
        if k < ROWED:
            kept[k][...] = weight
            for copy in copies(k, False):
                copy.start()
        for row in range(rows if k == 4 else 1):
            part = slice(row, row + 1) if k == 4 else slice(None)
            line = k + 1 + row + (k > 4)
            sums[pl.ds(line, 1)] += squares_of(weight[part])
            sums[pl.ds(8 + line, 1)] += squares_of(update[part])

    for k in range(6):
        pl.when(step == (6 + k if k < ROWED else k - 2) % steps)(functools.partial(tensor, k))

    @pl.when(step == steps - 1)
    def end():
        for k in range(ROWED):
            for copy in copies(k, False):
                copy.wait()


def moments(clip, sel, weights, grads, firsts, seconds, decays):
    width, height = weights[0].shape
    tall = tall_of(height)
    flat = [w.shape if w.ndim == 2 else w.shape[::2] for w in weights]

    def specs(arrays, results=False):
        out = [lined(width, tall)]
        for a in arrays[1:]:
            out.append(ANYWHERE if a.ndim == 3 else whole(a.shape))
        return out

    line = [jax.ShapeDtypeStruct(w.shape, jnp.float32) for w in weights]
    plain = [jax.ShapeDtypeStruct(s, jnp.float32 if k else LOW) for k, s in enumerate(flat)]
    kept = plain[1 : 1 + ROWED]
    out = pl.pallas_call(
        functools.partial(moments_kernel, decays),
        grid=(height // tall,),
        out_shape=line * 2 + plain + kept + [jax.ShapeDtypeStruct((16, 128), jnp.float32)],
        in_specs=[pl.BlockSpec(memory_space=pltpu.SMEM), whole(sel.shape)]
        + specs(weights)
        + specs(grads)
        + specs(firsts)
        + specs(seconds),
        out_specs=specs(line) * 2 + specs(plain) + [whole(s.shape) for s in kept] + [whole((16, 128))],
        scratch_shapes=[pltpu.VMEM(s.shape, jnp.float32) for s in kept for unused in range(5)]
        + [pltpu.SemaphoreType.DMA((ROWED, 3)), pltpu.SemaphoreType.DMA((ROWED, 2))],
        compiler_params=pltpu.CompilerParams(vmem_limit_bytes=60 * 2**20),
    )(clip[None], sel, *weights, *grads, *firsts, *seconds)
    return (out[:7], out[7:14], out[14:21], out[21 : 21 + ROWED], out[21 + ROWED])


def apply_kernel(scales, *refs):
    weights, updates, new, half = (refs[5 * k : 5 * k + 5] for k in range(4))
    staged, sem = (refs[20 : 20 + ROWED], refs[20 + ROWED])
    step, steps = (pl.program_id(0), pl.num_programs(0))

    def copy(k):
        return pltpu.make_async_copy(staged[k - 1], new[k].at[:, 0], sem.at[k - 1])

    def one(k):
        value = weights[k][...] - RATE * scales[k] * updates[k][...]
        half[k][...] = value.astype(LOW)
        if 0 < k <= ROWED:
            staged[k - 1][...] = value
            copy(k).start()
        else:
            new[k][...] = value

    one(0)
    for k in range(1, 5):
        pl.when(step == (k - 1) % steps)(functools.partial(one, k))

    @pl.when(step == steps - 1)
    def end():
        for k in range(1, 1 + ROWED):
            copy(k).wait()


def apply_updates(scales, weights, updates, shapes):
    width, height = weights[0].shape
    tall = tall_of(height)
    plain = [lined(width, tall)] + [whole(w.shape) for w in weights[1:]]
    out = pl.pallas_call(
        apply_kernel,
        grid=(height // tall,),
        out_shape=[jax.ShapeDtypeStruct(s, jnp.float32) for s in shapes]
        + [jax.ShapeDtypeStruct(w.shape, LOW) for w in weights],
        in_specs=[pl.BlockSpec(memory_space=pltpu.SMEM)] + plain * 2,
        out_specs=plain[:1] + [ANYWHERE] * ROWED + plain[1 + ROWED :] + plain,
        scratch_shapes=[pltpu.VMEM(w.shape, jnp.float32) for w in weights[1 : 1 + ROWED]]
        + [pltpu.SemaphoreType.DMA((ROWED,))],
        compiler_params=pltpu.CompilerParams(vmem_limit_bytes=56 * 2**20),
    )(scales, *weights, *updates)
    return (out[:5], out[5:])


EACH = HEADS // KV


def turned(x, cosine, sine):
    half = HD // 2
    u, w = (x[:half], x[half:])
    return jnp.concatenate([u * cosine - w * sine, w * cosine + u * sine], axis=0)


def query_blocks(scored):
    if scored:
        return [(0, scored, ((0, TOK_MB),))]
    out = [(0, PROMPT, ((0, PROMPT),))]
    for j in range(NCONT):
        first = PROMPT + j * CONT
        out.append((first, CONT, ((0, PROMPT), (first, CONT))))
    return out


def masks(place):
    out = []
    for first, count, ranges in query_blocks(0 if place is None else place.shape[1]):
        keys = sum(r[1] for r in ranges)
        row = lax.broadcasted_iota(jnp.int32, (keys, count), 0)
        if place is not None:
            at = place[pl.ds(0, 1)]
            seen = (row < PROMPT) | ((row >= place[pl.ds(1, 1)]) & (row <= at))
        else:
            seen = row - (keys - count) <= lax.broadcasted_iota(jnp.int32, (keys, count), 1)
        out.append(jnp.concatenate([jnp.where(seen, 0.0, -1e30)] * EACH, axis=1))
    return out


def rows_of(ranges, array):
    parts = [array[first : first + count] for first, count in ranges]
    return parts[0] if len(parts) == 1 else jnp.concatenate(parts, axis=0)


def head_rows(start):
    return pl.ds(pl.multiple_of(start, HD), HD)


def side_by_side(ref, group, first, count):
    return jnp.concatenate(
        [ref[head_rows((group * EACH + j) * HD), pl.ds(first, count)] for j in range(EACH)], axis=1
    )


def attend_kernel(scored, qkv, cosine, sine, *refs):
    pick, place = refs[:2] if scored else (None, None)
    low, out, top, share, *queries = refs[2:] if scored else refs
    queries = queries[0] if scored else low
    cos, sin = (cosine[...], sine[...])
    added = masks(place)

    def group_of(group, carry):
        key = turned(qkv[head_rows(WIDTH + group * HD)], cos, sin)
        low[head_rows(WIDTH + group * HD)] = key.astype(LOW)
        value = qkv[head_rows(WIDTH + KVW + group * HD)].astype(LOW)
        low[head_rows(WIDTH + KVW + group * HD)] = value
        for j in range(EACH):
            place_of = head_rows((group * EACH + j) * HD)
            query = turned(qkv[place_of], cos, sin).astype(LOW)
            low[place_of] = query
            if scored:
                queries[place_of] = dense_nt(query, pick[...]).astype(LOW)
        keys = key.T.astype(LOW)
        for (first, count, ranges), extra in zip(query_blocks(scored), added):
            query = side_by_side(queries, group, first, count)
            scores = dense(rows_of(ranges, keys), query) * SCALE + extra
            high = jnp.max(scores, axis=0, keepdims=True)
            expo = jnp.exp(scores - high)
            part = 1.0 / jnp.sum(expo, axis=0, keepdims=True)
            probs = (expo * part).astype(LOW)
            got, at = (0.0, 0)
            for start, length in ranges:
                got += dense(value[:, start : start + length], probs[at : at + length])
                at += length
            for j in range(EACH):
                column = slice(j * count, (j + 1) * count)
                out[head_rows((group * EACH + j) * HD), pl.ds(first, count)] = got[:, column].astype(LOW)
                top[group, j : j + 1, pl.ds(first, count)] = high[:, column]
                share[group, j : j + 1, pl.ds(first, count)] = part[:, column]
        return carry

    lax.fori_loop(0, KV, group_of, 0)


def attention(qkv, cosine, sine, chosen=()):
    tokens = qkv.shape[1]
    scored = chosen[0].shape[0] if chosen else 0
    count = scored or tokens
    stat = jax.ShapeDtypeStruct((KV, EACH, count), jnp.float32)
    heads = jax.ShapeDtypeStruct((WIDTH, count), LOW)
    results = [jax.ShapeDtypeStruct((WIDTH + 2 * KVW, tokens), LOW), heads, stat, stat]
    results += [heads] if scored else []
    return pl.pallas_call(
        functools.partial(attend_kernel, scored),
        out_shape=results,
        in_specs=[IN_VMEM] * (3 + len(chosen)),
        out_specs=[IN_VMEM] * len(results),
        compiler_params=pltpu.CompilerParams(vmem_limit_bytes=40 * 2**20),
    )(qkv, cosine, sine, *chosen)


def attend_back_kernel(scored, low, top, share, grad, cosine, sine, *refs):
    pick, place, queries = refs[:3] if scored else (None, None, low)
    out, key_sum, value_sum = refs[-3:]
    cos, sin = (cosine[...], sine[...])
    added = masks(place)
    spare = out.shape[0] - WIDTH - 2 * KVW
    out[pl.ds(WIDTH + 2 * KVW, spare)] = jnp.zeros((spare, out.shape[1]), LOW)

    def group_of(group, carry):
        key = low[head_rows(WIDTH + group * HD)]
        value = low[head_rows(WIDTH + KVW + group * HD)]
        keys = key.astype(jnp.float32).T.astype(LOW)
        values = value.astype(jnp.float32).T.astype(LOW)
        for number, ((first, count, ranges), extra) in enumerate(zip(query_blocks(scored), added)):
            sides = range(EACH)
            columns = pl.ds(first, count)
            query = side_by_side(queries, group, first, count)
            upstream = side_by_side(grad, group, first, count)
            high = jnp.concatenate([top[group, j : j + 1, columns] for j in sides], axis=1)
            part = jnp.concatenate([share[group, j : j + 1, columns] for j in sides], axis=1)
            scores = dense(rows_of(ranges, keys), query) * SCALE + extra
            probs = jnp.exp(scores - high) * part
            grad_probs = dense(rows_of(ranges, values), upstream)
            inner = jnp.sum(grad_probs * probs, axis=0, keepdims=True)
            grad_scores = (probs * (grad_probs - inner)).astype(LOW)
            probs = probs.astype(LOW)
            got, at = (0.0, 0)
            for start, length in ranges:
                piece = slice(at, at + length)
                got += dense(key[:, start : start + length], grad_scores[piece])
                here = pl.ds(start, length)
                more_key = dense_nt(query, grad_scores[piece])
                more_value = dense_nt(upstream, probs[piece])
                if number == 0 or start > 0:
                    key_sum[:, here] = more_key
                    value_sum[:, here] = more_value
                else:
                    key_sum[:, here] += more_key
                    value_sum[:, here] += more_value
                at += length
            for j in sides:
                turn = got[:, j * count : (j + 1) * count] * SCALE
                where = head_rows((group * EACH + j) * HD)
                if scored:
                    high_part = turn.astype(LOW)
                    rest = (turn - high_part.astype(jnp.float32)).astype(LOW)
                    turn = dense(high_part, pick[...]) + dense(rest, pick[...])
                    out[where] = turned(turn, cos, -sin).astype(LOW)
                else:
                    past = slice(first, first + count)
                    out[where, columns] = turned(turn, cos[:, past], -sin[:, past]).astype(LOW)
        out[head_rows(WIDTH + group * HD)] = turned(key_sum[...] * SCALE, cos, -sin).astype(LOW)
        out[head_rows(WIDTH + KVW + group * HD)] = value_sum[...].astype(LOW)
        return carry

    lax.fori_loop(0, KV, group_of, 0)


def attention_back(low, top, share, grad, cosine, sine, wide, chosen=()):
    tokens = low.shape[1]
    return pl.pallas_call(
        functools.partial(attend_back_kernel, chosen[0].shape[0] if chosen else 0),
        out_shape=jax.ShapeDtypeStruct((wide, tokens), LOW),
        in_specs=[IN_VMEM] * (6 + len(chosen)),
        out_specs=IN_VMEM,
        scratch_shapes=[pltpu.VMEM((HD, tokens), jnp.float32)] * 2,
        compiler_params=pltpu.CompilerParams(vmem_limit_bytes=48 * 2**20),
    )(low, top, share, grad, cosine, sine, *chosen)


def up16(count):
    return -(-count // 16) * 16


def dense(left, right):
    return jnp.dot(left, right, preferred_element_type=jnp.float32)


def dense_t(left, right):
    return lax.dot_general(
        left, right, (((0,), (0,)), ((), ())), preferred_element_type=jnp.float32
    )


def dense_nt(left, right):
    return lax.dot_general(
        left, right, (((1,), (1,)), ((), ())), preferred_element_type=jnp.float32
    )


def spread_matrix(parts, real, padded):
    feature = jnp.arange(parts * real)
    place = feature // real * padded + feature % real
    return (place[:, None] == jnp.arange(parts * padded)[None, :]).astype(LOW)


def inverse_rms(x, width):
    return lax.rsqrt(jnp.sum(x * x, axis=-1, keepdims=True) / width + EPS)


def norm_back(x, scale, gain, upstream, width):
    inner = upstream * gain
    grad_gain = jnp.sum(upstream * x * scale, axis=0)
    mean = jnp.sum(inner * x, axis=-1, keepdims=True) / width
    return (scale * inner - x * scale**3 * mean, grad_gain)


def rotary_angles():
    place = jnp.arange(TOK_MB)
    rotary = jnp.where(place >= PROMPT, PROMPT + (place - PROMPT) % CONT, place).astype(jnp.float32)
    freq = THETA ** (-2.0 * jnp.arange(HD // 2).astype(jnp.float32) / HD)
    angle = freq[:, None] * rotary[None, :]
    return (jnp.cos(angle), jnp.sin(angle))


def dense_tt(left, right):
    return lax.dot_general(
        left, right, (((0,), (1,)), ((), ())), preferred_element_type=jnp.float32
    )


def mlp(b, w_gu, w_down):
    gate_up = dense(b, w_gu)
    half = gate_up.shape[1] // 2
    gate, upper = (gate_up[:, :half], gate_up[:, half:])
    hidden = (jax.nn.silu(gate) * upper).astype(LOW)
    return (dense(hidden, w_down), gate, upper, hidden)


def mlp_back(branch, b, gate, upper, hidden, w_gu, w_down):
    grad_down = dense_t(hidden, branch)
    grad_hidden = dense_nt(branch, w_down)
    sig = jax.nn.sigmoid(gate)
    grad_gate = grad_hidden * upper * sig * (1.0 + gate * (1.0 - sig))
    grad_upper = grad_hidden * gate * sig
    grad_gate_up = jnp.concatenate([grad_gate, grad_upper], axis=1).astype(LOW)
    return (grad_down, dense_t(b, grad_gate_up), dense_nt(grad_gate_up, w_gu))


def lamb_parts(weight, grad, first, second, decay):
    first_new = BETA_ONE * first + (1.0 - BETA_ONE) * grad
    second_new = BETA_TWO * second + (1.0 - BETA_TWO) * grad * grad
    root = (1.0 - BETA_TWO**STEP) ** 0.5
    scale = root / (1.0 - BETA_ONE**STEP)
    update = first_new * scale / (second_new * lax.rsqrt(second_new) + ADAM_EPS * root) + decay * weight
    return (first_new, second_new, update)


def lookup_ranks(ids, vshard):
    place = jnp.arange(ids.shape[0])
    same = ids[:, None] == ids[None, :]
    first = jnp.min(jnp.where(same, place[None, :], ids.shape[0]), axis=1)
    owner = ids // vshard
    before = (
        (owner[:, None] == owner[None, :])
        & (first == place)[None, :]
        & (place[None, :] < first[:, None])
    )
    return (owner, jnp.sum(before.astype(jnp.int32), axis=1))


def lookup_round(ids, owner, rank, turn, slots, parts, vshard):
    slot = jnp.where(rank // slots == turn, owner * slots + rank - turn * slots, -1)
    onehot = slot[:, None] == jnp.arange(parts * slots)[None, :]
    wanted = jnp.max(jnp.where(onehot, (ids - owner * vshard)[:, None], -1), axis=0)
    return (onehot.astype(LOW), wanted)


def shards(
    token_ids,
    scored,
    targets,
    pairs,
    table,
    w_qkv,
    w_out,
    w_gu,
    w_down,
    gains,
    final_gain,
    first_table,
    first_qkv,
    first_out,
    first_gu,
    first_down,
    first_gains,
    first_final,
    second_table,
    second_qkv,
    second_out,
    second_gu,
    second_down,
    second_gains,
    second_final,
):
    n = lax.axis_size("fsdp")
    sections = lax.axis_size("section")
    section_index = lax.axis_index("section")
    fsdp_index = lax.axis_index("fsdp")
    leader = section_index == 0
    vshard, width = table.shape
    vstart = fsdp_index * vshard
    r = w_qkv.shape[1]
    rp = up16(r)
    rd = w_down.shape[1]
    rdp = up16(rd)
    wide = n * rp
    ffp = n * rdp
    slots = up16(768 // n)
    sel = spread_matrix(n, r, rp)
    sel_wide = jnp.pad(sel, ((0, wide - width), (0, 0)))
    fast = (sections, n) == (2, 16)
    qkv_wide = -(-w_qkv.shape[2] // 128) * 128

    qkv_block = jnp.pad(
        w_qkv[0].astype(LOW), ((0, rp - r), (0, qkv_wide - w_qkv.shape[2]))
    )
    out_block = jnp.pad(dense(w_out[0].astype(LOW), sel).astype(LOW), ((0, rp - r), (0, 0)))
    gu_block = w_gu[0].astype(LOW)
    if rdp != rd:
        gu_block = jnp.pad(gu_block.reshape(r, 2, n, rd), ((0, 0), (0, 0), (0, 0), (0, rdp - rd)))
    gu_block = jnp.pad(gu_block.reshape(r, 2 * ffp), ((0, rp - r), (0, 0)))
    down_block = jnp.pad(dense(w_down[0].astype(LOW), sel).astype(LOW), ((0, rdp - rd), (0, 0)))
    gain_block = jnp.pad(
        jnp.concatenate([gains[0], final_gain[None]], axis=0).astype(LOW),
        ((0, 13), (0, 128 - r)),
    )

    ids = token_ids[0]
    owner, rank = lookup_ranks(ids, vshard)
    onehot, wanted = lookup_round(ids, owner, rank, 0, slots, n, vshard)
    turns_here = jnp.max(rank) // slots + 1
    own_targets = lax.dynamic_slice_in_dim(targets[0], fsdp_index * NCONT, NCONT).reshape(-1)
    note = jnp.concatenate(
        [wanted, jnp.pad(own_targets, (0, 128 - NCONT * SCORED)), jnp.full((128,), turns_here, jnp.int32)]
    )
    if fast:
        notes = exchange(note.reshape(-1, 128), 0).reshape(sections * n, -1)
    else:
        notes = lax.all_gather(note, BOTH, axis=0)
    turns = jnp.max(notes[:, -1])
    wanted_rows = notes[:, n * slots : n * slots + NCONT * SCORED].reshape(-1)

    def asked(all_wanted):
        mine = lax.dynamic_slice_in_dim(all_wanted.reshape(sections, n, n, slots), fsdp_index, 1, 2)
        return mine[:, :, 0]

    asked_first = asked(notes[:, : n * slots])
    asked_here = lax.dynamic_index_in_dim(asked_first, section_index, 0, keepdims=False).reshape(-1)
    table_low, rows = padded_table(asked_here, sel_wide, table.T)
    rows = rows.reshape(n, slots, wide)

    blocks = (qkv_block, out_block, gu_block, down_block, gain_block)
    if fast:
        gathered = gather_all(blocks, WEIGHT_PIECES, 1, rows)
        got = gathered[10]
        gathered = (gathered[:5], gathered[5:10])
    else:
        got = lax.all_to_all(rows, "fsdp", 0, 0)
        gathered = [lax.all_gather(block, BOTH, axis=0) for block in blocks]
        gathered = [[g[k * n : (k + 1) * n] for g in gathered] for k in range(sections)]
    qkv_all, out_all, gu_all, down_all, gain_all = [
        [section[k].reshape(n * blocks[k].shape[0], -1) for section in gathered] for k in range(5)
    ]
    gain_all = jnp.stack([g.reshape(n, 16, 128)[:, :3, :rp] for g in gain_all])
    gain_all = jnp.moveaxis(gain_all, 2, 1).reshape(sections, 3, wide).astype(jnp.float32)
    final_all = gain_all[0, 2]
    x0 = dense(onehot, got.reshape(n * slots, wide))

    def fetch_more(state):
        turn, total = state
        choose, more = lookup_round(ids, owner, rank, turn, slots, n, vshard)
        here = asked(lax.all_gather(more, BOTH, axis=0))
        here = lax.dynamic_index_in_dim(here, section_index, 0, keepdims=False).reshape(-1)
        rows = dense(jnp.take(table_low, jnp.maximum(here, 0), axis=0), sel_wide).astype(LOW)
        got = lax.all_to_all(rows.reshape(n, slots, wide), "fsdp", 0, 0).reshape(n * slots, wide)
        return (turn + 1, total + dense(choose, got))

    x0 = lax.while_loop(lambda state: state[0] < turns, fetch_more, (jnp.int32(1), x0))[1]

    everyone = jnp.arange(TOK_MB)
    cosine, sine = rotary_angles()
    x = x0
    kept = []
    for layer in range(sections - 1):
        scale_a = inverse_rms(x, width)
        a = (x * scale_a * gain_all[layer, 0]).astype(LOW)
        low, attended, top, share = attention(dense_tt(qkv_all[layer], a), cosine, sine)
        attended = dense_t(attended, sel).astype(LOW)
        mixed = x + dense(attended, out_all[layer])
        scale_b = inverse_rms(mixed, width)
        b = (mixed * scale_b * gain_all[layer, 1]).astype(LOW)
        branch, gate, upper, hidden = mlp(b, gu_all[layer], down_all[layer])
        kept.append((x, scale_a, a, low, top, share, attended, mixed, scale_b, b, gate, upper, hidden))
        x = mixed + branch

    last = sections - 1
    place = (PROMPT + CONT * jnp.arange(NCONT)[:, None] + scored[0]).reshape(-1)
    taken = place.shape[0]
    place = jnp.pad(place, (0, -taken % 128), constant_values=PROMPT)
    real = jnp.arange(place.shape[0]) < taken
    pick = ((place[:, None] == everyone[None, :]) & real[:, None]).astype(LOW)
    pick32 = pick.astype(jnp.float32)
    picking = (pick, jnp.stack([place, PROMPT + (place - PROMPT) // CONT * CONT]))
    scale_last = inverse_rms(x, width)
    a_last = (x * scale_last * gain_all[last, 0]).astype(LOW)
    low_last, attended_s, top_s, share_s, queries = attention(
        dense_tt(qkv_all[last], a_last), cosine, sine, picking
    )
    x_s = jnp.dot(pick32, x, precision=HI)
    attended_s = dense_t(attended_s, sel).astype(LOW)
    mixed_s = x_s + dense(attended_s, out_all[last])
    scale_s = inverse_rms(mixed_s, width)
    b_s = (mixed_s * scale_s * gain_all[last, 1]).astype(LOW)
    branch_s, gate_s, upper_s, hidden_s = mlp(b_s, gu_all[last], down_all[last])
    y_s = mixed_s + branch_s
    scale_y = inverse_rms(y_s, width)
    head_in = dense_nt((y_s * scale_y * final_all).astype(LOW), sel_wide).astype(LOW)[:taken]

    if fast:
        rows_all = jnp.concatenate(gather_all([head_in], [(0, 16 * k, 16, k % 2) for k in range(4)], 2))
    else:
        rows_all = lax.all_gather(head_in, BOTH, axis=0)
    rows_all = rows_all.reshape(-1, wide)
    own_rows = rows_all.shape[0] // sections
    wanted_here = wanted_rows - vstart
    logits, top_here, total_here, target_here = logits_of(wanted_here, rows_all, table_low)
    stats = jnp.concatenate([top_here, total_here, target_here])
    if fast:
        stats = exchange(stats.reshape(-1, 128), 3, whole=False).reshape(n, 3, -1)
    else:
        stats = lax.all_gather(stats, "fsdp", axis=0)
    top = jnp.max(stats[:, 0], axis=0)
    total = jnp.sum(stats[:, 1] * jnp.exp(stats[:, 0] - top), axis=0)
    row_logp = jnp.sum(stats[:, 2], axis=0) - top - jnp.log(total)
    seq = jnp.sum(row_logp.reshape(-1, SCORED), axis=1)
    pair = pairs.reshape(-1, 2)
    conts = jnp.arange(seq.shape[0])
    chosen = (pair[:, 0][:, None] == conts[None, :]).astype(jnp.float32)
    passed = (pair[:, 1][:, None] == conts[None, :]).astype(jnp.float32)
    delta = jnp.sum((chosen - passed) * seq[None, :], axis=1)
    loss = jnp.sum(jax.nn.softplus(-BETA * delta))
    push = BETA * jax.nn.sigmoid(-BETA * delta)
    grad_seq = jnp.sum((passed - chosen) * push[:, None], axis=0)
    grad_row = jnp.repeat(grad_seq, SCORED)
    grad_logits, grad_rows = logits_back(
        section_index, wanted_here, top, grad_row / total, grad_row, logits, table_low, sections
    )
    if fast:
        halves = [[grad_rows[k * own_rows : (k + 1) * own_rows]] for k in range(sections)]
        grad_head = reduce_all(halves, 4, 1, tile=16)[0]
    else:
        grad_head = lax.psum_scatter(grad_rows, BOTH, scatter_dimension=0, tiled=True)
    grad_head = jnp.pad(grad_head.astype(jnp.float32), ((0, place.shape[0] - taken), (0, 0)))
    grad_z = jnp.dot(grad_head, sel_wide.astype(jnp.float32), precision=HI)
    grad_y, grad_final = norm_back(y_s, scale_y, final_all, grad_z, width)

    grads = [None] * sections
    g_down, g_gu, grad_b = mlp_back(
        grad_y.astype(LOW), b_s, gate_s, upper_s, hidden_s, gu_all[last], down_all[last]
    )
    grad_mid, gain_two = norm_back(mixed_s, scale_s, gain_all[last, 1], grad_b, width)
    grad_mixed = grad_mid + grad_y
    branch = grad_mixed.astype(LOW)
    g_out = dense_t(attended_s, branch)
    grad_att = dense_nt(sel, dense_nt(branch, out_all[last]).astype(LOW)).astype(LOW)
    grad_qkv = attention_back(
        low_last, top_s, share_s, grad_att, cosine, sine, qkv_wide, picking + (queries,)
    )
    g_qkv = dense_tt(a_last, grad_qkv)
    grad_in, gain_one = norm_back(
        x, scale_last, gain_all[last, 0], dense_tt(grad_qkv, qkv_all[last]), width
    )
    upstream = grad_in + lax.dot_general(pick32, grad_mixed, (((0,), (0,)), ((), ())), precision=HI)
    grads[last] = (g_qkv, g_out, g_gu, g_down, jnp.stack([gain_one, gain_two]))

    for layer in range(sections - 2, -1, -1):
        (x, scale_a, a, low, top, share, attended, mixed, scale_b, b, gate, upper, hidden) = kept[layer]
        g_down, g_gu, grad_b = mlp_back(
            upstream.astype(LOW), b, gate, upper, hidden, gu_all[layer], down_all[layer]
        )
        grad_mid, gain_two = norm_back(mixed, scale_b, gain_all[layer, 1], grad_b, width)
        grad_mixed = grad_mid + upstream
        branch = grad_mixed.astype(LOW)
        g_out = dense_t(attended, branch)
        grad_att = dense_nt(sel, dense_nt(branch, out_all[layer]).astype(LOW)).astype(LOW)
        grad_qkv = attention_back(low, top, share, grad_att, cosine, sine, qkv_wide)
        g_qkv = dense_tt(a, grad_qkv)
        grad_in, gain_one = norm_back(
            x, scale_a, gain_all[layer, 0], dense_tt(grad_qkv, qkv_all[layer]), width
        )
        upstream = grad_in + grad_mixed
        grads[layer] = (g_qkv, g_out, g_gu, g_down, jnp.stack([gain_one, gain_two]))

    grad_x0 = dense_nt(upstream.astype(LOW), sel_wide).astype(LOW)

    def give(all_asked, choose):
        rows = dense_t(choose, grad_x0).astype(LOW)
        got = lax.all_to_all(rows.reshape(n, slots, wide), "fsdp", 0, 0)
        return (all_asked.reshape(-1), lax.all_gather(got, "section", axis=0).reshape(-1, wide))

    def give_more(state):
        turn, grad, squares = state
        choose, more = lookup_round(ids, owner, rank, turn, slots, n, vshard)
        places, got = give(asked(lax.all_gather(more, BOTH, axis=0)), choose)
        place_of = (jnp.arange(vshard)[:, None] == places[None, :]).astype(LOW)
        new = grad.astype(jnp.float32) + lax.dot_general(
            got[:, :width], place_of, (((0,), (1,)), ((), ())), preferred_element_type=jnp.float32
        )
        every = squares[1] + jnp.where(leader, jnp.sum(new**2), 0.0)
        return (turn + 1, new.astype(LOW), squares.at[0].set(every))

    def gain_rows(layer):
        rows = jnp.concatenate([grads[layer][4], grad_final[None]], axis=0).reshape(3, n, rp)
        rows = jnp.pad(jnp.moveaxis(rows, 0, 1), ((0, 0), (0, TILE_R - 3), (0, 128 - rp)))
        return rows.reshape(n * TILE_R, 128)

    outward = [
        [g.astype(LOW) for g in grads[layer][:4] + (gain_rows(layer),)] for layer in range(sections)
    ]
    if fast:
        rows = dense_t(onehot, grad_x0).astype(LOW).reshape(n, slots, wide)
        *summed, got = reduce_all(outward, 5, 2, rows)
    else:
        summed = [
            lax.psum_scatter(
                jnp.concatenate(arrays, axis=0), BOTH, scatter_dimension=0, tiled=True
            ).astype(jnp.float32)
            for arrays in zip(*outward)
        ]
        got = give(asked_first, onehot)[1]
    if rdp != rd:
        summed[2] = summed[2].reshape(rp, 2, n, rdp)[:, :, :, :rd].reshape(rp, 2 * n * rd)
    grad_table, grad_squares = table_grad(
        leader.astype(jnp.float32),
        asked_first.reshape(-1),
        got.reshape(-1, wide).T,
        rows_all.T,
        grad_logits,
        summed,
        width,
    )
    grad_table, grad_squares = lax.while_loop(
        lambda state: state[0] < turns, give_more, (jnp.int32(1), grad_table, grad_squares)
    )[1:]

    def everyones(sums, name):
        if fast:
            return exchange(sums, name)
        return lax.all_gather(sums, BOTH, axis=0)

    grad_norm = jnp.sqrt(jnp.sum(everyones(grad_squares, 6)[:, 0, 0]))
    clip = jnp.minimum(1.0, CLIP / grad_norm)

    def views(arrays):
        out = [arrays[0].T] + [a.transpose(1, 0, 2) for a in arrays[1:4]]
        return out + [arrays[4][0], arrays[5][0], arrays[6][None]]

    weights_all = views((table, w_qkv, w_out, w_gu, w_down, gains, final_gain))
    grads_all = [grad_table] + summed[:4] + [summed[4][:2, :r], summed[4][2:3, :r]]
    new_firsts, new_seconds, updates, kept_weights, sums = moments(
        clip,
        sel,
        weights_all,
        grads_all,
        views((first_table, first_qkv, first_out, first_gu, first_down, first_gains, first_final)),
        views((second_table, second_qkv, second_out, second_gu, second_down, second_gains, second_final)),
        (DECAY,) * 5 + (0.0, 0.0),
    )
    sums = everyones(sums, 7)[:, :, 0].reshape(sections, n, 2, 8)
    sums = jnp.sum(sums, axis=1)
    layered = jnp.moveaxis(sums[:, :, 1:7], 1, 0).reshape(2, -1)
    matrix_norms = jnp.sqrt(jnp.concatenate([layered, sums[0, :, 0:1], sums[0, :, 7:8]], axis=1))
    trust_ratio = matrix_norms[0] / matrix_norms[1]
    own = lax.dynamic_slice_in_dim(trust_ratio, 6 * section_index, 6)
    last_two = trust_ratio[6 * sections :]
    new, half = apply_updates(
        jnp.concatenate([last_two[:1], own[:4]]),
        [weights_all[0], *kept_weights, weights_all[4]],
        updates[:5],
        [w.shape for w in weights_all[:5]],
    )
    new = list(new) + [
        weights_all[5] - RATE * own[4:6][:, None] * updates[5],
        weights_all[6] - RATE * last_two[1] * updates[6],
    ]

    def back(k, array):
        if k == 0:
            return array.T
        if k == 6:
            return array[0]
        return array.transpose(1, 0, 2) if array.ndim == 3 else array[None]

    outs = [loss, grad_norm, matrix_norms]
    for k in range(7):
        outs += [back(k, t[k]) for t in (new, new_firsts, new_seconds)]
    return tuple(outs + [back(k, half[k]) for k in range(5)])


def solution(mesh):
    tall, layered, gainy, flat = (
        P("fsdp", None),
        P("section", "fsdp", None),
        P("section", None, "fsdp"),
        P("fsdp"),
    )
    weights = (tall, layered, layered, layered, layered, gainy, flat)
    placed = (
        P("section", "fsdp"),
        P("section", "fsdp", None),
        P("section", None, None),
        P(),
    ) + weights * 3
    results = (P(), P(), P())
    for spec in weights:
        results += (spec, spec, spec)
    return jax.shard_map(
        shards, mesh=mesh, in_specs=placed, out_specs=results + weights[:5], check_vma=False
    )
```

```python
import functools

import jax
import jax.numpy as jnp
from jax import lax
from jax.experimental import pallas as pl
from jax.experimental.pallas import tpu as pltpu
from jax.sharding import PartitionSpec as P

HEADS = 15
KV = 5
HD = 64
FF = 2560
PROMPT = 256
NCONT = 2
CONT = 128
SCORED = 32
STEP = 10
TOK_MB = 512

EPS = 1e-05
SCALE = 0.125
THETA = 100000.0
BETA = 0.1
CLIP = 1.0
RATE = 0.3
BETA_ONE = 0.9
BETA_TWO = 0.99
ADAM_EPS = 1e-08
DECAY = 0.01

WIDTH = HEADS * HD
KVW = KV * HD
BOTH = ("section", "fsdp")
HI = lax.Precision.HIGHEST
LOW = jnp.bfloat16

WEIGHT_PIECES = [
    (0, 0, 64, 0),
    (1, 0, 64, 1),
    (2, 0, 16, 0),
    (2, 16, 16, 1),
    (2, 32, 16, 0),
    (2, 48, 16, 1),
    (3, 0, 80, 0),
    (3, 80, 80, 1),
    (4, 0, 16, 1),
]

MESH = pl.DeviceIdType.MESH
ANYWHERE = pl.BlockSpec(memory_space=pl.ANY)
IN_VMEM = pl.BlockSpec(memory_space=pltpu.VMEM)
TILE_R, TILE_C = 32, 1024


def coords():
    f = lax.axis_index("fsdp")
    return (lax.axis_index("section"), f // 4, f // 2 % 2, f % 2)


def device(y, z, x, c):
    return (y, z * 4 + x * 2 + c)


def greet(peers):
    barrier = pltpu.get_barrier_semaphore()
    for peer in peers:
        pl.semaphore_signal(barrier, inc=1, device_id=peer, device_id_type=MESH)
    pl.semaphore_wait(barrier, len(peers))


def send(src, dst, send_sem, recv_sem, peer):
    pltpu.make_async_remote_copy(
        src_ref=src,
        dst_ref=dst,
        send_sem=send_sem,
        recv_sem=recv_sem,
        device_id=peer,
        device_id_type=MESH,
    ).start()


def settle(ref, sem):
    pltpu.make_async_copy(ref, ref, sem).wait()


def gather_kernel(pieces, count, carried, *refs):
    y, f = (lax.axis_index("section"), lax.axis_index("fsdp"))
    z, x, c = coords()[1:]
    in_line = [((z + k) % 4) * 4 + x * 2 + c for k in range(1, 4)]
    near = [f + 2 - 4 * x, f + 1 - 2 * c]
    away = [(f + k) % 16 for k in range(1, 16)] if carried else in_line + near
    greet([device(1 - y, z, x, c)] + [(y, peer) for peer in away])
    moved = (refs[:count], refs[count + carried : 3 * count + carried])
    sems = refs[3 * count + carried + (2 if carried else 0) :][:4]

    def phase(name, p=None):
        for section in range(2):
            pl.when(y == section)(functools.partial(gather_section, section, pieces, moved, sems, name, p))

    phase("own")
    if not carried:
        for p in range(len(pieces)):
            phase("line", p)
        phase("rest")
        return
    asked, sel, table = refs[count : count + carried]
    low, got = refs[3 * count + carried : 3 * count + carried + 2]
    tiles, lows, total, rows, tile_sem, low_sem, carry_sem = refs[3 * count + carried + 6 :]
    width, tall = tiles.shape[1:]
    steps = table.shape[1] // tall
    columns = [pl.ds(i * tall, tall) for i in range(steps)]
    eye = lax.broadcasted_iota(jnp.int32, (tall, tall), 0) == lax.broadcasted_iota(jnp.int32, (tall, tall), 1)
    total[...] = jnp.zeros_like(total)
    lows[...] = jnp.zeros_like(lows)

    def tile_copy(i):
        return pltpu.make_async_copy(table.at[:, columns[i]], tiles.at[i % 2], tile_sem.at[i % 2])

    def low_copy(i):
        return pltpu.make_async_copy(lows.at[i % 2], low.at[columns[i]], low_sem.at[i % 2])

    def tile(i):
        if i + 1 < steps:
            tile_copy(i + 1).start()
        tile_copy(i).wait()
        if i >= 2:
            low_copy(i - 2).wait()
        lows[i % 2, :, pl.ds(0, width)] = dense_nt(eye.astype(LOW), tiles[i % 2].astype(LOW)).astype(LOW)
        place = lax.broadcasted_iota(jnp.int32, (asked.shape[0], tall), 1) + i * tall
        total[...] += dense((asked[...] == place).astype(LOW), lows[i % 2])
        low_copy(i).start()

    tile_copy(0).start()
    for p in range(len(pieces)):
        for i in (2 * p, 2 * p + 1):
            if i < steps:
                tile(i)
        if 2 * p + 2 == steps:
            rows[...] = dense(total[...].astype(LOW), sel[...]).astype(LOW).reshape(rows.shape)
            for k in range(1, 16):
                peer = (f + k) % 16
                send(rows.at[peer], got.at[f], carry_sem.at[0], carry_sem.at[1], (y, peer))
            pltpu.make_async_copy(rows.at[f], got.at[f], carry_sem.at[2]).start()
        phase("line", p)
    phase("rest")
    low_copy(steps - 2).wait()
    low_copy(steps - 1).wait()
    settle(rows.at[pl.ds(0, 15)], carry_sem.at[0])
    settle(rows.at[pl.ds(0, 15)], carry_sem.at[1])
    settle(rows.at[0], carry_sem.at[2])


def gather_section(y, pieces, moved, sems, name, number):
    blocks, outs = moved
    count = len(blocks)
    send_sem, recv_sem, sib_sem, own_sem = sems
    z, x, c = coords()[1:]
    to_x, to_y, to_sib = (device(y, z, 1 - x, c), device(1 - y, z, x, c), device(y, z, x, 1 - c))
    zs = [(z + k) % 4 for k in range(4)]

    def part(ref, p):
        return ref.at[pl.ds(pieces[p][1], pieces[p][2])]

    def there(p, o):
        return part(outs[o[0] * count + pieces[p][0]].at[o[1] * 4 + o[2] * 2 + c], p)

    def mark(p, o):
        return recv_sem.at[p, o[0] * 8 + o[1] * 2 + o[2]]

    def push(p, o, peer, own=False, sib=False):
        src = part(blocks[pieces[p][0]], p) if own else there(p, o)
        send(src, there(p, o), send_sem.at[p], sib_sem.at[p] if sib else mark(p, o), peer)

    every = range(len(pieces))
    for p in every if name == "own" else ():
        me = (y, z, x)
        push(p, me, to_x, own=True)
        push(p, me, to_y, own=True)
        for zz in zs[1:]:
            push(p, me, device(y, zz, x, c), own=True)
        push(p, me, to_sib, own=True, sib=True)
        pltpu.make_async_copy(part(blocks[pieces[p][0]], p), there(p, me), own_sem).start()
    def from_x(p, zz):
        o = (y, zz, 1 - x)
        settle(there(p, o), mark(p, o))
        if pieces[p][3] == 0:
            push(p, o, to_y)
        push(p, o, to_sib, sib=True)

    def from_y(p, zz):
        o = (1 - y, zz, x)
        settle(there(p, o), mark(p, o))
        if pieces[p][3] == 1:
            push(p, o, to_x)
        push(p, o, to_sib, sib=True)

    if name == "line":
        p = number
        for zz in zs[1:]:
            o = (y, zz, x)
            settle(there(p, o), mark(p, o))
            push(p, o, to_x)
            push(p, o, to_y)
            push(p, o, to_sib, sib=True)
        from_x(p, z)
        from_y(p, z)
    if name != "rest":
        return
    for p in every:
        for zz in zs[1:]:
            from_x(p, zz)
            from_y(p, zz)
    for p in every:
        for zz in zs:
            o = (1 - y, zz, 1 - x)
            settle(there(p, o), mark(p, o))
            push(p, o, to_sib, sib=True)
    for p in every:
        a, start, rows_each, unused = pieces[p]
        settle(part(blocks[a], p), own_sem)
        for times in (16, 15):
            settle(outs[a].at[pl.ds(0, times), pl.ds(start, rows_each)], send_sem.at[p])
        settle(outs[a].at[pl.ds(0, 16), pl.ds(start, rows_each)], sib_sem.at[p])


def gather_all(blocks, pieces, name, extra=(), slots=0):
    many = len(pieces)
    shapes = [jax.ShapeDtypeStruct((16,) + b.shape, b.dtype) for b in blocks] * 2
    scratch = [
        pltpu.SemaphoreType.DMA((many,)),
        pltpu.SemaphoreType.DMA((many, 16)),
        pltpu.SemaphoreType.DMA((many,)),
        pltpu.SemaphoreType.DMA,
    ]
    if extra:
        (deep, wide), (width, height) = (extra[1].shape, extra[2].shape)
        shapes += [jax.ShapeDtypeStruct((height, deep), LOW), jax.ShapeDtypeStruct((16, slots, wide), LOW)]
        tall = tall_of(height)
        scratch += [
            pltpu.VMEM((2, width, tall), jnp.float32),
            pltpu.VMEM((2, tall, deep), LOW),
            pltpu.VMEM((16 * slots, deep), jnp.float32),
            pltpu.VMEM((16, slots, wide), LOW),
            pltpu.SemaphoreType.DMA((2,)),
            pltpu.SemaphoreType.DMA((2,)),
            pltpu.SemaphoreType.DMA((3,)),
        ]
    return pl.pallas_call(
        functools.partial(gather_kernel, pieces, len(blocks), len(extra)),
        out_shape=shapes,
        in_specs=[ANYWHERE] * len(blocks) + [IN_VMEM, IN_VMEM, ANYWHERE][: len(extra)],
        out_specs=[ANYWHERE] * len(shapes),
        scratch_shapes=scratch,
        compiler_params=pltpu.CompilerParams(
            collective_id=name, has_side_effects=True, vmem_limit_bytes=32 * 2**20
        ),
    )(*blocks, *extra)


def reduce_pieces(shapes, tile):
    out = []
    for a, (rows, cols) in enumerate(shapes):
        for row in range(0, rows, tile):
            for col in range(0, cols, TILE_C):
                out.append((a, row, col, min(TILE_C, cols - col)))
    return out


RING = 8


def reduce_kernel(pieces, tile, count, carried, lag, *refs):
    many = len(pieces)
    ring = min(RING, many)
    grads = (refs[:count], refs[count : 2 * count])
    at = 2 * count + carried
    outs = refs[at : at + count]
    at += count
    if carried:
        rows, asked, head_rows_all, grad_logits = refs[2 * count : 2 * count + carried]
        theirs, got, grad_table, sums = refs[at : at + 4]
        at += 4
    held, from_one, from_two, from_z, mine, other = refs[at : at + 6]
    sib_recv, sib_send, recv_one, send_one, recv_two, send_two, recv_z, send_z, own_sem, other_sem = refs[
        at + 6 : at + 16
    ]
    if not carried:
        theirs = other
    y, z, x, c = coords()
    to_x, to_y, to_sib = (device(y, z, 1 - x, c), device(1 - y, z, x, c), device(y, z, x, 1 - c))
    zs = [(z + k) % 4 for k in range(4)]
    f = lax.axis_index("fsdp")
    me = y * 16 + f
    alike = [(y, (f + k) % 16) for k in range(1, 16)]
    others = [(1 - y, (f + k) % 16) for k in range(16)]
    near = [to_x, to_y, to_sib] + [device(y, zz, x, c) for zz in zs[1:]]
    greet(alike + others if carried else near)

    def source(p, yo, xo, core):
        a, row, col, cols = pieces[p]
        return grads[yo][a].at[:, xo, core, pl.ds(row, tile), pl.ds(col, cols)]

    def cut(ref, p):
        cols = pieces[p][3]
        return ref if cols == TILE_C else ref.at[..., pl.ds(0, cols)]

    def fetch(p):
        for yo in range(2):
            for xo in range(2):
                pltpu.make_async_copy(
                    source(p, yo, xo, c), cut(mine.at[p % 2, yo, xo], p), own_sem.at[p % 2]
                ).start()

    def fetch_other(p):
        settle(cut(theirs.at[p], p), sib_recv.at[p])
        if carried:
            pltpu.make_async_copy(cut(theirs.at[p], p), cut(other.at[p % 2], p), other_sem.at[p % 2]).start()

    for p in range(many):
        for yo in range(2):
            for xo in range(2):
                send(
                    source(p, yo, xo, 1 - c),
                    cut(theirs.at[p, yo, xo], p),
                    sib_send.at[p],
                    sib_recv.at[p],
                    to_sib,
                )
        if p == 0:
            fetch(0)

    def store_sum(dst, left, right, p):
        cols = pl.ds(0, pieces[p][3])
        dst[:, cols] = (left[:, cols].astype(jnp.float32) + right[:, cols].astype(jnp.float32)).astype(LOW)

    def settle_sends(p):
        settle(cut(from_one.at[p], p), send_one.at[p])
        settle(cut(from_two.at[p], p), send_two.at[p])
        settle(cut(from_z.at[p], p), send_z.at[p])

    def two_cores(p):
        if p == 0:
            fetch_other(0)
        if p + 1 < many:
            fetch(p + 1)
            fetch_other(p + 1)
        if p >= ring:
            settle_sends(p - ring)
        settle(cut(mine.at[p % 2], p), own_sem.at[p % 2])
        if carried:
            settle(cut(other.at[p % 2], p), other_sem.at[p % 2])
        right, left, here = (other.at[p % 2] if carried else theirs.at[p], mine.at[p % 2], held.at[p % ring])

        def each(i, carry):
            where = (i // 8, i // 4 % 2, i % 4)
            store_sum(here.at[where], left.at[where], right.at[where], p)
            return carry

        lax.fori_loop(0, 16, each, 0)
        if p % 2 == 0:
            send(cut(here.at[1 - y], p), cut(from_one.at[p], p), send_one.at[p], recv_one.at[p], to_y)
        else:
            for yo in range(2):
                send(
                    cut(here.at[yo, 1 - x], p),
                    cut(from_one.at[p, yo], p),
                    send_one.at[p],
                    recv_one.at[p],
                    to_x,
                )

    def first_axis(p):
        settle(cut(from_one.at[p], p), recv_one.at[p])
        here = held.at[p % ring]

        def each(i, carry):
            where = (y, i // 4, i % 4) if p % 2 == 0 else (i // 4, x, i % 4)
            store_sum(here.at[where], here.at[where], from_one.at[p, i // 4, i % 4], p)
            return carry

        lax.fori_loop(0, 8, each, 0)
        src, peer = (here.at[y, 1 - x], to_x) if p % 2 == 0 else (here.at[1 - y, x], to_y)
        send(cut(src, p), cut(from_two.at[p], p), send_two.at[p], recv_two.at[p], peer)

    def second_axis(p):
        settle(cut(from_two.at[p], p), recv_two.at[p])
        here = held.at[p % ring, y, x]

        def each(i, carry):
            store_sum(here.at[i], here.at[i], from_two.at[p, i], p)
            return carry

        lax.fori_loop(0, 4, each, 0)
        for k in range(1, 4):
            send(
                cut(here.at[zs[k]], p),
                cut(from_z.at[p, 3 - k], p),
                send_z.at[p],
                recv_z.at[p],
                device(y, zs[k], x, c),
            )

    def along_z(p):
        settle(cut(from_z.at[p], p), recv_z.at[p])
        a, row, col, cols = pieces[p]
        part = pl.ds(0, cols)
        total = held[p % ring, y, x, z, :, part].astype(jnp.float32)
        for k in range(3):
            total = total + from_z[p, k, :, part].astype(jnp.float32)
        outs[a][pl.ds(row, tile), pl.ds(col, cols)] = total

    between = [()] * (many + 3 * lag)
    if carried:
        natural, turned_rows, turned_got, tiles, made, squares, carry_sem, tile_sem, made_sem, sum_sem = refs[
            at + 16 :
        ]
        between = carried_work(
            (me, y, f, to_y, alike, others),
            (rows, asked, head_rows_all, grad_logits, got, grad_table, sums, outs),
            (natural, turned_rows, turned_got, tiles, made, squares),
            (carry_sem, tile_sem, made_sem, sum_sem),
            many + 3 * lag,
        )
    for step in range(many + 3 * lag):
        for work in between[step]:
            work()
        for k, stage in enumerate((two_cores, first_axis, second_axis, along_z)):
            if 0 <= step - k * lag < many:
                stage(step - k * lag)
    for p in range(many):
        settle(cut(theirs.at[p], p), sib_send.at[p])
        if p >= many - ring:
            settle_sends(p)
    if carried:
        between[-1]()


def carried_work(where, arrays, buffers, sems, steps):
    me, y, f, to_y, alike, others = where
    rows, asked, head_rows_all, grad_logits, got, grad_table, sums, outs = arrays
    natural, turned_rows, turned_got, tiles, made, squares = buffers
    carry_sem, tile_sem, made_sem, sum_sem = sems
    height, count = grad_logits.shape
    width = grad_table.shape[0]
    slots = rows.shape[1]
    wide = rows.shape[2]
    tall = tiles.shape[1]
    turns = height // tall
    leader = jnp.where(y == 0, 1.0, 0.0)
    eye = lax.broadcasted_iota(jnp.int32, (tall, tall), 0) == lax.broadcasted_iota(jnp.int32, (tall, tall), 1)

    def turn(source, target):
        for k in range(wide // tall):
            part = pl.ds(k * tall, tall)
            target[part] = dense_nt(eye.astype(LOW), source[:, part]).astype(LOW)

    def start():
        for peer in alike:
            send(rows.at[peer[1]], got.at[me], carry_sem.at[0], carry_sem.at[1], peer)
        pltpu.make_async_copy(rows.at[f], got.at[me], carry_sem.at[2]).start()
        pltpu.make_async_copy(head_rows_all, natural.at[pl.ds(0, count)], carry_sem.at[5]).start()

    def turn_rows():
        settle(natural.at[pl.ds(0, count)], carry_sem.at[5])
        turn(natural.at[pl.ds(0, count)], turned_rows)

    def pass_on():
        settle(rows.at[pl.ds(0, 15)], carry_sem.at[1])
        settle(rows.at[0], carry_sem.at[2])
        ours = got.at[pl.ds(y * 16, 16)]
        send(ours, ours, carry_sem.at[3], carry_sem.at[4], to_y)

    def load_got():
        settle(rows, carry_sem.at[4])
        for k in range(32):
            pltpu.make_async_copy(got.at[k], natural.at[pl.ds(k * slots, slots)], carry_sem.at[5]).start()
        tile_copy(0).start()

    def turn_got():
        settle(natural.at[pl.ds(0, 32 * slots)], carry_sem.at[5])
        turn(natural.at[pl.ds(0, 32 * slots)], turned_got)
        squares[...] = jnp.zeros_like(squares)

    def tile_copy(i):
        return pltpu.make_async_copy(grad_logits.at[pl.ds(i * tall, tall)], tiles.at[i % 2], tile_sem.at[i % 2])

    def made_copy(i):
        return pltpu.make_async_copy(made.at[i % 2], grad_table.at[:, pl.ds(i * tall, tall)], made_sem.at[i % 2])

    def table_tile(i):
        if i + 1 < turns:
            tile_copy(i + 1).start()
        tile_copy(i).wait()
        if i >= 2:
            made_copy(i - 2).wait()
        place = lax.broadcasted_iota(jnp.int32, (tall, asked.shape[1]), 0) + i * tall
        here = dense_nt(turned_rows[...], tiles[i % 2]) + dense_nt(
            turned_got[...], (asked[...] == place).astype(LOW)
        )
        here = here[:width]
        made[i % 2] = here.astype(LOW)
        squares[pl.ds(0, 1)] += leader * squares_of(here)
        made_copy(i).start()

    def end():
        gains = outs[-1][...]
        layers = squares_of(gains[:2]) + leader * squares_of(gains[2:3])
        for out in outs[:-1]:
            layers += squares_of(out[...])
        squares[pl.ds(0, 1)] += layers
        squares[pl.ds(1, 1)] += layers
        for peer in alike + others:
            send(squares, sums.at[me], sum_sem.at[0], sum_sem.at[1], peer)
        sums[me] = squares[...]
        made_copy(turns - 2).wait()
        made_copy(turns - 1).wait()
        settle(rows.at[pl.ds(0, 15)], carry_sem.at[0])
        settle(rows, carry_sem.at[3])
        settle(sums.at[pl.ds(0, 31)], sum_sem.at[0])
        settle(sums.at[pl.ds(0, 31)], sum_sem.at[1])

    plan = [[] for unused in range(steps)]
    plan[0].append(start)
    plan[3].append(turn_rows)
    plan[9].append(pass_on)
    plan[13].append(load_got)
    plan[14].append(turn_got)
    for i in range(turns):
        plan[15 + i * (steps - 16) // turns].append(functools.partial(table_tile, i))
    return plan + [end]


def reduce_all(grads, name, lag, tile=TILE_R, extra=(), width=0):
    count = len(grads[0])
    shapes = [(g.shape[0] // 16, g.shape[1]) for g in grads[0]]
    pieces = reduce_pieces(shapes, tile)
    many = len(pieces)
    views = [g.reshape(4, 2, 2, g.shape[0] // 16, g.shape[1]) for layer in grads for g in layer]
    results = [jax.ShapeDtypeStruct(s, jnp.float32) for s in shapes]
    piece = (2, 2, 4, tile, TILE_C)
    scratch = [
        pltpu.VMEM((min(RING, many),) + piece, LOW),
        pltpu.VMEM((many, 2, 4, tile, TILE_C), LOW),
        pltpu.VMEM((many, 4, tile, TILE_C), LOW),
        pltpu.VMEM((many, 3, tile, TILE_C), LOW),
        pltpu.VMEM((2,) + piece, LOW),
        pltpu.VMEM((2 if extra else many,) + piece, LOW),
    ]
    scratch += [pltpu.SemaphoreType.DMA((many,)) for unused in range(8)]
    scratch += [pltpu.SemaphoreType.DMA((2,)), pltpu.SemaphoreType.DMA((2,))]
    in_specs, out_specs = ([ANYWHERE] * len(views), [IN_VMEM] * count)
    if extra:
        rows, asked, scored_rows, grad_logits = extra
        slots, wide = rows.shape[1:]
        height, total = grad_logits.shape
        tall = tall_of(height)
        results += [
            jax.ShapeDtypeStruct((many,) + piece, LOW),
            jax.ShapeDtypeStruct((32, slots, wide), LOW),
            jax.ShapeDtypeStruct((width, height), LOW),
            jax.ShapeDtypeStruct((32, 8, 128), jnp.float32),
        ]
        in_specs += [ANYWHERE, IN_VMEM, ANYWHERE, ANYWHERE]
        out_specs += [ANYWHERE] * 3 + [IN_VMEM]
        scratch += [
            pltpu.VMEM((max(total, 32 * slots), wide), LOW),
            pltpu.VMEM((wide, total), LOW),
            pltpu.VMEM((wide, 32 * slots), LOW),
            pltpu.VMEM((2, tall, total), LOW),
            pltpu.VMEM((2, width, tall), LOW),
            pltpu.VMEM((8, 128), jnp.float32),
            pltpu.SemaphoreType.DMA((6,)),
            pltpu.SemaphoreType.DMA((2,)),
            pltpu.SemaphoreType.DMA((2,)),
            pltpu.SemaphoreType.DMA((2,)),
        ]
    return pl.pallas_call(
        functools.partial(reduce_kernel, pieces, tile, count, len(extra), lag),
        out_shape=results,
        in_specs=in_specs,
        out_specs=out_specs,
        scratch_shapes=scratch,
        compiler_params=pltpu.CompilerParams(
            collective_id=name, has_side_effects=True, vmem_limit_bytes=(60 if extra else 32) * 2**20
        ),
    )(*views, *extra)


def exchange_kernel(whole, src, out, send_sem, recv_sem, own_sem):
    y, f = (lax.axis_index("section"), lax.axis_index("fsdp"))
    count = 32 if whole else 16
    me = y * 16 + f if whole else f
    peers = [(me + k) % count for k in range(1, count)]
    where = [(p // 16, p % 16) if whole else (y, p) for p in peers]
    greet(where)
    for peer in where:
        send(src, out.at[me], send_sem, recv_sem, peer)
    own = pltpu.make_async_copy(src, out.at[me], own_sem)
    own.start()
    own.wait()
    settle(out.at[pl.ds(0, count - 1)], send_sem)
    settle(out.at[pl.ds(0, count - 1)], recv_sem)


def exchange(small, name, whole=True):
    return pl.pallas_call(
        functools.partial(exchange_kernel, whole),
        out_shape=jax.ShapeDtypeStruct((32 if whole else 16,) + small.shape, small.dtype),
        in_specs=[IN_VMEM],
        out_specs=IN_VMEM,
        scratch_shapes=[pltpu.SemaphoreType.DMA] * 3,
        compiler_params=pltpu.CompilerParams(collective_id=name, has_side_effects=True),
    )(small)


def tall_of(height, sections=2):
    return 256 if height % (256 * sections) == 0 else 128


def whole(shape):
    return pl.BlockSpec(shape, lambda *unused: (0,) * len(shape), pipeline_mode=pl.Buffered(1))


def striped(tall, cols):
    return pl.BlockSpec((tall, cols), lambda i: (i, 0))


def lined(rows, wide):
    return pl.BlockSpec((rows, wide), lambda i: (0, i))


def squares_of(value):
    return jnp.sum(jnp.sum(value * value, axis=1, keepdims=True), axis=0, keepdims=True)


def padded_table_kernel(asked, sel, table, low, rows, total):
    step = pl.program_id(0)

    @pl.when(step == 0)
    def start():
        total[...] = jnp.zeros_like(total)

    width, tall = table.shape
    low[:, pl.ds(low.shape[1] - 128, 128)] = jnp.zeros((tall, 128), LOW)
    eye = lax.broadcasted_iota(jnp.int32, (tall, tall), 0) == lax.broadcasted_iota(jnp.int32, (tall, tall), 1)
    low[:, pl.ds(0, width)] = dense_nt(eye.astype(LOW), table[...].astype(LOW)).astype(LOW)
    place = lax.broadcasted_iota(jnp.int32, (asked.shape[0], tall), 1) + step * tall
    total[...] += dense((asked[...] == place).astype(LOW), low[...])

    @pl.when(step == pl.num_programs(0) - 1)
    def end():
        rows[...] = dense(total[...].astype(LOW), sel[...]).astype(LOW)


def padded_table(asked, sel, table):
    width, height = table.shape
    wide = sel.shape[0]
    count = asked.shape[0]
    tall = tall_of(height)
    return pl.pallas_call(
        padded_table_kernel,
        grid=(height // tall,),
        out_shape=[
            jax.ShapeDtypeStruct((height, wide), LOW),
            jax.ShapeDtypeStruct((count, sel.shape[1]), LOW),
        ],
        in_specs=[whole((count, 1)), whole(sel.shape), lined(width, tall)],
        out_specs=[striped(tall, wide), whole((count, sel.shape[1]))],
        scratch_shapes=[pltpu.VMEM((count, wide), jnp.float32)],
        compiler_params=pltpu.CompilerParams(vmem_limit_bytes=48 * 2**20),
    )(asked[:, None], sel, table)


def logits_kernel(wanted, rows, table, logits, top, total, target):
    step = pl.program_id(0)

    @pl.when(step == 0)
    def start():
        top[...] = jnp.full_like(top, -jnp.inf)
        total[...] = jnp.zeros_like(total)
        target[...] = jnp.zeros_like(target)

    here = dense_nt(table[...], rows[...])
    logits[...] = here
    higher = jnp.maximum(top[...], jnp.max(here, axis=0, keepdims=True))
    total[...] = total[...] * jnp.exp(top[...] - higher) + jnp.sum(
        jnp.exp(here - higher), axis=0, keepdims=True
    )
    top[...] = higher
    place = lax.broadcasted_iota(jnp.int32, here.shape, 0) + step * here.shape[0]
    target[...] += jnp.sum(jnp.where(place == wanted[...], here, 0.0), axis=0, keepdims=True)


def logits_of(wanted, rows, table):
    height, wide = table.shape
    count = rows.shape[0]
    tall = tall_of(height)
    line = jax.ShapeDtypeStruct((1, count), jnp.float32)
    return pl.pallas_call(
        logits_kernel,
        grid=(height // tall,),
        out_shape=[jax.ShapeDtypeStruct((height, count), jnp.float32), line, line, line],
        in_specs=[whole((1, count)), whole(rows.shape), striped(tall, wide)],
        out_specs=[striped(tall, count)] + [whole((1, count))] * 3,
        compiler_params=pltpu.CompilerParams(vmem_limit_bytes=48 * 2**20),
    )(wanted[None], rows, table)


def logits_back_kernel(share, section, wanted, top, scale, push, logits, table, grad, rows, total):
    step = pl.program_id(1)
    mine = (step >= section[0] * share) & (step < (section[0] + 1) * share)

    @pl.when(step == 0)
    def start():
        total[...] = jnp.zeros_like(total)

    here = logits[...]
    place = lax.broadcasted_iota(jnp.int32, here.shape, 0) + step * here.shape[0]
    hit = jnp.where(place == wanted[...], push[...], 0.0)
    low = (hit - jnp.exp(here - top[...]) * scale[...]).astype(LOW)
    grad[...] = low

    @pl.when(mine)
    def add():
        total[...] += dense_t(low, table[...])

    @pl.when(step == pl.num_programs(1) - 1)
    def end():
        rows[...] = total[...].astype(LOW)


def logits_back(section, wanted, top, scale, push, logits, table, sections):
    height, wide = table.shape
    count = logits.shape[1]
    tall = tall_of(height, sections)
    block = min(count, 2048)
    line = pl.BlockSpec((1, block), lambda j, i: (0, j))
    tile = pl.BlockSpec((tall, block), lambda j, i: (i, j))
    return pl.pallas_call(
        functools.partial(logits_back_kernel, height // tall // sections),
        grid=(count // block, height // tall),
        out_shape=[
            jax.ShapeDtypeStruct((height, count), LOW),
            jax.ShapeDtypeStruct((count, wide), LOW),
        ],
        in_specs=[
            pl.BlockSpec(memory_space=pltpu.SMEM),
            line,
            line,
            line,
            line,
            tile,
            pl.BlockSpec((tall, wide), lambda j, i: (i, 0)),
        ],
        out_specs=[tile, pl.BlockSpec((block, wide), lambda j, i: (j, 0))],
        scratch_shapes=[pltpu.VMEM((block, wide), jnp.float32)],
        compiler_params=pltpu.CompilerParams(vmem_limit_bytes=56 * 2**20),
    )(section[None], wanted[None], top[None], scale[None], push[None], logits, table)


def table_grad_kernel(leader, asked, got, rows, grad_logits, *refs):
    *others, grad, squares = refs
    step = pl.program_id(0)

    @pl.when(step == 0)
    def start():
        gains = others[-1][...]
        total = squares_of(gains[:2]) + leader[0] * squares_of(gains[2:3])
        for other in others[:-1]:
            total += squares_of(other[...])
        squares[...] = jnp.broadcast_to(total, squares.shape)

    width, tall = grad.shape
    place = lax.broadcasted_iota(jnp.int32, (tall, asked.shape[1]), 0) + step * tall
    here = dense_nt(rows[...], grad_logits[...]) + dense_nt(got[...], (asked[...] == place).astype(LOW))
    here = here[:width]
    grad[...] = here.astype(LOW)
    squares[pl.ds(0, 1)] += leader[0] * squares_of(here)


def table_grad(leader, asked, got, rows, grad_logits, others, width):
    height, count = grad_logits.shape
    tall = tall_of(height)
    return pl.pallas_call(
        table_grad_kernel,
        grid=(height // tall,),
        out_shape=[
            jax.ShapeDtypeStruct((width, height), LOW),
            jax.ShapeDtypeStruct((8, 128), jnp.float32),
        ],
        in_specs=[
            pl.BlockSpec(memory_space=pltpu.SMEM),
            whole((1, asked.shape[0])),
            whole(got.shape),
            whole(rows.shape),
            striped(tall, count),
        ]
        + [whole(o.shape) for o in others],
        out_specs=[lined(width, tall), whole((8, 128))],
        compiler_params=pltpu.CompilerParams(vmem_limit_bytes=56 * 2**20),
    )(leader[None], asked[None], got, rows, grad_logits, *others)


def exact_product(left, onehot):
    high = left.astype(LOW)
    rest = left - high.astype(jnp.float32)
    middle = rest.astype(LOW)
    lowest = (rest - middle.astype(jnp.float32)).astype(LOW)
    return dense_nt(high, onehot) + (dense_nt(middle, onehot) + dense_nt(lowest, onehot))


ROWED = 3
SPREAD = (1, 3)


def moments_kernel(decays, clip, sel, *refs):
    weights, grads, firsts, seconds = (refs[7 * k : 7 * k + 7] for k in range(4))
    new_firsts, new_seconds, updates = (refs[28 + 7 * k : 35 + 7 * k] for k in range(3))
    kept, sums, *scratch = refs[49:49 + ROWED] , refs[49 + ROWED], *refs[50 + ROWED:]
    staged = [scratch[5 * k : 5 * k + 5] for k in range(ROWED)]
    in_sem, out_sem = scratch[5 * ROWED :]
    step, steps = (pl.program_id(0), pl.num_programs(0))

    def copies(k, inward):
        w, m, v, new_m, new_v = staged[k]
        if inward:
            pairs = [(weights[k + 1].at[:, 0], w), (firsts[k + 1].at[:, 0], m), (seconds[k + 1].at[:, 0], v)]
        else:
            pairs = [(new_m, new_firsts[k + 1].at[:, 0]), (new_v, new_seconds[k + 1].at[:, 0])]
        return [
            pltpu.make_async_copy(src, dst, (in_sem if inward else out_sem).at[k, i])
            for i, (src, dst) in enumerate(pairs)
        ]

    @pl.when(step == 0)
    def start():
        sums[...] = jnp.zeros_like(sums)
        for k in range(ROWED):
            for copy in copies(k, True):
                copy.start()

    def one(weight, grad, first, second, decay):
        return (weight,) + lamb_parts(weight, clip[0] * grad.astype(jnp.float32), first, second, decay)

    weight, new_firsts[0][...], new_seconds[0][...], update = one(
        weights[0][...], grads[0][...], firsts[0][...], seconds[0][...], decays[0]
    )
    updates[0][...] = update.astype(LOW)
    sums[pl.ds(0, 1)] += squares_of(weight)
    sums[pl.ds(8, 1)] += squares_of(update)

    def tensor(k):
        rows, cols = updates[k + 1].shape
        grad = grads[k + 1][pl.ds(0, rows)]
        grad = exact_product(grad, sel[...]) if k in SPREAD else grad[:, :cols]
        if k < ROWED:
            for copy in copies(k, True):
                copy.wait()
            w, m, v, new_m, new_v = staged[k]
        else:
            w, m, v, new_m, new_v = (t[k + 1] for t in (weights, firsts, seconds, new_firsts, new_seconds))
        weight, new_m[...], new_v[...], update = one(w[...], grad, m[...], v[...], decays[k + 1])
        updates[k + 1][...] = update
        if k < ROWED:
            kept[k][...] = weight
            for copy in copies(k, False):
                copy.start()
        for row in range(rows if k == 4 else 1):
            part = slice(row, row + 1) if k == 4 else slice(None)
            line = k + 1 + row + (k > 4)
            sums[pl.ds(line, 1)] += squares_of(weight[part])
            sums[pl.ds(8 + line, 1)] += squares_of(update[part])

    for k in range(6):
        pl.when(step == (6 + k if k < ROWED else k - 2) % steps)(functools.partial(tensor, k))

    @pl.when(step == steps - 1)
    def end():
        for k in range(ROWED):
            for copy in copies(k, False):
                copy.wait()


def moments(clip, sel, weights, grads, firsts, seconds, decays):
    width, height = weights[0].shape
    tall = tall_of(height)
    flat = [w.shape if w.ndim == 2 else w.shape[::2] for w in weights]

    def specs(arrays, results=False):
        out = [lined(width, tall)]
        for a in arrays[1:]:
            out.append(ANYWHERE if a.ndim == 3 else whole(a.shape))
        return out

    line = [jax.ShapeDtypeStruct(w.shape, jnp.float32) for w in weights]
    plain = [jax.ShapeDtypeStruct(s, jnp.float32 if k else LOW) for k, s in enumerate(flat)]
    kept = plain[1 : 1 + ROWED]
    out = pl.pallas_call(
        functools.partial(moments_kernel, decays),
        grid=(height // tall,),
        out_shape=line * 2 + plain + kept + [jax.ShapeDtypeStruct((16, 128), jnp.float32)],
        in_specs=[pl.BlockSpec(memory_space=pltpu.SMEM), whole(sel.shape)]
        + specs(weights)
        + specs(grads)
        + specs(firsts)
        + specs(seconds),
        out_specs=specs(line) * 2 + specs(plain) + [whole(s.shape) for s in kept] + [whole((16, 128))],
        scratch_shapes=[pltpu.VMEM(s.shape, jnp.float32) for s in kept for unused in range(5)]
        + [pltpu.SemaphoreType.DMA((ROWED, 3)), pltpu.SemaphoreType.DMA((ROWED, 2))],
        compiler_params=pltpu.CompilerParams(vmem_limit_bytes=60 * 2**20),
    )(clip[None], sel, *weights, *grads, *firsts, *seconds)
    return (out[:7], out[7:14], out[14:21], out[21 : 21 + ROWED], out[21 + ROWED])


def apply_kernel(scales, *refs):
    weights, updates, new, half = (refs[5 * k : 5 * k + 5] for k in range(4))
    staged, sem = (refs[20 : 20 + ROWED], refs[20 + ROWED])
    step, steps = (pl.program_id(0), pl.num_programs(0))

    def copy(k):
        return pltpu.make_async_copy(staged[k - 1], new[k].at[:, 0], sem.at[k - 1])

    def one(k):
        value = weights[k][...] - RATE * scales[k] * updates[k][...]
        half[k][...] = value.astype(LOW)
        if 0 < k <= ROWED:
            staged[k - 1][...] = value
            copy(k).start()
        else:
            new[k][...] = value

    one(0)
    for k in range(1, 5):
        pl.when(step == (k - 1) % steps)(functools.partial(one, k))

    @pl.when(step == steps - 1)
    def end():
        for k in range(1, 1 + ROWED):
            copy(k).wait()


def apply_updates(scales, weights, updates, shapes):
    width, height = weights[0].shape
    tall = tall_of(height)
    plain = [lined(width, tall)] + [whole(w.shape) for w in weights[1:]]
    out = pl.pallas_call(
        apply_kernel,
        grid=(height // tall,),
        out_shape=[jax.ShapeDtypeStruct(s, jnp.float32) for s in shapes]
        + [jax.ShapeDtypeStruct(w.shape, LOW) for w in weights],
        in_specs=[pl.BlockSpec(memory_space=pltpu.SMEM)] + plain * 2,
        out_specs=plain[:1] + [ANYWHERE] * ROWED + plain[1 + ROWED :] + plain,
        scratch_shapes=[pltpu.VMEM(w.shape, jnp.float32) for w in weights[1 : 1 + ROWED]]
        + [pltpu.SemaphoreType.DMA((ROWED,))],
        compiler_params=pltpu.CompilerParams(vmem_limit_bytes=56 * 2**20),
    )(scales, *weights, *updates)
    return (out[:5], out[5:])


EACH = HEADS // KV


def turned(x, cosine, sine):
    half = HD // 2
    u, w = (x[:half], x[half:])
    return jnp.concatenate([u * cosine - w * sine, w * cosine + u * sine], axis=0)


def query_blocks(scored):
    if scored:
        return [(0, scored, ((0, TOK_MB),))]
    out = [(0, PROMPT, ((0, PROMPT),))]
    for j in range(NCONT):
        first = PROMPT + j * CONT
        out.append((first, CONT, ((0, PROMPT), (first, CONT))))
    return out


def masks(place):
    out = []
    for first, count, ranges in query_blocks(0 if place is None else place.shape[1]):
        keys = sum(r[1] for r in ranges)
        row = lax.broadcasted_iota(jnp.int32, (keys, count), 0)
        if place is not None:
            at = place[pl.ds(0, 1)]
            seen = (row < PROMPT) | ((row >= place[pl.ds(1, 1)]) & (row <= at))
        else:
            seen = row - (keys - count) <= lax.broadcasted_iota(jnp.int32, (keys, count), 1)
        out.append(jnp.concatenate([jnp.where(seen, 0.0, -1e30)] * EACH, axis=1))
    return out


def rows_of(ranges, array):
    parts = [array[first : first + count] for first, count in ranges]
    return parts[0] if len(parts) == 1 else jnp.concatenate(parts, axis=0)


def head_rows(start):
    return pl.ds(pl.multiple_of(start, HD), HD)


def side_by_side(ref, group, first, count):
    return jnp.concatenate(
        [ref[head_rows((group * EACH + j) * HD), pl.ds(first, count)] for j in range(EACH)], axis=1
    )


def attend_kernel(scored, qkv, cosine, sine, *refs):
    pick, place = refs[:2] if scored else (None, None)
    low, out, top, share, *queries = refs[2:] if scored else refs
    queries = queries[0] if scored else low
    cos, sin = (cosine[...], sine[...])
    added = masks(place)

    def group_of(group, carry):
        key = turned(qkv[head_rows(WIDTH + group * HD)], cos, sin)
        low[head_rows(WIDTH + group * HD)] = key.astype(LOW)
        value = qkv[head_rows(WIDTH + KVW + group * HD)].astype(LOW)
        low[head_rows(WIDTH + KVW + group * HD)] = value
        for j in range(EACH):
            place_of = head_rows((group * EACH + j) * HD)
            query = turned(qkv[place_of], cos, sin).astype(LOW)
            low[place_of] = query
            if scored:
                queries[place_of] = dense_nt(query, pick[...]).astype(LOW)
        keys = key.T.astype(LOW)
        for (first, count, ranges), extra in zip(query_blocks(scored), added):
            query = side_by_side(queries, group, first, count)
            scores = dense(rows_of(ranges, keys), query) * SCALE + extra
            high = jnp.max(scores, axis=0, keepdims=True)
            expo = jnp.exp(scores - high)
            part = 1.0 / jnp.sum(expo, axis=0, keepdims=True)
            probs = (expo * part).astype(LOW)
            got, at = (0.0, 0)
            for start, length in ranges:
                got += dense(value[:, start : start + length], probs[at : at + length])
                at += length
            for j in range(EACH):
                column = slice(j * count, (j + 1) * count)
                out[head_rows((group * EACH + j) * HD), pl.ds(first, count)] = got[:, column].astype(LOW)
                top[group, j : j + 1, pl.ds(first, count)] = high[:, column]
                share[group, j : j + 1, pl.ds(first, count)] = part[:, column]
        return carry

    lax.fori_loop(0, KV, group_of, 0)


def attention(qkv, cosine, sine, chosen=()):
    tokens = qkv.shape[1]
    scored = chosen[0].shape[0] if chosen else 0
    count = scored or tokens
    stat = jax.ShapeDtypeStruct((KV, EACH, count), jnp.float32)
    heads = jax.ShapeDtypeStruct((WIDTH, count), LOW)
    results = [jax.ShapeDtypeStruct((WIDTH + 2 * KVW, tokens), LOW), heads, stat, stat]
    results += [heads] if scored else []
    return pl.pallas_call(
        functools.partial(attend_kernel, scored),
        out_shape=results,
        in_specs=[IN_VMEM] * (3 + len(chosen)),
        out_specs=[IN_VMEM] * len(results),
        compiler_params=pltpu.CompilerParams(vmem_limit_bytes=40 * 2**20),
    )(qkv, cosine, sine, *chosen)


def attend_back_kernel(scored, low, top, share, grad, cosine, sine, *refs):
    pick, place, queries = refs[:3] if scored else (None, None, low)
    out, key_sum, value_sum = refs[-3:]
    cos, sin = (cosine[...], sine[...])
    added = masks(place)
    spare = out.shape[0] - WIDTH - 2 * KVW
    out[pl.ds(WIDTH + 2 * KVW, spare)] = jnp.zeros((spare, out.shape[1]), LOW)

    def group_of(group, carry):
        key = low[head_rows(WIDTH + group * HD)]
        value = low[head_rows(WIDTH + KVW + group * HD)]
        keys = key.astype(jnp.float32).T.astype(LOW)
        values = value.astype(jnp.float32).T.astype(LOW)
        for number, ((first, count, ranges), extra) in enumerate(zip(query_blocks(scored), added)):
            sides = range(EACH)
            columns = pl.ds(first, count)
            query = side_by_side(queries, group, first, count)
            upstream = side_by_side(grad, group, first, count)
            high = jnp.concatenate([top[group, j : j + 1, columns] for j in sides], axis=1)
            part = jnp.concatenate([share[group, j : j + 1, columns] for j in sides], axis=1)
            scores = dense(rows_of(ranges, keys), query) * SCALE + extra
            probs = jnp.exp(scores - high) * part
            grad_probs = dense(rows_of(ranges, values), upstream)
            inner = jnp.sum(grad_probs * probs, axis=0, keepdims=True)
            grad_scores = (probs * (grad_probs - inner)).astype(LOW)
            probs = probs.astype(LOW)
            got, at = (0.0, 0)
            for start, length in ranges:
                piece = slice(at, at + length)
                got += dense(key[:, start : start + length], grad_scores[piece])
                here = pl.ds(start, length)
                more_key = dense_nt(query, grad_scores[piece])
                more_value = dense_nt(upstream, probs[piece])
                if number == 0 or start > 0:
                    key_sum[:, here] = more_key
                    value_sum[:, here] = more_value
                else:
                    key_sum[:, here] += more_key
                    value_sum[:, here] += more_value
                at += length
            for j in sides:
                turn = got[:, j * count : (j + 1) * count] * SCALE
                where = head_rows((group * EACH + j) * HD)
                if scored:
                    high_part = turn.astype(LOW)
                    rest = (turn - high_part.astype(jnp.float32)).astype(LOW)
                    turn = dense(high_part, pick[...]) + dense(rest, pick[...])
                    out[where] = turned(turn, cos, -sin).astype(LOW)
                else:
                    past = slice(first, first + count)
                    out[where, columns] = turned(turn, cos[:, past], -sin[:, past]).astype(LOW)
        out[head_rows(WIDTH + group * HD)] = turned(key_sum[...] * SCALE, cos, -sin).astype(LOW)
        out[head_rows(WIDTH + KVW + group * HD)] = value_sum[...].astype(LOW)
        return carry

    lax.fori_loop(0, KV, group_of, 0)


def attention_back(low, top, share, grad, cosine, sine, wide, chosen=()):
    tokens = low.shape[1]
    return pl.pallas_call(
        functools.partial(attend_back_kernel, chosen[0].shape[0] if chosen else 0),
        out_shape=jax.ShapeDtypeStruct((wide, tokens), LOW),
        in_specs=[IN_VMEM] * (6 + len(chosen)),
        out_specs=IN_VMEM,
        scratch_shapes=[pltpu.VMEM((HD, tokens), jnp.float32)] * 2,
        compiler_params=pltpu.CompilerParams(vmem_limit_bytes=48 * 2**20),
    )(low, top, share, grad, cosine, sine, *chosen)


def up16(count):
    return -(-count // 16) * 16


def dense(left, right):
    return jnp.dot(left, right, preferred_element_type=jnp.float32)


def dense_t(left, right):
    return lax.dot_general(
        left, right, (((0,), (0,)), ((), ())), preferred_element_type=jnp.float32
    )


def dense_nt(left, right):
    return lax.dot_general(
        left, right, (((1,), (1,)), ((), ())), preferred_element_type=jnp.float32
    )


def spread_matrix(parts, real, padded):
    feature = jnp.arange(parts * real)
    place = feature // real * padded + feature % real
    return (place[:, None] == jnp.arange(parts * padded)[None, :]).astype(LOW)


def inverse_rms(x, width):
    return lax.rsqrt(jnp.sum(x * x, axis=-1, keepdims=True) / width + EPS)


def norm_back(x, scale, gain, upstream, width):
    inner = upstream * gain
    grad_gain = jnp.sum(upstream * x * scale, axis=0)
    mean = jnp.sum(inner * x, axis=-1, keepdims=True) / width
    return (scale * inner - x * scale**3 * mean, grad_gain)


def rotary_angles():
    place = jnp.arange(TOK_MB)
    rotary = jnp.where(place >= PROMPT, PROMPT + (place - PROMPT) % CONT, place).astype(jnp.float32)
    freq = THETA ** (-2.0 * jnp.arange(HD // 2).astype(jnp.float32) / HD)
    angle = freq[:, None] * rotary[None, :]
    return (jnp.cos(angle), jnp.sin(angle))


def dense_tt(left, right):
    return lax.dot_general(
        left, right, (((0,), (1,)), ((), ())), preferred_element_type=jnp.float32
    )


def mlp(b, w_gu, w_down):
    gate_up = dense(b, w_gu)
    half = gate_up.shape[1] // 2
    gate, upper = (gate_up[:, :half], gate_up[:, half:])
    hidden = (jax.nn.silu(gate) * upper).astype(LOW)
    return (dense(hidden, w_down), gate, upper, hidden)


def mlp_back(branch, b, gate, upper, hidden, w_gu, w_down):
    grad_down = dense_t(hidden, branch)
    grad_hidden = dense_nt(branch, w_down)
    sig = jax.nn.sigmoid(gate)
    grad_gate = grad_hidden * upper * sig * (1.0 + gate * (1.0 - sig))
    grad_upper = grad_hidden * gate * sig
    grad_gate_up = jnp.concatenate([grad_gate, grad_upper], axis=1).astype(LOW)
    return (grad_down, dense_t(b, grad_gate_up), dense_nt(grad_gate_up, w_gu))


def lamb_parts(weight, grad, first, second, decay):
    first_new = BETA_ONE * first + (1.0 - BETA_ONE) * grad
    second_new = BETA_TWO * second + (1.0 - BETA_TWO) * grad * grad
    root = (1.0 - BETA_TWO**STEP) ** 0.5
    scale = root / (1.0 - BETA_ONE**STEP)
    update = first_new * scale / (second_new * lax.rsqrt(second_new) + ADAM_EPS * root) + decay * weight
    return (first_new, second_new, update)


def lookup_ranks(ids, vshard):
    place = jnp.arange(ids.shape[0])
    same = ids[:, None] == ids[None, :]
    first = jnp.min(jnp.where(same, place[None, :], ids.shape[0]), axis=1)
    owner = ids // vshard
    before = (
        (owner[:, None] == owner[None, :])
        & (first == place)[None, :]
        & (place[None, :] < first[:, None])
    )
    return (owner, jnp.sum(before.astype(jnp.int32), axis=1))


def lookup_round(ids, owner, rank, turn, slots, parts, vshard):
    slot = jnp.where(rank // slots == turn, owner * slots + rank - turn * slots, -1)
    onehot = slot[:, None] == jnp.arange(parts * slots)[None, :]
    wanted = jnp.max(jnp.where(onehot, (ids - owner * vshard)[:, None], -1), axis=0)
    return (onehot.astype(LOW), wanted)


def shards(
    token_ids,
    scored,
    targets,
    pairs,
    table,
    w_qkv,
    w_out,
    w_gu,
    w_down,
    gains,
    final_gain,
    first_table,
    first_qkv,
    first_out,
    first_gu,
    first_down,
    first_gains,
    first_final,
    second_table,
    second_qkv,
    second_out,
    second_gu,
    second_down,
    second_gains,
    second_final,
):
    n = lax.axis_size("fsdp")
    sections = lax.axis_size("section")
    section_index = lax.axis_index("section")
    fsdp_index = lax.axis_index("fsdp")
    leader = section_index == 0
    vshard, width = table.shape
    vstart = fsdp_index * vshard
    r = w_qkv.shape[1]
    rp = up16(r)
    rd = w_down.shape[1]
    rdp = up16(rd)
    wide = n * rp
    ffp = n * rdp
    slots = up16(768 // n)
    sel = spread_matrix(n, r, rp)
    sel_wide = jnp.pad(sel, ((0, wide - width), (0, 0)))
    fast = (sections, n) == (2, 16)
    qkv_wide = -(-w_qkv.shape[2] // 128) * 128

    qkv_block = jnp.pad(
        w_qkv[0].astype(LOW), ((0, rp - r), (0, qkv_wide - w_qkv.shape[2]))
    )
    out_block = jnp.pad(dense(w_out[0].astype(LOW), sel).astype(LOW), ((0, rp - r), (0, 0)))
    gu_block = w_gu[0].astype(LOW)
    if rdp != rd:
        gu_block = jnp.pad(gu_block.reshape(r, 2, n, rd), ((0, 0), (0, 0), (0, 0), (0, rdp - rd)))
    gu_block = jnp.pad(gu_block.reshape(r, 2 * ffp), ((0, rp - r), (0, 0)))
    down_block = jnp.pad(dense(w_down[0].astype(LOW), sel).astype(LOW), ((0, rdp - rd), (0, 0)))
    gain_block = jnp.pad(
        jnp.concatenate([gains[0], final_gain[None]], axis=0).astype(LOW),
        ((0, 13), (0, 128 - r)),
    )

    ids = token_ids[0]
    owner, rank = lookup_ranks(ids, vshard)
    onehot, wanted = lookup_round(ids, owner, rank, 0, slots, n, vshard)
    turns_here = jnp.max(rank) // slots + 1
    own_targets = lax.dynamic_slice_in_dim(targets[0], fsdp_index * NCONT, NCONT).reshape(-1)
    note = jnp.concatenate(
        [wanted, jnp.pad(own_targets, (0, 128 - NCONT * SCORED)), jnp.full((128,), turns_here, jnp.int32)]
    )
    if fast:
        notes = exchange(note.reshape(-1, 128), 0).reshape(sections * n, -1)
    else:
        notes = lax.all_gather(note, BOTH, axis=0)
    turns = jnp.max(notes[:, -1])
    wanted_rows = notes[:, n * slots : n * slots + NCONT * SCORED].reshape(-1)

    def asked(all_wanted):
        mine = lax.dynamic_slice_in_dim(all_wanted.reshape(sections, n, n, slots), fsdp_index, 1, 2)
        return mine[:, :, 0]

    asked_first = asked(notes[:, : n * slots])
    asked_here = lax.dynamic_index_in_dim(asked_first, section_index, 0, keepdims=False).reshape(-1)
    blocks = (qkv_block, out_block, gu_block, down_block, gain_block)
    if fast:
        extra = (asked_here[:, None], sel_wide, table.T)
        *gathered, table_low, got = gather_all(blocks, WEIGHT_PIECES, 1, extra, slots)
        gathered = (gathered[:5], gathered[5:])
    else:
        table_low, rows = padded_table(asked_here, sel_wide, table.T)
        got = lax.all_to_all(rows.reshape(n, slots, wide), "fsdp", 0, 0)
        gathered = [lax.all_gather(block, BOTH, axis=0) for block in blocks]
        gathered = [[g[k * n : (k + 1) * n] for g in gathered] for k in range(sections)]
    qkv_all, out_all, gu_all, down_all, gain_all = [
        [section[k].reshape(n * blocks[k].shape[0], -1) for section in gathered] for k in range(5)
    ]
    gain_all = jnp.stack([g.reshape(n, 16, 128)[:, :3, :rp] for g in gain_all])
    gain_all = jnp.moveaxis(gain_all, 2, 1).reshape(sections, 3, wide).astype(jnp.float32)
    final_all = gain_all[0, 2]
    x0 = dense(onehot, got.reshape(n * slots, wide))

    def fetch_more(state):
        turn, total = state
        choose, more = lookup_round(ids, owner, rank, turn, slots, n, vshard)
        here = asked(lax.all_gather(more, BOTH, axis=0))
        here = lax.dynamic_index_in_dim(here, section_index, 0, keepdims=False).reshape(-1)
        rows = dense(jnp.take(table_low, jnp.maximum(here, 0), axis=0), sel_wide).astype(LOW)
        got = lax.all_to_all(rows.reshape(n, slots, wide), "fsdp", 0, 0).reshape(n * slots, wide)
        return (turn + 1, total + dense(choose, got))

    x0 = lax.while_loop(lambda state: state[0] < turns, fetch_more, (jnp.int32(1), x0))[1]

    everyone = jnp.arange(TOK_MB)
    cosine, sine = rotary_angles()
    x = x0
    kept = []
    for layer in range(sections - 1):
        scale_a = inverse_rms(x, width)
        a = (x * scale_a * gain_all[layer, 0]).astype(LOW)
        low, attended, top, share = attention(dense_tt(qkv_all[layer], a), cosine, sine)
        attended = dense_t(attended, sel).astype(LOW)
        mixed = x + dense(attended, out_all[layer])
        scale_b = inverse_rms(mixed, width)
        b = (mixed * scale_b * gain_all[layer, 1]).astype(LOW)
        branch, gate, upper, hidden = mlp(b, gu_all[layer], down_all[layer])
        kept.append((x, scale_a, a, low, top, share, attended, mixed, scale_b, b, gate, upper, hidden))
        x = mixed + branch

    last = sections - 1
    place = (PROMPT + CONT * jnp.arange(NCONT)[:, None] + scored[0]).reshape(-1)
    taken = place.shape[0]
    place = jnp.pad(place, (0, -taken % 128), constant_values=PROMPT)
    real = jnp.arange(place.shape[0]) < taken
    pick = ((place[:, None] == everyone[None, :]) & real[:, None]).astype(LOW)
    pick32 = pick.astype(jnp.float32)
    picking = (pick, jnp.stack([place, PROMPT + (place - PROMPT) // CONT * CONT]))
    scale_last = inverse_rms(x, width)
    a_last = (x * scale_last * gain_all[last, 0]).astype(LOW)
    low_last, attended_s, top_s, share_s, queries = attention(
        dense_tt(qkv_all[last], a_last), cosine, sine, picking
    )
    x_s = jnp.dot(pick32, x, precision=HI)
    attended_s = dense_t(attended_s, sel).astype(LOW)
    mixed_s = x_s + dense(attended_s, out_all[last])
    scale_s = inverse_rms(mixed_s, width)
    b_s = (mixed_s * scale_s * gain_all[last, 1]).astype(LOW)
    branch_s, gate_s, upper_s, hidden_s = mlp(b_s, gu_all[last], down_all[last])
    y_s = mixed_s + branch_s
    scale_y = inverse_rms(y_s, width)
    head_in = dense_nt((y_s * scale_y * final_all).astype(LOW), sel_wide).astype(LOW)[:taken]

    if fast:
        rows_all = jnp.concatenate(gather_all([head_in], [(0, 16 * k, 16, k % 2) for k in range(4)], 2))
    else:
        rows_all = lax.all_gather(head_in, BOTH, axis=0)
    rows_all = rows_all.reshape(-1, wide)
    own_rows = rows_all.shape[0] // sections
    wanted_here = wanted_rows - vstart
    logits, top_here, total_here, target_here = logits_of(wanted_here, rows_all, table_low)
    stats = jnp.concatenate([top_here, total_here, target_here])
    if fast:
        stats = exchange(stats.reshape(-1, 128), 3, whole=False).reshape(n, 3, -1)
    else:
        stats = lax.all_gather(stats, "fsdp", axis=0)
    top = jnp.max(stats[:, 0], axis=0)
    total = jnp.sum(stats[:, 1] * jnp.exp(stats[:, 0] - top), axis=0)
    row_logp = jnp.sum(stats[:, 2], axis=0) - top - jnp.log(total)
    seq = jnp.sum(row_logp.reshape(-1, SCORED), axis=1)
    pair = pairs.reshape(-1, 2)
    conts = jnp.arange(seq.shape[0])
    chosen = (pair[:, 0][:, None] == conts[None, :]).astype(jnp.float32)
    passed = (pair[:, 1][:, None] == conts[None, :]).astype(jnp.float32)
    delta = jnp.sum((chosen - passed) * seq[None, :], axis=1)
    loss = jnp.sum(jax.nn.softplus(-BETA * delta))
    push = BETA * jax.nn.sigmoid(-BETA * delta)
    grad_seq = jnp.sum((passed - chosen) * push[:, None], axis=0)
    grad_row = jnp.repeat(grad_seq, SCORED)
    grad_logits, grad_rows = logits_back(
        section_index, wanted_here, top, grad_row / total, grad_row, logits, table_low, sections
    )
    if fast:
        halves = [[grad_rows[k * own_rows : (k + 1) * own_rows]] for k in range(sections)]
        grad_head = reduce_all(halves, 4, 1, tile=16)[0]
    else:
        grad_head = lax.psum_scatter(grad_rows, BOTH, scatter_dimension=0, tiled=True)
    grad_head = jnp.pad(grad_head.astype(jnp.float32), ((0, place.shape[0] - taken), (0, 0)))
    grad_z = jnp.dot(grad_head, sel_wide.astype(jnp.float32), precision=HI)
    grad_y, grad_final = norm_back(y_s, scale_y, final_all, grad_z, width)

    grads = [None] * sections
    g_down, g_gu, grad_b = mlp_back(
        grad_y.astype(LOW), b_s, gate_s, upper_s, hidden_s, gu_all[last], down_all[last]
    )
    grad_mid, gain_two = norm_back(mixed_s, scale_s, gain_all[last, 1], grad_b, width)
    grad_mixed = grad_mid + grad_y
    branch = grad_mixed.astype(LOW)
    g_out = dense_t(attended_s, branch)
    grad_att = dense_nt(sel, dense_nt(branch, out_all[last]).astype(LOW)).astype(LOW)
    grad_qkv = attention_back(
        low_last, top_s, share_s, grad_att, cosine, sine, qkv_wide, picking + (queries,)
    )
    g_qkv = dense_tt(a_last, grad_qkv)
    grad_in, gain_one = norm_back(
        x, scale_last, gain_all[last, 0], dense_tt(grad_qkv, qkv_all[last]), width
    )
    upstream = grad_in + lax.dot_general(pick32, grad_mixed, (((0,), (0,)), ((), ())), precision=HI)
    grads[last] = (g_qkv, g_out, g_gu, g_down, jnp.stack([gain_one, gain_two]))

    for layer in range(sections - 2, -1, -1):
        (x, scale_a, a, low, top, share, attended, mixed, scale_b, b, gate, upper, hidden) = kept[layer]
        g_down, g_gu, grad_b = mlp_back(
            upstream.astype(LOW), b, gate, upper, hidden, gu_all[layer], down_all[layer]
        )
        grad_mid, gain_two = norm_back(mixed, scale_b, gain_all[layer, 1], grad_b, width)
        grad_mixed = grad_mid + upstream
        branch = grad_mixed.astype(LOW)
        g_out = dense_t(attended, branch)
        grad_att = dense_nt(sel, dense_nt(branch, out_all[layer]).astype(LOW)).astype(LOW)
        grad_qkv = attention_back(low, top, share, grad_att, cosine, sine, qkv_wide)
        g_qkv = dense_tt(a, grad_qkv)
        grad_in, gain_one = norm_back(
            x, scale_a, gain_all[layer, 0], dense_tt(grad_qkv, qkv_all[layer]), width
        )
        upstream = grad_in + grad_mixed
        grads[layer] = (g_qkv, g_out, g_gu, g_down, jnp.stack([gain_one, gain_two]))

    grad_x0 = dense_nt(upstream.astype(LOW), sel_wide).astype(LOW)

    def give(all_asked, choose):
        rows = dense_t(choose, grad_x0).astype(LOW)
        got = lax.all_to_all(rows.reshape(n, slots, wide), "fsdp", 0, 0)
        return (all_asked.reshape(-1), lax.all_gather(got, "section", axis=0).reshape(-1, wide))

    def give_more(state):
        turn, grad, squares = state
        choose, more = lookup_round(ids, owner, rank, turn, slots, n, vshard)
        places, got = give(asked(lax.all_gather(more, BOTH, axis=0)), choose)
        place_of = (jnp.arange(vshard)[:, None] == places[None, :]).astype(LOW)
        new = grad.astype(jnp.float32) + lax.dot_general(
            got[:, :width], place_of, (((0,), (1,)), ((), ())), preferred_element_type=jnp.float32
        )
        every = lax.psum(jnp.where(leader, jnp.sum(new**2), 0.0), BOTH) + jnp.sum(squares[:, 1, 0])
        return (turn + 1, new.astype(LOW), squares.at[:, 0].set(every / (sections * n)))

    def gain_rows(layer):
        rows = jnp.concatenate([grads[layer][4], grad_final[None]], axis=0).reshape(3, n, rp)
        rows = jnp.pad(jnp.moveaxis(rows, 0, 1), ((0, 0), (0, TILE_R - 3), (0, 128 - rp)))
        return rows.reshape(n * TILE_R, 128)

    outward = [
        [g.astype(LOW) for g in grads[layer][:4] + (gain_rows(layer),)] for layer in range(sections)
    ]
    if fast:
        rows = dense_t(onehot, grad_x0).astype(LOW).reshape(n, slots, wide)
        extra = (rows, asked_first.reshape(1, -1), rows_all, grad_logits)
        *summed, unused, got, grad_table, grad_squares = reduce_all(outward, 5, 2, extra=extra, width=width)
    else:
        summed = [
            lax.psum_scatter(
                jnp.concatenate(arrays, axis=0), BOTH, scatter_dimension=0, tiled=True
            ).astype(jnp.float32)
            for arrays in zip(*outward)
        ]
        got = give(asked_first, onehot)[1]
        grad_table, grad_squares = table_grad(
            leader.astype(jnp.float32),
            asked_first.reshape(-1),
            got.T,
            rows_all.T,
            grad_logits,
            summed,
            width,
        )
        grad_squares = lax.all_gather(grad_squares, BOTH, axis=0)
    if rdp != rd:
        summed[2] = summed[2].reshape(rp, 2, n, rdp)[:, :, :, :rd].reshape(rp, 2 * n * rd)
    grad_table, grad_squares = lax.while_loop(
        lambda state: state[0] < turns, give_more, (jnp.int32(1), grad_table, grad_squares)
    )[1:]

    def everyones(sums, name):
        if fast:
            return exchange(sums, name)
        return lax.all_gather(sums, BOTH, axis=0)

    grad_norm = jnp.sqrt(jnp.sum(grad_squares[:, 0, 0]))
    clip = jnp.minimum(1.0, CLIP / grad_norm)

    def views(arrays):
        out = [arrays[0].T] + [a.transpose(1, 0, 2) for a in arrays[1:4]]
        return out + [arrays[4][0], arrays[5][0], arrays[6][None]]

    weights_all = views((table, w_qkv, w_out, w_gu, w_down, gains, final_gain))
    grads_all = [grad_table] + summed[:4] + [summed[4][:2, :r], summed[4][2:3, :r]]
    new_firsts, new_seconds, updates, kept_weights, sums = moments(
        clip,
        sel,
        weights_all,
        grads_all,
        views((first_table, first_qkv, first_out, first_gu, first_down, first_gains, first_final)),
        views((second_table, second_qkv, second_out, second_gu, second_down, second_gains, second_final)),
        (DECAY,) * 5 + (0.0, 0.0),
    )
    sums = everyones(sums, 7)[:, :, 0].reshape(sections, n, 2, 8)
    sums = jnp.sum(sums, axis=1)
    layered = jnp.moveaxis(sums[:, :, 1:7], 1, 0).reshape(2, -1)
    matrix_norms = jnp.sqrt(jnp.concatenate([layered, sums[0, :, 0:1], sums[0, :, 7:8]], axis=1))
    trust_ratio = matrix_norms[0] / matrix_norms[1]
    own = lax.dynamic_slice_in_dim(trust_ratio, 6 * section_index, 6)
    last_two = trust_ratio[6 * sections :]
    new, half = apply_updates(
        jnp.concatenate([last_two[:1], own[:4]]),
        [weights_all[0], *kept_weights, weights_all[4]],
        updates[:5],
        [w.shape for w in weights_all[:5]],
    )
    new = list(new) + [
        weights_all[5] - RATE * own[4:6][:, None] * updates[5],
        weights_all[6] - RATE * last_two[1] * updates[6],
    ]

    def back(k, array):
        if k == 0:
            return array.T
        if k == 6:
            return array[0]
        return array.transpose(1, 0, 2) if array.ndim == 3 else array[None]

    outs = [loss, grad_norm, matrix_norms]
    for k in range(7):
        outs += [back(k, t[k]) for t in (new, new_firsts, new_seconds)]
    return tuple(outs + [back(k, half[k]) for k in range(5)])


def solution(mesh):
    tall, layered, gainy, flat = (
        P("fsdp", None),
        P("section", "fsdp", None),
        P("section", None, "fsdp"),
        P("fsdp"),
    )
    weights = (tall, layered, layered, layered, layered, gainy, flat)
    placed = (
        P("section", "fsdp"),
        P("section", "fsdp", None),
        P("section", None, None),
        P(),
    ) + weights * 3
    results = (P(), P(), P())
    for spec in weights:
        results += (spec, spec, spec)
    return jax.shard_map(
        shards, mesh=mesh, in_specs=placed, out_specs=results + weights[:5], check_vma=False
    )
```

```python
import functools

import jax
import jax.numpy as jnp
from jax import lax
from jax.experimental import pallas as pl
from jax.experimental.pallas import tpu as pltpu
from jax.sharding import PartitionSpec as P

HEADS = 15
KV = 5
HD = 64
FF = 2560
PROMPT = 256
NCONT = 2
CONT = 128
SCORED = 32
STEP = 10
TOK_MB = 512

EPS = 1e-05
SCALE = 0.125
THETA = 100000.0
BETA = 0.1
CLIP = 1.0
RATE = 0.3
BETA_ONE = 0.9
BETA_TWO = 0.99
ADAM_EPS = 1e-08
DECAY = 0.01

WIDTH = HEADS * HD
KVW = KV * HD
BOTH = ("section", "fsdp")
HI = lax.Precision.HIGHEST
LOW = jnp.bfloat16

WEIGHT_PIECES = [
    (0, 0, 64, 0),
    (1, 0, 64, 1),
    (2, 0, 16, 0),
    (2, 16, 16, 1),
    (2, 32, 16, 0),
    (2, 48, 16, 1),
    (3, 0, 80, 0),
    (3, 80, 80, 1),
    (4, 0, 16, 1),
]

MESH = pl.DeviceIdType.MESH
ANYWHERE = pl.BlockSpec(memory_space=pl.ANY)
IN_VMEM = pl.BlockSpec(memory_space=pltpu.VMEM)
TILE_R, TILE_C = 32, 1024


def coords():
    f = lax.axis_index("fsdp")
    return (lax.axis_index("section"), f // 4, f // 2 % 2, f % 2)


def device(y, z, x, c):
    return (y, z * 4 + x * 2 + c)


def greet(peers):
    barrier = pltpu.get_barrier_semaphore()
    for peer in peers:
        pl.semaphore_signal(barrier, inc=1, device_id=peer, device_id_type=MESH)
    pl.semaphore_wait(barrier, len(peers))


def send(src, dst, send_sem, recv_sem, peer):
    pltpu.make_async_remote_copy(
        src_ref=src,
        dst_ref=dst,
        send_sem=send_sem,
        recv_sem=recv_sem,
        device_id=peer,
        device_id_type=MESH,
    ).start()


def settle(ref, sem):
    pltpu.make_async_copy(ref, ref, sem).wait()


def gather_kernel(pieces, count, carried, *refs):
    y, f = (lax.axis_index("section"), lax.axis_index("fsdp"))
    z, x, c = coords()[1:]
    in_line = [((z + k) % 4) * 4 + x * 2 + c for k in range(1, 4)]
    near = [f + 2 - 4 * x, f + 1 - 2 * c]
    away = [(f + k) % 16 for k in range(1, 16)] if carried else in_line + near
    greet([device(1 - y, z, x, c)] + [(y, peer) for peer in away])
    if not carried:
        outs = [ref.at[pl.ds(section * 16, 16)] for section in range(2) for ref in refs[count : 2 * count]]

        def everything(section):
            for name, p in [("own", None)] + [("line", p) for p in range(len(pieces))] + [("rest", None)]:
                gather_section(section, pieces, (refs[:count], outs), refs[2 * count :], name, p)

        for section in range(2):
            pl.when(y == section)(functools.partial(everything, section))
        return
    moved = (refs[:count], refs[count + carried : 3 * count + carried])
    sems = refs[3 * count + carried + 2 :][:4]

    def phase(name, p=None):
        for section in range(2):
            pl.when(y == section)(functools.partial(gather_section, section, pieces, moved, sems, name, p))

    phase("own")
    asked, sel, table = refs[count : count + carried]
    low, got = refs[3 * count + carried : 3 * count + carried + 2]
    tiles, lows, total, rows, tile_sem, low_sem, carry_sem = refs[3 * count + carried + 6 :]
    width, tall = tiles.shape[1:]
    steps = table.shape[1] // tall
    columns = [pl.ds(i * tall, tall) for i in range(steps)]
    eye = lax.broadcasted_iota(jnp.int32, (tall, tall), 0) == lax.broadcasted_iota(jnp.int32, (tall, tall), 1)
    total[...] = jnp.zeros_like(total)
    lows[...] = jnp.zeros_like(lows)

    def tile_copy(i):
        return pltpu.make_async_copy(table.at[:, columns[i]], tiles.at[i % 2], tile_sem.at[i % 2])

    def low_copy(i):
        return pltpu.make_async_copy(lows.at[i % 2], low.at[columns[i]], low_sem.at[i % 2])

    def tile(i):
        if i + 1 < steps:
            tile_copy(i + 1).start()
        tile_copy(i).wait()
        if i >= 2:
            low_copy(i - 2).wait()
        lows[i % 2, :, pl.ds(0, width)] = dense_nt(eye.astype(LOW), tiles[i % 2].astype(LOW)).astype(LOW)
        place = lax.broadcasted_iota(jnp.int32, (asked.shape[0], tall), 1) + i * tall
        total[...] += dense((asked[...] == place).astype(LOW), lows[i % 2])
        low_copy(i).start()

    tile_copy(0).start()
    for p in range(len(pieces)):
        for i in (2 * p, 2 * p + 1):
            if i < steps:
                tile(i)
        if 2 * p + 2 == steps:
            rows[...] = dense(total[...].astype(LOW), sel[...]).astype(LOW).reshape(rows.shape)
            for k in range(1, 16):
                peer = (f + k) % 16
                send(rows.at[peer], got.at[f], carry_sem.at[0], carry_sem.at[1], (y, peer))
            pltpu.make_async_copy(rows.at[f], got.at[f], carry_sem.at[2]).start()
        phase("line", p)
    phase("rest")
    low_copy(steps - 2).wait()
    low_copy(steps - 1).wait()
    settle(rows.at[pl.ds(0, 15)], carry_sem.at[0])
    settle(rows.at[pl.ds(0, 15)], carry_sem.at[1])
    settle(rows.at[0], carry_sem.at[2])


def gather_section(y, pieces, moved, sems, name, number):
    blocks, outs = moved
    count = len(blocks)
    send_sem, recv_sem, sib_sem, own_sem = sems
    z, x, c = coords()[1:]
    to_x, to_y, to_sib = (device(y, z, 1 - x, c), device(1 - y, z, x, c), device(y, z, x, 1 - c))
    zs = [(z + k) % 4 for k in range(4)]

    def part(ref, p):
        return ref.at[pl.ds(pieces[p][1], pieces[p][2])]

    def there(p, o):
        return part(outs[o[0] * count + pieces[p][0]].at[o[1] * 4 + o[2] * 2 + c], p)

    def mark(p, o):
        return recv_sem.at[p, o[0] * 8 + o[1] * 2 + o[2]]

    def push(p, o, peer, own=False, sib=False):
        src = part(blocks[pieces[p][0]], p) if own else there(p, o)
        send(src, there(p, o), send_sem.at[p], sib_sem.at[p] if sib else mark(p, o), peer)

    every = range(len(pieces))
    for p in every if name == "own" else ():
        me = (y, z, x)
        push(p, me, to_x, own=True)
        push(p, me, to_y, own=True)
        for zz in zs[1:]:
            push(p, me, device(y, zz, x, c), own=True)
        push(p, me, to_sib, own=True, sib=True)
        pltpu.make_async_copy(part(blocks[pieces[p][0]], p), there(p, me), own_sem).start()
    def from_x(p, zz):
        o = (y, zz, 1 - x)
        settle(there(p, o), mark(p, o))
        if pieces[p][3] == 0:
            push(p, o, to_y)
        push(p, o, to_sib, sib=True)

    def from_y(p, zz):
        o = (1 - y, zz, x)
        settle(there(p, o), mark(p, o))
        if pieces[p][3] == 1:
            push(p, o, to_x)
        push(p, o, to_sib, sib=True)

    if name == "line":
        p = number
        for zz in zs[1:]:
            o = (y, zz, x)
            settle(there(p, o), mark(p, o))
            push(p, o, to_x)
            push(p, o, to_y)
            push(p, o, to_sib, sib=True)
        from_x(p, z)
        from_y(p, z)
    if name != "rest":
        return
    for p in every:
        for zz in zs[1:]:
            from_x(p, zz)
            from_y(p, zz)
    for p in every:
        for zz in zs:
            o = (1 - y, zz, 1 - x)
            settle(there(p, o), mark(p, o))
            push(p, o, to_sib, sib=True)
    for p in every:
        a, start, rows_each, unused = pieces[p]
        settle(part(blocks[a], p), own_sem)
        for times in (16, 15):
            settle(outs[a].at[pl.ds(0, times), pl.ds(start, rows_each)], send_sem.at[p])
        settle(outs[a].at[pl.ds(0, 16), pl.ds(start, rows_each)], sib_sem.at[p])


def gather_all(blocks, pieces, name, extra=(), slots=0):
    many = len(pieces)
    shapes = [jax.ShapeDtypeStruct((16 if extra else 32,) + b.shape, b.dtype) for b in blocks]
    shapes = shapes * 2 if extra else shapes
    scratch = [
        pltpu.SemaphoreType.DMA((many,)),
        pltpu.SemaphoreType.DMA((many, 16)),
        pltpu.SemaphoreType.DMA((many,)),
        pltpu.SemaphoreType.DMA,
    ]
    if extra:
        (deep, wide), (width, height) = (extra[1].shape, extra[2].shape)
        shapes += [jax.ShapeDtypeStruct((height, deep), LOW), jax.ShapeDtypeStruct((16, slots, wide), LOW)]
        tall = tall_of(height)
        scratch += [
            pltpu.VMEM((2, width, tall), jnp.float32),
            pltpu.VMEM((2, tall, deep), LOW),
            pltpu.VMEM((16 * slots, deep), jnp.float32),
            pltpu.VMEM((16, slots, wide), LOW),
            pltpu.SemaphoreType.DMA((2,)),
            pltpu.SemaphoreType.DMA((2,)),
            pltpu.SemaphoreType.DMA((3,)),
        ]
    return pl.pallas_call(
        functools.partial(gather_kernel, pieces, len(blocks), len(extra)),
        out_shape=shapes,
        in_specs=[ANYWHERE] * len(blocks) + [IN_VMEM, IN_VMEM, ANYWHERE][: len(extra)],
        out_specs=[ANYWHERE] * len(shapes),
        scratch_shapes=scratch,
        compiler_params=pltpu.CompilerParams(
            collective_id=name, has_side_effects=True, vmem_limit_bytes=32 * 2**20 if extra else None
        ),
    )(*blocks, *extra)


def reduce_pieces(shapes, tile):
    out = []
    for a, (rows, cols) in enumerate(shapes):
        for row in range(0, rows, tile):
            for col in range(0, cols, TILE_C):
                out.append((a, row, col, min(TILE_C, cols - col)))
    return out


RING = 8


def reduce_kernel(pieces, tile, count, carried, lag, *refs):
    many = len(pieces)
    ring = min(RING, many)
    if carried:
        grads = (refs[:count], refs[count : 2 * count])
    else:
        grads = [[ref.at[section] for ref in refs[:count]] for section in range(2)]
    at = 2 * count + carried if carried else count
    outs = refs[at : at + count]
    at += count
    if carried:
        rows, asked, head_rows_all, grad_logits = refs[2 * count : 2 * count + carried]
        theirs, got, grad_table, sums = refs[at : at + 4]
        at += 4
    held, from_one, from_two, from_z, mine, other = refs[at : at + 6]
    sib_recv, sib_send, recv_one, send_one, recv_two, send_two, recv_z, send_z, own_sem, other_sem = refs[
        at + 6 : at + 16
    ]
    if not carried:
        theirs = other
    y, z, x, c = coords()
    to_x, to_y, to_sib = (device(y, z, 1 - x, c), device(1 - y, z, x, c), device(y, z, x, 1 - c))
    zs = [(z + k) % 4 for k in range(4)]
    f = lax.axis_index("fsdp")
    me = y * 16 + f
    alike = [(y, (f + k) % 16) for k in range(1, 16)]
    others = [(1 - y, (f + k) % 16) for k in range(16)]
    near = [to_x, to_y, to_sib] + [device(y, zz, x, c) for zz in zs[1:]]
    greet(alike + others if carried else near)

    def source(p, yo, xo, core):
        a, row, col, cols = pieces[p]
        return grads[yo][a].at[:, xo, core, pl.ds(row, tile), pl.ds(col, cols)]

    def cut(ref, p):
        cols = pieces[p][3]
        return ref if cols == TILE_C else ref.at[..., pl.ds(0, cols)]

    def fetch(p):
        for yo in range(2):
            for xo in range(2):
                pltpu.make_async_copy(
                    source(p, yo, xo, c), cut(mine.at[p % 2, yo, xo], p), own_sem.at[p % 2]
                ).start()

    def fetch_other(p):
        settle(cut(theirs.at[p], p), sib_recv.at[p])
        if carried:
            pltpu.make_async_copy(cut(theirs.at[p], p), cut(other.at[p % 2], p), other_sem.at[p % 2]).start()

    for p in range(many):
        for yo in range(2):
            for xo in range(2):
                send(
                    source(p, yo, xo, 1 - c),
                    cut(theirs.at[p, yo, xo], p),
                    sib_send.at[p],
                    sib_recv.at[p],
                    to_sib,
                )
        if p == 0:
            fetch(0)

    def store_sum(dst, left, right, p):
        cols = pl.ds(0, pieces[p][3])
        dst[:, cols] = (left[:, cols].astype(jnp.float32) + right[:, cols].astype(jnp.float32)).astype(LOW)

    def settle_sends(p):
        settle(cut(from_one.at[p], p), send_one.at[p])
        settle(cut(from_two.at[p], p), send_two.at[p])
        settle(cut(from_z.at[p], p), send_z.at[p])

    def two_cores(p):
        if p == 0:
            fetch_other(0)
        if p + 1 < many:
            fetch(p + 1)
            fetch_other(p + 1)
        if p >= ring:
            settle_sends(p - ring)
        settle(cut(mine.at[p % 2], p), own_sem.at[p % 2])
        if carried:
            settle(cut(other.at[p % 2], p), other_sem.at[p % 2])
        right, left, here = (other.at[p % 2] if carried else theirs.at[p], mine.at[p % 2], held.at[p % ring])

        def each(i, carry):
            where = (i // 8, i // 4 % 2, i % 4)
            store_sum(here.at[where], left.at[where], right.at[where], p)
            return carry

        lax.fori_loop(0, 16, each, 0)
        if p % 2 == 0:
            send(cut(here.at[1 - y], p), cut(from_one.at[p], p), send_one.at[p], recv_one.at[p], to_y)
        else:
            for yo in range(2):
                send(
                    cut(here.at[yo, 1 - x], p),
                    cut(from_one.at[p, yo], p),
                    send_one.at[p],
                    recv_one.at[p],
                    to_x,
                )

    def first_axis(p):
        settle(cut(from_one.at[p], p), recv_one.at[p])
        here = held.at[p % ring]

        def each(i, carry):
            where = (y, i // 4, i % 4) if p % 2 == 0 else (i // 4, x, i % 4)
            store_sum(here.at[where], here.at[where], from_one.at[p, i // 4, i % 4], p)
            return carry

        lax.fori_loop(0, 8, each, 0)
        src, peer = (here.at[y, 1 - x], to_x) if p % 2 == 0 else (here.at[1 - y, x], to_y)
        send(cut(src, p), cut(from_two.at[p], p), send_two.at[p], recv_two.at[p], peer)

    def second_axis(p):
        settle(cut(from_two.at[p], p), recv_two.at[p])
        here = held.at[p % ring, y, x]

        def each(i, carry):
            store_sum(here.at[i], here.at[i], from_two.at[p, i], p)
            return carry

        lax.fori_loop(0, 4, each, 0)
        for k in range(1, 4):
            send(
                cut(here.at[zs[k]], p),
                cut(from_z.at[p, 3 - k], p),
                send_z.at[p],
                recv_z.at[p],
                device(y, zs[k], x, c),
            )

    def along_z(p):
        settle(cut(from_z.at[p], p), recv_z.at[p])
        a, row, col, cols = pieces[p]
        part = pl.ds(0, cols)
        total = held[p % ring, y, x, z, :, part].astype(jnp.float32)
        for k in range(3):
            total = total + from_z[p, k, :, part].astype(jnp.float32)
        outs[a][pl.ds(row, tile), pl.ds(col, cols)] = total

    between = [()] * (many + 3 * lag)
    if carried:
        natural, turned_rows, turned_got, tiles, made, squares, carry_sem, tile_sem, made_sem, sum_sem = refs[
            at + 16 :
        ]
        between = carried_work(
            (me, y, f, to_y, alike, others),
            (rows, asked, head_rows_all, grad_logits, got, grad_table, sums, outs),
            (natural, turned_rows, turned_got, tiles, made, squares),
            (carry_sem, tile_sem, made_sem, sum_sem),
            many + 3 * lag,
        )
    for step in range(many + 3 * lag):
        for work in between[step]:
            work()
        for k, stage in enumerate((two_cores, first_axis, second_axis, along_z)):
            if 0 <= step - k * lag < many:
                stage(step - k * lag)
    for p in range(many):
        settle(cut(theirs.at[p], p), sib_send.at[p])
        if p >= many - ring:
            settle_sends(p)
    if carried:
        between[-1]()


def carried_work(where, arrays, buffers, sems, steps):
    me, y, f, to_y, alike, others = where
    rows, asked, head_rows_all, grad_logits, got, grad_table, sums, outs = arrays
    natural, turned_rows, turned_got, tiles, made, squares = buffers
    carry_sem, tile_sem, made_sem, sum_sem = sems
    height, count = grad_logits.shape
    width = grad_table.shape[0]
    slots = rows.shape[1]
    wide = rows.shape[2]
    tall = tiles.shape[1]
    turns = height // tall
    leader = jnp.where(y == 0, 1.0, 0.0)
    eye = lax.broadcasted_iota(jnp.int32, (tall, tall), 0) == lax.broadcasted_iota(jnp.int32, (tall, tall), 1)

    def turn(source, target):
        for k in range(wide // tall):
            part = pl.ds(k * tall, tall)
            target[part] = dense_nt(eye.astype(LOW), source[:, part]).astype(LOW)

    def start():
        for peer in alike:
            send(rows.at[peer[1]], got.at[me], carry_sem.at[0], carry_sem.at[1], peer)
        pltpu.make_async_copy(rows.at[f], got.at[me], carry_sem.at[2]).start()
        pltpu.make_async_copy(head_rows_all, natural.at[pl.ds(0, count)], carry_sem.at[5]).start()

    def turn_rows():
        settle(natural.at[pl.ds(0, count)], carry_sem.at[5])
        turn(natural.at[pl.ds(0, count)], turned_rows)

    def pass_on():
        settle(rows.at[pl.ds(0, 15)], carry_sem.at[1])
        settle(rows.at[0], carry_sem.at[2])
        ours = got.at[pl.ds(y * 16, 16)]
        send(ours, ours, carry_sem.at[3], carry_sem.at[4], to_y)

    def load_got():
        settle(rows, carry_sem.at[4])
        for k in range(32):
            pltpu.make_async_copy(got.at[k], natural.at[pl.ds(k * slots, slots)], carry_sem.at[5]).start()
        tile_copy(0).start()

    def turn_got():
        settle(natural.at[pl.ds(0, 32 * slots)], carry_sem.at[5])
        turn(natural.at[pl.ds(0, 32 * slots)], turned_got)
        squares[...] = jnp.zeros_like(squares)

    def tile_copy(i):
        return pltpu.make_async_copy(grad_logits.at[pl.ds(i * tall, tall)], tiles.at[i % 2], tile_sem.at[i % 2])

    def made_copy(i):
        return pltpu.make_async_copy(made.at[i % 2], grad_table.at[:, pl.ds(i * tall, tall)], made_sem.at[i % 2])

    def table_tile(i):
        if i + 1 < turns:
            tile_copy(i + 1).start()
        tile_copy(i).wait()
        if i >= 2:
            made_copy(i - 2).wait()
        place = lax.broadcasted_iota(jnp.int32, (tall, asked.shape[1]), 0) + i * tall
        here = dense_nt(turned_rows[...], tiles[i % 2]) + dense_nt(
            turned_got[...], (asked[...] == place).astype(LOW)
        )
        here = here[:width]
        made[i % 2] = here.astype(LOW)
        squares[pl.ds(0, 1)] += leader * squares_of(here)
        made_copy(i).start()

    def end():
        gains = outs[-1][...]
        layers = squares_of(gains[:2]) + leader * squares_of(gains[2:3])
        for out in outs[:-1]:
            layers += squares_of(out[...])
        squares[pl.ds(0, 1)] += layers
        squares[pl.ds(1, 1)] += layers
        for peer in alike + others:
            send(squares, sums.at[me], sum_sem.at[0], sum_sem.at[1], peer)
        sums[me] = squares[...]
        made_copy(turns - 2).wait()
        made_copy(turns - 1).wait()
        settle(rows.at[pl.ds(0, 15)], carry_sem.at[0])
        settle(rows, carry_sem.at[3])
        settle(sums.at[pl.ds(0, 31)], sum_sem.at[0])
        settle(sums.at[pl.ds(0, 31)], sum_sem.at[1])

    plan = [[] for unused in range(steps)]
    plan[0].append(start)
    plan[3].append(turn_rows)
    plan[9].append(pass_on)
    plan[13].append(load_got)
    plan[14].append(turn_got)
    for i in range(turns):
        plan[15 + i * (steps - 16) // turns].append(functools.partial(table_tile, i))
    return plan + [end]


def reduce_all(grads, name, lag, tile=TILE_R, extra=(), width=0):
    first = grads[0] if extra else grads
    count = len(first)
    shapes = [(g.shape[0] // (16 if extra else 32), g.shape[1]) for g in first]
    pieces = reduce_pieces(shapes, tile)
    many = len(pieces)
    if extra:
        views = [g.reshape(4, 2, 2, g.shape[0] // 16, g.shape[1]) for layer in grads for g in layer]
    else:
        views = [g.reshape(2, 4, 2, 2, *s) for g, s in zip(grads, shapes)]
    results = [jax.ShapeDtypeStruct(s, jnp.float32) for s in shapes]
    piece = (2, 2, 4, tile, TILE_C)
    scratch = [
        pltpu.VMEM((min(RING, many),) + piece, LOW),
        pltpu.VMEM((many, 2, 4, tile, TILE_C), LOW),
        pltpu.VMEM((many, 4, tile, TILE_C), LOW),
        pltpu.VMEM((many, 3, tile, TILE_C), LOW),
        pltpu.VMEM((2,) + piece, LOW),
        pltpu.VMEM((2 if extra else many,) + piece, LOW),
    ]
    scratch += [pltpu.SemaphoreType.DMA((many,)) for unused in range(8)]
    scratch += [pltpu.SemaphoreType.DMA((2,)), pltpu.SemaphoreType.DMA((2,))]
    in_specs, out_specs = ([ANYWHERE] * len(views), [IN_VMEM] * count)
    if extra:
        rows, asked, scored_rows, grad_logits = extra
        slots, wide = rows.shape[1:]
        height, total = grad_logits.shape
        tall = tall_of(height)
        results += [
            jax.ShapeDtypeStruct((many,) + piece, LOW),
            jax.ShapeDtypeStruct((32, slots, wide), LOW),
            jax.ShapeDtypeStruct((width, height), LOW),
            jax.ShapeDtypeStruct((32, 8, 128), jnp.float32),
        ]
        in_specs += [ANYWHERE, IN_VMEM, ANYWHERE, ANYWHERE]
        out_specs += [ANYWHERE] * 3 + [IN_VMEM]
        scratch += [
            pltpu.VMEM((max(total, 32 * slots), wide), LOW),
            pltpu.VMEM((wide, total), LOW),
            pltpu.VMEM((wide, 32 * slots), LOW),
            pltpu.VMEM((2, tall, total), LOW),
            pltpu.VMEM((2, width, tall), LOW),
            pltpu.VMEM((8, 128), jnp.float32),
            pltpu.SemaphoreType.DMA((6,)),
            pltpu.SemaphoreType.DMA((2,)),
            pltpu.SemaphoreType.DMA((2,)),
            pltpu.SemaphoreType.DMA((2,)),
        ]
    return pl.pallas_call(
        functools.partial(reduce_kernel, pieces, tile, count, len(extra), lag),
        out_shape=results,
        in_specs=in_specs,
        out_specs=out_specs,
        scratch_shapes=scratch,
        compiler_params=pltpu.CompilerParams(
            collective_id=name, has_side_effects=True, vmem_limit_bytes=(60 if extra else 32) * 2**20
        ),
    )(*views, *extra)


def exchange_kernel(whole, src, out, send_sem, recv_sem, own_sem):
    y, f = (lax.axis_index("section"), lax.axis_index("fsdp"))
    count = 32 if whole else 16
    me = y * 16 + f if whole else f
    peers = [(me + k) % count for k in range(1, count)]
    where = [(p // 16, p % 16) if whole else (y, p) for p in peers]
    greet(where)
    for peer in where:
        send(src, out.at[me], send_sem, recv_sem, peer)
    own = pltpu.make_async_copy(src, out.at[me], own_sem)
    own.start()
    own.wait()
    settle(out.at[pl.ds(0, count - 1)], send_sem)
    settle(out.at[pl.ds(0, count - 1)], recv_sem)


def exchange(small, name, whole=True):
    return pl.pallas_call(
        functools.partial(exchange_kernel, whole),
        out_shape=jax.ShapeDtypeStruct((32 if whole else 16,) + small.shape, small.dtype),
        in_specs=[IN_VMEM],
        out_specs=IN_VMEM,
        scratch_shapes=[pltpu.SemaphoreType.DMA] * 3,
        compiler_params=pltpu.CompilerParams(collective_id=name, has_side_effects=True),
    )(small)


def tall_of(height, sections=2, most=256):
    while height % (most * sections):
        most //= 2
    return most


def whole(shape):
    return pl.BlockSpec(shape, lambda *unused: (0,) * len(shape), pipeline_mode=pl.Buffered(1))


def striped(tall, cols):
    return pl.BlockSpec((tall, cols), lambda i: (i, 0))


def lined(rows, wide):
    return pl.BlockSpec((rows, wide), lambda i: (0, i))


def squares_of(value):
    return jnp.sum(jnp.sum(value * value, axis=1, keepdims=True), axis=0, keepdims=True)


def padded_table_kernel(asked, sel, table, low, rows, total):
    step = pl.program_id(0)

    @pl.when(step == 0)
    def start():
        total[...] = jnp.zeros_like(total)

    width, tall = table.shape
    low[:, pl.ds(low.shape[1] - 128, 128)] = jnp.zeros((tall, 128), LOW)
    eye = lax.broadcasted_iota(jnp.int32, (tall, tall), 0) == lax.broadcasted_iota(jnp.int32, (tall, tall), 1)
    low[:, pl.ds(0, width)] = dense_nt(eye.astype(LOW), table[...].astype(LOW)).astype(LOW)
    place = lax.broadcasted_iota(jnp.int32, (asked.shape[0], tall), 1) + step * tall
    total[...] += dense((asked[...] == place).astype(LOW), low[...])

    @pl.when(step == pl.num_programs(0) - 1)
    def end():
        rows[...] = dense(total[...].astype(LOW), sel[...]).astype(LOW)


def padded_table(asked, sel, table):
    width, height = table.shape
    wide = sel.shape[0]
    count = asked.shape[0]
    tall = tall_of(height)
    return pl.pallas_call(
        padded_table_kernel,
        grid=(height // tall,),
        out_shape=[
            jax.ShapeDtypeStruct((height, wide), LOW),
            jax.ShapeDtypeStruct((count, sel.shape[1]), LOW),
        ],
        in_specs=[whole((count, 1)), whole(sel.shape), lined(width, tall)],
        out_specs=[striped(tall, wide), whole((count, sel.shape[1]))],
        scratch_shapes=[pltpu.VMEM((count, wide), jnp.float32)],
        compiler_params=pltpu.CompilerParams(vmem_limit_bytes=48 * 2**20),
    )(asked[:, None], sel, table)


def logits_kernel(wanted, rows, table, logits, top, total, target):
    step = pl.program_id(0)

    @pl.when(step == 0)
    def start():
        top[...] = jnp.full_like(top, -jnp.inf)
        total[...] = jnp.zeros_like(total)
        target[...] = jnp.zeros_like(target)

    here = dense_nt(table[...], rows[...])
    logits[...] = here
    higher = jnp.maximum(top[...], jnp.max(here, axis=0, keepdims=True))
    total[...] = total[...] * jnp.exp(top[...] - higher) + jnp.sum(
        jnp.exp(here - higher), axis=0, keepdims=True
    )
    top[...] = higher
    place = lax.broadcasted_iota(jnp.int32, here.shape, 0) + step * here.shape[0]
    target[...] += jnp.sum(jnp.where(place == wanted[...], here, 0.0), axis=0, keepdims=True)


def logits_of(wanted, rows, table):
    height, wide = table.shape
    count = rows.shape[0]
    tall = tall_of(height, most=512 if count <= 2048 else 256)
    line = jax.ShapeDtypeStruct((1, count), jnp.float32)
    return pl.pallas_call(
        logits_kernel,
        grid=(height // tall,),
        out_shape=[jax.ShapeDtypeStruct((height, count), jnp.float32), line, line, line],
        in_specs=[whole((1, count)), whole(rows.shape), striped(tall, wide)],
        out_specs=[striped(tall, count)] + [whole((1, count))] * 3,
        compiler_params=pltpu.CompilerParams(vmem_limit_bytes=48 * 2**20),
    )(wanted[None], rows, table)


def logits_back_kernel(share, section, wanted, top, scale, push, logits, table, grad, rows, total):
    step = pl.program_id(1)
    mine = (step >= section[0] * share) & (step < (section[0] + 1) * share)

    @pl.when(step == 0)
    def start():
        total[...] = jnp.zeros_like(total)

    here = logits[...]
    place = lax.broadcasted_iota(jnp.int32, here.shape, 0) + step * here.shape[0]
    hit = jnp.where(place == wanted[...], push[...], 0.0)
    low = (hit - jnp.exp(here - top[...]) * scale[...]).astype(LOW)
    grad[...] = low

    @pl.when(mine)
    def add():
        total[...] += dense_t(low, table[...])

    @pl.when(step == pl.num_programs(1) - 1)
    def end():
        rows[...] = total[...].astype(LOW)


def logits_back(section, wanted, top, scale, push, logits, table, sections):
    height, wide = table.shape
    count = logits.shape[1]
    tall = tall_of(height, sections, 512)
    block = min(count, 2048)
    line = pl.BlockSpec((1, block), lambda j, i: (0, j))
    tile = pl.BlockSpec((tall, block), lambda j, i: (i, j))
    return pl.pallas_call(
        functools.partial(logits_back_kernel, height // tall // sections),
        grid=(count // block, height // tall),
        out_shape=[
            jax.ShapeDtypeStruct((height, count), LOW),
            jax.ShapeDtypeStruct((count, wide), LOW),
        ],
        in_specs=[
            pl.BlockSpec(memory_space=pltpu.SMEM),
            line,
            line,
            line,
            line,
            tile,
            pl.BlockSpec((tall, wide), lambda j, i: (i, 0)),
        ],
        out_specs=[tile, pl.BlockSpec((block, wide), lambda j, i: (j, 0))],
        scratch_shapes=[pltpu.VMEM((block, wide), jnp.float32)],
        compiler_params=pltpu.CompilerParams(vmem_limit_bytes=56 * 2**20),
    )(section[None], wanted[None], top[None], scale[None], push[None], logits, table)


def table_grad_kernel(leader, asked, got, rows, grad_logits, *refs):
    *others, grad, squares = refs
    step = pl.program_id(0)

    @pl.when(step == 0)
    def start():
        gains = others[-1][...]
        total = squares_of(gains[:2]) + leader[0] * squares_of(gains[2:3])
        for other in others[:-1]:
            total += squares_of(other[...])
        squares[...] = jnp.broadcast_to(total, squares.shape)

    width, tall = grad.shape
    place = lax.broadcasted_iota(jnp.int32, (tall, asked.shape[1]), 0) + step * tall
    here = dense_nt(rows[...], grad_logits[...]) + dense_nt(got[...], (asked[...] == place).astype(LOW))
    here = here[:width]
    grad[...] = here.astype(LOW)
    squares[pl.ds(0, 1)] += leader[0] * squares_of(here)


def table_grad(leader, asked, got, rows, grad_logits, others, width):
    height, count = grad_logits.shape
    tall = tall_of(height)
    return pl.pallas_call(
        table_grad_kernel,
        grid=(height // tall,),
        out_shape=[
            jax.ShapeDtypeStruct((width, height), LOW),
            jax.ShapeDtypeStruct((8, 128), jnp.float32),
        ],
        in_specs=[
            pl.BlockSpec(memory_space=pltpu.SMEM),
            whole((1, asked.shape[0])),
            whole(got.shape),
            whole(rows.shape),
            striped(tall, count),
        ]
        + [whole(o.shape) for o in others],
        out_specs=[lined(width, tall), whole((8, 128))],
        compiler_params=pltpu.CompilerParams(vmem_limit_bytes=56 * 2**20),
    )(leader[None], asked[None], got, rows, grad_logits, *others)


def exact_product(left, onehot):
    high = left.astype(LOW)
    rest = left - high.astype(jnp.float32)
    middle = rest.astype(LOW)
    lowest = (rest - middle.astype(jnp.float32)).astype(LOW)
    return dense_nt(high, onehot) + (dense_nt(middle, onehot) + dense_nt(lowest, onehot))


ROWED = 3
BAND = 160
SPREAD = (1, 3)


def moments_kernel(decays, clip, sel, *refs):
    weights, grads, firsts, seconds = (refs[7 * k : 7 * k + 7] for k in range(4))
    new_firsts, new_seconds, updates = (refs[28 + 7 * k : 35 + 7 * k] for k in range(3))
    kept, sums, *scratch = refs[49:49 + ROWED] , refs[49 + ROWED], *refs[50 + ROWED:]
    staged = [scratch[5 * k : 5 * k + 5] for k in range(ROWED)]
    in_sem, out_sem = scratch[5 * ROWED :]
    step, steps = (pl.program_id(0), pl.num_programs(0))

    def copies(k, inward):
        w, m, v, new_m, new_v = staged[k]
        if inward:
            pairs = [(weights[k + 1].at[:, 0], w), (firsts[k + 1].at[:, 0], m), (seconds[k + 1].at[:, 0], v)]
        else:
            pairs = [(new_m, new_firsts[k + 1].at[:, 0]), (new_v, new_seconds[k + 1].at[:, 0])]
        return [
            pltpu.make_async_copy(src, dst, (in_sem if inward else out_sem).at[k, i])
            for i, (src, dst) in enumerate(pairs)
        ]

    @pl.when(step == 0)
    def start():
        sums[...] = jnp.zeros_like(sums)
        for k in range(ROWED):
            for copy in copies(k, True):
                copy.start()

    def one(weight, grad, first, second, decay):
        return (weight,) + lamb_parts(weight, clip[0] * grad.astype(jnp.float32), first, second, decay)

    weight, new_firsts[0][...], new_seconds[0][...], update = one(
        weights[0][...], grads[0][...], firsts[0][...], seconds[0][...], decays[0]
    )
    updates[0][...] = update.astype(LOW)
    sums[pl.ds(0, 1)] += squares_of(weight)
    sums[pl.ds(8, 1)] += squares_of(update)

    def tensor(k):
        rows, cols = updates[k + 1].shape
        grad = grads[k + 1][pl.ds(0, rows)]
        grad = exact_product(grad, sel[...]) if k in SPREAD else grad[:, :cols]
        if k < ROWED:
            for copy in copies(k, True):
                copy.wait()
            w, m, v, new_m, new_v = staged[k]
        else:
            w, m, v, new_m, new_v = (t[k + 1] for t in (weights, firsts, seconds, new_firsts, new_seconds))
        weight, new_m[...], new_v[...], update = one(w[...], grad, m[...], v[...], decays[k + 1])
        updates[k + 1][...] = update
        if k < ROWED:
            kept[k][...] = weight
            for copy in copies(k, False):
                copy.start()
        for row in range(rows if k == 4 else 1):
            part = slice(row, row + 1) if k == 4 else slice(None)
            line = k + 1 + row + (k > 4)
            sums[pl.ds(line, 1)] += squares_of(weight[part])
            sums[pl.ds(8 + line, 1)] += squares_of(update[part])

    for k in range(6):
        pl.when(step == (steps // 2 + k if k < ROWED else k - 2) % steps)(functools.partial(tensor, k))

    @pl.when(step == steps - 1)
    def end():
        for k in range(ROWED):
            for copy in copies(k, False):
                copy.wait()


def moments(clip, sel, weights, grads, firsts, seconds, decays):
    width, height = weights[0].shape
    band = pl.BlockSpec((BAND, height), lambda i: (i, 0))
    flat = [w.shape if w.ndim == 2 else w.shape[::2] for w in weights]

    def specs(arrays, results=False):
        out = [band]
        for a in arrays[1:]:
            out.append(ANYWHERE if a.ndim == 3 else whole(a.shape))
        return out

    line = [jax.ShapeDtypeStruct(w.shape, jnp.float32) for w in weights]
    plain = [jax.ShapeDtypeStruct(s, jnp.float32 if k else LOW) for k, s in enumerate(flat)]
    kept = plain[1 : 1 + ROWED]
    out = pl.pallas_call(
        functools.partial(moments_kernel, decays),
        grid=(width // BAND,),
        out_shape=line * 2 + plain + kept + [jax.ShapeDtypeStruct((16, 128), jnp.float32)],
        in_specs=[pl.BlockSpec(memory_space=pltpu.SMEM), whole(sel.shape)]
        + specs(weights)
        + specs(grads)
        + specs(firsts)
        + specs(seconds),
        out_specs=specs(line) * 2 + specs(plain) + [whole(s.shape) for s in kept] + [whole((16, 128))],
        scratch_shapes=[pltpu.VMEM(s.shape, jnp.float32) for s in kept for unused in range(5)]
        + [pltpu.SemaphoreType.DMA((ROWED, 3)), pltpu.SemaphoreType.DMA((ROWED, 2))],
        compiler_params=pltpu.CompilerParams(vmem_limit_bytes=60 * 2**20),
    )(clip[None], sel, *weights, *grads, *firsts, *seconds)
    return (out[:7], out[7:14], out[14:21], out[21 : 21 + ROWED], out[21 + ROWED])


def apply_kernel(scales, *refs):
    weights, updates, new, half = (refs[5 * k : 5 * k + 5] for k in range(4))
    staged, sem = (refs[20 : 20 + ROWED], refs[20 + ROWED])
    step, steps = (pl.program_id(0), pl.num_programs(0))

    def copy(k):
        return pltpu.make_async_copy(staged[k - 1], new[k].at[:, 0], sem.at[k - 1])

    def one(k):
        value = weights[k][...] - RATE * scales[k] * updates[k][...]
        half[k][...] = value.astype(LOW)
        if 0 < k <= ROWED:
            staged[k - 1][...] = value
            copy(k).start()
        else:
            new[k][...] = value

    one(0)
    for k in range(1, 5):
        pl.when(step == (k - 1) % steps)(functools.partial(one, k))

    @pl.when(step == steps - 1)
    def end():
        for k in range(1, 1 + ROWED):
            copy(k).wait()


def apply_updates(scales, weights, updates, shapes):
    width, height = weights[0].shape
    plain = [pl.BlockSpec((BAND, height), lambda i: (i, 0))] + [whole(w.shape) for w in weights[1:]]
    out = pl.pallas_call(
        apply_kernel,
        grid=(width // BAND,),
        out_shape=[jax.ShapeDtypeStruct(s, jnp.float32) for s in shapes]
        + [jax.ShapeDtypeStruct(w.shape, LOW) for w in weights],
        in_specs=[pl.BlockSpec(memory_space=pltpu.SMEM)] + plain * 2,
        out_specs=plain[:1] + [ANYWHERE] * ROWED + plain[1 + ROWED :] + plain,
        scratch_shapes=[pltpu.VMEM(w.shape, jnp.float32) for w in weights[1 : 1 + ROWED]]
        + [pltpu.SemaphoreType.DMA((ROWED,))],
        compiler_params=pltpu.CompilerParams(vmem_limit_bytes=56 * 2**20),
    )(scales, *weights, *updates)
    return (out[:5], out[5:])


EACH = HEADS // KV


def turned(x, cosine, sine):
    half = HD // 2
    u, w = (x[:half], x[half:])
    return jnp.concatenate([u * cosine - w * sine, w * cosine + u * sine], axis=0)


def query_blocks(scored):
    if scored:
        return [(0, scored, ((0, TOK_MB),))]
    out = [(0, PROMPT, ((0, PROMPT),))]
    for j in range(NCONT):
        first = PROMPT + j * CONT
        out.append((first, CONT, ((0, PROMPT), (first, CONT))))
    return out


def masks(place):
    out = []
    for first, count, ranges in query_blocks(0 if place is None else place.shape[1]):
        keys = sum(r[1] for r in ranges)
        row = lax.broadcasted_iota(jnp.int32, (keys, count), 0)
        if place is not None:
            at = place[pl.ds(0, 1)]
            seen = (row < PROMPT) | ((row >= place[pl.ds(1, 1)]) & (row <= at))
        else:
            seen = row - (keys - count) <= lax.broadcasted_iota(jnp.int32, (keys, count), 1)
        out.append(jnp.concatenate([jnp.where(seen, 0.0, -1e30)] * EACH, axis=1))
    return out


def rows_of(ranges, array):
    parts = [array[first : first + count] for first, count in ranges]
    return parts[0] if len(parts) == 1 else jnp.concatenate(parts, axis=0)


def head_rows(start):
    return pl.ds(pl.multiple_of(start, HD), HD)


def side_by_side(ref, group, first, count):
    return jnp.concatenate(
        [ref[head_rows((group * EACH + j) * HD), pl.ds(first, count)] for j in range(EACH)], axis=1
    )


def attend_kernel(scored, qkv, cosine, sine, *refs):
    pick, place = refs[:2] if scored else (None, None)
    low, out, top, share, *queries = refs[2:] if scored else refs
    queries = queries[0] if scored else low
    cos, sin = (cosine[...], sine[...])
    added = masks(place)

    def group_of(group, carry):
        key = turned(qkv[head_rows(WIDTH + group * HD)], cos, sin)
        low[head_rows(WIDTH + group * HD)] = key.astype(LOW)
        value = qkv[head_rows(WIDTH + KVW + group * HD)].astype(LOW)
        low[head_rows(WIDTH + KVW + group * HD)] = value
        for j in range(EACH):
            place_of = head_rows((group * EACH + j) * HD)
            query = turned(qkv[place_of], cos, sin).astype(LOW)
            low[place_of] = query
            if scored:
                queries[place_of] = dense_nt(query, pick[...]).astype(LOW)
        keys = key.T.astype(LOW)
        for (first, count, ranges), extra in zip(query_blocks(scored), added):
            query = side_by_side(queries, group, first, count)
            scores = dense(rows_of(ranges, keys), query) * SCALE + extra
            high = jnp.max(scores, axis=0, keepdims=True)
            expo = jnp.exp(scores - high)
            part = 1.0 / jnp.sum(expo, axis=0, keepdims=True)
            probs = (expo * part).astype(LOW)
            got, at = (0.0, 0)
            for start, length in ranges:
                got += dense(value[:, start : start + length], probs[at : at + length])
                at += length
            for j in range(EACH):
                column = slice(j * count, (j + 1) * count)
                out[head_rows((group * EACH + j) * HD), pl.ds(first, count)] = got[:, column].astype(LOW)
                top[group, j : j + 1, pl.ds(first, count)] = high[:, column]
                share[group, j : j + 1, pl.ds(first, count)] = part[:, column]
        return carry

    lax.fori_loop(0, KV, group_of, 0)


def attention(qkv, cosine, sine, chosen=()):
    tokens = qkv.shape[1]
    scored = chosen[0].shape[0] if chosen else 0
    count = scored or tokens
    stat = jax.ShapeDtypeStruct((KV, EACH, count), jnp.float32)
    heads = jax.ShapeDtypeStruct((WIDTH, count), LOW)
    results = [jax.ShapeDtypeStruct((WIDTH + 2 * KVW, tokens), LOW), heads, stat, stat]
    results += [heads] if scored else []
    return pl.pallas_call(
        functools.partial(attend_kernel, scored),
        out_shape=results,
        in_specs=[IN_VMEM] * (3 + len(chosen)),
        out_specs=[IN_VMEM] * len(results),
        compiler_params=pltpu.CompilerParams(vmem_limit_bytes=40 * 2**20),
    )(qkv, cosine, sine, *chosen)


def attend_back_kernel(scored, low, top, share, grad, cosine, sine, *refs):
    pick, place, queries = refs[:3] if scored else (None, None, low)
    out, key_sum, value_sum = refs[-3:]
    cos, sin = (cosine[...], sine[...])
    added = masks(place)
    spare = out.shape[0] - WIDTH - 2 * KVW
    out[pl.ds(WIDTH + 2 * KVW, spare)] = jnp.zeros((spare, out.shape[1]), LOW)

    def group_of(group, carry):
        key = low[head_rows(WIDTH + group * HD)]
        value = low[head_rows(WIDTH + KVW + group * HD)]
        keys = key.astype(jnp.float32).T.astype(LOW)
        values = value.astype(jnp.float32).T.astype(LOW)
        for number, ((first, count, ranges), extra) in enumerate(zip(query_blocks(scored), added)):
            sides = range(EACH)
            columns = pl.ds(first, count)
            query = side_by_side(queries, group, first, count)
            upstream = side_by_side(grad, group, first, count)
            high = jnp.concatenate([top[group, j : j + 1, columns] for j in sides], axis=1)
            part = jnp.concatenate([share[group, j : j + 1, columns] for j in sides], axis=1)
            scores = dense(rows_of(ranges, keys), query) * SCALE + extra
            probs = jnp.exp(scores - high) * part
            grad_probs = dense(rows_of(ranges, values), upstream)
            inner = jnp.sum(grad_probs * probs, axis=0, keepdims=True)
            grad_scores = (probs * (grad_probs - inner)).astype(LOW)
            probs = probs.astype(LOW)
            got, at = (0.0, 0)
            for start, length in ranges:
                piece = slice(at, at + length)
                got += dense(key[:, start : start + length], grad_scores[piece])
                here = pl.ds(start, length)
                more_key = dense_nt(query, grad_scores[piece])
                more_value = dense_nt(upstream, probs[piece])
                if number == 0 or start > 0:
                    key_sum[:, here] = more_key
                    value_sum[:, here] = more_value
                else:
                    key_sum[:, here] += more_key
                    value_sum[:, here] += more_value
                at += length
            for j in sides:
                turn = got[:, j * count : (j + 1) * count] * SCALE
                where = head_rows((group * EACH + j) * HD)
                if scored:
                    high_part = turn.astype(LOW)
                    rest = (turn - high_part.astype(jnp.float32)).astype(LOW)
                    turn = dense(high_part, pick[...]) + dense(rest, pick[...])
                    out[where] = turned(turn, cos, -sin).astype(LOW)
                else:
                    past = slice(first, first + count)
                    out[where, columns] = turned(turn, cos[:, past], -sin[:, past]).astype(LOW)
        out[head_rows(WIDTH + group * HD)] = turned(key_sum[...] * SCALE, cos, -sin).astype(LOW)
        out[head_rows(WIDTH + KVW + group * HD)] = value_sum[...].astype(LOW)
        return carry

    lax.fori_loop(0, KV, group_of, 0)


def attention_back(low, top, share, grad, cosine, sine, wide, chosen=()):
    tokens = low.shape[1]
    return pl.pallas_call(
        functools.partial(attend_back_kernel, chosen[0].shape[0] if chosen else 0),
        out_shape=jax.ShapeDtypeStruct((wide, tokens), LOW),
        in_specs=[IN_VMEM] * (6 + len(chosen)),
        out_specs=IN_VMEM,
        scratch_shapes=[pltpu.VMEM((HD, tokens), jnp.float32)] * 2,
        compiler_params=pltpu.CompilerParams(vmem_limit_bytes=48 * 2**20),
    )(low, top, share, grad, cosine, sine, *chosen)


def up16(count):
    return -(-count // 16) * 16


def dense(left, right):
    return jnp.dot(left, right, preferred_element_type=jnp.float32)


def dense_t(left, right):
    return lax.dot_general(
        left, right, (((0,), (0,)), ((), ())), preferred_element_type=jnp.float32
    )


def dense_nt(left, right):
    return lax.dot_general(
        left, right, (((1,), (1,)), ((), ())), preferred_element_type=jnp.float32
    )


def spread_matrix(parts, real, padded):
    feature = jnp.arange(parts * real)
    place = feature // real * padded + feature % real
    return (place[:, None] == jnp.arange(parts * padded)[None, :]).astype(LOW)


def inverse_rms(x, width):
    return lax.rsqrt(jnp.sum(x * x, axis=-1, keepdims=True) / width + EPS)


def norm_back(x, scale, gain, upstream, width):
    inner = upstream * gain
    grad_gain = jnp.sum(upstream * x * scale, axis=0)
    mean = jnp.sum(inner * x, axis=-1, keepdims=True) / width
    return (scale * inner - x * scale**3 * mean, grad_gain)


def rotary_angles():
    place = jnp.arange(TOK_MB)
    rotary = jnp.where(place >= PROMPT, PROMPT + (place - PROMPT) % CONT, place).astype(jnp.float32)
    freq = THETA ** (-2.0 * jnp.arange(HD // 2).astype(jnp.float32) / HD)
    angle = freq[:, None] * rotary[None, :]
    return (jnp.cos(angle), jnp.sin(angle))


def dense_tt(left, right):
    return lax.dot_general(
        left, right, (((0,), (1,)), ((), ())), preferred_element_type=jnp.float32
    )


def mlp(b, w_gu, w_down):
    gate_up = dense(b, w_gu)
    half = gate_up.shape[1] // 2
    gate, upper = (gate_up[:, :half], gate_up[:, half:])
    hidden = (jax.nn.silu(gate) * upper).astype(LOW)
    return (dense(hidden, w_down), gate, upper, hidden)


def mlp_back(branch, b, gate, upper, hidden, w_gu, w_down):
    grad_down = dense_t(hidden, branch)
    grad_hidden = dense_nt(branch, w_down)
    sig = jax.nn.sigmoid(gate)
    grad_gate = grad_hidden * upper * sig * (1.0 + gate * (1.0 - sig))
    grad_upper = grad_hidden * gate * sig
    grad_gate_up = jnp.concatenate([grad_gate, grad_upper], axis=1).astype(LOW)
    return (grad_down, dense_t(b, grad_gate_up), dense_nt(grad_gate_up, w_gu))


def lamb_parts(weight, grad, first, second, decay):
    first_new = BETA_ONE * first + (1.0 - BETA_ONE) * grad
    second_new = BETA_TWO * second + (1.0 - BETA_TWO) * grad * grad
    root = (1.0 - BETA_TWO**STEP) ** 0.5
    scale = root / (1.0 - BETA_ONE**STEP)
    update = first_new * scale / (second_new * lax.rsqrt(second_new) + ADAM_EPS * root) + decay * weight
    return (first_new, second_new, update)


def lookup_ranks(ids, vshard):
    place = jnp.arange(ids.shape[0])
    same = ids[:, None] == ids[None, :]
    first = jnp.min(jnp.where(same, place[None, :], ids.shape[0]), axis=1)
    owner = ids // vshard
    before = (
        (owner[:, None] == owner[None, :])
        & (first == place)[None, :]
        & (place[None, :] < first[:, None])
    )
    return (owner, jnp.sum(before.astype(jnp.int32), axis=1))


def lookup_round(ids, owner, rank, turn, slots, parts, vshard):
    slot = jnp.where(rank // slots == turn, owner * slots + rank - turn * slots, -1)
    onehot = slot[:, None] == jnp.arange(parts * slots)[None, :]
    wanted = jnp.max(jnp.where(onehot, (ids - owner * vshard)[:, None], -1), axis=0)
    return (onehot.astype(LOW), wanted)


def shards(
    token_ids,
    scored,
    targets,
    pairs,
    table,
    w_qkv,
    w_out,
    w_gu,
    w_down,
    gains,
    final_gain,
    first_table,
    first_qkv,
    first_out,
    first_gu,
    first_down,
    first_gains,
    first_final,
    second_table,
    second_qkv,
    second_out,
    second_gu,
    second_down,
    second_gains,
    second_final,
):
    n = lax.axis_size("fsdp")
    sections = lax.axis_size("section")
    section_index = lax.axis_index("section")
    fsdp_index = lax.axis_index("fsdp")
    leader = section_index == 0
    vshard, width = table.shape
    vstart = fsdp_index * vshard
    r = w_qkv.shape[1]
    rp = up16(r)
    rd = w_down.shape[1]
    rdp = up16(rd)
    wide = n * rp
    ffp = n * rdp
    slots = up16(768 // n)
    sel = spread_matrix(n, r, rp)
    sel_wide = jnp.pad(sel, ((0, wide - width), (0, 0)))
    fast = (sections, n) == (2, 16)
    qkv_wide = -(-w_qkv.shape[2] // 128) * 128

    qkv_block = jnp.pad(
        w_qkv[0].astype(LOW), ((0, rp - r), (0, qkv_wide - w_qkv.shape[2]))
    )
    out_block = jnp.pad(dense(w_out[0].astype(LOW), sel).astype(LOW), ((0, rp - r), (0, 0)))
    gu_block = w_gu[0].astype(LOW)
    if rdp != rd:
        gu_block = jnp.pad(gu_block.reshape(r, 2, n, rd), ((0, 0), (0, 0), (0, 0), (0, rdp - rd)))
    gu_block = jnp.pad(gu_block.reshape(r, 2 * ffp), ((0, rp - r), (0, 0)))
    down_block = jnp.pad(dense(w_down[0].astype(LOW), sel).astype(LOW), ((0, rdp - rd), (0, 0)))
    gain_block = jnp.pad(
        jnp.concatenate([gains[0], final_gain[None]], axis=0).astype(LOW),
        ((0, 13), (0, 128 - r)),
    )

    ids = token_ids[0]
    owner, rank = lookup_ranks(ids, vshard)
    onehot, wanted = lookup_round(ids, owner, rank, 0, slots, n, vshard)
    turns_here = jnp.max(rank) // slots + 1
    own_targets = lax.dynamic_slice_in_dim(targets[0], fsdp_index * NCONT, NCONT).reshape(-1)
    note = jnp.concatenate(
        [wanted, jnp.pad(own_targets, (0, 128 - NCONT * SCORED)), jnp.full((128,), turns_here, jnp.int32)]
    )
    if fast:
        notes = exchange(note.reshape(-1, 128), 0).reshape(sections * n, -1)
    else:
        notes = lax.all_gather(note, BOTH, axis=0)
    turns = jnp.max(notes[:, -1])
    wanted_rows = notes[:, n * slots : n * slots + NCONT * SCORED].reshape(-1)

    def asked(all_wanted):
        mine = lax.dynamic_slice_in_dim(all_wanted.reshape(sections, n, n, slots), fsdp_index, 1, 2)
        return mine[:, :, 0]

    asked_first = asked(notes[:, : n * slots])
    asked_here = lax.dynamic_index_in_dim(asked_first, section_index, 0, keepdims=False).reshape(-1)
    blocks = (qkv_block, out_block, gu_block, down_block, gain_block)
    if fast:
        extra = (asked_here[:, None], sel_wide, table.T)
        *gathered, table_low, got = gather_all(blocks, WEIGHT_PIECES, 1, extra, slots)
        gathered = (gathered[:5], gathered[5:])
    else:
        table_low, rows = padded_table(asked_here, sel_wide, table.T)
        got = lax.all_to_all(rows.reshape(n, slots, wide), "fsdp", 0, 0)
        gathered = [lax.all_gather(block, BOTH, axis=0) for block in blocks]
        gathered = [[g[k * n : (k + 1) * n] for g in gathered] for k in range(sections)]
    qkv_all, out_all, gu_all, down_all, gain_all = [
        [section[k].reshape(n * blocks[k].shape[0], -1) for section in gathered] for k in range(5)
    ]
    gain_all = jnp.stack([g.reshape(n, 16, 128)[:, :3, :rp] for g in gain_all])
    gain_all = jnp.moveaxis(gain_all, 2, 1).reshape(sections, 3, wide).astype(jnp.float32)
    final_all = gain_all[0, 2]
    x0 = dense(onehot, got.reshape(n * slots, wide))

    def fetch_more(state):
        turn, total = state
        choose, more = lookup_round(ids, owner, rank, turn, slots, n, vshard)
        here = asked(lax.all_gather(more, BOTH, axis=0))
        here = lax.dynamic_index_in_dim(here, section_index, 0, keepdims=False).reshape(-1)
        rows = dense(jnp.take(table_low, jnp.maximum(here, 0), axis=0), sel_wide).astype(LOW)
        got = lax.all_to_all(rows.reshape(n, slots, wide), "fsdp", 0, 0).reshape(n * slots, wide)
        return (turn + 1, total + dense(choose, got))

    x0 = lax.while_loop(lambda state: state[0] < turns, fetch_more, (jnp.int32(1), x0))[1]

    everyone = jnp.arange(TOK_MB)
    cosine, sine = rotary_angles()
    x = x0
    kept = []
    for layer in range(sections - 1):
        scale_a = inverse_rms(x, width)
        a = (x * scale_a * gain_all[layer, 0]).astype(LOW)
        low, attended, top, share = attention(dense_tt(qkv_all[layer], a), cosine, sine)
        attended = dense_t(attended, sel).astype(LOW)
        mixed = x + dense(attended, out_all[layer])
        scale_b = inverse_rms(mixed, width)
        b = (mixed * scale_b * gain_all[layer, 1]).astype(LOW)
        branch, gate, upper, hidden = mlp(b, gu_all[layer], down_all[layer])
        kept.append((x, scale_a, a, low, top, share, attended, mixed, scale_b, b, gate, upper, hidden))
        x = mixed + branch

    last = sections - 1
    place = (PROMPT + CONT * jnp.arange(NCONT)[:, None] + scored[0]).reshape(-1)
    taken = place.shape[0]
    place = jnp.pad(place, (0, -taken % 128), constant_values=PROMPT)
    real = jnp.arange(place.shape[0]) < taken
    pick = ((place[:, None] == everyone[None, :]) & real[:, None]).astype(LOW)
    pick32 = pick.astype(jnp.float32)
    picking = (pick, jnp.stack([place, PROMPT + (place - PROMPT) // CONT * CONT]))
    scale_last = inverse_rms(x, width)
    a_last = (x * scale_last * gain_all[last, 0]).astype(LOW)
    low_last, attended_s, top_s, share_s, queries = attention(
        dense_tt(qkv_all[last], a_last), cosine, sine, picking
    )
    x_s = jnp.dot(pick32, x, precision=HI)
    attended_s = dense_t(attended_s, sel).astype(LOW)
    mixed_s = x_s + dense(attended_s, out_all[last])
    scale_s = inverse_rms(mixed_s, width)
    b_s = (mixed_s * scale_s * gain_all[last, 1]).astype(LOW)
    branch_s, gate_s, upper_s, hidden_s = mlp(b_s, gu_all[last], down_all[last])
    y_s = mixed_s + branch_s
    scale_y = inverse_rms(y_s, width)
    head_in = dense_nt((y_s * scale_y * final_all).astype(LOW), sel_wide).astype(LOW)[:taken]

    if fast:
        rows_all = gather_all([head_in], [(0, 16 * k, 16, k % 2) for k in range(4)], 2)[0]
    else:
        rows_all = lax.all_gather(head_in, BOTH, axis=0)
    rows_all = rows_all.reshape(-1, wide)
    own_rows = rows_all.shape[0] // sections
    wanted_here = wanted_rows - vstart
    logits, top_here, total_here, target_here = logits_of(wanted_here, rows_all, table_low)
    stats = jnp.concatenate([top_here + jnp.log(total_here), target_here])
    if fast:
        stats = exchange(stats.reshape(-1, 128), 3, whole=False).reshape(n, 2, -1)
    else:
        stats = lax.all_gather(stats, "fsdp", axis=0)
    top = jnp.max(stats[:, 0], axis=0)
    total = jnp.sum(jnp.exp(stats[:, 0] - top), axis=0)
    row_logp = jnp.sum(stats[:, 1], axis=0) - top - jnp.log(total)
    seq = jnp.sum(row_logp.reshape(-1, SCORED), axis=1)
    pair = pairs.reshape(-1, 2)
    conts = jnp.arange(seq.shape[0])
    chosen = (pair[:, 0][:, None] == conts[None, :]).astype(jnp.float32)
    passed = (pair[:, 1][:, None] == conts[None, :]).astype(jnp.float32)
    delta = jnp.sum((chosen - passed) * seq[None, :], axis=1)
    loss = jnp.sum(jax.nn.softplus(-BETA * delta))
    push = BETA * jax.nn.sigmoid(-BETA * delta)
    grad_seq = jnp.sum((passed - chosen) * push[:, None], axis=0)
    grad_row = jnp.repeat(grad_seq, SCORED)
    grad_logits, grad_rows = logits_back(
        section_index, wanted_here, top, grad_row / total, grad_row, logits, table_low, sections
    )
    if fast:
        grad_head = reduce_all([grad_rows], 4, 1, tile=16)[0]
    else:
        grad_head = lax.psum_scatter(grad_rows, BOTH, scatter_dimension=0, tiled=True)
    grad_head = jnp.pad(grad_head.astype(jnp.float32), ((0, place.shape[0] - taken), (0, 0)))
    grad_z = jnp.dot(grad_head, sel_wide.astype(jnp.float32), precision=HI)
    grad_y, grad_final = norm_back(y_s, scale_y, final_all, grad_z, width)

    grads = [None] * sections
    g_down, g_gu, grad_b = mlp_back(
        grad_y.astype(LOW), b_s, gate_s, upper_s, hidden_s, gu_all[last], down_all[last]
    )
    grad_mid, gain_two = norm_back(mixed_s, scale_s, gain_all[last, 1], grad_b, width)
    grad_mixed = grad_mid + grad_y
    branch = grad_mixed.astype(LOW)
    g_out = dense_t(attended_s, branch)
    grad_att = dense_nt(sel, dense_nt(branch, out_all[last]).astype(LOW)).astype(LOW)
    grad_qkv = attention_back(
        low_last, top_s, share_s, grad_att, cosine, sine, qkv_wide, picking + (queries,)
    )
    g_qkv = dense_tt(a_last, grad_qkv)
    grad_in, gain_one = norm_back(
        x, scale_last, gain_all[last, 0], dense_tt(grad_qkv, qkv_all[last]), width
    )
    upstream = grad_in + lax.dot_general(pick32, grad_mixed, (((0,), (0,)), ((), ())), precision=HI)
    grads[last] = (g_qkv, g_out, g_gu, g_down, jnp.stack([gain_one, gain_two]))

    for layer in range(sections - 2, -1, -1):
        (x, scale_a, a, low, top, share, attended, mixed, scale_b, b, gate, upper, hidden) = kept[layer]
        g_down, g_gu, grad_b = mlp_back(
            upstream.astype(LOW), b, gate, upper, hidden, gu_all[layer], down_all[layer]
        )
        grad_mid, gain_two = norm_back(mixed, scale_b, gain_all[layer, 1], grad_b, width)
        grad_mixed = grad_mid + upstream
        branch = grad_mixed.astype(LOW)
        g_out = dense_t(attended, branch)
        grad_att = dense_nt(sel, dense_nt(branch, out_all[layer]).astype(LOW)).astype(LOW)
        grad_qkv = attention_back(low, top, share, grad_att, cosine, sine, qkv_wide)
        g_qkv = dense_tt(a, grad_qkv)
        grad_in, gain_one = norm_back(
            x, scale_a, gain_all[layer, 0], dense_tt(grad_qkv, qkv_all[layer]), width
        )
        upstream = grad_in + grad_mixed
        grads[layer] = (g_qkv, g_out, g_gu, g_down, jnp.stack([gain_one, gain_two]))

    grad_x0 = dense_nt(upstream.astype(LOW), sel_wide).astype(LOW)

    def give(all_asked, choose):
        rows = dense_t(choose, grad_x0).astype(LOW)
        got = lax.all_to_all(rows.reshape(n, slots, wide), "fsdp", 0, 0)
        return (all_asked.reshape(-1), lax.all_gather(got, "section", axis=0).reshape(-1, wide))

    def give_more(state):
        turn, grad, squares = state
        choose, more = lookup_round(ids, owner, rank, turn, slots, n, vshard)
        places, got = give(asked(lax.all_gather(more, BOTH, axis=0)), choose)
        place_of = (jnp.arange(vshard)[:, None] == places[None, :]).astype(LOW)
        new = grad.astype(jnp.float32) + lax.dot_general(
            got[:, :width], place_of, (((0,), (1,)), ((), ())), preferred_element_type=jnp.float32
        )
        every = lax.psum(jnp.where(leader, jnp.sum(new**2), 0.0), BOTH) + jnp.sum(squares[:, 1, 0])
        return (turn + 1, new.astype(LOW), squares.at[:, 0].set(every / (sections * n)))

    def gain_rows(layer):
        rows = jnp.concatenate([grads[layer][4], grad_final[None]], axis=0).reshape(3, n, rp)
        rows = jnp.pad(jnp.moveaxis(rows, 0, 1), ((0, 0), (0, TILE_R - 3), (0, 128 - rp)))
        return rows.reshape(n * TILE_R, 128)

    outward = [
        [g.astype(LOW) for g in grads[layer][:4] + (gain_rows(layer),)] for layer in range(sections)
    ]
    if fast:
        rows = dense_t(onehot, grad_x0).astype(LOW).reshape(n, slots, wide)
        extra = (rows, asked_first.reshape(1, -1), rows_all, grad_logits)
        *summed, unused, got, grad_table, grad_squares = reduce_all(outward, 5, 2, extra=extra, width=width)
    else:
        summed = [
            lax.psum_scatter(
                jnp.concatenate(arrays, axis=0), BOTH, scatter_dimension=0, tiled=True
            ).astype(jnp.float32)
            for arrays in zip(*outward)
        ]
        got = give(asked_first, onehot)[1]
        grad_table, grad_squares = table_grad(
            leader.astype(jnp.float32),
            asked_first.reshape(-1),
            got.T,
            rows_all.T,
            grad_logits,
            summed,
            width,
        )
        grad_squares = lax.all_gather(grad_squares, BOTH, axis=0)
    if rdp != rd:
        summed[2] = summed[2].reshape(rp, 2, n, rdp)[:, :, :, :rd].reshape(rp, 2 * n * rd)
    grad_table, grad_squares = lax.while_loop(
        lambda state: state[0] < turns, give_more, (jnp.int32(1), grad_table, grad_squares)
    )[1:]

    def everyones(sums, name):
        if fast:
            return exchange(sums, name)
        return lax.all_gather(sums, BOTH, axis=0)

    grad_norm = jnp.sqrt(jnp.sum(grad_squares[:, 0, 0]))
    clip = jnp.minimum(1.0, CLIP / grad_norm)

    def views(arrays):
        out = [arrays[0].T] + [a.transpose(1, 0, 2) for a in arrays[1:4]]
        return out + [arrays[4][0], arrays[5][0], arrays[6][None]]

    weights_all = views((table, w_qkv, w_out, w_gu, w_down, gains, final_gain))
    grads_all = [grad_table] + summed[:4] + [summed[4][:2, :r], summed[4][2:3, :r]]
    new_firsts, new_seconds, updates, kept_weights, sums = moments(
        clip,
        sel,
        weights_all,
        grads_all,
        views((first_table, first_qkv, first_out, first_gu, first_down, first_gains, first_final)),
        views((second_table, second_qkv, second_out, second_gu, second_down, second_gains, second_final)),
        (DECAY,) * 5 + (0.0, 0.0),
    )
    sums = everyones(sums, 7)[:, :, 0].reshape(sections, n, 2, 8)
    sums = jnp.sum(sums, axis=1)
    layered = jnp.moveaxis(sums[:, :, 1:7], 1, 0).reshape(2, -1)
    matrix_norms = jnp.sqrt(jnp.concatenate([layered, sums[0, :, 0:1], sums[0, :, 7:8]], axis=1))
    trust_ratio = matrix_norms[0] / matrix_norms[1]
    own = lax.dynamic_slice_in_dim(trust_ratio, 6 * section_index, 6)
    last_two = trust_ratio[6 * sections :]
    new, half = apply_updates(
        jnp.concatenate([last_two[:1], own[:4]]),
        [weights_all[0], *kept_weights, weights_all[4]],
        updates[:5],
        [w.shape for w in weights_all[:5]],
    )
    new = list(new) + [
        weights_all[5] - RATE * own[4:6][:, None] * updates[5],
        weights_all[6] - RATE * last_two[1] * updates[6],
    ]

    def back(k, array):
        if k == 0:
            return array.T
        if k == 6:
            return array[0]
        return array.transpose(1, 0, 2) if array.ndim == 3 else array[None]

    outs = [loss, grad_norm, matrix_norms]
    for k in range(7):
        outs += [back(k, t[k]) for t in (new, new_firsts, new_seconds)]
    return tuple(outs + [back(k, half[k]) for k in range(5)])


def solution(mesh):
    tall, layered, gainy, flat = (
        P("fsdp", None),
        P("section", "fsdp", None),
        P("section", None, "fsdp"),
        P("fsdp"),
    )
    weights = (tall, layered, layered, layered, layered, gainy, flat)
    placed = (
        P("section", "fsdp"),
        P("section", "fsdp", None),
        P("section", None, None),
        P(),
    ) + weights * 3
    results = (P(), P(), P())
    for spec in weights:
        results += (spec, spec, spec)
    return jax.shard_map(
        shards, mesh=mesh, in_specs=placed, out_specs=results + weights[:5], check_vma=False
    )
```

```python
import functools

import jax
import jax.numpy as jnp
from jax import lax
from jax.experimental import pallas as pl
from jax.experimental.pallas import tpu as pltpu
from jax.sharding import PartitionSpec as P

HEADS = 15
KV = 5
HD = 64
FF = 2560
PROMPT = 256
NCONT = 2
CONT = 128
SCORED = 32
STEP = 10
TOK_MB = 512

EPS = 1e-05
SCALE = 0.125
THETA = 100000.0
BETA = 0.1
CLIP = 1.0
RATE = 0.3
BETA_ONE = 0.9
BETA_TWO = 0.99
ADAM_EPS = 1e-08
DECAY = 0.01

WIDTH = HEADS * HD
KVW = KV * HD
BOTH = ("section", "fsdp")
HI = lax.Precision.HIGHEST
LOW = jnp.bfloat16

WEIGHT_PIECES = [
    (0, 0, 64, 0),
    (1, 0, 64, 1),
    (2, 0, 16, 0),
    (2, 16, 16, 1),
    (2, 32, 16, 0),
    (2, 48, 16, 1),
    (3, 0, 80, 0),
    (3, 80, 80, 1),
    (4, 0, 16, 1),
]

MESH = pl.DeviceIdType.MESH
ANYWHERE = pl.BlockSpec(memory_space=pl.ANY)
IN_VMEM = pl.BlockSpec(memory_space=pltpu.VMEM)
TILE_R, TILE_C = 32, 1024


def coords():
    f = lax.axis_index("fsdp")
    return (lax.axis_index("section"), f // 4, f // 2 % 2, f % 2)


def device(y, z, x, c):
    return (y, z * 4 + x * 2 + c)


def greet(peers):
    barrier = pltpu.get_barrier_semaphore()
    for peer in peers:
        pl.semaphore_signal(barrier, inc=1, device_id=peer, device_id_type=MESH)
    pl.semaphore_wait(barrier, len(peers))


def send(src, dst, send_sem, recv_sem, peer):
    pltpu.make_async_remote_copy(
        src_ref=src,
        dst_ref=dst,
        send_sem=send_sem,
        recv_sem=recv_sem,
        device_id=peer,
        device_id_type=MESH,
    ).start()


def settle(ref, sem):
    pltpu.make_async_copy(ref, ref, sem).wait()


def gather_kernel(pieces, count, carried, *refs):
    y, f = (lax.axis_index("section"), lax.axis_index("fsdp"))
    z, x, c = coords()[1:]
    in_line = [((z + k) % 4) * 4 + x * 2 + c for k in range(1, 4)]
    near = [f + 2 - 4 * x, f + 1 - 2 * c]
    away = [(f + k) % 16 for k in range(1, 16)] if carried else in_line + near
    greet([device(1 - y, z, x, c)] + [(y, peer) for peer in away])
    if not carried:
        outs = [ref.at[pl.ds(section * 16, 16)] for section in range(2) for ref in refs[count : 2 * count]]

        def everything(section):
            for name, p in [("own", None)] + [("line", p) for p in range(len(pieces))] + [("rest", None)]:
                gather_section(section, pieces, (refs[:count], outs), refs[2 * count :], name, p)

        for section in range(2):
            pl.when(y == section)(functools.partial(everything, section))
        return
    moved = (refs[:count], refs[count + carried : 3 * count + carried])
    sems = refs[3 * count + carried + 2 :][:4]

    def phase(name, p=None):
        for section in range(2):
            pl.when(y == section)(functools.partial(gather_section, section, pieces, moved, sems, name, p))

    phase("own")
    asked, sel, table = refs[count : count + carried]
    low, got = refs[3 * count + carried : 3 * count + carried + 2]
    tiles, lows, total, rows, tile_sem, low_sem, carry_sem = refs[3 * count + carried + 6 :]
    width, tall = tiles.shape[1:]
    steps = table.shape[1] // tall
    columns = [pl.ds(i * tall, tall) for i in range(steps)]
    eye = lax.broadcasted_iota(jnp.int32, (tall, tall), 0) == lax.broadcasted_iota(jnp.int32, (tall, tall), 1)
    total[...] = jnp.zeros_like(total)
    lows[...] = jnp.zeros_like(lows)

    def tile_copy(i):
        return pltpu.make_async_copy(table.at[:, columns[i]], tiles.at[i % 2], tile_sem.at[i % 2])

    def low_copy(i):
        return pltpu.make_async_copy(lows.at[i % 2], low.at[columns[i]], low_sem.at[i % 2])

    def tile(i):
        if i + 1 < steps:
            tile_copy(i + 1).start()
        tile_copy(i).wait()
        if i >= 2:
            low_copy(i - 2).wait()
        lows[i % 2, :, pl.ds(0, width)] = dense_nt(eye.astype(LOW), tiles[i % 2].astype(LOW)).astype(LOW)
        place = lax.broadcasted_iota(jnp.int32, (asked.shape[0], tall), 1) + i * tall
        total[...] += dense((asked[...] == place).astype(LOW), lows[i % 2])
        low_copy(i).start()

    tile_copy(0).start()
    for p in range(len(pieces)):
        for i in (2 * p, 2 * p + 1):
            if i < steps:
                tile(i)
        if 2 * p + 2 == steps:
            rows[...] = dense(total[...].astype(LOW), sel[...]).astype(LOW).reshape(rows.shape)
            for k in range(1, 16):
                peer = (f + k) % 16
                send(rows.at[peer], got.at[f], carry_sem.at[0], carry_sem.at[1], (y, peer))
            pltpu.make_async_copy(rows.at[f], got.at[f], carry_sem.at[2]).start()
        phase("line", p)
    phase("rest")
    low_copy(steps - 2).wait()
    low_copy(steps - 1).wait()
    settle(rows.at[pl.ds(0, 15)], carry_sem.at[0])
    settle(rows.at[pl.ds(0, 15)], carry_sem.at[1])
    settle(rows.at[0], carry_sem.at[2])


def gather_section(y, pieces, moved, sems, name, number):
    blocks, outs = moved
    count = len(blocks)
    send_sem, recv_sem, sib_sem, own_sem = sems
    z, x, c = coords()[1:]
    to_x, to_y, to_sib = (device(y, z, 1 - x, c), device(1 - y, z, x, c), device(y, z, x, 1 - c))
    zs = [(z + k) % 4 for k in range(4)]

    def part(ref, p):
        return ref.at[pl.ds(pieces[p][1], pieces[p][2])]

    def there(p, o):
        return part(outs[o[0] * count + pieces[p][0]].at[o[1] * 4 + o[2] * 2 + c], p)

    def mark(p, o):
        return recv_sem.at[p, o[0] * 8 + o[1] * 2 + o[2]]

    def push(p, o, peer, own=False, sib=False):
        src = part(blocks[pieces[p][0]], p) if own else there(p, o)
        send(src, there(p, o), send_sem.at[p], sib_sem.at[p] if sib else mark(p, o), peer)

    every = range(len(pieces))
    for p in every if name == "own" else ():
        me = (y, z, x)
        push(p, me, to_x, own=True)
        push(p, me, to_y, own=True)
        for zz in zs[1:]:
            push(p, me, device(y, zz, x, c), own=True)
        push(p, me, to_sib, own=True, sib=True)
        pltpu.make_async_copy(part(blocks[pieces[p][0]], p), there(p, me), own_sem).start()
    def from_x(p, zz):
        o = (y, zz, 1 - x)
        settle(there(p, o), mark(p, o))
        if pieces[p][3] == 0:
            push(p, o, to_y)
        push(p, o, to_sib, sib=True)

    def from_y(p, zz):
        o = (1 - y, zz, x)
        settle(there(p, o), mark(p, o))
        if pieces[p][3] == 1:
            push(p, o, to_x)
        push(p, o, to_sib, sib=True)

    if name == "line":
        p = number
        for zz in zs[1:]:
            o = (y, zz, x)
            settle(there(p, o), mark(p, o))
            push(p, o, to_x)
            push(p, o, to_y)
            push(p, o, to_sib, sib=True)
        from_x(p, z)
        from_y(p, z)
    if name != "rest":
        return
    for p in every:
        for zz in zs[1:]:
            from_x(p, zz)
            from_y(p, zz)
    for p in every:
        for zz in zs:
            o = (1 - y, zz, 1 - x)
            settle(there(p, o), mark(p, o))
            push(p, o, to_sib, sib=True)
    for p in every:
        a, start, rows_each, unused = pieces[p]
        settle(part(blocks[a], p), own_sem)
        for times in (16, 15):
            settle(outs[a].at[pl.ds(0, times), pl.ds(start, rows_each)], send_sem.at[p])
        settle(outs[a].at[pl.ds(0, 16), pl.ds(start, rows_each)], sib_sem.at[p])


def gather_all(blocks, pieces, name, extra=(), slots=0):
    many = len(pieces)
    shapes = [jax.ShapeDtypeStruct((16 if extra else 32,) + b.shape, b.dtype) for b in blocks]
    shapes = shapes * 2 if extra else shapes
    scratch = [
        pltpu.SemaphoreType.DMA((many,)),
        pltpu.SemaphoreType.DMA((many, 16)),
        pltpu.SemaphoreType.DMA((many,)),
        pltpu.SemaphoreType.DMA,
    ]
    if extra:
        (deep, wide), (width, height) = (extra[1].shape, extra[2].shape)
        shapes += [jax.ShapeDtypeStruct((height, deep), LOW), jax.ShapeDtypeStruct((16, slots, wide), LOW)]
        tall = tall_of(height)
        scratch += [
            pltpu.VMEM((2, width, tall), jnp.float32),
            pltpu.VMEM((2, tall, deep), LOW),
            pltpu.VMEM((16 * slots, deep), jnp.float32),
            pltpu.VMEM((16, slots, wide), LOW),
            pltpu.SemaphoreType.DMA((2,)),
            pltpu.SemaphoreType.DMA((2,)),
            pltpu.SemaphoreType.DMA((3,)),
        ]
    return pl.pallas_call(
        functools.partial(gather_kernel, pieces, len(blocks), len(extra)),
        out_shape=shapes,
        in_specs=[ANYWHERE] * len(blocks) + [IN_VMEM, IN_VMEM, ANYWHERE][: len(extra)],
        out_specs=[ANYWHERE] * len(shapes),
        scratch_shapes=scratch,
        compiler_params=pltpu.CompilerParams(
            collective_id=name, has_side_effects=True, vmem_limit_bytes=32 * 2**20 if extra else None
        ),
    )(*blocks, *extra)


def reduce_pieces(shapes, tile):
    out = []
    for a, (rows, cols) in enumerate(shapes):
        for row in range(0, rows, tile):
            for col in range(0, cols, TILE_C):
                out.append((a, row, col, min(TILE_C, cols - col)))
    return out


RING = 8


def reduce_kernel(pieces, tile, count, carried, lag, *refs):
    many = len(pieces)
    ring = min(RING, many)
    if carried:
        grads = (refs[:count], refs[count : 2 * count])
    else:
        grads = [[ref.at[section] for ref in refs[:count]] for section in range(2)]
    at = 2 * count + carried if carried else count
    outs = refs[at : at + count]
    at += count
    if carried:
        rows, asked, head_rows_all, grad_logits = refs[2 * count : 2 * count + carried]
        theirs, got, grad_table, sums = refs[at : at + 4]
        at += 4
    held, from_one, from_two, from_z, mine, other = refs[at : at + 6]
    sib_recv, sib_send, recv_one, send_one, recv_two, send_two, recv_z, send_z, own_sem, other_sem = refs[
        at + 6 : at + 16
    ]
    if not carried:
        theirs = other
    y, z, x, c = coords()
    to_x, to_y, to_sib = (device(y, z, 1 - x, c), device(1 - y, z, x, c), device(y, z, x, 1 - c))
    zs = [(z + k) % 4 for k in range(4)]
    f = lax.axis_index("fsdp")
    me = y * 16 + f
    alike = [(y, (f + k) % 16) for k in range(1, 16)]
    others = [(1 - y, (f + k) % 16) for k in range(16)]
    near = [to_x, to_y, to_sib] + [device(y, zz, x, c) for zz in zs[1:]]
    greet(alike + others if carried else near)

    def source(p, yo, xo, core):
        a, row, col, cols = pieces[p]
        return grads[yo][a].at[:, xo, core, pl.ds(row, tile), pl.ds(col, cols)]

    def cut(ref, p):
        cols = pieces[p][3]
        return ref if cols == TILE_C else ref.at[..., pl.ds(0, cols)]

    def fetch(p):
        for yo in range(2):
            for xo in range(2):
                pltpu.make_async_copy(
                    source(p, yo, xo, c), cut(mine.at[p % 2, yo, xo], p), own_sem.at[p % 2]
                ).start()

    def fetch_other(p):
        settle(cut(theirs.at[p], p), sib_recv.at[p])
        if carried:
            pltpu.make_async_copy(cut(theirs.at[p], p), cut(other.at[p % 2], p), other_sem.at[p % 2]).start()

    for p in range(many):
        for yo in range(2):
            for xo in range(2):
                send(
                    source(p, yo, xo, 1 - c),
                    cut(theirs.at[p, yo, xo], p),
                    sib_send.at[p],
                    sib_recv.at[p],
                    to_sib,
                )
        if p == 0:
            fetch(0)

    def store_sum(dst, left, right, p):
        cols = pl.ds(0, pieces[p][3])
        dst[:, cols] = (left[:, cols].astype(jnp.float32) + right[:, cols].astype(jnp.float32)).astype(LOW)

    def settle_sends(p):
        settle(cut(from_one.at[p], p), send_one.at[p])
        settle(cut(from_two.at[p], p), send_two.at[p])
        settle(cut(from_z.at[p], p), send_z.at[p])

    def two_cores(p):
        if p == 0:
            fetch_other(0)
        if p + 1 < many:
            fetch(p + 1)
            fetch_other(p + 1)
        if p >= ring:
            settle_sends(p - ring)
        settle(cut(mine.at[p % 2], p), own_sem.at[p % 2])
        if carried:
            settle(cut(other.at[p % 2], p), other_sem.at[p % 2])
        right, left, here = (other.at[p % 2] if carried else theirs.at[p], mine.at[p % 2], held.at[p % ring])

        def each(i, carry):
            where = (i // 8, i // 4 % 2, i % 4)
            store_sum(here.at[where], left.at[where], right.at[where], p)
            return carry

        lax.fori_loop(0, 16, each, 0)
        if p % 2 == 0:
            send(cut(here.at[1 - y], p), cut(from_one.at[p], p), send_one.at[p], recv_one.at[p], to_y)
        else:
            for yo in range(2):
                send(
                    cut(here.at[yo, 1 - x], p),
                    cut(from_one.at[p, yo], p),
                    send_one.at[p],
                    recv_one.at[p],
                    to_x,
                )

    def first_axis(p):
        settle(cut(from_one.at[p], p), recv_one.at[p])
        here = held.at[p % ring]

        def each(i, carry):
            where = (y, i // 4, i % 4) if p % 2 == 0 else (i // 4, x, i % 4)
            store_sum(here.at[where], here.at[where], from_one.at[p, i // 4, i % 4], p)
            return carry

        lax.fori_loop(0, 8, each, 0)
        src, peer = (here.at[y, 1 - x], to_x) if p % 2 == 0 else (here.at[1 - y, x], to_y)
        send(cut(src, p), cut(from_two.at[p], p), send_two.at[p], recv_two.at[p], peer)

    def second_axis(p):
        settle(cut(from_two.at[p], p), recv_two.at[p])
        here = held.at[p % ring, y, x]

        def each(i, carry):
            store_sum(here.at[i], here.at[i], from_two.at[p, i], p)
            return carry

        lax.fori_loop(0, 4, each, 0)
        for k in range(1, 4):
            send(
                cut(here.at[zs[k]], p),
                cut(from_z.at[p, 3 - k], p),
                send_z.at[p],
                recv_z.at[p],
                device(y, zs[k], x, c),
            )

    def along_z(p):
        settle(cut(from_z.at[p], p), recv_z.at[p])
        a, row, col, cols = pieces[p]
        part = pl.ds(0, cols)
        total = held[p % ring, y, x, z, :, part].astype(jnp.float32)
        for k in range(3):
            total = total + from_z[p, k, :, part].astype(jnp.float32)
        outs[a][pl.ds(row, tile), pl.ds(col, cols)] = total

    between = [()] * (many + 3 * lag)
    if carried:
        natural, turned_rows, turned_got, tiles, made, squares, carry_sem, tile_sem, made_sem, sum_sem = refs[
            at + 16 :
        ]
        between = carried_work(
            (me, y, f, to_y, alike, others),
            (rows, asked, head_rows_all, grad_logits, got, grad_table, sums, outs),
            (natural, turned_rows, turned_got, tiles, made, squares),
            (carry_sem, tile_sem, made_sem, sum_sem),
            many + 3 * lag,
        )
    for step in range(many + 3 * lag):
        for work in between[step]:
            work()
        for k, stage in enumerate((two_cores, first_axis, second_axis, along_z)):
            if 0 <= step - k * lag < many:
                stage(step - k * lag)
    for p in range(many):
        settle(cut(theirs.at[p], p), sib_send.at[p])
        if p >= many - ring:
            settle_sends(p)
    if carried:
        between[-1]()


def carried_work(where, arrays, buffers, sems, steps):
    me, y, f, to_y, alike, others = where
    rows, asked, head_rows_all, grad_logits, got, grad_table, sums, outs = arrays
    natural, turned_rows, turned_got, tiles, made, squares = buffers
    carry_sem, tile_sem, made_sem, sum_sem = sems
    height, count = grad_logits.shape
    width = grad_table.shape[0]
    slots = rows.shape[1]
    wide = rows.shape[2]
    tall = tiles.shape[1]
    turns = height // tall
    leader = jnp.where(y == 0, 1.0, 0.0)
    eye = lax.broadcasted_iota(jnp.int32, (tall, tall), 0) == lax.broadcasted_iota(jnp.int32, (tall, tall), 1)

    def turn(source, target):
        for k in range(wide // tall):
            part = pl.ds(k * tall, tall)
            target[part] = dense_nt(eye.astype(LOW), source[:, part]).astype(LOW)

    def start():
        for peer in alike:
            send(rows.at[peer[1]], got.at[me], carry_sem.at[0], carry_sem.at[1], peer)
        pltpu.make_async_copy(rows.at[f], got.at[me], carry_sem.at[2]).start()
        pltpu.make_async_copy(head_rows_all, natural.at[pl.ds(0, count)], carry_sem.at[5]).start()

    def turn_rows():
        settle(natural.at[pl.ds(0, count)], carry_sem.at[5])
        turn(natural.at[pl.ds(0, count)], turned_rows)

    def pass_on():
        settle(rows.at[pl.ds(0, 15)], carry_sem.at[1])
        settle(rows.at[0], carry_sem.at[2])
        ours = got.at[pl.ds(y * 16, 16)]
        send(ours, ours, carry_sem.at[3], carry_sem.at[4], to_y)

    def load_got():
        settle(rows, carry_sem.at[4])
        for k in range(32):
            pltpu.make_async_copy(got.at[k], natural.at[pl.ds(k * slots, slots)], carry_sem.at[5]).start()
        tile_copy(0).start()

    def turn_got():
        settle(natural.at[pl.ds(0, 32 * slots)], carry_sem.at[5])
        turn(natural.at[pl.ds(0, 32 * slots)], turned_got)
        squares[...] = jnp.zeros_like(squares)

    def tile_copy(i):
        return pltpu.make_async_copy(grad_logits.at[pl.ds(i * tall, tall)], tiles.at[i % 2], tile_sem.at[i % 2])

    def made_copy(i):
        return pltpu.make_async_copy(made.at[i % 2], grad_table.at[:, pl.ds(i * tall, tall)], made_sem.at[i % 2])

    def table_tile(i):
        if i + 1 < turns:
            tile_copy(i + 1).start()
        tile_copy(i).wait()
        if i >= 2:
            made_copy(i - 2).wait()
        place = lax.broadcasted_iota(jnp.int32, (tall, asked.shape[1]), 0) + i * tall
        here = dense_nt(turned_rows[...], tiles[i % 2]) + dense_nt(
            turned_got[...], (asked[...] == place).astype(LOW)
        )
        here = here[:width]
        made[i % 2] = here.astype(LOW)
        squares[pl.ds(0, 1)] += leader * squares_of(here)
        made_copy(i).start()

    def end():
        gains = outs[-1][...]
        layers = squares_of(gains[:2]) + leader * squares_of(gains[2:3])
        for out in outs[:-1]:
            layers += squares_of(out[...])
        squares[pl.ds(0, 1)] += layers
        squares[pl.ds(1, 1)] += layers
        for peer in alike + others:
            send(squares, sums.at[me], sum_sem.at[0], sum_sem.at[1], peer)
        sums[me] = squares[...]
        made_copy(turns - 2).wait()
        made_copy(turns - 1).wait()
        settle(rows.at[pl.ds(0, 15)], carry_sem.at[0])
        settle(rows, carry_sem.at[3])
        settle(sums.at[pl.ds(0, 31)], sum_sem.at[0])
        settle(sums.at[pl.ds(0, 31)], sum_sem.at[1])

    plan = [[] for unused in range(steps)]
    plan[0].append(start)
    plan[3].append(turn_rows)
    plan[6].append(pass_on)
    plan[10].append(load_got)
    plan[11].append(turn_got)
    for i in range(turns):
        plan[12 + i * (steps - 16) // turns].append(functools.partial(table_tile, i))
    return plan + [end]


def reduce_all(grads, name, lag, tile=TILE_R, extra=(), width=0):
    first = grads[0] if extra else grads
    count = len(first)
    shapes = [(g.shape[0] // (16 if extra else 32), g.shape[1]) for g in first]
    pieces = reduce_pieces(shapes, tile)
    many = len(pieces)
    if extra:
        views = [g.reshape(4, 2, 2, g.shape[0] // 16, g.shape[1]) for layer in grads for g in layer]
    else:
        views = [g.reshape(2, 4, 2, 2, *s) for g, s in zip(grads, shapes)]
    results = [jax.ShapeDtypeStruct(s, jnp.float32) for s in shapes]
    piece = (2, 2, 4, tile, TILE_C)
    scratch = [
        pltpu.VMEM((min(RING, many),) + piece, LOW),
        pltpu.VMEM((many, 2, 4, tile, TILE_C), LOW),
        pltpu.VMEM((many, 4, tile, TILE_C), LOW),
        pltpu.VMEM((many, 3, tile, TILE_C), LOW),
        pltpu.VMEM((2,) + piece, LOW),
        pltpu.VMEM((2 if extra else many,) + piece, LOW),
    ]
    scratch += [pltpu.SemaphoreType.DMA((many,)) for unused in range(8)]
    scratch += [pltpu.SemaphoreType.DMA((2,)), pltpu.SemaphoreType.DMA((2,))]
    in_specs, out_specs = ([ANYWHERE] * len(views), [IN_VMEM] * count)
    if extra:
        rows, asked, scored_rows, grad_logits = extra
        slots, wide = rows.shape[1:]
        height, total = grad_logits.shape
        tall = tall_of(height)
        results += [
            jax.ShapeDtypeStruct((many,) + piece, LOW),
            jax.ShapeDtypeStruct((32, slots, wide), LOW),
            jax.ShapeDtypeStruct((width, height), LOW),
            jax.ShapeDtypeStruct((32, 8, 128), jnp.float32),
        ]
        in_specs += [ANYWHERE, IN_VMEM, ANYWHERE, ANYWHERE]
        out_specs += [ANYWHERE] * 3 + [IN_VMEM]
        scratch += [
            pltpu.VMEM((max(total, 32 * slots), wide), LOW),
            pltpu.VMEM((wide, total), LOW),
            pltpu.VMEM((wide, 32 * slots), LOW),
            pltpu.VMEM((2, tall, total), LOW),
            pltpu.VMEM((2, width, tall), LOW),
            pltpu.VMEM((8, 128), jnp.float32),
            pltpu.SemaphoreType.DMA((6,)),
            pltpu.SemaphoreType.DMA((2,)),
            pltpu.SemaphoreType.DMA((2,)),
            pltpu.SemaphoreType.DMA((2,)),
        ]
    return pl.pallas_call(
        functools.partial(reduce_kernel, pieces, tile, count, len(extra), lag),
        out_shape=results,
        in_specs=in_specs,
        out_specs=out_specs,
        scratch_shapes=scratch,
        compiler_params=pltpu.CompilerParams(
            collective_id=name, has_side_effects=True, vmem_limit_bytes=(60 if extra else 32) * 2**20
        ),
    )(*views, *extra)


def exchange_kernel(whole, src, out, send_sem, recv_sem, own_sem):
    y, f = (lax.axis_index("section"), lax.axis_index("fsdp"))
    count = 32 if whole else 16
    me = y * 16 + f if whole else f
    peers = [(me + k) % count for k in range(1, count)]
    where = [(p // 16, p % 16) if whole else (y, p) for p in peers]
    greet(where)
    for peer in where:
        send(src, out.at[me], send_sem, recv_sem, peer)
    own = pltpu.make_async_copy(src, out.at[me], own_sem)
    own.start()
    own.wait()
    settle(out.at[pl.ds(0, count - 1)], send_sem)
    settle(out.at[pl.ds(0, count - 1)], recv_sem)


def exchange(small, name, whole=True):
    return pl.pallas_call(
        functools.partial(exchange_kernel, whole),
        out_shape=jax.ShapeDtypeStruct((32 if whole else 16,) + small.shape, small.dtype),
        in_specs=[IN_VMEM],
        out_specs=IN_VMEM,
        scratch_shapes=[pltpu.SemaphoreType.DMA] * 3,
        compiler_params=pltpu.CompilerParams(collective_id=name, has_side_effects=True),
    )(small)


def tall_of(height, sections=2, most=256):
    while height % (most * sections):
        most //= 2
    return most


def whole(shape):
    return pl.BlockSpec(shape, lambda *unused: (0,) * len(shape), pipeline_mode=pl.Buffered(1))


def striped(tall, cols):
    return pl.BlockSpec((tall, cols), lambda i: (i, 0))


def lined(rows, wide):
    return pl.BlockSpec((rows, wide), lambda i: (0, i))


def squares_of(value):
    return jnp.sum(jnp.sum(value * value, axis=1, keepdims=True), axis=0, keepdims=True)


def padded_table_kernel(asked, sel, table, low, rows, total):
    step = pl.program_id(0)

    @pl.when(step == 0)
    def start():
        total[...] = jnp.zeros_like(total)

    width, tall = table.shape
    low[:, pl.ds(low.shape[1] - 128, 128)] = jnp.zeros((tall, 128), LOW)
    eye = lax.broadcasted_iota(jnp.int32, (tall, tall), 0) == lax.broadcasted_iota(jnp.int32, (tall, tall), 1)
    low[:, pl.ds(0, width)] = dense_nt(eye.astype(LOW), table[...].astype(LOW)).astype(LOW)
    place = lax.broadcasted_iota(jnp.int32, (asked.shape[0], tall), 1) + step * tall
    total[...] += dense((asked[...] == place).astype(LOW), low[...])

    @pl.when(step == pl.num_programs(0) - 1)
    def end():
        rows[...] = dense(total[...].astype(LOW), sel[...]).astype(LOW)


def padded_table(asked, sel, table):
    width, height = table.shape
    wide = sel.shape[0]
    count = asked.shape[0]
    tall = tall_of(height)
    return pl.pallas_call(
        padded_table_kernel,
        grid=(height // tall,),
        out_shape=[
            jax.ShapeDtypeStruct((height, wide), LOW),
            jax.ShapeDtypeStruct((count, sel.shape[1]), LOW),
        ],
        in_specs=[whole((count, 1)), whole(sel.shape), lined(width, tall)],
        out_specs=[striped(tall, wide), whole((count, sel.shape[1]))],
        scratch_shapes=[pltpu.VMEM((count, wide), jnp.float32)],
        compiler_params=pltpu.CompilerParams(vmem_limit_bytes=48 * 2**20),
    )(asked[:, None], sel, table)


def logits_kernel(wanted, rows, table, logits, top, total, target):
    step = pl.program_id(0)

    @pl.when(step == 0)
    def start():
        top[...] = jnp.full_like(top, -jnp.inf)
        total[...] = jnp.zeros_like(total)
        target[...] = jnp.zeros_like(target)

    here = dense_nt(table[...], rows[...])
    logits[...] = here
    higher = jnp.maximum(top[...], jnp.max(here, axis=0, keepdims=True))
    total[...] = total[...] * jnp.exp(top[...] - higher) + jnp.sum(
        jnp.exp(here - higher), axis=0, keepdims=True
    )
    top[...] = higher
    place = lax.broadcasted_iota(jnp.int32, here.shape, 0) + step * here.shape[0]
    target[...] += jnp.sum(jnp.where(place == wanted[...], here, 0.0), axis=0, keepdims=True)


def logits_of(wanted, rows, table):
    height, wide = table.shape
    count = rows.shape[0]
    tall = tall_of(height, most=512 if count <= 2048 else 256)
    line = jax.ShapeDtypeStruct((1, count), jnp.float32)
    return pl.pallas_call(
        logits_kernel,
        grid=(height // tall,),
        out_shape=[jax.ShapeDtypeStruct((height, count), jnp.float32), line, line, line],
        in_specs=[whole((1, count)), whole(rows.shape), striped(tall, wide)],
        out_specs=[striped(tall, count)] + [whole((1, count))] * 3,
        compiler_params=pltpu.CompilerParams(vmem_limit_bytes=48 * 2**20),
    )(wanted[None], rows, table)


def logits_back_kernel(share, section, wanted, top, scale, push, logits, table, grad, rows, total):
    step = pl.program_id(1)
    mine = (step >= section[0] * share) & (step < (section[0] + 1) * share)

    @pl.when(step == 0)
    def start():
        total[...] = jnp.zeros_like(total)

    here = logits[...]
    place = lax.broadcasted_iota(jnp.int32, here.shape, 0) + step * here.shape[0]
    hit = jnp.where(place == wanted[...], push[...], 0.0)
    low = (hit - jnp.exp(here - top[...]) * scale[...]).astype(LOW)
    grad[...] = low

    @pl.when(mine)
    def add():
        total[...] += dense_t(low, table[...])

    @pl.when(step == pl.num_programs(1) - 1)
    def end():
        rows[...] = total[...].astype(LOW)


def logits_back(section, wanted, top, scale, push, logits, table, sections):
    height, wide = table.shape
    count = logits.shape[1]
    tall = tall_of(height, sections, 512)
    block = min(count, 2048)
    line = pl.BlockSpec((1, block), lambda j, i: (0, j))
    tile = pl.BlockSpec((tall, block), lambda j, i: (i, j))
    return pl.pallas_call(
        functools.partial(logits_back_kernel, height // tall // sections),
        grid=(count // block, height // tall),
        out_shape=[
            jax.ShapeDtypeStruct((height, count), LOW),
            jax.ShapeDtypeStruct((count, wide), LOW),
        ],
        in_specs=[
            pl.BlockSpec(memory_space=pltpu.SMEM),
            line,
            line,
            line,
            line,
            tile,
            pl.BlockSpec((tall, wide), lambda j, i: (i, 0)),
        ],
        out_specs=[tile, pl.BlockSpec((block, wide), lambda j, i: (j, 0))],
        scratch_shapes=[pltpu.VMEM((block, wide), jnp.float32)],
        compiler_params=pltpu.CompilerParams(vmem_limit_bytes=56 * 2**20),
    )(section[None], wanted[None], top[None], scale[None], push[None], logits, table)


def table_grad_kernel(leader, asked, got, rows, grad_logits, *refs):
    *others, grad, squares = refs
    step = pl.program_id(0)

    @pl.when(step == 0)
    def start():
        gains = others[-1][...]
        total = squares_of(gains[:2]) + leader[0] * squares_of(gains[2:3])
        for other in others[:-1]:
            total += squares_of(other[...])
        squares[...] = jnp.broadcast_to(total, squares.shape)

    width, tall = grad.shape
    place = lax.broadcasted_iota(jnp.int32, (tall, asked.shape[1]), 0) + step * tall
    here = dense_nt(rows[...], grad_logits[...]) + dense_nt(got[...], (asked[...] == place).astype(LOW))
    here = here[:width]
    grad[...] = here.astype(LOW)
    squares[pl.ds(0, 1)] += leader[0] * squares_of(here)


def table_grad(leader, asked, got, rows, grad_logits, others, width):
    height, count = grad_logits.shape
    tall = tall_of(height)
    return pl.pallas_call(
        table_grad_kernel,
        grid=(height // tall,),
        out_shape=[
            jax.ShapeDtypeStruct((width, height), LOW),
            jax.ShapeDtypeStruct((8, 128), jnp.float32),
        ],
        in_specs=[
            pl.BlockSpec(memory_space=pltpu.SMEM),
            whole((1, asked.shape[0])),
            whole(got.shape),
            whole(rows.shape),
            striped(tall, count),
        ]
        + [whole(o.shape) for o in others],
        out_specs=[lined(width, tall), whole((8, 128))],
        compiler_params=pltpu.CompilerParams(vmem_limit_bytes=56 * 2**20),
    )(leader[None], asked[None], got, rows, grad_logits, *others)


def exact_product(left, onehot):
    high = left.astype(LOW)
    rest = left - high.astype(jnp.float32)
    middle = rest.astype(LOW)
    lowest = (rest - middle.astype(jnp.float32)).astype(LOW)
    return dense_nt(high, onehot) + (dense_nt(middle, onehot) + dense_nt(lowest, onehot))


ROWED = 3
BAND = 160
SPREAD = (1, 3)


def moments_kernel(decays, clip, sel, *refs):
    weights, grads, firsts, seconds = (refs[7 * k : 7 * k + 7] for k in range(4))
    new_firsts, new_seconds, updates = (refs[28 + 7 * k : 35 + 7 * k] for k in range(3))
    kept, sums, *scratch = refs[49:49 + ROWED] , refs[49 + ROWED], *refs[50 + ROWED:]
    staged = [scratch[5 * k : 5 * k + 5] for k in range(ROWED)]
    in_sem, out_sem = scratch[5 * ROWED :]
    step, steps = (pl.program_id(0), pl.num_programs(0))

    def copies(k, inward):
        w, m, v, new_m, new_v = staged[k]
        if inward:
            pairs = [(weights[k + 1].at[:, 0], w), (firsts[k + 1].at[:, 0], m), (seconds[k + 1].at[:, 0], v)]
        else:
            pairs = [(new_m, new_firsts[k + 1].at[:, 0]), (new_v, new_seconds[k + 1].at[:, 0])]
        return [
            pltpu.make_async_copy(src, dst, (in_sem if inward else out_sem).at[k, i])
            for i, (src, dst) in enumerate(pairs)
        ]

    @pl.when(step == 0)
    def start():
        sums[...] = jnp.zeros_like(sums)
        for k in range(ROWED):
            for copy in copies(k, True):
                copy.start()

    def one(weight, grad, first, second, decay):
        return (weight,) + lamb_parts(weight, clip[0] * grad.astype(jnp.float32), first, second, decay)

    weight, new_firsts[0][...], new_seconds[0][...], update = one(
        weights[0][...], grads[0][...], firsts[0][...], seconds[0][...], decays[0]
    )
    updates[0][...] = update.astype(LOW)
    sums[pl.ds(0, 1)] += squares_of(weight)
    sums[pl.ds(8, 1)] += squares_of(update)

    def tensor(k):
        rows, cols = updates[k + 1].shape
        grad = grads[k + 1][pl.ds(0, rows)]
        grad = exact_product(grad, sel[...]) if k in SPREAD else grad[:, :cols]
        if k < ROWED:
            for copy in copies(k, True):
                copy.wait()
            w, m, v, new_m, new_v = staged[k]
        else:
            w, m, v, new_m, new_v = (t[k + 1] for t in (weights, firsts, seconds, new_firsts, new_seconds))
        weight, new_m[...], new_v[...], update = one(w[...], grad, m[...], v[...], decays[k + 1])
        updates[k + 1][...] = update
        if k < ROWED:
            kept[k][...] = weight
            for copy in copies(k, False):
                copy.start()
        for row in range(rows if k == 4 else 1):
            part = slice(row, row + 1) if k == 4 else slice(None)
            line = k + 1 + row + (k > 4)
            sums[pl.ds(line, 1)] += squares_of(weight[part])
            sums[pl.ds(8 + line, 1)] += squares_of(update[part])

    for k in range(6):
        pl.when(step == (steps // 2 + k if k < ROWED else k - 2) % steps)(functools.partial(tensor, k))

    @pl.when(step == steps - 1)
    def end():
        for k in range(ROWED):
            for copy in copies(k, False):
                copy.wait()


def moments(clip, sel, weights, grads, firsts, seconds, decays):
    width, height = weights[0].shape
    band = pl.BlockSpec((BAND, height), lambda i: (i, 0))
    flat = [w.shape if w.ndim == 2 else w.shape[::2] for w in weights]

    def specs(arrays, results=False):
        out = [band]
        for a in arrays[1:]:
            out.append(ANYWHERE if a.ndim == 3 else whole(a.shape))
        return out

    line = [jax.ShapeDtypeStruct(w.shape, jnp.float32) for w in weights]
    plain = [jax.ShapeDtypeStruct(s, jnp.float32 if k else LOW) for k, s in enumerate(flat)]
    kept = plain[1 : 1 + ROWED]
    out = pl.pallas_call(
        functools.partial(moments_kernel, decays),
        grid=(width // BAND,),
        out_shape=line * 2 + plain + kept + [jax.ShapeDtypeStruct((16, 128), jnp.float32)],
        in_specs=[pl.BlockSpec(memory_space=pltpu.SMEM), whole(sel.shape)]
        + specs(weights)
        + specs(grads)
        + specs(firsts)
        + specs(seconds),
        out_specs=specs(line) * 2 + specs(plain) + [whole(s.shape) for s in kept] + [whole((16, 128))],
        scratch_shapes=[pltpu.VMEM(s.shape, jnp.float32) for s in kept for unused in range(5)]
        + [pltpu.SemaphoreType.DMA((ROWED, 3)), pltpu.SemaphoreType.DMA((ROWED, 2))],
        compiler_params=pltpu.CompilerParams(vmem_limit_bytes=60 * 2**20),
    )(clip[None], sel, *weights, *grads, *firsts, *seconds)
    return (out[:7], out[7:14], out[14:21], out[21 : 21 + ROWED], out[21 + ROWED])


def apply_kernel(scales, *refs):
    weights, updates, new, half = (refs[5 * k : 5 * k + 5] for k in range(4))
    staged, sem = (refs[20 : 20 + ROWED], refs[20 + ROWED])
    step, steps = (pl.program_id(0), pl.num_programs(0))

    def copy(k):
        return pltpu.make_async_copy(staged[k - 1], new[k].at[:, 0], sem.at[k - 1])

    def one(k):
        value = weights[k][...] - RATE * scales[k] * updates[k][...]
        half[k][...] = value.astype(LOW)
        if 0 < k <= ROWED:
            staged[k - 1][...] = value
            copy(k).start()
        else:
            new[k][...] = value

    one(0)
    for k in range(1, 5):
        pl.when(step == (k - 1) % steps)(functools.partial(one, k))

    @pl.when(step == steps - 1)
    def end():
        for k in range(1, 1 + ROWED):
            copy(k).wait()


def apply_updates(scales, weights, updates, shapes):
    width, height = weights[0].shape
    plain = [pl.BlockSpec((BAND, height), lambda i: (i, 0))] + [whole(w.shape) for w in weights[1:]]
    out = pl.pallas_call(
        apply_kernel,
        grid=(width // BAND,),
        out_shape=[jax.ShapeDtypeStruct(s, jnp.float32) for s in shapes]
        + [jax.ShapeDtypeStruct(w.shape, LOW) for w in weights],
        in_specs=[pl.BlockSpec(memory_space=pltpu.SMEM)] + plain * 2,
        out_specs=plain[:1] + [ANYWHERE] * ROWED + plain[1 + ROWED :] + plain,
        scratch_shapes=[pltpu.VMEM(w.shape, jnp.float32) for w in weights[1 : 1 + ROWED]]
        + [pltpu.SemaphoreType.DMA((ROWED,))],
        compiler_params=pltpu.CompilerParams(vmem_limit_bytes=56 * 2**20),
    )(scales, *weights, *updates)
    return (out[:5], out[5:])


EACH = HEADS // KV


def turned(x, cosine, sine):
    half = HD // 2
    u, w = (x[:half], x[half:])
    return jnp.concatenate([u * cosine - w * sine, w * cosine + u * sine], axis=0)


def query_blocks(scored):
    if scored:
        return [(0, scored, ((0, TOK_MB),))]
    out = [(0, PROMPT, ((0, PROMPT),))]
    for j in range(NCONT):
        first = PROMPT + j * CONT
        out.append((first, CONT, ((0, PROMPT), (first, CONT))))
    return out


def masks(place):
    out = []
    for first, count, ranges in query_blocks(0 if place is None else place.shape[1]):
        keys = sum(r[1] for r in ranges)
        row = lax.broadcasted_iota(jnp.int32, (keys, count), 0)
        if place is not None:
            at = place[pl.ds(0, 1)]
            seen = (row < PROMPT) | ((row >= place[pl.ds(1, 1)]) & (row <= at))
        else:
            seen = row - (keys - count) <= lax.broadcasted_iota(jnp.int32, (keys, count), 1)
        out.append(jnp.concatenate([jnp.where(seen, 0.0, -1e30)] * EACH, axis=1))
    return out


def rows_of(ranges, array):
    parts = [array[first : first + count] for first, count in ranges]
    return parts[0] if len(parts) == 1 else jnp.concatenate(parts, axis=0)


def head_rows(start):
    return pl.ds(pl.multiple_of(start, HD), HD)


def side_by_side(ref, group, first, count):
    return jnp.concatenate(
        [ref[head_rows((group * EACH + j) * HD), pl.ds(first, count)] for j in range(EACH)], axis=1
    )


def attend_kernel(scored, qkv, cosine, sine, *refs):
    pick, place = refs[:2] if scored else (None, None)
    low, out, top, share, *queries = refs[2:] if scored else refs
    queries = queries[0] if scored else low
    cos, sin = (cosine[...], sine[...])
    added = masks(place)

    def group_of(group, carry):
        key = turned(qkv[head_rows(WIDTH + group * HD)], cos, sin)
        low[head_rows(WIDTH + group * HD)] = key.astype(LOW)
        value = qkv[head_rows(WIDTH + KVW + group * HD)].astype(LOW)
        low[head_rows(WIDTH + KVW + group * HD)] = value
        for j in range(EACH):
            place_of = head_rows((group * EACH + j) * HD)
            query = turned(qkv[place_of], cos, sin).astype(LOW)
            low[place_of] = query
            if scored:
                queries[place_of] = dense_nt(query, pick[...]).astype(LOW)
        keys = key.T.astype(LOW)
        for (first, count, ranges), extra in zip(query_blocks(scored), added):
            query = side_by_side(queries, group, first, count)
            scores = dense(rows_of(ranges, keys), query) * SCALE + extra
            high = jnp.max(scores, axis=0, keepdims=True)
            expo = jnp.exp(scores - high)
            part = 1.0 / jnp.sum(expo, axis=0, keepdims=True)
            probs = (expo * part).astype(LOW)
            got, at = (0.0, 0)
            for start, length in ranges:
                got += dense(value[:, start : start + length], probs[at : at + length])
                at += length
            for j in range(EACH):
                column = slice(j * count, (j + 1) * count)
                out[head_rows((group * EACH + j) * HD), pl.ds(first, count)] = got[:, column].astype(LOW)
                top[group, j : j + 1, pl.ds(first, count)] = high[:, column]
                share[group, j : j + 1, pl.ds(first, count)] = part[:, column]
        return carry

    lax.fori_loop(0, KV, group_of, 0)


def attention(qkv, cosine, sine, chosen=()):
    tokens = qkv.shape[1]
    scored = chosen[0].shape[0] if chosen else 0
    count = scored or tokens
    stat = jax.ShapeDtypeStruct((KV, EACH, count), jnp.float32)
    heads = jax.ShapeDtypeStruct((WIDTH, count), LOW)
    results = [jax.ShapeDtypeStruct((WIDTH + 2 * KVW, tokens), LOW), heads, stat, stat]
    results += [heads] if scored else []
    return pl.pallas_call(
        functools.partial(attend_kernel, scored),
        out_shape=results,
        in_specs=[IN_VMEM] * (3 + len(chosen)),
        out_specs=[IN_VMEM] * len(results),
        compiler_params=pltpu.CompilerParams(vmem_limit_bytes=40 * 2**20),
    )(qkv, cosine, sine, *chosen)


def attend_back_kernel(scored, low, top, share, grad, cosine, sine, *refs):
    pick, place, queries = refs[:3] if scored else (None, None, low)
    out, key_sum, value_sum = refs[-3:]
    cos, sin = (cosine[...], sine[...])
    added = masks(place)
    spare = out.shape[0] - WIDTH - 2 * KVW
    out[pl.ds(WIDTH + 2 * KVW, spare)] = jnp.zeros((spare, out.shape[1]), LOW)

    def group_of(group, carry):
        key = low[head_rows(WIDTH + group * HD)]
        value = low[head_rows(WIDTH + KVW + group * HD)]
        keys = key.astype(jnp.float32).T.astype(LOW)
        values = value.astype(jnp.float32).T.astype(LOW)
        for number, ((first, count, ranges), extra) in enumerate(zip(query_blocks(scored), added)):
            sides = range(EACH)
            columns = pl.ds(first, count)
            query = side_by_side(queries, group, first, count)
            upstream = side_by_side(grad, group, first, count)
            high = jnp.concatenate([top[group, j : j + 1, columns] for j in sides], axis=1)
            part = jnp.concatenate([share[group, j : j + 1, columns] for j in sides], axis=1)
            scores = dense(rows_of(ranges, keys), query) * SCALE + extra
            probs = jnp.exp(scores - high) * part
            grad_probs = dense(rows_of(ranges, values), upstream)
            inner = jnp.sum(grad_probs * probs, axis=0, keepdims=True)
            grad_scores = (probs * (grad_probs - inner)).astype(LOW)
            probs = probs.astype(LOW)
            got, at = (0.0, 0)
            for start, length in ranges:
                piece = slice(at, at + length)
                got += dense(key[:, start : start + length], grad_scores[piece])
                here = pl.ds(start, length)
                more_key = dense_nt(query, grad_scores[piece])
                more_value = dense_nt(upstream, probs[piece])
                if number == 0 or start > 0:
                    key_sum[:, here] = more_key
                    value_sum[:, here] = more_value
                else:
                    key_sum[:, here] += more_key
                    value_sum[:, here] += more_value
                at += length
            for j in sides:
                turn = got[:, j * count : (j + 1) * count] * SCALE
                where = head_rows((group * EACH + j) * HD)
                if scored:
                    high_part = turn.astype(LOW)
                    rest = (turn - high_part.astype(jnp.float32)).astype(LOW)
                    turn = dense(high_part, pick[...]) + dense(rest, pick[...])
                    out[where] = turned(turn, cos, -sin).astype(LOW)
                else:
                    past = slice(first, first + count)
                    out[where, columns] = turned(turn, cos[:, past], -sin[:, past]).astype(LOW)
        out[head_rows(WIDTH + group * HD)] = turned(key_sum[...] * SCALE, cos, -sin).astype(LOW)
        out[head_rows(WIDTH + KVW + group * HD)] = value_sum[...].astype(LOW)
        return carry

    lax.fori_loop(0, KV, group_of, 0)


def attention_back(low, top, share, grad, cosine, sine, wide, chosen=()):
    tokens = low.shape[1]
    return pl.pallas_call(
        functools.partial(attend_back_kernel, chosen[0].shape[0] if chosen else 0),
        out_shape=jax.ShapeDtypeStruct((wide, tokens), LOW),
        in_specs=[IN_VMEM] * (6 + len(chosen)),
        out_specs=IN_VMEM,
        scratch_shapes=[pltpu.VMEM((HD, tokens), jnp.float32)] * 2,
        compiler_params=pltpu.CompilerParams(vmem_limit_bytes=48 * 2**20),
    )(low, top, share, grad, cosine, sine, *chosen)


def up16(count):
    return -(-count // 16) * 16


def dense(left, right):
    return jnp.dot(left, right, preferred_element_type=jnp.float32)


def dense_t(left, right):
    return lax.dot_general(
        left, right, (((0,), (0,)), ((), ())), preferred_element_type=jnp.float32
    )


def dense_nt(left, right):
    return lax.dot_general(
        left, right, (((1,), (1,)), ((), ())), preferred_element_type=jnp.float32
    )


def spread_matrix(parts, real, padded):
    feature = jnp.arange(parts * real)
    place = feature // real * padded + feature % real
    return (place[:, None] == jnp.arange(parts * padded)[None, :]).astype(LOW)


def inverse_rms(x, width):
    return lax.rsqrt(jnp.sum(x * x, axis=-1, keepdims=True) / width + EPS)


def norm_back(x, scale, gain, upstream, width):
    inner = upstream * gain
    grad_gain = jnp.sum(upstream * x * scale, axis=0)
    mean = jnp.sum(inner * x, axis=-1, keepdims=True) / width
    return (scale * inner - x * scale**3 * mean, grad_gain)


def rotary_angles():
    place = jnp.arange(TOK_MB)
    rotary = jnp.where(place >= PROMPT, PROMPT + (place - PROMPT) % CONT, place).astype(jnp.float32)
    freq = THETA ** (-2.0 * jnp.arange(HD // 2).astype(jnp.float32) / HD)
    angle = freq[:, None] * rotary[None, :]
    return (jnp.cos(angle), jnp.sin(angle))


def dense_tt(left, right):
    return lax.dot_general(
        left, right, (((0,), (1,)), ((), ())), preferred_element_type=jnp.float32
    )


def mlp(b, w_gu, w_down):
    gate_up = dense(b, w_gu)
    half = gate_up.shape[1] // 2
    gate, upper = (gate_up[:, :half], gate_up[:, half:])
    hidden = (jax.nn.silu(gate) * upper).astype(LOW)
    return (dense(hidden, w_down), gate, upper, hidden)


def mlp_back(branch, b, gate, upper, hidden, w_gu, w_down):
    grad_down = dense_t(hidden, branch)
    grad_hidden = dense_nt(branch, w_down)
    sig = jax.nn.sigmoid(gate)
    grad_gate = grad_hidden * upper * sig * (1.0 + gate * (1.0 - sig))
    grad_upper = grad_hidden * gate * sig
    grad_gate_up = jnp.concatenate([grad_gate, grad_upper], axis=1).astype(LOW)
    return (grad_down, dense_t(b, grad_gate_up), dense_nt(grad_gate_up, w_gu))


def lamb_parts(weight, grad, first, second, decay):
    first_new = BETA_ONE * first + (1.0 - BETA_ONE) * grad
    second_new = BETA_TWO * second + (1.0 - BETA_TWO) * grad * grad
    root = (1.0 - BETA_TWO**STEP) ** 0.5
    scale = root / (1.0 - BETA_ONE**STEP)
    update = first_new * scale / (second_new * lax.rsqrt(second_new) + ADAM_EPS * root) + decay * weight
    return (first_new, second_new, update)


def lookup_ranks(ids, vshard):
    place = jnp.arange(ids.shape[0])
    same = ids[:, None] == ids[None, :]
    first = jnp.min(jnp.where(same, place[None, :], ids.shape[0]), axis=1)
    owner = ids // vshard
    before = (
        (owner[:, None] == owner[None, :])
        & (first == place)[None, :]
        & (place[None, :] < first[:, None])
    )
    return (owner, jnp.sum(before.astype(jnp.int32), axis=1))


def lookup_round(ids, owner, rank, turn, slots, parts, vshard):
    slot = jnp.where(rank // slots == turn, owner * slots + rank - turn * slots, -1)
    onehot = slot[:, None] == jnp.arange(parts * slots)[None, :]
    wanted = jnp.max(jnp.where(onehot, (ids - owner * vshard)[:, None], -1), axis=0)
    return (onehot.astype(LOW), wanted)


def shards(
    token_ids,
    scored,
    targets,
    pairs,
    table,
    w_qkv,
    w_out,
    w_gu,
    w_down,
    gains,
    final_gain,
    first_table,
    first_qkv,
    first_out,
    first_gu,
    first_down,
    first_gains,
    first_final,
    second_table,
    second_qkv,
    second_out,
    second_gu,
    second_down,
    second_gains,
    second_final,
):
    n = lax.axis_size("fsdp")
    sections = lax.axis_size("section")
    section_index = lax.axis_index("section")
    fsdp_index = lax.axis_index("fsdp")
    leader = section_index == 0
    vshard, width = table.shape
    vstart = fsdp_index * vshard
    r = w_qkv.shape[1]
    rp = up16(r)
    rd = w_down.shape[1]
    rdp = up16(rd)
    wide = n * rp
    ffp = n * rdp
    slots = up16(768 // n)
    sel = spread_matrix(n, r, rp)
    sel_wide = jnp.pad(sel, ((0, wide - width), (0, 0)))
    fast = (sections, n) == (2, 16)
    qkv_wide = -(-w_qkv.shape[2] // 128) * 128

    qkv_block = jnp.pad(
        w_qkv[0].astype(LOW), ((0, rp - r), (0, qkv_wide - w_qkv.shape[2]))
    )
    out_block = jnp.pad(dense(w_out[0].astype(LOW), sel).astype(LOW), ((0, rp - r), (0, 0)))
    gu_block = w_gu[0].astype(LOW)
    if rdp != rd:
        gu_block = jnp.pad(gu_block.reshape(r, 2, n, rd), ((0, 0), (0, 0), (0, 0), (0, rdp - rd)))
    gu_block = jnp.pad(gu_block.reshape(r, 2 * ffp), ((0, rp - r), (0, 0)))
    down_block = jnp.pad(dense(w_down[0].astype(LOW), sel).astype(LOW), ((0, rdp - rd), (0, 0)))
    gain_block = jnp.pad(
        jnp.concatenate([gains[0], final_gain[None]], axis=0).astype(LOW),
        ((0, 13), (0, 128 - r)),
    )

    ids = token_ids[0]
    owner, rank = lookup_ranks(ids, vshard)
    onehot, wanted = lookup_round(ids, owner, rank, 0, slots, n, vshard)
    turns_here = jnp.max(rank) // slots + 1
    own_targets = lax.dynamic_slice_in_dim(targets[0], fsdp_index * NCONT, NCONT).reshape(-1)
    note = jnp.concatenate(
        [wanted, jnp.pad(own_targets, (0, 128 - NCONT * SCORED)), jnp.full((128,), turns_here, jnp.int32)]
    )
    if fast:
        notes = exchange(note.reshape(-1, 128), 0).reshape(sections * n, -1)
    else:
        notes = lax.all_gather(note, BOTH, axis=0)
    turns = jnp.max(notes[:, -1])
    wanted_rows = notes[:, n * slots : n * slots + NCONT * SCORED].reshape(-1)

    def asked(all_wanted):
        mine = lax.dynamic_slice_in_dim(all_wanted.reshape(sections, n, n, slots), fsdp_index, 1, 2)
        return mine[:, :, 0]

    asked_first = asked(notes[:, : n * slots])
    asked_here = lax.dynamic_index_in_dim(asked_first, section_index, 0, keepdims=False).reshape(-1)
    blocks = (qkv_block, out_block, gu_block, down_block, gain_block)
    if fast:
        extra = (asked_here[:, None], sel_wide, table.T)
        *gathered, table_low, got = gather_all(blocks, WEIGHT_PIECES, 1, extra, slots)
        gathered = (gathered[:5], gathered[5:])
    else:
        table_low, rows = padded_table(asked_here, sel_wide, table.T)
        got = lax.all_to_all(rows.reshape(n, slots, wide), "fsdp", 0, 0)
        gathered = [lax.all_gather(block, BOTH, axis=0) for block in blocks]
        gathered = [[g[k * n : (k + 1) * n] for g in gathered] for k in range(sections)]
    qkv_all, out_all, gu_all, down_all, gain_all = [
        [section[k].reshape(n * blocks[k].shape[0], -1) for section in gathered] for k in range(5)
    ]
    gain_all = jnp.stack([g.reshape(n, 16, 128)[:, :3, :rp] for g in gain_all])
    gain_all = jnp.moveaxis(gain_all, 2, 1).reshape(sections, 3, wide).astype(jnp.float32)
    final_all = gain_all[0, 2]
    x0 = dense(onehot, got.reshape(n * slots, wide))

    def fetch_more(state):
        turn, total = state
        choose, more = lookup_round(ids, owner, rank, turn, slots, n, vshard)
        here = asked(lax.all_gather(more, BOTH, axis=0))
        here = lax.dynamic_index_in_dim(here, section_index, 0, keepdims=False).reshape(-1)
        rows = dense(jnp.take(table_low, jnp.maximum(here, 0), axis=0), sel_wide).astype(LOW)
        got = lax.all_to_all(rows.reshape(n, slots, wide), "fsdp", 0, 0).reshape(n * slots, wide)
        return (turn + 1, total + dense(choose, got))

    x0 = lax.while_loop(lambda state: state[0] < turns, fetch_more, (jnp.int32(1), x0))[1]

    everyone = jnp.arange(TOK_MB)
    cosine, sine = rotary_angles()
    x = x0
    kept = []
    for layer in range(sections - 1):
        scale_a = inverse_rms(x, width)
        a = (x * scale_a * gain_all[layer, 0]).astype(LOW)
        low, attended, top, share = attention(dense_tt(qkv_all[layer], a), cosine, sine)
        attended = dense_t(attended, sel).astype(LOW)
        mixed = x + dense(attended, out_all[layer])
        scale_b = inverse_rms(mixed, width)
        b = (mixed * scale_b * gain_all[layer, 1]).astype(LOW)
        branch, gate, upper, hidden = mlp(b, gu_all[layer], down_all[layer])
        kept.append((x, scale_a, a, low, top, share, attended, mixed, scale_b, b, gate, upper, hidden))
        x = mixed + branch

    last = sections - 1
    place = (PROMPT + CONT * jnp.arange(NCONT)[:, None] + scored[0]).reshape(-1)
    taken = place.shape[0]
    place = jnp.pad(place, (0, -taken % 128), constant_values=PROMPT)
    real = jnp.arange(place.shape[0]) < taken
    pick = ((place[:, None] == everyone[None, :]) & real[:, None]).astype(LOW)
    pick32 = pick.astype(jnp.float32)
    picking = (pick, jnp.stack([place, PROMPT + (place - PROMPT) // CONT * CONT]))
    scale_last = inverse_rms(x, width)
    a_last = (x * scale_last * gain_all[last, 0]).astype(LOW)
    low_last, attended_s, top_s, share_s, queries = attention(
        dense_tt(qkv_all[last], a_last), cosine, sine, picking
    )
    x_s = jnp.dot(pick32, x, precision=HI)
    attended_s = dense_t(attended_s, sel).astype(LOW)
    mixed_s = x_s + dense(attended_s, out_all[last])
    scale_s = inverse_rms(mixed_s, width)
    b_s = (mixed_s * scale_s * gain_all[last, 1]).astype(LOW)
    branch_s, gate_s, upper_s, hidden_s = mlp(b_s, gu_all[last], down_all[last])
    y_s = mixed_s + branch_s
    scale_y = inverse_rms(y_s, width)
    head_in = dense_nt((y_s * scale_y * final_all).astype(LOW), sel_wide).astype(LOW)[:taken]

    if fast:
        rows_all = gather_all([head_in], [(0, 16 * k, 16, k % 2) for k in range(4)], 2)[0]
    else:
        rows_all = lax.all_gather(head_in, BOTH, axis=0)
    rows_all = rows_all.reshape(-1, wide)
    own_rows = rows_all.shape[0] // sections
    wanted_here = wanted_rows - vstart
    logits, top_here, total_here, target_here = logits_of(wanted_here, rows_all, table_low)
    stats = jnp.concatenate([top_here + jnp.log(total_here), target_here])
    if fast:
        stats = exchange(stats.reshape(-1, 128), 3, whole=False).reshape(n, 2, -1)
    else:
        stats = lax.all_gather(stats, "fsdp", axis=0)
    top = jnp.max(stats[:, 0], axis=0)
    total = jnp.sum(jnp.exp(stats[:, 0] - top), axis=0)
    row_logp = jnp.sum(stats[:, 1], axis=0) - top - jnp.log(total)
    seq = jnp.sum(row_logp.reshape(-1, SCORED), axis=1)
    pair = pairs.reshape(-1, 2)
    conts = jnp.arange(seq.shape[0])
    chosen = (pair[:, 0][:, None] == conts[None, :]).astype(jnp.float32)
    passed = (pair[:, 1][:, None] == conts[None, :]).astype(jnp.float32)
    delta = jnp.sum((chosen - passed) * seq[None, :], axis=1)
    loss = jnp.sum(jax.nn.softplus(-BETA * delta))
    push = BETA * jax.nn.sigmoid(-BETA * delta)
    grad_seq = jnp.sum((passed - chosen) * push[:, None], axis=0)
    grad_row = jnp.repeat(grad_seq, SCORED)
    grad_logits, grad_rows = logits_back(
        section_index, wanted_here, top, grad_row / total, grad_row, logits, table_low, sections
    )
    if fast:
        grad_head = reduce_all([grad_rows], 4, 2, tile=16)[0]
    else:
        grad_head = lax.psum_scatter(grad_rows, BOTH, scatter_dimension=0, tiled=True)
    grad_head = jnp.pad(grad_head.astype(jnp.float32), ((0, place.shape[0] - taken), (0, 0)))
    grad_z = jnp.dot(grad_head, sel_wide.astype(jnp.float32), precision=HI)
    grad_y, grad_final = norm_back(y_s, scale_y, final_all, grad_z, width)

    grads = [None] * sections
    g_down, g_gu, grad_b = mlp_back(
        grad_y.astype(LOW), b_s, gate_s, upper_s, hidden_s, gu_all[last], down_all[last]
    )
    grad_mid, gain_two = norm_back(mixed_s, scale_s, gain_all[last, 1], grad_b, width)
    grad_mixed = grad_mid + grad_y
    branch = grad_mixed.astype(LOW)
    g_out = dense_t(attended_s, branch)
    grad_att = dense_nt(sel, dense_nt(branch, out_all[last]).astype(LOW)).astype(LOW)
    grad_qkv = attention_back(
        low_last, top_s, share_s, grad_att, cosine, sine, qkv_wide, picking + (queries,)
    )
    g_qkv = dense_tt(a_last, grad_qkv)
    grad_in, gain_one = norm_back(
        x, scale_last, gain_all[last, 0], dense_tt(grad_qkv, qkv_all[last]), width
    )
    upstream = grad_in + lax.dot_general(pick32, grad_mixed, (((0,), (0,)), ((), ())), precision=HI)
    grads[last] = (g_qkv, g_out, g_gu, g_down, jnp.stack([gain_one, gain_two]))

    for layer in range(sections - 2, -1, -1):
        (x, scale_a, a, low, top, share, attended, mixed, scale_b, b, gate, upper, hidden) = kept[layer]
        g_down, g_gu, grad_b = mlp_back(
            upstream.astype(LOW), b, gate, upper, hidden, gu_all[layer], down_all[layer]
        )
        grad_mid, gain_two = norm_back(mixed, scale_b, gain_all[layer, 1], grad_b, width)
        grad_mixed = grad_mid + upstream
        branch = grad_mixed.astype(LOW)
        g_out = dense_t(attended, branch)
        grad_att = dense_nt(sel, dense_nt(branch, out_all[layer]).astype(LOW)).astype(LOW)
        grad_qkv = attention_back(low, top, share, grad_att, cosine, sine, qkv_wide)
        g_qkv = dense_tt(a, grad_qkv)
        grad_in, gain_one = norm_back(
            x, scale_a, gain_all[layer, 0], dense_tt(grad_qkv, qkv_all[layer]), width
        )
        upstream = grad_in + grad_mixed
        grads[layer] = (g_qkv, g_out, g_gu, g_down, jnp.stack([gain_one, gain_two]))

    grad_x0 = dense_nt(upstream.astype(LOW), sel_wide).astype(LOW)

    def give(all_asked, choose):
        rows = dense_t(choose, grad_x0).astype(LOW)
        got = lax.all_to_all(rows.reshape(n, slots, wide), "fsdp", 0, 0)
        return (all_asked.reshape(-1), lax.all_gather(got, "section", axis=0).reshape(-1, wide))

    def give_more(state):
        turn, grad, squares = state
        choose, more = lookup_round(ids, owner, rank, turn, slots, n, vshard)
        places, got = give(asked(lax.all_gather(more, BOTH, axis=0)), choose)
        place_of = (jnp.arange(vshard)[:, None] == places[None, :]).astype(LOW)
        new = grad.astype(jnp.float32) + lax.dot_general(
            got[:, :width], place_of, (((0,), (1,)), ((), ())), preferred_element_type=jnp.float32
        )
        every = lax.psum(jnp.where(leader, jnp.sum(new**2), 0.0), BOTH) + jnp.sum(squares[:, 1, 0])
        return (turn + 1, new.astype(LOW), squares.at[:, 0].set(every / (sections * n)))

    def gain_rows(layer):
        rows = jnp.concatenate([grads[layer][4], grad_final[None]], axis=0).reshape(3, n, rp)
        rows = jnp.pad(jnp.moveaxis(rows, 0, 1), ((0, 0), (0, TILE_R - 3), (0, 128 - rp)))
        return rows.reshape(n * TILE_R, 128)

    outward = [
        [g.astype(LOW) for g in grads[layer][:4] + (gain_rows(layer),)] for layer in range(sections)
    ]
    if fast:
        rows = dense_t(onehot, grad_x0).astype(LOW).reshape(n, slots, wide)
        extra = (rows, asked_first.reshape(1, -1), rows_all, grad_logits)
        *summed, unused, got, grad_table, grad_squares = reduce_all(outward, 5, 2, extra=extra, width=width)
    else:
        summed = [
            lax.psum_scatter(
                jnp.concatenate(arrays, axis=0), BOTH, scatter_dimension=0, tiled=True
            ).astype(jnp.float32)
            for arrays in zip(*outward)
        ]
        got = give(asked_first, onehot)[1]
        grad_table, grad_squares = table_grad(
            leader.astype(jnp.float32),
            asked_first.reshape(-1),
            got.T,
            rows_all.T,
            grad_logits,
            summed,
            width,
        )
        grad_squares = lax.all_gather(grad_squares, BOTH, axis=0)
    if rdp != rd:
        summed[2] = summed[2].reshape(rp, 2, n, rdp)[:, :, :, :rd].reshape(rp, 2 * n * rd)
    grad_table, grad_squares = lax.while_loop(
        lambda state: state[0] < turns, give_more, (jnp.int32(1), grad_table, grad_squares)
    )[1:]

    def everyones(sums, name):
        if fast:
            return exchange(sums, name)
        return lax.all_gather(sums, BOTH, axis=0)

    grad_norm = jnp.sqrt(jnp.sum(grad_squares[:, 0, 0]))
    clip = jnp.minimum(1.0, CLIP / grad_norm)

    def views(arrays):
        out = [arrays[0].T] + [a.transpose(1, 0, 2) for a in arrays[1:4]]
        return out + [arrays[4][0], arrays[5][0], arrays[6][None]]

    weights_all = views((table, w_qkv, w_out, w_gu, w_down, gains, final_gain))
    grads_all = [grad_table] + summed[:4] + [summed[4][:2, :r], summed[4][2:3, :r]]
    new_firsts, new_seconds, updates, kept_weights, sums = moments(
        clip,
        sel,
        weights_all,
        grads_all,
        views((first_table, first_qkv, first_out, first_gu, first_down, first_gains, first_final)),
        views((second_table, second_qkv, second_out, second_gu, second_down, second_gains, second_final)),
        (DECAY,) * 5 + (0.0, 0.0),
    )
    sums = everyones(sums, 7)[:, :, 0].reshape(sections, n, 2, 8)
    sums = jnp.sum(sums, axis=1)
    layered = jnp.moveaxis(sums[:, :, 1:7], 1, 0).reshape(2, -1)
    matrix_norms = jnp.sqrt(jnp.concatenate([layered, sums[0, :, 0:1], sums[0, :, 7:8]], axis=1))
    trust_ratio = matrix_norms[0] / matrix_norms[1]
    own = lax.dynamic_slice_in_dim(trust_ratio, 6 * section_index, 6)
    last_two = trust_ratio[6 * sections :]
    new, half = apply_updates(
        jnp.concatenate([last_two[:1], own[:4]]),
        [weights_all[0], *kept_weights, weights_all[4]],
        updates[:5],
        [w.shape for w in weights_all[:5]],
    )
    new = list(new) + [
        weights_all[5] - RATE * own[4:6][:, None] * updates[5],
        weights_all[6] - RATE * last_two[1] * updates[6],
    ]

    def back(k, array):
        if k == 0:
            return array.T
        if k == 6:
            return array[0]
        return array.transpose(1, 0, 2) if array.ndim == 3 else array[None]

    outs = [loss, grad_norm, matrix_norms]
    for k in range(7):
        outs += [back(k, t[k]) for t in (new, new_firsts, new_seconds)]
    return tuple(outs + [back(k, half[k]) for k in range(5)])


def solution(mesh):
    tall, layered, gainy, flat = (
        P("fsdp", None),
        P("section", "fsdp", None),
        P("section", None, "fsdp"),
        P("fsdp"),
    )
    weights = (tall, layered, layered, layered, layered, gainy, flat)
    placed = (
        P("section", "fsdp"),
        P("section", "fsdp", None),
        P("section", None, None),
        P(),
    ) + weights * 3
    results = (P(), P(), P())
    for spec in weights:
        results += (spec, spec, spec)
    return jax.shard_map(
        shards, mesh=mesh, in_specs=placed, out_specs=results + weights[:5], check_vma=False
    )
```
